256 devices in a mesh: blk: 32 (over z, y_lo, core), pw: 8 (over y_hi, x).
Axes of the slice: x: 4, y: 4 (y_hi: 2, y_lo: 2; y = y_hi * 2 + y_lo), z: 8, core: 2. Of those that a mesh axis runs over, the one named last changes fastest.
Arguments:
- occupied_states: bfloat16 [2, 128, 72, 10368], P(None, 'blk', 'pw'), may hold values from -0.025512695 to 0.025512695
- empty_states: bfloat16 [2, 256, 72, 10368], P(None, 'blk', 'pw'), may hold values from -0.025512695 to 0.025512695
- occ_energy: bfloat16 [128], P('blk'), may hold values from -2 to -0.099609375
- empty_energy: bfloat16 [256], P('blk'), may hold values from 0.099609375 to 2
- gvectors: int32 [3, 4096], replicated, may hold values from -16 to 16
Outputs:
- response: float32 [4096, 2, 4096], P('blk', None, 'pw')
The draws below stay inside these ranges and needn't reach their ends.
Inputs may be any that keep to these rules, and one draw needn't show every extreme that they name: `gvectors`: each plane wave's three components lie within 16 of zero.
All inputs are finite; a program needn't handle non-finite values.
Results may differ from the reference program's by a relative error of at most 0.011.
Values may be sent and summed in bfloat16 or wider, within the bound.
A program may use at most 192 MiB of HBM per device.

```python
import math
import jax
import jax.numpy as jnp
from jax import lax

GX = 72
GY = 72
GZ = 144
KMAX = 16
NG = 4096
NV_DEV = 4
NC_DEV = 8
NV = 128
NC = 256
N_BLK = 32


def touch_ends(drawn, key, low, largest):
    longest = drawn.shape.index(max(drawn.shape))
    spots = []
    for shift in (0, 1):
        where = [jax.random.randint(jax.random.fold_in(key, axis), (), 0, length) for axis, length in enumerate(drawn.shape)]
        where[longest] = (where[longest] + shift) % drawn.shape[longest]
        spots.append(tuple(where))
    return drawn.at[spots[0]].set(low).at[spots[1]].set(largest)


def steps_of(key, dims, cuts, smallest, largest):
    gain, own = 1.0, jax.random.fold_in(key, 6)
    for position, blocks in cuts:
        draws = jnp.exp(jax.random.uniform(jax.random.fold_in(own, position), (blocks,), jnp.float32, smallest / len(cuts), largest / len(cuts)))
        gain = gain * jnp.repeat(draws, dims[position] // blocks).reshape([-1 if axis == position else 1 for axis in range(len(dims))])
    return gain


def bell_draw(stream_key, dims, scale, reach, cuts=(), kind=jnp.bfloat16):
    drawn = scale * jax.random.normal(stream_key, dims, jnp.float32)
    if cuts:
        drawn = drawn * steps_of(stream_key, dims, cuts, -0.22, 0.18)
    return jnp.clip(drawn, -reach, reach).astype(kind)


def setup_inputs(seed: int = 0) -> dict:
    arg_keys = jax.random.split(jax.random.key(seed), 6)
    occupied_states = bell_draw(arg_keys[0], (2, NV, GX, GY * GZ), ((4 * NV_DEV * N_BLK * NC_DEV * GX * GY * GZ) ** -0.25), 0.025512695, ((1, 32), (2, 8)))
    empty_states = bell_draw(arg_keys[1], (2, NC, GX, GY * GZ), ((4 * NV_DEV * N_BLK * NC_DEV * GX * GY * GZ) ** -0.25), 0.025512695, ((1, 32), (2, 8)))
    occ_energy = jnp.clip(-2.0 + 1.9003906 * jax.random.uniform(arg_keys[2], (NV,), jnp.float32) ** steps_of(arg_keys[2], (NV,), ((0, 32),), -0.2, 0.2), -2.0, -0.099609375).astype(jnp.bfloat16)
    empty_energy = jnp.clip(0.099609375 + 1.9003906 * jax.random.uniform(arg_keys[3], (NC,), jnp.float32) ** steps_of(arg_keys[3], (NC,), ((0, 32),), -0.2, 0.2), 0.099609375, 2.0).astype(jnp.bfloat16)
    gvectors = touch_ends(jax.random.randint(arg_keys[4], (3, NG), -KMAX, KMAX + 1), jax.random.fold_in(arg_keys[4], 1), -KMAX, KMAX).astype(jnp.int32)
    return dict(occupied_states=occupied_states, empty_states=empty_states, occ_energy=occ_energy, empty_energy=empty_energy, gvectors=gvectors)


omega_shift = 0.5


def axis_tables(length, count_half):
    grid_steps = jnp.arange(length, dtype=jnp.int32)
    values = jnp.arange(2 * count_half + 1, dtype=jnp.int32) - count_half
    phase_steps = (grid_steps[:, None] * values[None, :]) % length
    angles = phase_steps.astype(jnp.float32) * (2.0 * math.pi / length)
    return jnp.cos(angles).astype(jnp.bfloat16), jnp.sin(angles).astype(jnp.bfloat16)


def depth_table():
    cosines, sine_table = axis_tables(GZ, KMAX)
    upper = jnp.concatenate([cosines, -sine_table], axis=1)
    lower = jnp.concatenate([sine_table, cosines], axis=1)
    return jnp.concatenate([upper, lower], axis=0)


def row_table():
    cosines, sine_table = axis_tables(GY, KMAX)
    from_real = jnp.stack([cosines, -sine_table], axis=1)
    from_imag = jnp.stack([sine_table, cosines], axis=1)
    return jnp.stack([from_real, from_imag], axis=0)


def pair_planes(occ_state, partners):
    occ_real = occ_state[0].astype(jnp.float32)[None]
    occ_imag = occ_state[1].astype(jnp.float32)[None]
    emp_real = partners[0].astype(jnp.float32)
    emp_imag = partners[1].astype(jnp.float32)
    real_part = occ_real * emp_real + occ_imag * emp_imag
    imag_part = occ_real * emp_imag - occ_imag * emp_real
    line_total = partners.shape[1] * partners.shape[2] * GY
    joined = jnp.concatenate([real_part.reshape(line_total, GZ), imag_part.reshape(line_total, GZ)], axis=1)
    return joined.astype(jnp.bfloat16)


def plane_sections(occ_state, partners, z_table, y_table):
    pair_rows = pair_planes(occ_state, partners)
    depth_out = jnp.dot(pair_rows, z_table, preferred_element_type=jnp.float32).astype(jnp.bfloat16)
    pair_count = partners.shape[1]
    plane_count = partners.shape[2]
    side = 2 * KMAX + 1
    depth_out = depth_out.reshape(pair_count, plane_count, GY, 2, side)
    row_out = jnp.einsum("kxyiq,iyop->kxopq", depth_out.astype(jnp.float32), y_table.astype(jnp.float32))
    return row_out.astype(jnp.bfloat16).reshape(pair_count, plane_count, 2, side * side)


def wave_sums(planes, wave_rows, first_plane):
    side = 2 * KMAX + 1
    pick_index = (wave_rows[1] + KMAX) * side + (wave_rows[2] + KMAX)
    picked = jnp.take(planes, pick_index, axis=3).astype(jnp.float32)
    plane_ids = first_plane + jnp.arange(planes.shape[1], dtype=jnp.int32)
    phase_steps = (plane_ids[:, None] * wave_rows[0][None, :]) % GX
    angles = phase_steps.astype(jnp.float32) * (2.0 * math.pi / GX)
    cosines = jnp.cos(angles)
    sine_table = jnp.sin(angles)
    real_part = jnp.sum(picked[:, :, 0] * cosines + picked[:, :, 1] * sine_table, axis=1)
    imag_part = jnp.sum(picked[:, :, 1] * cosines - picked[:, :, 0] * sine_table, axis=1)
    return jnp.stack([real_part, imag_part], axis=1)


def pair_weights(occ_level, emp_level):
    energy_gap = emp_level.astype(jnp.float32)[None, :] - occ_level.astype(jnp.float32)[:, None] + omega_shift
    return (-2.0 / energy_gap).reshape(-1)


def right_rows(weighted):
    real_cols = jnp.concatenate([weighted[:, 0, :], weighted[:, 1, :]], axis=1)
    imag_cols = jnp.concatenate([weighted[:, 1, :], -weighted[:, 0, :]], axis=1)
    return jnp.stack([real_cols, imag_cols], axis=0).reshape(-1, real_cols.shape[1])


def product_rows(density_low, right_side):
    row_total = density_low.shape[0]
    left_side = density_low.reshape(row_total, -1)
    product = jnp.dot(left_side, right_side.T, preferred_element_type=jnp.float32)
    return product.reshape(row_total, 2, -1)


def reference(occupied_states, empty_states, occ_energy, empty_energy, gvectors):
    blocks = N_BLK
    z_table = depth_table()
    y_table = row_table()

    def accumulate(running, block_index):
        occ_block = lax.dynamic_slice_in_dim(occupied_states, block_index * NV_DEV, NV_DEV, 1)
        occ_level = lax.dynamic_slice_in_dim(occ_energy, block_index * NV_DEV, NV_DEV, 0)
        first_start = ((block_index - 1) % blocks) * NC_DEV
        second_start = ((block_index - 2) % blocks) * NC_DEV
        partners = jnp.concatenate([lax.dynamic_slice_in_dim(empty_states, first_start, NC_DEV, 1),
                                    lax.dynamic_slice_in_dim(empty_states, second_start, NC_DEV, 1)], axis=1)
        partner_levels = jnp.concatenate([lax.dynamic_slice_in_dim(empty_energy, first_start, NC_DEV, 0),
                                          lax.dynamic_slice_in_dim(empty_energy, second_start, NC_DEV, 0)], axis=0)

        def one_state(state_index):
            occ_state = lax.dynamic_index_in_dim(occ_block, state_index, 1, keepdims=False)
            planes = plane_sections(occ_state, partners, z_table, y_table)
            return wave_sums(planes, gvectors, 0)

        density = lax.map(one_state, jnp.arange(NV_DEV, dtype=jnp.int32))
        density = jnp.transpose(density.reshape(-1, 2, NG), (2, 1, 0))
        density_low = density.astype(jnp.bfloat16)
        factor = pair_weights(occ_level, partner_levels)
        weighted = (density_low.astype(jnp.float32) * factor).astype(jnp.bfloat16)
        running = running + product_rows(density_low, right_rows(weighted))
        return running, None

    start_sum = jnp.zeros((NG, 2, NG), jnp.float32)
    running, unused = lax.scan(accumulate, start_sum, jnp.arange(blocks, dtype=jnp.int32))
    return running
```

```python
import functools
import math

import jax
import jax.numpy as jnp
import numpy as np
from jax import lax
from jax.experimental import pallas as pl
from jax.experimental.pallas import tpu as pltpu
from jax.sharding import PartitionSpec as P
import ml_dtypes

GX = 72
GY = 72
GZ = 144
KMAX = 16
SIDE = 2 * KMAX + 1
PLANES = 9
CELLS = GY * GZ
NG = 4096
GROUPS = 9
GROUP_CELLS = 8 * GZ
Z_ROWS = SIDE * 8
ROWS_X = 80
DEPTH = PLANES * ROWS_X
HALF = (SIDE * SIDE + 1) // 2
WAVE_ROWS = 1104
Q_SLOTS = 34
LANES = 128
omega_shift = 0.5


def z_table():
    z = np.arange(GZ)
    out = np.zeros((Z_ROWS, GROUP_CELLS), np.float64)
    for q in range(KMAX + 1):
        angle = 2 * np.pi * ((q * z) % GZ) / GZ
        for y in range(8):
            out[q * 8 + y, y * GZ : (y + 1) * GZ] = np.cos(angle)
            if q:
                out[(KMAX + q) * 8 + y, y * GZ : (y + 1) * GZ] = np.sin(angle)
    return out.astype(np.float32).astype(ml_dtypes.bfloat16)


def plane_table(groups):
    h = np.arange(HALF)
    p = (h + KMAX) // SIDE
    a = h - SIDE * p
    out = np.zeros((groups, WAVE_ROWS, PLANES, ROWS_X), np.float64)
    y = np.arange(GY)
    for group in range(groups):
        for plane in range(PLANES):
            x = group * PLANES + plane
            steps = (p[:, None] * y[None, :] + a[:, None] * x) % GX
            out[group, 0 : 2 * HALF : 2, plane, :GY] = np.cos(2 * np.pi * steps / GX)
            out[group, 1 : 2 * HALF : 2, plane, :GY] = np.sin(2 * np.pi * steps / GX)
    return out.reshape(groups, WAVE_ROWS, DEPTH).astype(np.float32).astype(ml_dtypes.bfloat16)


def turned(value):
    lane = lax.broadcasted_iota(jnp.int32, value.shape, 1)
    ahead = pltpu.roll(value, LANES - 8, 1)
    behind = pltpu.roll(value, 8, 1)
    return jnp.where((lane & 8) == 0, ahead, -behind)


def density_kernel(
    index_ref, emp_ref, near_ref, far_ref, ztab_ref, xytab_ref, sign_ref, scale_ref,
    out_ref, occ_f, pairs, depth_out, sections, waves, picked,
):
    plane = pl.program_id(0)

    occ_f[0:8, :] = near_ref[0].astype(jnp.float32)
    occ_f[8:16, :] = far_ref[0].astype(jnp.float32)

    def group_pairs(group, carry):
        for part in range(3):
            start = pl.multiple_of(group * GROUP_CELLS + part * 384, 128)
            cells = pl.ds(start, 384)
            emp = emp_ref[0, :, cells].astype(jnp.float32)
            emp_re, emp_im = emp[0:8], emp[8:16]
            for v in range(8):
                row = v if v < 4 else v + 4
                occ_re = occ_f[row : row + 1, cells]
                occ_im = occ_f[row + 4 : row + 5, cells]
                both = jnp.concatenate(
                    [occ_re * emp_re + occ_im * emp_im, occ_re * emp_im - occ_im * emp_re], axis=0
                )
                rows = pl.ds(pl.multiple_of(group * LANES + v * 16, 16), 16)
                pairs[rows, part * 384 : part * 384 + 384] = both.astype(jnp.bfloat16)
        return carry

    lax.fori_loop(0, GROUPS, group_pairs, 0)
    depth_out[...] = lax.dot_general(
        ztab_ref[...], pairs[...], (((1,), (1,)), ((), ())), preferred_element_type=jnp.float32
    )
    spot = pl.ds(pl.multiple_of(plane * ROWS_X, 16), ROWS_X)
    blank = jnp.zeros((ROWS_X - GY, LANES), jnp.float32)

    def rows_of(first):
        parts = [depth_out[first : first + 8, t * LANES : (t + 1) * LANES] for t in range(GROUPS)]
        return jnp.concatenate(parts + [blank], axis=0)

    def put(slot, value):
        half = slot % 2
        sections[slot // 2, spot, half * LANES : (half + 1) * LANES] = value.astype(jnp.bfloat16)

    put(KMAX, rows_of(0))
    for q in range(1, KMAX + 1):
        cosine = rows_of(q * 8)
        sine = turned(rows_of((KMAX + q) * 8))
        put(KMAX + q, cosine + sine)
        put(KMAX - q, cosine - sine)

    @pl.when(plane == PLANES - 1)
    def _():
        sections[Q_SLOTS // 2 - 1, :, LANES:] = jnp.zeros((DEPTH, LANES), jnp.bfloat16)

        def slot_pair(k, carry):
            product = jnp.dot(xytab_ref[...], sections[k], preferred_element_type=jnp.float32)
            first = pl.multiple_of(k * 2 * WAVE_ROWS, 16)
            waves[pl.ds(first, WAVE_ROWS), :] = product[:, :LANES]
            waves[pl.ds(first + WAVE_ROWS, WAVE_ROWS), :] = product[:, LANES:]
            return carry

        lax.fori_loop(0, Q_SLOTS // 2, slot_pair, 0)

        def pick(step, carry):
            first = step * 16
            for i in range(16):
                picked[pl.ds((first + i) * 2, 2), :] = waves[pl.ds(index_ref[first + i], 2), :]
            return carry

        lax.fori_loop(0, NG // 16, pick, 0)

        def finish(step, carry):
            first = step * 128
            cosine = picked[pl.ds(first * 2, 128, stride=2), :]
            sine = picked[pl.ds(first * 2 + 1, 128, stride=2), :]
            rows = pl.ds(pl.multiple_of(first, 128), 128)
            total = (cosine + sign_ref[rows, :] * turned(sine)) * scale_ref[...]
            out_ref[rows, :] = total.astype(out_ref.dtype)
            return carry

        lax.fori_loop(0, NG // 128, finish, 0)


def partial_density(index, emp, near, far, ztab, xytab, sign, scale, interpret=False):
    whole = lambda *shape: pl.BlockSpec(shape, lambda i: (0,) * len(shape))
    plane = lambda rows: pl.BlockSpec((1, rows, CELLS), lambda i: (i, 0, 0))
    return pl.pallas_call(
        density_kernel,
        grid=(PLANES,),
        out_shape=jax.ShapeDtypeStruct((NG, LANES), jnp.float32),
        in_specs=[
            pl.BlockSpec(memory_space=pltpu.SMEM),
            plane(16),
            plane(8),
            plane(8),
            whole(Z_ROWS, GROUP_CELLS),
            whole(WAVE_ROWS, DEPTH),
            whole(NG, 1),
            whole(1, LANES),
        ],
        out_specs=whole(NG, LANES),
        scratch_shapes=[
            pltpu.VMEM((16, CELLS), jnp.float32),
            pltpu.VMEM((GROUPS * LANES, GROUP_CELLS), jnp.bfloat16),
            pltpu.VMEM((Z_ROWS, GROUPS * LANES), jnp.float32),
            pltpu.VMEM((Q_SLOTS // 2, DEPTH, 2 * LANES), jnp.bfloat16),
            pltpu.VMEM((Q_SLOTS * WAVE_ROWS, LANES), jnp.float32),
            pltpu.VMEM((2 * NG, LANES), jnp.float32),
        ],
        compiler_params=pltpu.CompilerParams(vmem_limit_bytes=60 * 2**20),
        cost_estimate=pl.CostEstimate(
            flops=15_000_000_000, bytes_accessed=12_000_000, transcendentals=0
        ),
        interpret=interpret,
    )(index, emp, near, far, ztab, xytab, sign, scale)


def from_ahead(value, axis, steps):
    count = lax.axis_size(axis)
    pairs = [((target + steps) % count, target) for target in range(count)]
    return lax.ppermute(value, axis, pairs)


def plane_rows(states):
    moved = jnp.transpose(states, (2, 0, 1, 3))
    return moved.reshape(moved.shape[0], -1, moved.shape[3])


def pair_scale(occ_levels, emp_level):
    gap = (
        emp_level.astype(jnp.float32)[None, :]
        - occ_levels.astype(jnp.float32)[:, None]
        + omega_shift
    )
    root = jnp.sqrt(2.0 / gap)
    return jnp.broadcast_to(root[:, None, :], (8, 2, 8)).reshape(1, LANES)


def wave_index(gvectors):
    flat = SIDE * gvectors[1] + gvectors[0]
    index = (gvectors[2] + KMAX) * WAVE_ROWS + 2 * jnp.abs(flat)
    sign = jnp.where(flat < 0, -1.0, 1.0).astype(jnp.float32)
    return index, sign[:, None]


def shards(ztab, xytabs, occupied_states, empty_states, occ_energy, empty_energy, gvectors):
    occ = plane_rows(occupied_states)
    emp = plane_rows(empty_states)
    near, near_level = from_ahead(occ, "blk", 1), from_ahead(occ_energy, "blk", 1)
    far, far_level = from_ahead(occ, "blk", 2), from_ahead(occ_energy, "blk", 2)
    scale = pair_scale(jnp.concatenate([near_level, far_level]), empty_energy)
    index, sign = wave_index(gvectors)
    xytab = lax.dynamic_index_in_dim(xytabs, lax.axis_index("pw"), 0, keepdims=False)
    partial_sums = partial_density(index, emp, near, far, ztab, xytab, sign, scale)
    rho = lax.psum_scatter(partial_sums, "pw", scatter_dimension=0, tiled=True)
    rho = rho.astype(jnp.bfloat16)
    right = lax.all_gather(rho, "blk", axis=1, tiled=True)
    column = lax.all_gather(rho, "pw", axis=0, tiled=True)
    left = lax.all_to_all(column, "blk", split_axis=0, concat_axis=1, tiled=True)
    parts = left.reshape(left.shape[0], -1, 2, 8)
    side = jnp.stack([-parts[:, :, 1], parts[:, :, 0]], axis=2).reshape(left.shape)
    both = jnp.stack([left, side], axis=1).reshape(-1, left.shape[1])
    product = lax.dot_general(
        -both, right, (((1,), (1,)), ((), ())), preferred_element_type=jnp.float32
    )
    return product.reshape(left.shape[0], 2, -1)


def solution(mesh):
    ztab = z_table()
    xytabs = plane_table(mesh.shape["pw"])
    return jax.shard_map(
        lambda *args: shards(jnp.asarray(ztab), jnp.asarray(xytabs), *args),
        mesh=mesh,
        in_specs=(P(None, "blk", "pw", None), P(None, "blk", "pw", None), P("blk"), P("blk"), P()),
        out_specs=P("blk", None, "pw"),
        check_vma=False,
    )
```

```python
import functools
import math

import jax
import jax.numpy as jnp
import numpy as np
from jax import lax
from jax.experimental import pallas as pl
from jax.experimental.pallas import tpu as pltpu
from jax.sharding import PartitionSpec as P
import ml_dtypes

GX = 72
GY = 72
GZ = 144
KMAX = 16
SIDE = 2 * KMAX + 1
PLANES = 9
CELLS = GY * GZ
NG = 4096
GROUPS = 9
GROUP_CELLS = 8 * GZ
Z_ROWS = SIDE * 8
ROWS_X = 80
DEPTH = PLANES * ROWS_X
HALF = (SIDE * SIDE + 1) // 2
WAVE_ROWS = 1104
Q_SLOTS = 34
LANES = 128
omega_shift = 0.5


def z_table():
    z = np.arange(GZ)
    out = np.zeros((Z_ROWS, GROUP_CELLS), np.float64)
    for q in range(KMAX + 1):
        angle = 2 * np.pi * ((q * z) % GZ) / GZ
        for y in range(8):
            out[q * 8 + y, y * GZ : (y + 1) * GZ] = np.cos(angle)
            if q:
                out[(KMAX + q) * 8 + y, y * GZ : (y + 1) * GZ] = np.sin(angle)
    return out.astype(np.float32).astype(ml_dtypes.bfloat16)


def plane_table(groups):
    h = np.arange(HALF)
    p = (h + KMAX) // SIDE
    a = h - SIDE * p
    out = np.zeros((groups, WAVE_ROWS, PLANES, ROWS_X), np.float64)
    y = np.arange(GY)
    for group in range(groups):
        for plane in range(PLANES):
            x = group * PLANES + plane
            steps = (p[:, None] * y[None, :] + a[:, None] * x) % GX
            out[group, 0 : 2 * HALF : 2, plane, :GY] = np.cos(2 * np.pi * steps / GX)
            out[group, 1 : 2 * HALF : 2, plane, :GY] = np.sin(2 * np.pi * steps / GX)
    return out.reshape(groups, WAVE_ROWS, DEPTH).astype(np.float32).astype(ml_dtypes.bfloat16)


def turned(value):
    lane = lax.broadcasted_iota(jnp.int32, value.shape, 1)
    ahead = pltpu.roll(value, LANES - 8, 1)
    behind = pltpu.roll(value, 8, 1)
    return jnp.where((lane & 8) == 0, ahead, -behind)


def density_kernel(
    index_ref, emp_ref, near_ref, far_ref, ztab_ref, xytab_ref, sign_ref, scale_ref,
    out_ref, occ_f, pairs, depth_out, sections, waves, picked,
):
    plane = pl.program_id(0)

    occ_f[0:8, :] = near_ref[0].astype(jnp.float32)
    occ_f[8:16, :] = far_ref[0].astype(jnp.float32)

    def group_pairs(group, carry):
        for part in range(3):
            start = pl.multiple_of(group * GROUP_CELLS + part * 384, 128)
            cells = pl.ds(start, 384)
            emp = emp_ref[0, :, cells].astype(jnp.float32)
            emp_re, emp_im = emp[0:8], emp[8:16]
            for v in range(8):
                row = v if v < 4 else v + 4
                occ_re = occ_f[row : row + 1, cells]
                occ_im = occ_f[row + 4 : row + 5, cells]
                both = jnp.concatenate(
                    [occ_re * emp_re + occ_im * emp_im, occ_re * emp_im - occ_im * emp_re], axis=0
                )
                rows = pl.ds(pl.multiple_of(group * LANES + v * 16, 16), 16)
                pairs[rows, part * 384 : part * 384 + 384] = both.astype(jnp.bfloat16)
        return carry

    lax.fori_loop(0, GROUPS, group_pairs, 0)
    depth_out[...] = lax.dot_general(
        ztab_ref[...], pairs[...], (((1,), (1,)), ((), ())), preferred_element_type=jnp.float32
    )
    spot = pl.ds(pl.multiple_of(plane * ROWS_X, 16), ROWS_X)
    blank = jnp.zeros((ROWS_X - GY, LANES), jnp.float32)

    def rows_of(first):
        parts = [depth_out[first : first + 8, t * LANES : (t + 1) * LANES] for t in range(GROUPS)]
        return jnp.concatenate(parts + [blank], axis=0)

    def put(slot, value):
        half = slot % 2
        sections[slot // 2, spot, half * LANES : (half + 1) * LANES] = value.astype(jnp.bfloat16)

    put(KMAX, rows_of(0))
    for q in range(1, KMAX + 1):
        cosine = rows_of(q * 8)
        sine = turned(rows_of((KMAX + q) * 8))
        put(KMAX + q, cosine + sine)
        put(KMAX - q, cosine - sine)

    @pl.when(plane == PLANES - 1)
    def _():
        sections[Q_SLOTS // 2 - 1, :, LANES:] = jnp.zeros((DEPTH, LANES), jnp.bfloat16)

        def slot_pair(k, carry):
            product = jnp.dot(xytab_ref[...], sections[k], preferred_element_type=jnp.float32)
            first = pl.multiple_of(k * 2 * WAVE_ROWS, 16)
            waves[pl.ds(first, WAVE_ROWS), :] = product[:, :LANES]
            waves[pl.ds(first + WAVE_ROWS, WAVE_ROWS), :] = product[:, LANES:]
            return carry

        lax.fori_loop(0, Q_SLOTS // 2, slot_pair, 0)

        def pick(step, carry):
            first = step * 16
            for i in range(16):
                picked[pl.ds((first + i) * 2, 2), :] = waves[pl.ds(index_ref[first + i], 2), :]
            return carry

        lax.fori_loop(0, NG // 16, pick, 0)

        def finish(step, carry):
            first = step * 128
            cosine = picked[pl.ds(first * 2, 128, stride=2), :]
            sine = picked[pl.ds(first * 2 + 1, 128, stride=2), :]
            rows = pl.ds(pl.multiple_of(first, 128), 128)
            total = (cosine + sign_ref[rows, :] * turned(sine)) * scale_ref[...]
            out_ref[rows, :] = total.astype(out_ref.dtype)
            return carry

        lax.fori_loop(0, NG // 128, finish, 0)


def partial_density(index, emp, near, far, ztab, xytab, sign, scale, interpret=False):
    whole = lambda *shape: pl.BlockSpec(shape, lambda i: (0,) * len(shape))
    plane = lambda rows: pl.BlockSpec((1, rows, CELLS), lambda i: (i, 0, 0))
    return pl.pallas_call(
        density_kernel,
        grid=(PLANES,),
        out_shape=jax.ShapeDtypeStruct((NG, LANES), jnp.bfloat16),
        in_specs=[
            pl.BlockSpec(memory_space=pltpu.SMEM),
            plane(16),
            plane(8),
            plane(8),
            whole(Z_ROWS, GROUP_CELLS),
            whole(WAVE_ROWS, DEPTH),
            whole(NG, 1),
            whole(1, LANES),
        ],
        out_specs=whole(NG, LANES),
        scratch_shapes=[
            pltpu.VMEM((16, CELLS), jnp.float32),
            pltpu.VMEM((GROUPS * LANES, GROUP_CELLS), jnp.bfloat16),
            pltpu.VMEM((Z_ROWS, GROUPS * LANES), jnp.float32),
            pltpu.VMEM((Q_SLOTS // 2, DEPTH, 2 * LANES), jnp.bfloat16),
            pltpu.VMEM((Q_SLOTS * WAVE_ROWS, LANES), jnp.float32),
            pltpu.VMEM((2 * NG, LANES), jnp.float32),
        ],
        compiler_params=pltpu.CompilerParams(vmem_limit_bytes=60 * 2**20),
        cost_estimate=pl.CostEstimate(
            flops=15_000_000_000, bytes_accessed=12_000_000, transcendentals=0
        ),
        interpret=interpret,
    )(index, emp, near, far, ztab, xytab, sign, scale)


def share_kernel(rows, part_ref, out_ref, everyone, left, relay, passed, arrived, plane_sum, other,
                 send_sems, sum_sems, ring_sems, side_sems, left_sems):
    half_rows, quarter = rows // 2, rows // 4
    blk, pw = lax.axis_index("blk"), lax.axis_index("pw")
    z, y, core = blk // 4, (blk // 2) % 2, blk % 2
    x, y_hi = pw % 4, pw // 4
    n_z = lax.axis_size("blk") // 4

    def place(z=z, y=y, core=core, x=x, y_hi=y_hi):
        return {"blk": z * 4 + y * 2 + core, "pw": y_hi * 4 + x}

    x_next, x_last = place(x=(x + 1) % 4), place(x=(x + 3) % 4)
    z_next, z_last = place(z=(z + 1) % n_z), place(z=(z + n_z - 1) % n_z)
    sibling, beside = place(core=1 - core), place(y=1 - y)
    facing, across = place(y_hi=1 - y_hi), place(y=1 - y, y_hi=1 - y_hi)

    sends = []

    def copy(source, target, arrival, device):
        return pltpu.make_async_remote_copy(
            src_ref=source, dst_ref=target, send_sem=send_sems.at[len(sends)], recv_sem=arrival,
            device_id=device, device_id_type=pl.DeviceIdType.MESH,
        )

    def send(source, target, arrival, device):
        moving = copy(source, target, arrival, device)
        moving.start()
        sends.append(moving)

    def landed(target, arrival):
        pltpu.make_async_copy(target, target, arrival).wait()

    barrier = pltpu.get_barrier_semaphore()
    neighbours = (x_next, x_last, z_next, z_last, sibling, beside, facing, across)
    for device in neighbours:
        pl.semaphore_signal(barrier, inc=1, device_id=device, device_id_type=pl.DeviceIdType.MESH)
    pl.semaphore_wait(barrier, len(neighbours))

    xn, xl, xo = (x + 1) % 4, (x + 3) % 4, (x + 2) % 4
    send(part_ref.at[:, xo, 0], relay.at[0], sum_sems.at[0], x_next)
    send(part_ref.at[:, xo, 1], relay.at[1], sum_sems.at[1], x_last)
    send(part_ref.at[:, xn, 1], arrived.at[0], sum_sems.at[2], x_next)
    send(part_ref.at[:, xl, 0], arrived.at[1], sum_sems.at[3], x_last)
    f32 = jnp.float32
    landed(relay.at[0], sum_sems.at[0])
    passed[0] = (part_ref[:, xn, 0].astype(f32) + relay[0].astype(f32)).astype(jnp.bfloat16)
    send(passed.at[0], arrived.at[2], sum_sems.at[4], x_next)
    landed(relay.at[1], sum_sems.at[1])
    passed[1] = (part_ref[:, xl, 1].astype(f32) + relay[1].astype(f32)).astype(jnp.bfloat16)
    send(passed.at[1], arrived.at[3], sum_sems.at[5], x_last)
    landed(arrived.at[0], sum_sems.at[2])
    landed(arrived.at[1], sum_sems.at[3])
    landed(arrived.at[2], sum_sems.at[4])
    landed(arrived.at[3], sum_sems.at[5])

    def x_total(y_hi, half):
        first, second = (2, 1) if half == 0 else (0, 3)
        return (
            part_ref[y_hi, x, half].astype(f32)
            + arrived[first, y_hi].astype(f32)
            + arrived[second, y_hi].astype(f32)
        )

    for half in range(2):
        plane_sum[half] = x_total(1 - y_hi, half).astype(jnp.bfloat16)
    send(plane_sum, other, sum_sems.at[6], facing)
    landed(other, sum_sems.at[6])
    mine = everyone.at[z, y, core]
    for half in range(2):
        total = x_total(y_hi, half) + other[half].astype(f32)
        everyone[z, y, core, half] = total.astype(jnp.bfloat16)

    send(mine, mine, side_sems.at[0], beside)
    send(mine, mine, side_sems.at[1], sibling)
    upper = lambda zz: everyone.at[zz, :, core, 0]
    lower = lambda zz, yy: everyone.at[zz, yy, core, 1]
    send(lower(z, y), lower(z, y), ring_sems.at[1, 0, 1], z_next)
    send(lower(z, y), lower(z, y), ring_sems.at[1, 1, 1], z_last)
    theirs = everyone.at[z, 1 - y, core]
    landed(theirs, side_sems.at[0])
    send(upper(z), upper(z), ring_sems.at[0, 0, 1], z_next)
    send(upper(z), upper(z), ring_sems.at[0, 1, 1], z_last)
    send(theirs, theirs, side_sems.at[2], sibling)

    longest = {(0, 0): n_z // 2, (0, 1): n_z // 2 - 1, (1, 0): n_z // 2 - 1, (1, 1): n_z // 2}

    def ring_step(step):
        for half in (1, 0):
            for way in (0, 1):
                if step > longest[half, way]:
                    continue
                origin = (z + n_z - step) % n_z if way == 0 else (z + step) % n_z
                piece = upper(origin) if half == 0 else lower(origin, y)
                landed(piece, ring_sems.at[half, way, step])
                if step < longest[half, way]:
                    send(piece, piece, ring_sems.at[half, way, step + 1], z_next if way == 0 else z_last)
                if half == 1:
                    send(piece, piece, ring_sems.at[2, way, step], beside)
                send(piece, piece, ring_sems.at[3 + half, way, step], sibling)

    def side_step(step):
        for way in (0, 1):
            if step > longest[1, way]:
                continue
            origin = (z + n_z - step) % n_z if way == 0 else (z + step) % n_z
            piece = lower(origin, 1 - y)
            landed(piece, ring_sems.at[2, way, step])
            send(piece, piece, ring_sems.at[5, way, step], sibling)

    def rest_step(step):
        if step == 0:
            for yy, spot in ((y, 1), (1 - y, 2)):
                landed(everyone.at[z, yy, 1 - core], side_sems.at[spot])
            return
        for way in (0, 1):
            origin = (z + n_z - step) % n_z if way == 0 else (z + step) % n_z
            if step <= longest[0, way]:
                landed(everyone.at[origin, :, 1 - core, 0], ring_sems.at[3, way, step])
            if step <= longest[1, way]:
                landed(everyone.at[origin, y, 1 - core, 1], ring_sems.at[4, way, step])
                landed(everyone.at[origin, 1 - y, 1 - core, 1], ring_sems.at[5, way, step])

    dx = (x + 4 - z % 4) % 4
    root = z // 4 == y_hi
    first = core * quarter
    eighth = quarter // 2

    def group_origins(step):
        if step == 0:
            return ((z, 0),)
        if step == n_z // 2:
            return (((z + step) % n_z, step),)
        return (((z + n_z - step) % n_z, step), ((z + step) % n_z, n_z - step))

    held = lambda zz, part: left.at[zz, :, :, pl.ds(part * eighth, eighth)]
    late = []

    def left_step(step):
        for zz, tag in group_origins(step):
            base = len(sends)

            def numbered(source, target, arrival, device, offset):
                return pltpu.make_async_remote_copy(
                    src_ref=source, dst_ref=target, send_sem=send_sems.at[base + offset],
                    recv_sem=arrival, device_id=device, device_id_type=pl.DeviceIdType.MESH,
                )

            rows_at = lambda half, start, count: everyone.at[zz, :, :, half, pl.ds(start, count)]
            to_next = numbered(held(zz, 0), held(zz, 0), left_sems.at[0, tag], x_next, 0)
            to_last = numbered(held(zz, 1), held(zz, 1), left_sems.at[1, tag], x_last, 1)
            to_across = numbered(
                rows_at(1 - y, first, quarter), left.at[zz], left_sems.at[2, tag], across, 2
            )

            @pl.when(dx == 0)
            def _():
                @pl.when(root)
                def _():
                    to_across.start()
                    left[zz] = everyone[zz, :, :, y, pl.ds(first, quarter)]

                @pl.when(jnp.logical_not(root))
                def _():
                    landed(left.at[zz], left_sems.at[2, tag])

                to_next.start()
                to_last.start()

            @pl.when((dx == 1) | (dx == 2))
            def _():
                landed(held(zz, 0), left_sems.at[0, tag])
                to_next.start()

            @pl.when((dx == 3) | (dx == 2))
            def _():
                landed(held(zz, 1), left_sems.at[1, tag])
                to_last.start()

            late.append((zz, tag, to_next, to_last, to_across))
            sends.extend([None] * 3)

    def left_end():
        for zz, tag, to_next, to_last, to_across in late:
            pl.when(dx == 1)(lambda: landed(held(zz, 1), left_sems.at[1, tag]))
            pl.when(dx == 3)(lambda: landed(held(zz, 0), left_sems.at[0, tag]))

    rest_step(0)
    ring_step(1)
    left_step(0)
    ring_step(2)
    side_step(1)
    rest_step(1)
    left_step(1)
    ring_step(3)
    side_step(2)
    rest_step(2)
    left_step(2)
    ring_step(4)
    side_step(3)
    rest_step(3)
    left_step(3)
    side_step(4)
    rest_step(4)
    left_step(4)
    left_end()

    def joined(value):
        return jnp.concatenate([value[0, 0], value[0, 1], value[1, 0], value[1, 1]], axis=1)

    def group_product(zz, carry):
        straight = [left[zz, i // 2, i % 2].astype(f32) for i in range(4)]
        side = jnp.concatenate([turned(value) for value in straight], axis=1)
        both = jnp.concatenate([-jnp.concatenate(straight, axis=1), side], axis=0)
        both = both.astype(jnp.bfloat16)
        for half in range(2):
            right = jnp.concatenate([everyone[zz, i // 2, i % 2, half] for i in range(4)], axis=1)
            product = lax.dot_general(
                both, right, (((1,), (1,)), ((), ())), preferred_element_type=f32
            )
            for part in range(2):
                spot = (part, slice(None), slice(half * half_rows, (half + 1) * half_rows))
                out_ref[spot] += product[part * quarter : (part + 1) * quarter]
        return carry

    out_ref[...] = jnp.zeros_like(out_ref)
    lax.fori_loop(0, n_z, group_product, 0)

    for moving in sends:
        if moving is not None:
            moving.wait_send()
    for zz, tag, to_next, to_last, to_across in late:
        pl.when(dx != 3)(lambda: to_next.wait_send())
        pl.when(dx != 1)(lambda: to_last.wait_send())
        pl.when((dx == 0) & root)(lambda: to_across.wait_send())


def shared_response(partial_sums, n_z):
    rows = partial_sums.shape[0] // 8
    half = rows // 2
    bf16 = jnp.bfloat16
    part = partial_sums.reshape(2, 4, 2, half, LANES)
    return pl.pallas_call(
        functools.partial(share_kernel, rows),
        out_shape=jax.ShapeDtypeStruct((2, rows // 4, rows), jnp.float32),
        in_specs=[pl.BlockSpec(memory_space=pltpu.VMEM)],
        out_specs=pl.BlockSpec(memory_space=pltpu.VMEM),
        scratch_shapes=[
            pltpu.VMEM((n_z, 2, 2, 2, half, LANES), bf16),
            pltpu.VMEM((n_z, 2, 2, rows // 4, LANES), bf16),
            pltpu.VMEM((2, 2, half, LANES), bf16),
            pltpu.VMEM((2, 2, half, LANES), bf16),
            pltpu.VMEM((4, 2, half, LANES), bf16),
            pltpu.VMEM((2, half, LANES), bf16),
            pltpu.VMEM((2, half, LANES), bf16),
            pltpu.SemaphoreType.DMA((128,)),
            pltpu.SemaphoreType.DMA((8,)),
            pltpu.SemaphoreType.DMA((6, 2, n_z // 2 + 1)),
            pltpu.SemaphoreType.DMA((3,)),
            pltpu.SemaphoreType.DMA((3, n_z)),
        ],
        compiler_params=pltpu.CompilerParams(
            collective_id=0, has_side_effects=True, vmem_limit_bytes=40 * 2**20
        ),
        cost_estimate=pl.CostEstimate(
            flops=1_100_000_000, bytes_accessed=2_000_000, transcendentals=0
        ),
    )(part)


def from_ahead(value, axis, steps):
    count = lax.axis_size(axis)
    pairs = [((target + steps) % count, target) for target in range(count)]
    return lax.ppermute(value, axis, pairs)


def plane_rows(states):
    moved = jnp.transpose(states, (2, 0, 1, 3))
    return moved.reshape(moved.shape[0], -1, moved.shape[3])


def pair_scale(occ_levels, emp_level):
    gap = (
        emp_level.astype(jnp.float32)[None, :]
        - occ_levels.astype(jnp.float32)[:, None]
        + omega_shift
    )
    root = jnp.sqrt(2.0 / gap)
    return jnp.broadcast_to(root[:, None, :], (8, 2, 8)).reshape(1, LANES)


def wave_index(gvectors):
    flat = SIDE * gvectors[1] + gvectors[0]
    index = (gvectors[2] + KMAX) * WAVE_ROWS + 2 * jnp.abs(flat)
    sign = jnp.where(flat < 0, -1.0, 1.0).astype(jnp.float32)
    return index, sign[:, None]


def shards(ztab, xytabs, occupied_states, empty_states, occ_energy, empty_energy, gvectors):
    occ = plane_rows(occupied_states)
    emp = plane_rows(empty_states)
    near, near_level = from_ahead(occ, "blk", 1), from_ahead(occ_energy, "blk", 1)
    far, far_level = from_ahead(occ, "blk", 2), from_ahead(occ_energy, "blk", 2)
    scale = pair_scale(jnp.concatenate([near_level, far_level]), empty_energy)
    index, sign = wave_index(gvectors)
    xytab = lax.dynamic_index_in_dim(xytabs, lax.axis_index("pw"), 0, keepdims=False)
    partial_sums = partial_density(index, emp, near, far, ztab, xytab, sign, scale)
    n_z = lax.axis_size("blk") // 4
    return jnp.transpose(shared_response(partial_sums, n_z), (1, 0, 2))


def solution(mesh):
    ztab = z_table()
    xytabs = plane_table(mesh.shape["pw"])
    return jax.shard_map(
        lambda *args: shards(jnp.asarray(ztab), jnp.asarray(xytabs), *args),
        mesh=mesh,
        in_specs=(P(None, "blk", "pw", None), P(None, "blk", "pw", None), P("blk"), P("blk"), P()),
        out_specs=P("blk", None, "pw"),
        check_vma=False,
    )
```

```python
import functools
import math

import jax
import jax.numpy as jnp
import numpy as np
from jax import lax
from jax.experimental import pallas as pl
from jax.experimental.pallas import tpu as pltpu
from jax.sharding import PartitionSpec as P
import ml_dtypes

GX = 72
GY = 72
GZ = 144
KMAX = 16
SIDE = 2 * KMAX + 1
PLANES = 9
CELLS = GY * GZ
NG = 4096
GROUPS = 9
GROUP_CELLS = 8 * GZ
Z_ROWS = SIDE * 8
ROWS_X = 80
BATCH = 3
DEPTH = BATCH * ROWS_X
HALF = (SIDE * SIDE + 1) // 2
WAVE_ROWS = 1096
Q_SLOTS = 34
LANES = 128
omega_shift = 0.5


def z_table():
    z = np.arange(GZ)
    out = np.zeros((Z_ROWS, GROUP_CELLS), np.float64)
    for q in range(KMAX + 1):
        angle = 2 * np.pi * ((q * z) % GZ) / GZ
        for y in range(8):
            out[q * 8 + y, y * GZ : (y + 1) * GZ] = np.cos(angle)
            if q:
                out[(KMAX + q) * 8 + y, y * GZ : (y + 1) * GZ] = np.sin(angle)
    return out.astype(np.float32).astype(ml_dtypes.bfloat16)


def plane_table(groups):
    h = np.arange(HALF)
    p = (h + KMAX) // SIDE
    a = h - SIDE * p
    out = np.zeros((groups, WAVE_ROWS, PLANES, ROWS_X), np.float64)
    y = np.arange(GY)
    for group in range(groups):
        for plane in range(PLANES):
            x = group * PLANES + plane
            steps = (p[:, None] * y[None, :] + a[:, None] * x) % GX
            out[group, 0 : 2 * HALF : 2, plane, :GY] = np.cos(2 * np.pi * steps / GX)
            out[group, 1 : 2 * HALF : 2, plane, :GY] = np.sin(2 * np.pi * steps / GX)
    out = out.reshape(groups, WAVE_ROWS, PLANES // BATCH, DEPTH).transpose(0, 2, 1, 3)
    return out.astype(np.float32).astype(ml_dtypes.bfloat16)


def turned(value):
    lane = lax.broadcasted_iota(jnp.int32, value.shape, 1)
    ahead = pltpu.roll(value, LANES - 8, 1)
    behind = pltpu.roll(value, 8, 1)
    return jnp.where((lane & 8) == 0, ahead, -behind)


MESH = pl.DeviceIdType.MESH


def density_kernel(
    occ_ref, emp_ref, wave_ref, level_ref, ztab_ref, xytab_ref, out_ref,
    near, far, near_level, far_level, emp, ztab, xytab, occ_f, pairs, depth_out, sections, waves,
    picked, index_v, index_s, sign_v, ahead_sems, far_sems, pass_sems, near_sems, load_sems,
):
    blk, pw = lax.axis_index("blk"), lax.axis_index("pw")
    count = lax.axis_size("blk")
    core = blk % 2
    behind, ahead = {"blk": (blk + count - 2) % count}, {"blk": (blk + 2) % count}
    sibling = {"blk": blk + 1 - 2 * core}
    barrier = pltpu.get_barrier_semaphore()
    for device in (behind, ahead, sibling):
        pl.semaphore_signal(barrier, inc=1, device_id=device, device_id_type=MESH)
    pl.semaphore_wait(barrier, 3)

    def to_behind(source, target, spot):
        return pltpu.make_async_remote_copy(
            src_ref=source, dst_ref=target, send_sem=ahead_sems.at[spot],
            recv_sem=far_sems.at[spot], device_id=behind, device_id_type=MESH,
        )

    def to_sibling(source, target, spot):
        return pltpu.make_async_remote_copy(
            src_ref=source, dst_ref=target, send_sem=pass_sems.at[spot],
            recv_sem=near_sems.at[spot], device_id=sibling, device_id_type=MESH,
        )

    def landed(target, arrival):
        pltpu.make_async_copy(target, target, arrival).wait()

    def send_plane(x, carry):
        to_behind(occ_ref.at[:, x], far.at[x], x).start()
        return carry

    def pass_plane(x, carry):
        to_sibling(occ_ref.at[:, x], near.at[x], x).start()
        return carry

    to_behind(level_ref, far_level, PLANES).start()
    lax.fori_loop(0, PLANES, send_plane, 0)

    @pl.when(core == 1)
    def _():
        to_sibling(level_ref, near_level, PLANES).start()
        lax.fori_loop(0, PLANES, pass_plane, 0)

    loads = [
        pltpu.make_async_copy(emp_ref, emp, load_sems.at[0]),
        pltpu.make_async_copy(ztab_ref, ztab, load_sems.at[1]),
        pltpu.make_async_copy(xytab_ref.at[pw], xytab, load_sems.at[2]),
    ]
    for load in loads:
        load.start()

    flat = SIDE * wave_ref[1:2, :] + wave_ref[0:1, :]
    index_v[...] = (wave_ref[2:3, :] + KMAX) * WAVE_ROWS + 2 * jnp.abs(flat)
    sign_v[...] = jnp.where(flat < 0, -1.0, 1.0).astype(jnp.float32)
    index_move = pltpu.make_async_copy(index_v, index_s, load_sems.at[3])
    index_move.start()
    landed(far_level, far_sems.at[PLANES])

    @pl.when(core == 0)
    def _():
        to_sibling(far_level, near_level, PLANES).start()

    for load in loads:
        load.wait()
    index_move.wait()

    def group_pairs(x, group):
        for part in range(3):
            start = pl.multiple_of(group * GROUP_CELLS + part * 384, 128)
            cells = pl.ds(start, 384)
            emp_re = emp[0, x, :, cells].astype(jnp.float32)
            emp_im = emp[1, x, :, cells].astype(jnp.float32)
            for v in range(8):
                row = v if v < 4 else v + 4
                occ_re = occ_f[row : row + 1, cells]
                occ_im = occ_f[row + 4 : row + 5, cells]
                both = jnp.concatenate(
                    [occ_re * emp_re + occ_im * emp_im, occ_re * emp_im - occ_im * emp_re], axis=0
                )
                rows = pl.ds(pl.multiple_of(group * LANES + v * 16, 16), 16)
                pairs[rows, part * 384 : part * 384 + 384] = both.astype(jnp.bfloat16)

    blank = jnp.zeros((ROWS_X - GY, LANES), jnp.float32)

    def rows_of(first):
        parts = [depth_out[first : first + 8, t * LANES : (t + 1) * LANES] for t in range(GROUPS)]
        return jnp.concatenate(parts + [blank], axis=0)

    def one_plane(x, spot):
        landed(far.at[x], far_sems.at[x])

        @pl.when(core == 0)
        def _():
            to_sibling(far.at[x], near.at[x], x).start()

        landed(near.at[x], near_sems.at[x])
        for part in range(2):
            occ_f[part * 4 : part * 4 + 4, :] = near[x, part].astype(jnp.float32)
            occ_f[part * 4 + 8 : part * 4 + 12, :] = far[x, part].astype(jnp.float32)

        def each_group(group, carry):
            group_pairs(x, group)
            return carry

        lax.fori_loop(0, GROUPS, each_group, 0)
        depth_out[...] = lax.dot_general(
            ztab[...], pairs[...], (((1,), (1,)), ((), ())), preferred_element_type=jnp.float32
        )
        rows = pl.ds(pl.multiple_of(spot * ROWS_X, 16), ROWS_X)

        def put(slot, value):
            half = slot % 2
            sections[slot // 2, rows, half * LANES : (half + 1) * LANES] = value.astype(jnp.bfloat16)

        put(KMAX, rows_of(0))
        for q in range(1, KMAX + 1):
            cosine = rows_of(q * 8)
            sine = turned(rows_of((KMAX + q) * 8))
            put(KMAX + q, cosine + sine)
            put(KMAX - q, cosine - sine)

    sections[Q_SLOTS // 2 - 1, :, LANES:] = jnp.zeros((DEPTH, LANES), jnp.bfloat16)
    for batch in range(PLANES // BATCH):

        def each_plane(spot, carry):
            one_plane(batch * BATCH + spot, spot)
            return carry

        lax.fori_loop(0, BATCH, each_plane, 0)

        def slot_pair(k, carry):
            product = jnp.dot(xytab[batch], sections[k], preferred_element_type=jnp.float32)
            first = pl.multiple_of(k * 2 * WAVE_ROWS, 8)
            for half in range(2):
                rows = pl.ds(first + half * WAVE_ROWS, WAVE_ROWS)
                value = product[:, half * LANES : (half + 1) * LANES]
                waves[rows, :] = value if batch == 0 else waves[rows, :] + value
            return carry

        lax.fori_loop(0, Q_SLOTS // 2, slot_pair, 0)

    landed(near_level, near_sems.at[PLANES])
    lane = lax.broadcasted_iota(jnp.int32, (1, LANES), 1)
    occ_level = jnp.where(lane < LANES // 2, near_level[0:1, :], far_level[0:1, :])
    scale = jnp.sqrt(2.0 / (level_ref[1:2, :] - occ_level + omega_shift))

    def chunk(w, carry):
        def pick(step, carry):
            first = step * 16
            for i in range(16):
                row = index_s[0, w * 512 + first + i]
                picked[pl.ds((first + i) * 2, 2), :] = waves[pl.ds(row, 2), :]
            return carry

        lax.fori_loop(0, 32, pick, 0)
        for part in range(4):
            cosine = picked[pl.ds(part * 256, 128, stride=2), :]
            sine = picked[pl.ds(part * 256 + 1, 128, stride=2), :]
            first = pl.multiple_of(w * 512 + part * 128, 128)
            sign = jnp.broadcast_to(sign_v[:, pl.ds(first, 128)], (128, LANES)).T
            total = (cosine + sign * turned(sine)) * scale
            out_ref[pl.ds(first, 128), :] = total.astype(out_ref.dtype)
        return carry

    lax.fori_loop(0, NG // 512, chunk, 0)

    def sent_plane(x, carry):
        to_behind(occ_ref.at[:, x], far.at[x], x).wait_send()
        return carry

    def passed_plane(x, carry):
        to_sibling(occ_ref.at[:, x], near.at[x], x).wait_send()
        return carry

    def passed_far(x, carry):
        to_sibling(far.at[x], near.at[x], x).wait_send()
        return carry

    to_behind(level_ref, far_level, PLANES).wait_send()
    lax.fori_loop(0, PLANES, sent_plane, 0)

    @pl.when(core == 1)
    def _():
        to_sibling(level_ref, near_level, PLANES).wait_send()
        lax.fori_loop(0, PLANES, passed_plane, 0)

    @pl.when(core == 0)
    def _():
        to_sibling(far_level, near_level, PLANES).wait_send()
        lax.fori_loop(0, PLANES, passed_far, 0)


def partial_density(occ, emp, gvectors, levels, ztab, xytabs):
    bf16, f32 = jnp.bfloat16, jnp.float32
    anywhere, vmem = pl.BlockSpec(memory_space=pl.ANY), pl.BlockSpec(memory_space=pltpu.VMEM)
    return pl.pallas_call(
        density_kernel,
        out_shape=jax.ShapeDtypeStruct((NG, LANES), bf16),
        in_specs=[anywhere, anywhere, vmem, vmem, anywhere, anywhere],
        out_specs=vmem,
        scratch_shapes=[
            pltpu.VMEM((PLANES, 2, 4, CELLS), bf16),
            pltpu.VMEM((PLANES, 2, 4, CELLS), bf16),
            pltpu.VMEM((8, LANES), f32),
            pltpu.VMEM((8, LANES), f32),
            pltpu.VMEM((2, PLANES, 8, CELLS), bf16),
            pltpu.VMEM((Z_ROWS, GROUP_CELLS), bf16),
            pltpu.VMEM((PLANES // BATCH, WAVE_ROWS, DEPTH), bf16),
            pltpu.VMEM((16, CELLS), f32),
            pltpu.VMEM((GROUPS * LANES, GROUP_CELLS), bf16),
            pltpu.VMEM((Z_ROWS, GROUPS * LANES), f32),
            pltpu.VMEM((Q_SLOTS // 2, DEPTH, 2 * LANES), bf16),
            pltpu.VMEM((Q_SLOTS * WAVE_ROWS, LANES), f32),
            pltpu.VMEM((1024, LANES), f32),
            pltpu.VMEM((1, NG), jnp.int32),
            pltpu.SMEM((1, NG), jnp.int32),
            pltpu.VMEM((1, NG), f32),
            pltpu.SemaphoreType.DMA((PLANES + 1,)),
            pltpu.SemaphoreType.DMA((PLANES + 1,)),
            pltpu.SemaphoreType.DMA((PLANES + 1,)),
            pltpu.SemaphoreType.DMA((PLANES + 1,)),
            pltpu.SemaphoreType.DMA((4,)),
        ],
        compiler_params=pltpu.CompilerParams(
            collective_id=1, has_side_effects=True, vmem_limit_bytes=60 * 2**20
        ),
        cost_estimate=pl.CostEstimate(
            flops=15_000_000_000, bytes_accessed=12_000_000, transcendentals=0
        ),
    )(occ, emp, gvectors, levels, ztab, xytabs)


def share_kernel(rows, part_ref, out_ref, everyone, left, relay, passed, arrived, plane_sum, other,
                 send_sems, sum_sems, ring_sems, side_sems, left_sems):
    half_rows, quarter = rows // 2, rows // 4
    blk, pw = lax.axis_index("blk"), lax.axis_index("pw")
    z, y, core = blk // 4, (blk // 2) % 2, blk % 2
    x, y_hi = pw % 4, pw // 4
    n_z = lax.axis_size("blk") // 4

    def place(z=z, y=y, core=core, x=x, y_hi=y_hi):
        return {"blk": z * 4 + y * 2 + core, "pw": y_hi * 4 + x}

    x_next, x_last = place(x=(x + 1) % 4), place(x=(x + 3) % 4)
    z_next, z_last = place(z=(z + 1) % n_z), place(z=(z + n_z - 1) % n_z)
    sibling, beside = place(core=1 - core), place(y=1 - y)
    facing, across = place(y_hi=1 - y_hi), place(y=1 - y, y_hi=1 - y_hi)

    sends = []

    def copy(source, target, arrival, device):
        return pltpu.make_async_remote_copy(
            src_ref=source, dst_ref=target, send_sem=send_sems.at[len(sends)], recv_sem=arrival,
            device_id=device, device_id_type=pl.DeviceIdType.MESH,
        )

    def send(source, target, arrival, device):
        moving = copy(source, target, arrival, device)
        moving.start()
        sends.append(moving)

    def landed(target, arrival):
        pltpu.make_async_copy(target, target, arrival).wait()

    barrier = pltpu.get_barrier_semaphore()
    neighbours = (x_next, x_last, z_next, z_last, sibling, beside, facing, across)
    for device in neighbours:
        pl.semaphore_signal(barrier, inc=1, device_id=device, device_id_type=pl.DeviceIdType.MESH)
    pl.semaphore_wait(barrier, len(neighbours))

    xn, xl, xo = (x + 1) % 4, (x + 3) % 4, (x + 2) % 4
    send(part_ref.at[:, xo, 0], relay.at[0], sum_sems.at[0], x_next)
    send(part_ref.at[:, xo, 1], relay.at[1], sum_sems.at[1], x_last)
    send(part_ref.at[:, xn, 1], arrived.at[0], sum_sems.at[2], x_next)
    send(part_ref.at[:, xl, 0], arrived.at[1], sum_sems.at[3], x_last)
    f32 = jnp.float32
    landed(relay.at[0], sum_sems.at[0])
    passed[0] = (part_ref[:, xn, 0].astype(f32) + relay[0].astype(f32)).astype(jnp.bfloat16)
    send(passed.at[0], arrived.at[2], sum_sems.at[4], x_next)
    landed(relay.at[1], sum_sems.at[1])
    passed[1] = (part_ref[:, xl, 1].astype(f32) + relay[1].astype(f32)).astype(jnp.bfloat16)
    send(passed.at[1], arrived.at[3], sum_sems.at[5], x_last)
    landed(arrived.at[0], sum_sems.at[2])
    landed(arrived.at[1], sum_sems.at[3])
    landed(arrived.at[2], sum_sems.at[4])
    landed(arrived.at[3], sum_sems.at[5])

    def x_total(y_hi, half):
        first, second = (2, 1) if half == 0 else (0, 3)
        return (
            part_ref[y_hi, x, half].astype(f32)
            + arrived[first, y_hi].astype(f32)
            + arrived[second, y_hi].astype(f32)
        )

    for half in range(2):
        plane_sum[half] = x_total(1 - y_hi, half).astype(jnp.bfloat16)
    send(plane_sum, other, sum_sems.at[6], facing)
    landed(other, sum_sems.at[6])
    mine = everyone.at[z, y, core]
    for half in range(2):
        total = x_total(y_hi, half) + other[half].astype(f32)
        everyone[z, y, core, half] = total.astype(jnp.bfloat16)

    send(mine, mine, side_sems.at[0], beside)
    send(mine, mine, side_sems.at[1], sibling)
    upper = lambda zz: everyone.at[zz, :, core, 0]
    lower = lambda zz, yy: everyone.at[zz, yy, core, 1]
    send(lower(z, y), lower(z, y), ring_sems.at[1, 0, 1], z_next)
    send(lower(z, y), lower(z, y), ring_sems.at[1, 1, 1], z_last)
    theirs = everyone.at[z, 1 - y, core]
    landed(theirs, side_sems.at[0])
    send(upper(z), upper(z), ring_sems.at[0, 0, 1], z_next)
    send(upper(z), upper(z), ring_sems.at[0, 1, 1], z_last)
    send(theirs, theirs, side_sems.at[2], sibling)

    longest = {(0, 0): n_z // 2, (0, 1): n_z // 2 - 1, (1, 0): n_z // 2 - 1, (1, 1): n_z // 2}

    def ring_step(step):
        for half in (1, 0):
            for way in (0, 1):
                if step > longest[half, way]:
                    continue
                origin = (z + n_z - step) % n_z if way == 0 else (z + step) % n_z
                piece = upper(origin) if half == 0 else lower(origin, y)
                landed(piece, ring_sems.at[half, way, step])
                if step < longest[half, way]:
                    send(piece, piece, ring_sems.at[half, way, step + 1], z_next if way == 0 else z_last)
                if half == 1:
                    send(piece, piece, ring_sems.at[2, way, step], beside)
                send(piece, piece, ring_sems.at[3 + half, way, step], sibling)

    def side_step(step):
        for way in (0, 1):
            if step > longest[1, way]:
                continue
            origin = (z + n_z - step) % n_z if way == 0 else (z + step) % n_z
            piece = lower(origin, 1 - y)
            landed(piece, ring_sems.at[2, way, step])
            send(piece, piece, ring_sems.at[5, way, step], sibling)

    def rest_step(step):
        if step == 0:
            for yy, spot in ((y, 1), (1 - y, 2)):
                landed(everyone.at[z, yy, 1 - core], side_sems.at[spot])
            return
        for way in (0, 1):
            origin = (z + n_z - step) % n_z if way == 0 else (z + step) % n_z
            if step <= longest[0, way]:
                landed(everyone.at[origin, :, 1 - core, 0], ring_sems.at[3, way, step])
            if step <= longest[1, way]:
                landed(everyone.at[origin, y, 1 - core, 1], ring_sems.at[4, way, step])
                landed(everyone.at[origin, 1 - y, 1 - core, 1], ring_sems.at[5, way, step])

    dx = (x + 4 - z % 4) % 4
    root = z // 4 == y_hi
    first = core * quarter
    eighth = quarter // 2

    def group_origins(step):
        if step == 0:
            return ((z, 0),)
        if step == n_z // 2:
            return (((z + step) % n_z, step),)
        return (((z + n_z - step) % n_z, step), ((z + step) % n_z, n_z - step))

    held = lambda zz, part: left.at[zz, :, :, pl.ds(part * eighth, eighth)]
    late = []

    def left_step(step):
        for zz, tag in group_origins(step):
            base = len(sends)

            def numbered(source, target, arrival, device, offset):
                return pltpu.make_async_remote_copy(
                    src_ref=source, dst_ref=target, send_sem=send_sems.at[base + offset],
                    recv_sem=arrival, device_id=device, device_id_type=pl.DeviceIdType.MESH,
                )

            rows_at = lambda half, start, count: everyone.at[zz, :, :, half, pl.ds(start, count)]
            to_next = numbered(held(zz, 0), held(zz, 0), left_sems.at[0, tag], x_next, 0)
            to_last = numbered(held(zz, 1), held(zz, 1), left_sems.at[1, tag], x_last, 1)
            to_across = numbered(
                rows_at(1 - y, first, quarter), left.at[zz], left_sems.at[2, tag], across, 2
            )

            @pl.when(dx == 0)
            def _():
                @pl.when(root)
                def _():
                    to_across.start()
                    left[zz] = everyone[zz, :, :, y, pl.ds(first, quarter)]

                @pl.when(jnp.logical_not(root))
                def _():
                    landed(left.at[zz], left_sems.at[2, tag])

                to_next.start()
                to_last.start()

            @pl.when((dx == 1) | (dx == 2))
            def _():
                landed(held(zz, 0), left_sems.at[0, tag])
                to_next.start()

            @pl.when((dx == 3) | (dx == 2))
            def _():
                landed(held(zz, 1), left_sems.at[1, tag])
                to_last.start()

            late.append((zz, tag, to_next, to_last, to_across))
            sends.extend([None] * 3)

    def left_end():
        for zz, tag, to_next, to_last, to_across in late:
            pl.when(dx == 1)(lambda: landed(held(zz, 1), left_sems.at[1, tag]))
            pl.when(dx == 3)(lambda: landed(held(zz, 0), left_sems.at[0, tag]))

    rest_step(0)
    ring_step(1)
    left_step(0)
    ring_step(2)
    side_step(1)
    rest_step(1)
    left_step(1)
    ring_step(3)
    side_step(2)
    rest_step(2)
    left_step(2)
    ring_step(4)
    side_step(3)
    rest_step(3)
    left_step(3)
    side_step(4)
    rest_step(4)
    left_step(4)
    left_end()

    def joined(value):
        return jnp.concatenate([value[0, 0], value[0, 1], value[1, 0], value[1, 1]], axis=1)

    def group_product(zz, carry):
        straight = [left[zz, i // 2, i % 2].astype(f32) for i in range(4)]
        side = jnp.concatenate([turned(value) for value in straight], axis=1)
        both = jnp.concatenate([-jnp.concatenate(straight, axis=1), side], axis=0)
        both = both.astype(jnp.bfloat16)
        for half in range(2):
            right = jnp.concatenate([everyone[zz, i // 2, i % 2, half] for i in range(4)], axis=1)
            product = lax.dot_general(
                both, right, (((1,), (1,)), ((), ())), preferred_element_type=f32
            )
            for part in range(2):
                spot = (part, slice(None), slice(half * half_rows, (half + 1) * half_rows))
                out_ref[spot] += product[part * quarter : (part + 1) * quarter]
        return carry

    out_ref[...] = jnp.zeros_like(out_ref)
    lax.fori_loop(0, n_z, group_product, 0)

    for moving in sends:
        if moving is not None:
            moving.wait_send()
    for zz, tag, to_next, to_last, to_across in late:
        pl.when(dx != 3)(lambda: to_next.wait_send())
        pl.when(dx != 1)(lambda: to_last.wait_send())
        pl.when((dx == 0) & root)(lambda: to_across.wait_send())


def shared_response(partial_sums, n_z):
    rows = partial_sums.shape[0] // 8
    half = rows // 2
    bf16 = jnp.bfloat16
    part = partial_sums.reshape(2, 4, 2, half, LANES)
    return pl.pallas_call(
        functools.partial(share_kernel, rows),
        out_shape=jax.ShapeDtypeStruct((2, rows // 4, rows), jnp.float32),
        in_specs=[pl.BlockSpec(memory_space=pltpu.VMEM)],
        out_specs=pl.BlockSpec(memory_space=pltpu.VMEM),
        scratch_shapes=[
            pltpu.VMEM((n_z, 2, 2, 2, half, LANES), bf16),
            pltpu.VMEM((n_z, 2, 2, rows // 4, LANES), bf16),
            pltpu.VMEM((2, 2, half, LANES), bf16),
            pltpu.VMEM((2, 2, half, LANES), bf16),
            pltpu.VMEM((4, 2, half, LANES), bf16),
            pltpu.VMEM((2, half, LANES), bf16),
            pltpu.VMEM((2, half, LANES), bf16),
            pltpu.SemaphoreType.DMA((128,)),
            pltpu.SemaphoreType.DMA((8,)),
            pltpu.SemaphoreType.DMA((6, 2, n_z // 2 + 1)),
            pltpu.SemaphoreType.DMA((3,)),
            pltpu.SemaphoreType.DMA((3, n_z)),
        ],
        compiler_params=pltpu.CompilerParams(
            collective_id=0, has_side_effects=True, vmem_limit_bytes=40 * 2**20
        ),
        cost_estimate=pl.CostEstimate(
            flops=1_100_000_000, bytes_accessed=2_000_000, transcendentals=0
        ),
    )(part)


def lane_levels(occ_energy, empty_energy):
    occ = jnp.broadcast_to(occ_energy.astype(jnp.float32)[None, :, None], (2, 4, 16))
    emp = jnp.broadcast_to(empty_energy.astype(jnp.float32)[None, :], (16, 8))
    rows = jnp.stack([occ.reshape(LANES), emp.reshape(LANES)])
    return jnp.concatenate([rows, jnp.zeros((6, LANES), jnp.float32)])


def shards(ztab, xytabs, occupied_states, empty_states, occ_energy, empty_energy, gvectors):
    occ = jnp.transpose(occupied_states, (0, 2, 1, 3))
    emp = jnp.transpose(empty_states, (0, 2, 1, 3))
    levels = lane_levels(occ_energy, empty_energy)
    partial_sums = partial_density(occ, emp, gvectors, levels, ztab, xytabs)
    n_z = lax.axis_size("blk") // 4
    return jnp.transpose(shared_response(partial_sums, n_z), (1, 0, 2))


def solution(mesh):
    ztab = z_table()
    xytabs = plane_table(mesh.shape["pw"])
    return jax.shard_map(
        lambda *args: shards(jnp.asarray(ztab), jnp.asarray(xytabs), *args),
        mesh=mesh,
        in_specs=(P(None, "blk", "pw", None), P(None, "blk", "pw", None), P("blk"), P("blk"), P()),
        out_specs=P("blk", None, "pw"),
        check_vma=False,
    )
```

```python
import math

import jax
import jax.numpy as jnp
import numpy as np
from jax import lax
from jax.experimental import pallas as pl
from jax.experimental.pallas import tpu as pltpu
from jax.sharding import PartitionSpec as P
import ml_dtypes

GX = 72
GY = 72
GZ = 144
KMAX = 16
SIDE = 2 * KMAX + 1
PLANES = 9
CELLS = GY * GZ
NG = 4096
GROUPS = 9
GROUP_CELLS = 8 * GZ
Z_ROWS = SIDE * 8
ROWS_X = 80
BATCH = 3
DEPTH = BATCH * ROWS_X
HALF = (SIDE * SIDE + 1) // 2
WAVE_ROWS = 1096
Q_SLOTS = 34
LANES = 128
omega_shift = 0.5


def z_table():
    z = np.arange(GZ)
    out = np.zeros((Z_ROWS, GROUP_CELLS), np.float64)
    for q in range(KMAX + 1):
        angle = 2 * np.pi * ((q * z) % GZ) / GZ
        for y in range(8):
            out[q * 8 + y, y * GZ : (y + 1) * GZ] = np.cos(angle)
            if q:
                out[(KMAX + q) * 8 + y, y * GZ : (y + 1) * GZ] = np.sin(angle)
    return out.astype(np.float32).astype(ml_dtypes.bfloat16)


def plane_table(groups):
    h = np.arange(HALF)
    p = (h + KMAX) // SIDE
    a = h - SIDE * p
    out = np.zeros((groups, WAVE_ROWS, PLANES, ROWS_X), np.float64)
    y = np.arange(GY)
    for group in range(groups):
        for plane in range(PLANES):
            x = group * PLANES + plane
            steps = (p[:, None] * y[None, :] + a[:, None] * x) % GX
            out[group, 0 : 2 * HALF : 2, plane, :GY] = np.cos(2 * np.pi * steps / GX)
            out[group, 1 : 2 * HALF : 2, plane, :GY] = np.sin(2 * np.pi * steps / GX)
    out = out.reshape(groups, WAVE_ROWS, PLANES // BATCH, DEPTH).transpose(0, 2, 1, 3)
    return out.astype(np.float32).astype(ml_dtypes.bfloat16)


def turned(value):
    lane = lax.broadcasted_iota(jnp.int32, value.shape, 1)
    ahead = pltpu.roll(value, LANES - 8, 1)
    behind = pltpu.roll(value, 8, 1)
    return jnp.where((lane & 8) == 0, ahead, -behind)


MESH = pl.DeviceIdType.MESH


def response_kernel(
    occ_ref, emp_ref, wave_ref, occ_energy_ref, emp_energy_ref, ztab_ref, xytab_ref, out_ref,
    near, far, level_ref, near_level, far_level, emp, ztab, xytab, occ_f, pairs, depth_out, sections, waves,
    picked, index_v, index_s, sign_v, part_ref, everyone, left, relay, passed, arrived, plane_sum,
    other, ahead_sems, far_sems, pass_sems, near_sems, load_sems, send_sems, sum_sems, ring_sems,
    side_sems, left_sems,
):
    blk, pw = lax.axis_index("blk"), lax.axis_index("pw")
    count = lax.axis_size("blk")
    n_z = count // 4
    z, y, core = blk // 4, (blk // 2) % 2, blk % 2
    x, y_hi = pw % 4, pw // 4
    f32, bf16 = jnp.float32, jnp.bfloat16

    def place(z=z, y=y, core=core, x=x, y_hi=y_hi):
        return {"blk": z * 4 + y * 2 + core, "pw": y_hi * 4 + x}

    x_next, x_last = place(x=(x + 1) % 4), place(x=(x + 3) % 4)
    z_next, z_last = place(z=(z + 1) % n_z), place(z=(z + n_z - 1) % n_z)
    sibling, beside = place(core=1 - core), place(y=1 - y)
    facing, across = place(y_hi=1 - y_hi), place(y=1 - y, y_hi=1 - y_hi)
    behind = {"blk": (blk + count - 2) % count, "pw": pw}
    ahead = {"blk": (blk + 2) % count, "pw": pw}

    barrier = pltpu.get_barrier_semaphore()
    neighbours = (
        x_next, x_last, z_next, z_last, sibling, beside, facing, across, behind, ahead
    )
    for device in neighbours:
        pl.semaphore_signal(barrier, inc=1, device_id=device, device_id_type=MESH)
    pl.semaphore_wait(barrier, len(neighbours))

    def to_behind(source, target, spot):
        return pltpu.make_async_remote_copy(
            src_ref=source, dst_ref=target, send_sem=ahead_sems.at[spot],
            recv_sem=far_sems.at[spot], device_id=behind, device_id_type=MESH,
        )

    def to_sibling(source, target, spot):
        return pltpu.make_async_remote_copy(
            src_ref=source, dst_ref=target, send_sem=pass_sems.at[spot],
            recv_sem=near_sems.at[spot], device_id=sibling, device_id_type=MESH,
        )

    def landed(target, arrival):
        pltpu.make_async_copy(target, target, arrival).wait()

    def send_plane(x, carry):
        to_behind(occ_ref.at[:, x], far.at[x], x).start()
        return carry

    def pass_plane(x, carry):
        to_sibling(occ_ref.at[:, x], near.at[x], x).start()
        return carry

    lax.fori_loop(0, PLANES, send_plane, 0)
    lane = lax.broadcasted_iota(jnp.int32, (8, LANES), 1)
    occ_energy = occ_energy_ref[...].astype(f32)
    emp_energy = emp_energy_ref[...].astype(f32)
    spread = jnp.zeros((8, LANES), f32)
    for v in range(4):
        spread = jnp.where((lane // 16) % 4 == v, occ_energy[:, v : v + 1], spread)
    level_ref[...] = spread
    emp_level = jnp.zeros((8, LANES), f32)
    for c in range(8):
        emp_level = jnp.where(lane % 8 == c, emp_energy[:, c : c + 1], emp_level)
    to_behind(level_ref, far_level, PLANES).start()

    @pl.when(core == 1)
    def _():
        to_sibling(level_ref, near_level, PLANES).start()
        lax.fori_loop(0, PLANES, pass_plane, 0)

    loads = [
        pltpu.make_async_copy(emp_ref, emp, load_sems.at[0]),
        pltpu.make_async_copy(ztab_ref, ztab, load_sems.at[1]),
        pltpu.make_async_copy(xytab_ref.at[pw], xytab, load_sems.at[2]),
    ]
    for load in loads:
        load.start()

    flat = SIDE * wave_ref[1:2, :] + wave_ref[0:1, :]
    index_v[...] = (wave_ref[2:3, :] + KMAX) * WAVE_ROWS + 2 * jnp.abs(flat)
    sign_v[...] = jnp.where(flat < 0, -1.0, 1.0).astype(jnp.float32)
    index_move = pltpu.make_async_copy(index_v, index_s, load_sems.at[3])
    index_move.start()
    landed(far_level, far_sems.at[PLANES])

    @pl.when(core == 0)
    def _():
        to_sibling(far_level, near_level, PLANES).start()

    for load in loads:
        load.wait()
    index_move.wait()

    def group_pairs(x, group):
        for part in range(3):
            start = pl.multiple_of(group * GROUP_CELLS + part * 384, 128)
            cells = pl.ds(start, 384)
            emp_re = emp[0, x, :, cells].astype(jnp.float32)
            emp_im = emp[1, x, :, cells].astype(jnp.float32)
            for v in range(8):
                row = v if v < 4 else v + 4
                occ_re = occ_f[row : row + 1, cells]
                occ_im = occ_f[row + 4 : row + 5, cells]
                both = jnp.concatenate(
                    [occ_re * emp_re + occ_im * emp_im, occ_re * emp_im - occ_im * emp_re], axis=0
                )
                rows = pl.ds(pl.multiple_of(group * LANES + v * 16, 16), 16)
                pairs[rows, part * 384 : part * 384 + 384] = both.astype(jnp.bfloat16)

    blank = jnp.zeros((ROWS_X - GY, LANES), jnp.float32)

    def rows_of(first):
        parts = [depth_out[first : first + 8, t * LANES : (t + 1) * LANES] for t in range(GROUPS)]
        return jnp.concatenate(parts + [blank], axis=0)

    def one_plane(x, spot):
        landed(far.at[x], far_sems.at[x])

        @pl.when(core == 0)
        def _():
            to_sibling(far.at[x], near.at[x], x).start()

        landed(near.at[x], near_sems.at[x])
        for part in range(2):
            occ_f[part * 4 : part * 4 + 4, :] = near[x, part].astype(jnp.float32)
            occ_f[part * 4 + 8 : part * 4 + 12, :] = far[x, part].astype(jnp.float32)

        def each_group(group, carry):
            group_pairs(x, group)
            return carry

        lax.fori_loop(0, GROUPS, each_group, 0)
        depth_out[...] = lax.dot_general(
            ztab[...], pairs[...], (((1,), (1,)), ((), ())), preferred_element_type=jnp.float32
        )
        rows = pl.ds(pl.multiple_of(spot * ROWS_X, 16), ROWS_X)

        def put(slot, value):
            half = slot % 2
            sections[slot // 2, rows, half * LANES : (half + 1) * LANES] = value.astype(jnp.bfloat16)

        put(KMAX, rows_of(0))
        for q in range(1, KMAX + 1):
            cosine = rows_of(q * 8)
            sine = turned(rows_of((KMAX + q) * 8))
            put(KMAX + q, cosine + sine)
            put(KMAX - q, cosine - sine)

    sections[Q_SLOTS // 2 - 1, :, LANES:] = jnp.zeros((DEPTH, LANES), jnp.bfloat16)
    for batch in range(PLANES // BATCH):

        def each_plane(spot, carry):
            one_plane(batch * BATCH + spot, spot)
            return carry

        lax.fori_loop(0, BATCH, each_plane, 0)

        def slot_pair(k, carry):
            product = jnp.dot(xytab[batch], sections[k], preferred_element_type=jnp.float32)
            first = pl.multiple_of(k * 2 * WAVE_ROWS, 8)
            for half in range(2):
                rows = pl.ds(first + half * WAVE_ROWS, WAVE_ROWS)
                value = product[:, half * LANES : (half + 1) * LANES]
                waves[rows, :] = value if batch == 0 else waves[rows, :] + value
            return carry

        lax.fori_loop(0, Q_SLOTS // 2, slot_pair, 0)

    landed(near_level, near_sems.at[PLANES])
    occ_level = jnp.where(lane < LANES // 2, near_level[...], far_level[...])
    scale = jnp.sqrt(2.0 / (emp_level - occ_level + omega_shift))[0:1]

    def chunk(yy, xx):
        base = (yy * 4 + xx) * 512

        def pick(step, carry):
            first = step * 16
            for i in range(16):
                row = index_s[0, base + first + i]
                picked[pl.ds((first + i) * 2, 2), :] = waves[pl.ds(row, 2), :]
            return carry

        lax.fori_loop(0, 32, pick, 0)
        for part in range(4):
            cosine = picked[pl.ds(part * 256, 128, stride=2), :]
            sine = picked[pl.ds(part * 256 + 1, 128, stride=2), :]
            first = pl.multiple_of(base + part * 128, 128)
            sign = jnp.broadcast_to(sign_v[:, pl.ds(first, 128)], (128, LANES)).T
            total = (cosine + sign * turned(sine)) * scale
            rows = slice((part % 2) * 128, (part % 2) * 128 + 128)
            part_ref[yy, xx, part // 2, rows, :] = total.astype(bf16)

    def both_chunks(xx):
        def one(yy, carry):
            chunk(yy, xx)
            return carry

        lax.fori_loop(0, 2, one, 0)

    sends = []

    def copy(source, target, arrival, device):
        return pltpu.make_async_remote_copy(
            src_ref=source, dst_ref=target, send_sem=send_sems.at[len(sends)], recv_sem=arrival,
            device_id=device, device_id_type=MESH,
        )

    def send(source, target, arrival, device):
        moving = copy(source, target, arrival, device)
        moving.start()
        sends.append(moving)

    out_ref[...] = jnp.zeros_like(out_ref)
    rows = everyone.shape[4] * 2
    half_rows, quarter = rows // 2, rows // 4

    xn, xl, xo = (x + 1) % 4, (x + 3) % 4, (x + 2) % 4
    both_chunks(xo)
    send(part_ref.at[:, xo, 0], relay.at[0], sum_sems.at[0], x_next)
    send(part_ref.at[:, xo, 1], relay.at[1], sum_sems.at[1], x_last)
    both_chunks(xn)
    send(part_ref.at[:, xn, 1], arrived.at[0], sum_sems.at[2], x_next)
    both_chunks(xl)
    send(part_ref.at[:, xl, 0], arrived.at[1], sum_sems.at[3], x_last)
    landed(relay.at[0], sum_sems.at[0])
    passed[0] = (part_ref[:, xn, 0].astype(f32) + relay[0].astype(f32)).astype(bf16)
    send(passed.at[0], arrived.at[2], sum_sems.at[4], x_next)
    landed(relay.at[1], sum_sems.at[1])
    passed[1] = (part_ref[:, xl, 1].astype(f32) + relay[1].astype(f32)).astype(bf16)
    send(passed.at[1], arrived.at[3], sum_sems.at[5], x_last)
    both_chunks(x)
    landed(arrived.at[0], sum_sems.at[2])
    landed(arrived.at[1], sum_sems.at[3])
    landed(arrived.at[2], sum_sems.at[4])
    landed(arrived.at[3], sum_sems.at[5])

    def x_total(y_hi, half):
        first, second = (2, 1) if half == 0 else (0, 3)
        return (
            part_ref[y_hi, x, half].astype(f32)
            + arrived[first, y_hi].astype(f32)
            + arrived[second, y_hi].astype(f32)
        )

    for half in range(2):
        plane_sum[half] = x_total(1 - y_hi, half).astype(bf16)
    send(plane_sum, other, sum_sems.at[6], facing)
    landed(other, sum_sems.at[6])
    mine = everyone.at[z, y, core]
    for half in range(2):
        total = x_total(y_hi, half) + other[half].astype(f32)
        everyone[z, y, core, half] = total.astype(bf16)

    send(mine, mine, side_sems.at[0], beside)
    send(mine, mine, side_sems.at[1], sibling)
    upper = lambda zz: everyone.at[zz, :, core, 0]
    lower = lambda zz, yy: everyone.at[zz, yy, core, 1]
    send(lower(z, y), lower(z, y), ring_sems.at[1, 0, 1], z_next)
    send(lower(z, y), lower(z, y), ring_sems.at[1, 1, 1], z_last)
    theirs = everyone.at[z, 1 - y, core]
    landed(theirs, side_sems.at[0])
    send(upper(z), upper(z), ring_sems.at[0, 0, 1], z_next)
    send(upper(z), upper(z), ring_sems.at[0, 1, 1], z_last)
    send(theirs, theirs, side_sems.at[2], sibling)

    longest = {(0, 0): n_z // 2, (0, 1): n_z // 2 - 1, (1, 0): n_z // 2 - 1, (1, 1): n_z // 2}

    def ring_step(step):
        for half in (1, 0):
            for way in (0, 1):
                if step > longest[half, way]:
                    continue
                origin = (z + n_z - step) % n_z if way == 0 else (z + step) % n_z
                piece = upper(origin) if half == 0 else lower(origin, y)
                landed(piece, ring_sems.at[half, way, step])
                if step < longest[half, way]:
                    send(piece, piece, ring_sems.at[half, way, step + 1], z_next if way == 0 else z_last)
                if half == 1:
                    send(piece, piece, ring_sems.at[2, way, step], beside)
                send(piece, piece, ring_sems.at[3 + half, way, step], sibling)

    def side_step(step):
        for way in (0, 1):
            if step > longest[1, way]:
                continue
            origin = (z + n_z - step) % n_z if way == 0 else (z + step) % n_z
            piece = lower(origin, 1 - y)
            landed(piece, ring_sems.at[2, way, step])
            send(piece, piece, ring_sems.at[5, way, step], sibling)

    def rest_step(step):
        if step == 0:
            for yy, spot in ((y, 1), (1 - y, 2)):
                landed(everyone.at[z, yy, 1 - core], side_sems.at[spot])
            return
        for way in (0, 1):
            origin = (z + n_z - step) % n_z if way == 0 else (z + step) % n_z
            if step <= longest[0, way]:
                landed(everyone.at[origin, :, 1 - core, 0], ring_sems.at[3, way, step])
            if step <= longest[1, way]:
                landed(everyone.at[origin, y, 1 - core, 1], ring_sems.at[4, way, step])
                landed(everyone.at[origin, 1 - y, 1 - core, 1], ring_sems.at[5, way, step])

    dx = (x + 4 - z % 4) % 4
    root = z // 4 == y_hi
    first = core * quarter
    eighth = quarter // 2

    def group_origins(step):
        if step == 0:
            return ((z, 0),)
        if step == n_z // 2:
            return (((z + step) % n_z, step),)
        return (((z + n_z - step) % n_z, step), ((z + step) % n_z, n_z - step))

    held = lambda zz, part: left.at[zz, :, :, pl.ds(part * eighth, eighth)]
    late = []

    def left_step(step):
        for zz, tag in group_origins(step):
            base = len(sends)

            def numbered(source, target, arrival, device, offset):
                return pltpu.make_async_remote_copy(
                    src_ref=source, dst_ref=target, send_sem=send_sems.at[base + offset],
                    recv_sem=arrival, device_id=device, device_id_type=MESH,
                )

            rows_at = lambda half, start, count: everyone.at[zz, :, :, half, pl.ds(start, count)]
            to_next = numbered(held(zz, 0), held(zz, 0), left_sems.at[0, tag], x_next, 0)
            to_last = numbered(held(zz, 1), held(zz, 1), left_sems.at[1, tag], x_last, 1)
            to_across = numbered(
                rows_at(1 - y, first, quarter), left.at[zz], left_sems.at[2, tag], across, 2
            )

            @pl.when(dx == 0)
            def _():
                @pl.when(root)
                def _():
                    to_across.start()
                    left[zz] = everyone[zz, :, :, y, pl.ds(first, quarter)]

                @pl.when(jnp.logical_not(root))
                def _():
                    landed(left.at[zz], left_sems.at[2, tag])

                to_next.start()
                to_last.start()

            @pl.when((dx == 1) | (dx == 2))
            def _():
                landed(held(zz, 0), left_sems.at[0, tag])
                to_next.start()

            @pl.when((dx == 3) | (dx == 2))
            def _():
                landed(held(zz, 1), left_sems.at[1, tag])
                to_last.start()

            late.append((zz, tag, to_next, to_last, to_across))
            sends.extend([None] * 3)

    rest_step(0)
    ring_step(1)
    left_step(0)
    ring_step(2)
    side_step(1)
    rest_step(1)
    left_step(1)
    ring_step(3)
    side_step(2)
    rest_step(2)
    left_step(2)
    ring_step(4)
    side_step(3)
    rest_step(3)
    left_step(3)
    side_step(4)
    rest_step(4)
    left_step(4)

    def group_product(k, carry):
        odd = k % 2
        tag = (odd * ((k + 1) // 2) + (1 - odd) * (n_z - k // 2)) % n_z
        zz = (z + n_z - tag) % n_z

        @pl.when(dx == 1)
        def _():
            landed(held(zz, 1), left_sems.at[1, tag])

        @pl.when(dx == 3)
        def _():
            landed(held(zz, 0), left_sems.at[0, tag])

        straight = [left[zz, i // 2, i % 2].astype(f32) for i in range(4)]
        side = jnp.concatenate([turned(value) for value in straight], axis=1)
        both = jnp.concatenate([-jnp.concatenate(straight, axis=1), side], axis=0)
        both = both.astype(bf16)
        for half in range(2):
            right = jnp.concatenate([everyone[zz, i // 2, i % 2, half] for i in range(4)], axis=1)
            product = lax.dot_general(
                both, right, (((1,), (1,)), ((), ())), preferred_element_type=f32
            )
            for part in range(2):
                spot = (part, slice(None), slice(half * half_rows, (half + 1) * half_rows))
                out_ref[spot] += product[part * quarter : (part + 1) * quarter]
        return carry

    lax.fori_loop(0, n_z, group_product, 0)

    for moving in sends:
        if moving is not None:
            moving.wait_send()
    for zz, tag, to_next, to_last, to_across in late:
        pl.when(dx != 3)(lambda: to_next.wait_send())
        pl.when(dx != 1)(lambda: to_last.wait_send())
        pl.when((dx == 0) & root)(lambda: to_across.wait_send())

    def sent_plane(x, carry):
        to_behind(occ_ref.at[:, x], far.at[x], x).wait_send()
        return carry

    def passed_plane(x, carry):
        to_sibling(occ_ref.at[:, x], near.at[x], x).wait_send()
        return carry

    def passed_far(x, carry):
        to_sibling(far.at[x], near.at[x], x).wait_send()
        return carry

    to_behind(level_ref, far_level, PLANES).wait_send()
    lax.fori_loop(0, PLANES, sent_plane, 0)

    @pl.when(core == 1)
    def _():
        to_sibling(level_ref, near_level, PLANES).wait_send()
        lax.fori_loop(0, PLANES, passed_plane, 0)

    @pl.when(core == 0)
    def _():
        to_sibling(far_level, near_level, PLANES).wait_send()
        lax.fori_loop(0, PLANES, passed_far, 0)


def whole_response(occ, emp, gvectors, energies, ztab, xytabs, n_z):
    bf16, f32 = jnp.bfloat16, jnp.float32
    half = NG // 16
    anywhere, vmem = pl.BlockSpec(memory_space=pl.ANY), pl.BlockSpec(memory_space=pltpu.VMEM)
    return pl.pallas_call(
        response_kernel,
        out_shape=jax.ShapeDtypeStruct((2, half // 2, 2 * half), f32),
        in_specs=[anywhere, anywhere, vmem, vmem, vmem, anywhere, anywhere],
        out_specs=vmem,
        scratch_shapes=[
            pltpu.VMEM((PLANES, 2, 4, CELLS), bf16),
            pltpu.VMEM((PLANES, 2, 4, CELLS), bf16),
            pltpu.VMEM((8, LANES), f32),
            pltpu.VMEM((8, LANES), f32),
            pltpu.VMEM((8, LANES), f32),
            pltpu.VMEM((2, PLANES, 8, CELLS), bf16),
            pltpu.VMEM((Z_ROWS, GROUP_CELLS), bf16),
            pltpu.VMEM((PLANES // BATCH, WAVE_ROWS, DEPTH), bf16),
            pltpu.VMEM((16, CELLS), f32),
            pltpu.VMEM((GROUPS * LANES, GROUP_CELLS), bf16),
            pltpu.VMEM((Z_ROWS, GROUPS * LANES), f32),
            pltpu.VMEM((Q_SLOTS // 2, DEPTH, 2 * LANES), bf16),
            pltpu.VMEM((Q_SLOTS * WAVE_ROWS, LANES), f32),
            pltpu.VMEM((1024, LANES), f32),
            pltpu.VMEM((1, NG), jnp.int32),
            pltpu.SMEM((1, NG), jnp.int32),
            pltpu.VMEM((1, NG), f32),
            pltpu.VMEM((2, 4, 2, half, LANES), bf16),
            pltpu.VMEM((n_z, 2, 2, 2, half, LANES), bf16),
            pltpu.VMEM((n_z, 2, 2, half // 2, LANES), bf16),
            pltpu.VMEM((2, 2, half, LANES), bf16),
            pltpu.VMEM((2, 2, half, LANES), bf16),
            pltpu.VMEM((4, 2, half, LANES), bf16),
            pltpu.VMEM((2, half, LANES), bf16),
            pltpu.VMEM((2, half, LANES), bf16),
            pltpu.SemaphoreType.DMA((PLANES + 1,)),
            pltpu.SemaphoreType.DMA((PLANES + 1,)),
            pltpu.SemaphoreType.DMA((PLANES + 1,)),
            pltpu.SemaphoreType.DMA((PLANES + 1,)),
            pltpu.SemaphoreType.DMA((4,)),
            pltpu.SemaphoreType.DMA((128,)),
            pltpu.SemaphoreType.DMA((8,)),
            pltpu.SemaphoreType.DMA((6, 2, n_z // 2 + 1)),
            pltpu.SemaphoreType.DMA((3,)),
            pltpu.SemaphoreType.DMA((3, n_z)),
        ],
        compiler_params=pltpu.CompilerParams(
            collective_id=0, has_side_effects=True, vmem_limit_bytes=60 * 2**20
        ),
        cost_estimate=pl.CostEstimate(
            flops=16_000_000_000, bytes_accessed=12_000_000, transcendentals=0
        ),
    )(occ, emp, gvectors, *energies, ztab, xytabs)


def shards(ztab, xytabs, occupied_states, empty_states, occ_energy, empty_energy, gvectors):
    occ = jnp.transpose(occupied_states, (0, 2, 1, 3))
    emp = jnp.transpose(empty_states, (0, 2, 1, 3))
    energies = occ_energy.reshape(1, -1), empty_energy.reshape(1, -1)
    n_z = lax.axis_size("blk") // 4
    out = whole_response(occ, emp, gvectors, energies, ztab, xytabs, n_z)
    return jnp.transpose(out, (1, 0, 2))


def solution(mesh):
    ztab = z_table()
    xytabs = plane_table(mesh.shape["pw"])
    return jax.shard_map(
        lambda *args: shards(jnp.asarray(ztab), jnp.asarray(xytabs), *args),
        mesh=mesh,
        in_specs=(P(None, "blk", "pw", None), P(None, "blk", "pw", None), P("blk"), P("blk"), P()),
        out_specs=P("blk", None, "pw"),
        check_vma=False,
    )
```

```python
import functools
import math

import jax
import jax.numpy as jnp
import numpy as np
from jax import lax
from jax.experimental import pallas as pl
from jax.experimental.pallas import tpu as pltpu
from jax.sharding import PartitionSpec as P
import ml_dtypes

GX = 72
GY = 72
GZ = 144
KMAX = 16
SIDE = 2 * KMAX + 1
PLANES = 9
CELLS = GY * GZ
NG = 4096
GROUPS = 9
GROUP_CELLS = 8 * GZ
Z_ROWS = SIDE * 8
ROWS_X = 80
BATCH = 3
DEPTH = BATCH * ROWS_X
HALF = (SIDE * SIDE + 1) // 2
WAVE_ROWS = 1096
Q_SLOTS = 34
LANES = 128
omega_shift = 0.5


def z_table():
    z = np.arange(GZ)
    out = np.zeros((Z_ROWS, GROUP_CELLS), np.float64)
    for q in range(KMAX + 1):
        angle = 2 * np.pi * ((q * z) % GZ) / GZ
        for y in range(8):
            out[q * 8 + y, y * GZ : (y + 1) * GZ] = np.cos(angle)
            if q:
                out[(KMAX + q) * 8 + y, y * GZ : (y + 1) * GZ] = np.sin(angle)
    return out.astype(np.float32).astype(ml_dtypes.bfloat16)


def plane_table(groups):
    h = np.arange(HALF)
    p = (h + KMAX) // SIDE
    a = h - SIDE * p
    out = np.zeros((groups, WAVE_ROWS, PLANES, ROWS_X), np.float64)
    y = np.arange(GY)
    for group in range(groups):
        for plane in range(PLANES):
            x = group * PLANES + plane
            steps = (p[:, None] * y[None, :] + a[:, None] * x) % GX
            out[group, 0 : 2 * HALF : 2, plane, :GY] = np.cos(2 * np.pi * steps / GX)
            out[group, 1 : 2 * HALF : 2, plane, :GY] = np.sin(2 * np.pi * steps / GX)
    out = out.reshape(groups, WAVE_ROWS, PLANES // BATCH, DEPTH).transpose(0, 2, 1, 3)
    return out.astype(np.float32).astype(ml_dtypes.bfloat16)


def turned(value):
    lane = lax.broadcasted_iota(jnp.int32, value.shape, 1)
    ahead = pltpu.roll(value, LANES - 8, 1)
    behind = pltpu.roll(value, 8, 1)
    return jnp.where((lane & 8) == 0, ahead, -behind)


MESH = pl.DeviceIdType.MESH


def density_kernel(
    occ_ref, emp_ref, wave_ref, occ_energy_ref, emp_energy_ref, ztab_ref, xytab_ref, out_ref,
    near, far, level_ref, near_level, far_level, emp, ztab, xytab, occ_f, pairs, depth_out, sections, waves,
    picked, index_v, index_s, sign_v, ahead_sems, far_sems, pass_sems, near_sems, load_sems,
):
    blk, pw = lax.axis_index("blk"), lax.axis_index("pw")
    count = lax.axis_size("blk")
    core = blk % 2
    behind, ahead = {"blk": (blk + count - 2) % count}, {"blk": (blk + 2) % count}
    sibling = {"blk": blk + 1 - 2 * core}
    barrier = pltpu.get_barrier_semaphore()
    for device in (behind, ahead, sibling):
        pl.semaphore_signal(barrier, inc=1, device_id=device, device_id_type=MESH)
    pl.semaphore_wait(barrier, 3)

    def to_behind(source, target, spot):
        return pltpu.make_async_remote_copy(
            src_ref=source, dst_ref=target, send_sem=ahead_sems.at[spot],
            recv_sem=far_sems.at[spot], device_id=behind, device_id_type=MESH,
        )

    def to_sibling(source, target, spot):
        return pltpu.make_async_remote_copy(
            src_ref=source, dst_ref=target, send_sem=pass_sems.at[spot],
            recv_sem=near_sems.at[spot], device_id=sibling, device_id_type=MESH,
        )

    def landed(target, arrival):
        pltpu.make_async_copy(target, target, arrival).wait()

    def send_plane(x, carry):
        to_behind(occ_ref.at[:, x], far.at[x], x).start()
        return carry

    def pass_plane(x, carry):
        to_sibling(occ_ref.at[:, x], near.at[x], x).start()
        return carry

    lax.fori_loop(0, PLANES, send_plane, 0)
    lane = lax.broadcasted_iota(jnp.int32, (8, LANES), 1)
    occ_energy = occ_energy_ref[...].astype(jnp.float32)
    emp_energy = emp_energy_ref[...].astype(jnp.float32)
    spread = jnp.zeros((8, LANES), jnp.float32)
    for v in range(4):
        spread = jnp.where((lane // 16) % 4 == v, occ_energy[:, v : v + 1], spread)
    level_ref[...] = spread
    emp_level = jnp.zeros((8, LANES), jnp.float32)
    for c in range(8):
        emp_level = jnp.where(lane % 8 == c, emp_energy[:, c : c + 1], emp_level)
    to_behind(level_ref, far_level, PLANES).start()

    @pl.when(core == 1)
    def _():
        to_sibling(level_ref, near_level, PLANES).start()
        lax.fori_loop(0, PLANES, pass_plane, 0)

    loads = [
        pltpu.make_async_copy(emp_ref, emp, load_sems.at[0]),
        pltpu.make_async_copy(ztab_ref, ztab, load_sems.at[1]),
        pltpu.make_async_copy(xytab_ref.at[pw], xytab, load_sems.at[2]),
    ]
    for load in loads:
        load.start()

    flat = SIDE * wave_ref[1:2, :] + wave_ref[0:1, :]
    index_v[...] = (wave_ref[2:3, :] + KMAX) * WAVE_ROWS + 2 * jnp.abs(flat)
    sign_v[...] = jnp.where(flat < 0, -1.0, 1.0).astype(jnp.float32)
    index_move = pltpu.make_async_copy(index_v, index_s, load_sems.at[3])
    index_move.start()
    landed(far_level, far_sems.at[PLANES])

    @pl.when(core == 0)
    def _():
        to_sibling(far_level, near_level, PLANES).start()

    for load in loads:
        load.wait()
    index_move.wait()

    def group_pairs(x, group):
        for part in range(3):
            start = pl.multiple_of(group * GROUP_CELLS + part * 384, 128)
            cells = pl.ds(start, 384)
            emp_re = emp[0, x, :, cells].astype(jnp.float32)
            emp_im = emp[1, x, :, cells].astype(jnp.float32)
            for v in range(8):
                row = v if v < 4 else v + 4
                occ_re = occ_f[row : row + 1, cells]
                occ_im = occ_f[row + 4 : row + 5, cells]
                both = jnp.concatenate(
                    [occ_re * emp_re + occ_im * emp_im, occ_re * emp_im - occ_im * emp_re], axis=0
                )
                rows = pl.ds(pl.multiple_of(group * LANES + v * 16, 16), 16)
                pairs[rows, part * 384 : part * 384 + 384] = both.astype(jnp.bfloat16)

    blank = jnp.zeros((ROWS_X - GY, LANES), jnp.float32)

    def rows_of(first):
        parts = [depth_out[first : first + 8, t * LANES : (t + 1) * LANES] for t in range(GROUPS)]
        return jnp.concatenate(parts + [blank], axis=0)

    def one_plane(x, spot):
        landed(far.at[x], far_sems.at[x])

        @pl.when(core == 0)
        def _():
            to_sibling(far.at[x], near.at[x], x).start()

        landed(near.at[x], near_sems.at[x])
        for part in range(2):
            occ_f[part * 4 : part * 4 + 4, :] = near[x, part].astype(jnp.float32)
            occ_f[part * 4 + 8 : part * 4 + 12, :] = far[x, part].astype(jnp.float32)

        def each_group(group, carry):
            group_pairs(x, group)
            return carry

        lax.fori_loop(0, GROUPS, each_group, 0)
        depth_out[...] = lax.dot_general(
            ztab[...], pairs[...], (((1,), (1,)), ((), ())), preferred_element_type=jnp.float32
        )
        rows = pl.ds(pl.multiple_of(spot * ROWS_X, 16), ROWS_X)

        def put(slot, value):
            half = slot % 2
            sections[slot // 2, rows, half * LANES : (half + 1) * LANES] = value.astype(jnp.bfloat16)

        put(KMAX, rows_of(0))
        for q in range(1, KMAX + 1):
            cosine = rows_of(q * 8)
            sine = turned(rows_of((KMAX + q) * 8))
            put(KMAX + q, cosine + sine)
            put(KMAX - q, cosine - sine)

    sections[Q_SLOTS // 2 - 1, :, LANES:] = jnp.zeros((DEPTH, LANES), jnp.bfloat16)

    def clear(k, carry):
        rows = pl.ds(pl.multiple_of(k * WAVE_ROWS, 8), WAVE_ROWS)
        waves[rows, :] = jnp.zeros((WAVE_ROWS, LANES), jnp.float32)
        return carry

    lax.fori_loop(0, Q_SLOTS, clear, 0)

    def each_batch(batch, carry):
        def each_plane(spot, carry):
            one_plane(batch * BATCH + spot, spot)
            return carry

        lax.fori_loop(0, BATCH, each_plane, 0)

        def slot_pair(k, carry):
            product = jnp.dot(xytab[batch], sections[k], preferred_element_type=jnp.float32)
            first = pl.multiple_of(k * 2 * WAVE_ROWS, 8)
            for half in range(2):
                rows = pl.ds(first + half * WAVE_ROWS, WAVE_ROWS)
                waves[rows, :] += product[:, half * LANES : (half + 1) * LANES]
            return carry

        lax.fori_loop(0, Q_SLOTS // 2, slot_pair, 0)
        return carry

    lax.fori_loop(0, PLANES // BATCH, each_batch, 0)
    landed(near_level, near_sems.at[PLANES])
    occ_level = jnp.where(lane < LANES // 2, near_level[...], far_level[...])
    scale = jnp.sqrt(2.0 / (emp_level - occ_level + omega_shift))[0:1]

    def chunk(w, carry):
        def pick(step, carry):
            first = step * 16
            for i in range(16):
                row = index_s[0, w * 512 + first + i]
                picked[pl.ds((first + i) * 2, 2), :] = waves[pl.ds(row, 2), :]
            return carry

        lax.fori_loop(0, 32, pick, 0)
        for part in range(4):
            cosine = picked[pl.ds(part * 256, 128, stride=2), :]
            sine = picked[pl.ds(part * 256 + 1, 128, stride=2), :]
            first = pl.multiple_of(w * 512 + part * 128, 128)
            sign = jnp.broadcast_to(sign_v[:, pl.ds(first, 128)], (128, LANES)).T
            total = (cosine + sign * turned(sine)) * scale
            out_ref[pl.ds(first, 128), :] = total.astype(out_ref.dtype)
        return carry

    lax.fori_loop(0, NG // 512, chunk, 0)

    def sent_plane(x, carry):
        to_behind(occ_ref.at[:, x], far.at[x], x).wait_send()
        return carry

    def passed_plane(x, carry):
        to_sibling(occ_ref.at[:, x], near.at[x], x).wait_send()
        return carry

    def passed_far(x, carry):
        to_sibling(far.at[x], near.at[x], x).wait_send()
        return carry

    to_behind(level_ref, far_level, PLANES).wait_send()
    lax.fori_loop(0, PLANES, sent_plane, 0)

    @pl.when(core == 1)
    def _():
        to_sibling(level_ref, near_level, PLANES).wait_send()
        lax.fori_loop(0, PLANES, passed_plane, 0)

    @pl.when(core == 0)
    def _():
        to_sibling(far_level, near_level, PLANES).wait_send()
        lax.fori_loop(0, PLANES, passed_far, 0)


def partial_density(occ, emp, gvectors, energies, ztab, xytabs):
    bf16, f32 = jnp.bfloat16, jnp.float32
    anywhere, vmem = pl.BlockSpec(memory_space=pl.ANY), pl.BlockSpec(memory_space=pltpu.VMEM)
    return pl.pallas_call(
        density_kernel,
        out_shape=jax.ShapeDtypeStruct((NG, LANES), bf16),
        in_specs=[anywhere, anywhere, vmem, vmem, vmem, anywhere, anywhere],
        out_specs=vmem,
        scratch_shapes=[
            pltpu.VMEM((PLANES, 2, 4, CELLS), bf16),
            pltpu.VMEM((PLANES, 2, 4, CELLS), bf16),
            pltpu.VMEM((8, LANES), f32),
            pltpu.VMEM((8, LANES), f32),
            pltpu.VMEM((8, LANES), f32),
            pltpu.VMEM((2, PLANES, 8, CELLS), bf16),
            pltpu.VMEM((Z_ROWS, GROUP_CELLS), bf16),
            pltpu.VMEM((PLANES // BATCH, WAVE_ROWS, DEPTH), bf16),
            pltpu.VMEM((16, CELLS), f32),
            pltpu.VMEM((GROUPS * LANES, GROUP_CELLS), bf16),
            pltpu.VMEM((Z_ROWS, GROUPS * LANES), f32),
            pltpu.VMEM((Q_SLOTS // 2, DEPTH, 2 * LANES), bf16),
            pltpu.VMEM((Q_SLOTS * WAVE_ROWS, LANES), f32),
            pltpu.VMEM((1024, LANES), f32),
            pltpu.VMEM((1, NG), jnp.int32),
            pltpu.SMEM((1, NG), jnp.int32),
            pltpu.VMEM((1, NG), f32),
            pltpu.SemaphoreType.DMA((PLANES + 1,)),
            pltpu.SemaphoreType.DMA((PLANES + 1,)),
            pltpu.SemaphoreType.DMA((PLANES + 1,)),
            pltpu.SemaphoreType.DMA((PLANES + 1,)),
            pltpu.SemaphoreType.DMA((4,)),
        ],
        compiler_params=pltpu.CompilerParams(
            collective_id=1, has_side_effects=True, vmem_limit_bytes=60 * 2**20
        ),
        cost_estimate=pl.CostEstimate(
            flops=15_000_000_000, bytes_accessed=12_000_000, transcendentals=0
        ),
    )(occ, emp, gvectors, *energies, ztab, xytabs)


def share_kernel(rows, part_ref, out_ref, everyone, left, relay, passed, arrived, own, plane_sum,
                 other, send_sems, sum_sems, own_sems, ring_sems, side_sems, left_sems):
    half_rows, quarter = rows // 2, rows // 4
    blk, pw = lax.axis_index("blk"), lax.axis_index("pw")
    z, y, core = blk // 4, (blk // 2) % 2, blk % 2
    x, y_hi = pw % 4, pw // 4
    n_z = lax.axis_size("blk") // 4

    def place(z=z, y=y, core=core, x=x, y_hi=y_hi):
        return {"blk": z * 4 + y * 2 + core, "pw": y_hi * 4 + x}

    x_next, x_last = place(x=(x + 1) % 4), place(x=(x + 3) % 4)
    z_next, z_last = place(z=(z + 1) % n_z), place(z=(z + n_z - 1) % n_z)
    sibling, beside = place(core=1 - core), place(y=1 - y)
    facing, across = place(y_hi=1 - y_hi), place(y=1 - y, y_hi=1 - y_hi)

    sends = []

    def copy(source, target, arrival, device):
        return pltpu.make_async_remote_copy(
            src_ref=source, dst_ref=target, send_sem=send_sems.at[len(sends)], recv_sem=arrival,
            device_id=device, device_id_type=MESH,
        )

    def send(source, target, arrival, device):
        moving = copy(source, target, arrival, device)
        moving.start()
        sends.append(moving)

    def landed(target, arrival):
        pltpu.make_async_copy(target, target, arrival).wait()

    barrier = pltpu.get_barrier_semaphore()
    neighbours = (x_next, x_last, z_next, z_last, sibling, beside, facing, across)
    for device in neighbours:
        pl.semaphore_signal(barrier, inc=1, device_id=device, device_id_type=MESH)
    pl.semaphore_wait(barrier, len(neighbours))

    xn, xl, xo = (x + 1) % 4, (x + 3) % 4, (x + 2) % 4
    send(part_ref.at[:, xo, 0], relay.at[0], sum_sems.at[0], x_next)
    send(part_ref.at[:, xo, 1], relay.at[1], sum_sems.at[1], x_last)
    send(part_ref.at[:, xn, 1], arrived.at[0], sum_sems.at[2], x_next)
    send(part_ref.at[:, xl, 0], arrived.at[1], sum_sems.at[3], x_last)
    f32 = jnp.float32
    moves = [
        pltpu.make_async_copy(part_ref.at[:, xn, 0], passed.at[0], own_sems.at[0]),
        pltpu.make_async_copy(part_ref.at[:, xl, 1], passed.at[1], own_sems.at[1]),
        pltpu.make_async_copy(part_ref.at[:, x], own, own_sems.at[2]),
    ]
    for move in moves:
        move.start()
    out_ref[...] = jnp.zeros_like(out_ref)
    for move in moves:
        move.wait()
    landed(relay.at[0], sum_sems.at[0])
    passed[0] = (passed[0].astype(f32) + relay[0].astype(f32)).astype(jnp.bfloat16)
    send(passed.at[0], arrived.at[2], sum_sems.at[4], x_next)
    landed(relay.at[1], sum_sems.at[1])
    passed[1] = (passed[1].astype(f32) + relay[1].astype(f32)).astype(jnp.bfloat16)
    send(passed.at[1], arrived.at[3], sum_sems.at[5], x_last)
    landed(arrived.at[0], sum_sems.at[2])
    landed(arrived.at[1], sum_sems.at[3])
    landed(arrived.at[2], sum_sems.at[4])
    landed(arrived.at[3], sum_sems.at[5])

    def x_total(y_hi, half):
        first, second = (2, 1) if half == 0 else (0, 3)
        return (
            own[y_hi, half].astype(f32)
            + arrived[first, y_hi].astype(f32)
            + arrived[second, y_hi].astype(f32)
        )

    for half in range(2):
        plane_sum[half] = x_total(1 - y_hi, half).astype(jnp.bfloat16)
    send(plane_sum, other, sum_sems.at[6], facing)
    landed(other, sum_sems.at[6])
    mine = everyone.at[z, y, core]
    for half in range(2):
        total = x_total(y_hi, half) + other[half].astype(f32)
        everyone[z, y, core, half] = total.astype(jnp.bfloat16)

    send(mine, mine, side_sems.at[0], beside)
    send(mine, mine, side_sems.at[1], sibling)
    upper = lambda zz: everyone.at[zz, :, core, 0]
    lower = lambda zz, yy: everyone.at[zz, yy, core, 1]
    send(lower(z, y), lower(z, y), ring_sems.at[1, 0, 1], z_next)
    send(lower(z, y), lower(z, y), ring_sems.at[1, 1, 1], z_last)
    theirs = everyone.at[z, 1 - y, core]
    landed(theirs, side_sems.at[0])
    send(upper(z), upper(z), ring_sems.at[0, 0, 1], z_next)
    send(upper(z), upper(z), ring_sems.at[0, 1, 1], z_last)
    send(theirs, theirs, side_sems.at[2], sibling)

    longest = {(0, 0): n_z // 2, (0, 1): n_z // 2 - 1, (1, 0): n_z // 2 - 1, (1, 1): n_z // 2}

    def ring_step(step):
        for half in (1, 0):
            for way in (0, 1):
                if step > longest[half, way]:
                    continue
                origin = (z + n_z - step) % n_z if way == 0 else (z + step) % n_z
                piece = upper(origin) if half == 0 else lower(origin, y)
                landed(piece, ring_sems.at[half, way, step])
                if step < longest[half, way]:
                    send(piece, piece, ring_sems.at[half, way, step + 1], z_next if way == 0 else z_last)
                if half == 1:
                    send(piece, piece, ring_sems.at[2, way, step], beside)
                send(piece, piece, ring_sems.at[3 + half, way, step], sibling)

    def side_step(step):
        for way in (0, 1):
            if step > longest[1, way]:
                continue
            origin = (z + n_z - step) % n_z if way == 0 else (z + step) % n_z
            piece = lower(origin, 1 - y)
            landed(piece, ring_sems.at[2, way, step])
            send(piece, piece, ring_sems.at[5, way, step], sibling)

    def rest_step(step):
        if step == 0:
            for yy, spot in ((y, 1), (1 - y, 2)):
                landed(everyone.at[z, yy, 1 - core], side_sems.at[spot])
            return
        for way in (0, 1):
            origin = (z + n_z - step) % n_z if way == 0 else (z + step) % n_z
            if step <= longest[0, way]:
                landed(everyone.at[origin, :, 1 - core, 0], ring_sems.at[3, way, step])
            if step <= longest[1, way]:
                landed(everyone.at[origin, y, 1 - core, 1], ring_sems.at[4, way, step])
                landed(everyone.at[origin, 1 - y, 1 - core, 1], ring_sems.at[5, way, step])

    dx = (x + 4 - z % 4) % 4
    root = z // 4 == y_hi
    first = core * quarter
    eighth = quarter // 2

    def group_origins(step):
        if step == 0:
            return ((z, 0),)
        if step == n_z // 2:
            return (((z + step) % n_z, step),)
        return (((z + n_z - step) % n_z, step), ((z + step) % n_z, n_z - step))

    held = lambda zz, part: left.at[zz, :, :, pl.ds(part * eighth, eighth)]
    late = []

    def left_copies(step):
        made = []
        for zz, tag in group_origins(step):
            base = len(sends)

            def numbered(source, target, arrival, device, offset):
                return pltpu.make_async_remote_copy(
                    src_ref=source, dst_ref=target, send_sem=send_sems.at[base + offset],
                    recv_sem=arrival, device_id=device, device_id_type=MESH,
                )

            there = everyone.at[zz, :, :, 1 - y, pl.ds(first, quarter)]
            to_next = numbered(held(zz, 0), held(zz, 0), left_sems.at[0, tag], x_next, 0)
            to_last = numbered(held(zz, 1), held(zz, 1), left_sems.at[1, tag], x_last, 1)
            to_across = numbered(there, left.at[zz], left_sems.at[2, tag], across, 2)
            made.append((zz, tag, to_next, to_last, to_across))
            sends.extend([None] * 3)
        late.extend(made)
        return made

    def left_from_root(made):
        @pl.when((dx == 0) & root)
        def _():
            for zz, tag, to_next, to_last, to_across in made:
                to_across.start()
                left[zz] = everyone[zz, :, :, y, pl.ds(first, quarter)]
                to_next.start()
                to_last.start()

    def left_onward(made):
        @pl.when((dx == 0) & jnp.logical_not(root))
        def _():
            for zz, tag, to_next, to_last, to_across in made:
                landed(left.at[zz], left_sems.at[2, tag])
                to_next.start()
                to_last.start()

        @pl.when(dx == 1)
        def _():
            for zz, tag, to_next, to_last, to_across in made:
                landed(held(zz, 0), left_sems.at[0, tag])
                to_next.start()

        @pl.when(dx == 3)
        def _():
            for zz, tag, to_next, to_last, to_across in made:
                landed(held(zz, 1), left_sems.at[1, tag])
                to_last.start()

    def left_middle(made):
        @pl.when(dx == 2)
        def _():
            for zz, tag, to_next, to_last, to_across in made:
                landed(held(zz, 0), left_sems.at[0, tag])
                to_next.start()
                landed(held(zz, 1), left_sems.at[1, tag])
                to_last.start()

    parts = [left_copies(step) for step in range(n_z // 2 + 1)]
    rest_step(0)
    ring_step(1)
    left_from_root(parts[0])
    ring_step(2)
    side_step(1)
    rest_step(1)
    left_from_root(parts[1])
    ring_step(3)
    side_step(2)
    rest_step(2)
    left_from_root(parts[2])
    left_onward(parts[0])
    ring_step(4)
    side_step(3)
    rest_step(3)
    left_from_root(parts[3])
    left_onward(parts[1])
    left_middle(parts[0])
    side_step(4)
    rest_step(4)
    left_from_root(parts[4])
    for step in range(2, n_z // 2 + 1):
        left_onward(parts[step])
        left_middle(parts[step - 1])
    left_middle(parts[n_z // 2])

    def group_product(k, carry):
        odd = k % 2
        tag = (odd * ((k + 1) // 2) + (1 - odd) * (n_z - k // 2)) % n_z
        zz = (z + n_z - tag) % n_z

        @pl.when(dx == 1)
        def _():
            landed(held(zz, 1), left_sems.at[1, tag])

        @pl.when(dx == 3)
        def _():
            landed(held(zz, 0), left_sems.at[0, tag])

        straight = [left[zz, i // 2, i % 2].astype(f32) for i in range(4)]
        side = jnp.concatenate([turned(value) for value in straight], axis=1)
        both = jnp.concatenate([-jnp.concatenate(straight, axis=1), side], axis=0)
        both = both.astype(jnp.bfloat16)
        for half in range(2):
            right = jnp.concatenate([everyone[zz, i // 2, i % 2, half] for i in range(4)], axis=1)
            product = lax.dot_general(
                both, right, (((1,), (1,)), ((), ())), preferred_element_type=f32
            )
            for part in range(2):
                spot = (part, slice(None), slice(half * half_rows, (half + 1) * half_rows))
                out_ref[spot] += product[part * quarter : (part + 1) * quarter]
        return carry

    lax.fori_loop(0, n_z, group_product, 0)

    for moving in sends:
        if moving is not None:
            moving.wait_send()
    for zz, tag, to_next, to_last, to_across in late:
        pl.when(dx != 3)(lambda: to_next.wait_send())
        pl.when(dx != 1)(lambda: to_last.wait_send())
        pl.when((dx == 0) & root)(lambda: to_across.wait_send())


def shared_response(partial_sums, n_z):
    rows = partial_sums.shape[0] // 8
    half = rows // 2
    bf16 = jnp.bfloat16
    part = partial_sums.reshape(2, 4, 2, half, LANES)
    return pl.pallas_call(
        functools.partial(share_kernel, rows),
        out_shape=jax.ShapeDtypeStruct((2, rows // 4, rows), jnp.float32),
        in_specs=[pl.BlockSpec(memory_space=pl.ANY)],
        out_specs=pl.BlockSpec(memory_space=pltpu.VMEM),
        scratch_shapes=[
            pltpu.VMEM((n_z, 2, 2, 2, half, LANES), bf16),
            pltpu.VMEM((n_z, 2, 2, rows // 4, LANES), bf16),
            pltpu.VMEM((2, 2, half, LANES), bf16),
            pltpu.VMEM((2, 2, half, LANES), bf16),
            pltpu.VMEM((4, 2, half, LANES), bf16),
            pltpu.VMEM((2, 2, half, LANES), bf16),
            pltpu.VMEM((2, half, LANES), bf16),
            pltpu.VMEM((2, half, LANES), bf16),
            pltpu.SemaphoreType.DMA((128,)),
            pltpu.SemaphoreType.DMA((8,)),
            pltpu.SemaphoreType.DMA((3,)),
            pltpu.SemaphoreType.DMA((6, 2, n_z // 2 + 1)),
            pltpu.SemaphoreType.DMA((3,)),
            pltpu.SemaphoreType.DMA((3, n_z)),
        ],
        compiler_params=pltpu.CompilerParams(
            collective_id=0, has_side_effects=True, vmem_limit_bytes=60 * 2**20
        ),
        cost_estimate=pl.CostEstimate(
            flops=1_100_000_000, bytes_accessed=2_000_000, transcendentals=0
        ),
    )(part)


def shards(ztab, xytabs, occupied_states, empty_states, occ_energy, empty_energy, gvectors):
    occ = jnp.transpose(occupied_states, (0, 2, 1, 3))
    emp = jnp.transpose(empty_states, (0, 2, 1, 3))
    energies = occ_energy.reshape(1, -1), empty_energy.reshape(1, -1)
    partial_sums = partial_density(occ, emp, gvectors, energies, ztab, xytabs)
    n_z = lax.axis_size("blk") // 4
    return jnp.transpose(shared_response(partial_sums, n_z), (1, 0, 2))


def solution(mesh):
    ztab = z_table()
    xytabs = plane_table(mesh.shape["pw"])
    return jax.shard_map(
        lambda *args: shards(jnp.asarray(ztab), jnp.asarray(xytabs), *args),
        mesh=mesh,
        in_specs=(P(None, "blk", "pw", None), P(None, "blk", "pw", None), P("blk"), P("blk"), P()),
        out_specs=P("blk", None, "pw"),
        check_vma=False,
    )
```

```python
import math

import jax
import jax.numpy as jnp
import numpy as np
from jax import lax
from jax.experimental import pallas as pl
from jax.experimental.pallas import tpu as pltpu
from jax.sharding import PartitionSpec as P
import ml_dtypes

GX = 72
GY = 72
GZ = 144
KMAX = 16
SIDE = 2 * KMAX + 1
PLANES = 9
CELLS = GY * GZ
NG = 4096
GROUPS = 9
GROUP_CELLS = 8 * GZ
Z_ROWS = SIDE * 8
ROWS_X = 80
BATCH = 3
DEPTH = BATCH * ROWS_X
HALF = (SIDE * SIDE + 1) // 2
WAVE_ROWS = 1096
Q_SLOTS = 34
LANES = 128
omega_shift = 0.5


def z_table():
    z = np.arange(GZ)
    out = np.zeros((Z_ROWS, GROUP_CELLS), np.float64)
    for q in range(KMAX + 1):
        angle = 2 * np.pi * ((q * z) % GZ) / GZ
        for y in range(8):
            out[q * 8 + y, y * GZ : (y + 1) * GZ] = np.cos(angle)
            if q:
                out[(KMAX + q) * 8 + y, y * GZ : (y + 1) * GZ] = np.sin(angle)
    return out.astype(np.float32).astype(ml_dtypes.bfloat16)


def plane_table(groups):
    h = np.arange(HALF)
    p = (h + KMAX) // SIDE
    a = h - SIDE * p
    out = np.zeros((groups, WAVE_ROWS, PLANES, ROWS_X), np.float64)
    y = np.arange(GY)
    for group in range(groups):
        for plane in range(PLANES):
            x = group * PLANES + plane
            steps = (p[:, None] * y[None, :] + a[:, None] * x) % GX
            out[group, 0 : 2 * HALF : 2, plane, :GY] = np.cos(2 * np.pi * steps / GX)
            out[group, 1 : 2 * HALF : 2, plane, :GY] = np.sin(2 * np.pi * steps / GX)
    out = out.reshape(groups, WAVE_ROWS, PLANES // BATCH, DEPTH).transpose(0, 2, 1, 3)
    return out.astype(np.float32).astype(ml_dtypes.bfloat16)


def turned(value):
    lane = lax.broadcasted_iota(jnp.int32, value.shape, 1)
    ahead = pltpu.roll(value, LANES - 8, 1)
    behind = pltpu.roll(value, 8, 1)
    return jnp.where((lane & 8) == 0, ahead, -behind)


MESH = pl.DeviceIdType.MESH


def response_kernel(
    occ_ref, emp_ref, wave_ref, occ_energy_ref, emp_energy_ref, ztab_ref, xytab_ref, out_ref,
    near, far, level_ref, near_level, far_level, emp, ztab, xytab, occ_f, pairs, depth_out, sections, waves,
    picked, index_v, index_s, sign_v, part_ref, everyone, left, relay, passed, arrived, plane_sum,
    other, ahead_sems, far_sems, pass_sems, near_sems, load_sems, send_sems, sum_sems, ring_sems,
    side_sems, left_sems,
):
    blk, pw = lax.axis_index("blk"), lax.axis_index("pw")
    count = lax.axis_size("blk")
    n_z = count // 4
    z, y, core = blk // 4, (blk // 2) % 2, blk % 2
    x, y_hi = pw % 4, pw // 4
    f32, bf16 = jnp.float32, jnp.bfloat16

    def place(z=z, y=y, core=core, x=x, y_hi=y_hi):
        return {"blk": z * 4 + y * 2 + core, "pw": y_hi * 4 + x}

    x_next, x_last = place(x=(x + 1) % 4), place(x=(x + 3) % 4)
    z_next, z_last = place(z=(z + 1) % n_z), place(z=(z + n_z - 1) % n_z)
    sibling, beside = place(core=1 - core), place(y=1 - y)
    facing, across = place(y_hi=1 - y_hi), place(y=1 - y, y_hi=1 - y_hi)
    behind = {"blk": (blk + count - 2) % count, "pw": pw}
    ahead = {"blk": (blk + 2) % count, "pw": pw}

    barrier = pltpu.get_barrier_semaphore()
    neighbours = (
        x_next, x_last, z_next, z_last, sibling, beside, facing, across, behind, ahead
    )
    for device in neighbours:
        pl.semaphore_signal(barrier, inc=1, device_id=device, device_id_type=MESH)
    pl.semaphore_wait(barrier, len(neighbours))

    def to_behind(source, target, spot):
        return pltpu.make_async_remote_copy(
            src_ref=source, dst_ref=target, send_sem=ahead_sems.at[spot],
            recv_sem=far_sems.at[spot], device_id=behind, device_id_type=MESH,
        )

    def to_sibling(source, target, spot):
        return pltpu.make_async_remote_copy(
            src_ref=source, dst_ref=target, send_sem=pass_sems.at[spot],
            recv_sem=near_sems.at[spot], device_id=sibling, device_id_type=MESH,
        )

    def landed(target, arrival):
        pltpu.make_async_copy(target, target, arrival).wait()

    def send_plane(x, carry):
        to_behind(occ_ref.at[:, x], far.at[x], x).start()
        return carry

    def pass_plane(x, carry):
        to_sibling(occ_ref.at[:, x], near.at[x], x).start()
        return carry

    lane = lax.broadcasted_iota(jnp.int32, (8, LANES), 1)
    occ_energy = occ_energy_ref[...].astype(f32)
    emp_energy = emp_energy_ref[...].astype(f32)
    spread = jnp.zeros((8, LANES), f32)
    for v in range(4):
        spread = jnp.where((lane // 16) % 4 == v, occ_energy[:, v : v + 1], spread)
    level_ref[...] = spread
    emp_level = jnp.zeros((8, LANES), f32)
    for c in range(8):
        emp_level = jnp.where(lane % 8 == c, emp_energy[:, c : c + 1], emp_level)
    to_behind(level_ref, far_level, PLANES).start()
    lax.fori_loop(0, PLANES, send_plane, 0)

    @pl.when(core == 1)
    def _():
        to_sibling(level_ref, near_level, PLANES).start()
        lax.fori_loop(0, PLANES, pass_plane, 0)

    loads = [
        pltpu.make_async_copy(emp_ref, emp, load_sems.at[0]),
        pltpu.make_async_copy(ztab_ref, ztab, load_sems.at[1]),
        pltpu.make_async_copy(xytab_ref.at[pw], xytab, load_sems.at[2]),
    ]
    for load in loads:
        load.start()

    flat = SIDE * wave_ref[1:2, :] + wave_ref[0:1, :]
    index_v[...] = (wave_ref[2:3, :] + KMAX) * WAVE_ROWS + 2 * jnp.abs(flat)
    sign_v[...] = jnp.where(flat < 0, -1.0, 1.0).astype(jnp.float32)
    index_move = pltpu.make_async_copy(index_v, index_s, load_sems.at[3])
    index_move.start()
    for load in loads:
        load.wait()
    index_move.wait()

    def group_pairs(x, group):
        for part in range(3):
            start = pl.multiple_of(group * GROUP_CELLS + part * 384, 128)
            cells = pl.ds(start, 384)
            emp_re = emp[0, x, :, cells].astype(jnp.float32)
            emp_im = emp[1, x, :, cells].astype(jnp.float32)
            for v in range(8):
                row = v if v < 4 else v + 4
                occ_re = occ_f[row : row + 1, cells]
                occ_im = occ_f[row + 4 : row + 5, cells]
                both = jnp.concatenate(
                    [occ_re * emp_re + occ_im * emp_im, occ_re * emp_im - occ_im * emp_re], axis=0
                )
                rows = pl.ds(pl.multiple_of(group * LANES + v * 16, 16), 16)
                pairs[rows, part * 384 : part * 384 + 384] = both.astype(jnp.bfloat16)

    blank = jnp.zeros((ROWS_X - GY, LANES), jnp.float32)

    def rows_of(first):
        parts = [depth_out[first : first + 8, t * LANES : (t + 1) * LANES] for t in range(GROUPS)]
        return jnp.concatenate(parts + [blank], axis=0)

    def one_plane(x, spot):
        landed(far.at[x], far_sems.at[x])

        @pl.when(core == 0)
        def _():
            to_sibling(far.at[x], near.at[x], x).start()

        landed(near.at[x], near_sems.at[x])
        for part in range(2):
            occ_f[part * 4 : part * 4 + 4, :] = near[x, part].astype(jnp.float32)
            occ_f[part * 4 + 8 : part * 4 + 12, :] = far[x, part].astype(jnp.float32)

        def each_group(group, carry):
            group_pairs(x, group)
            return carry

        lax.fori_loop(0, GROUPS, each_group, 0)
        depth_out[...] = lax.dot_general(
            ztab[...], pairs[...], (((1,), (1,)), ((), ())), preferred_element_type=jnp.float32
        )
        rows = pl.ds(pl.multiple_of(spot * ROWS_X, 16), ROWS_X)

        def put(slot, value):
            half = slot % 2
            sections[slot // 2, rows, half * LANES : (half + 1) * LANES] = value.astype(jnp.bfloat16)

        put(KMAX, rows_of(0))
        for q in range(1, KMAX + 1):
            cosine = rows_of(q * 8)
            sine = turned(rows_of((KMAX + q) * 8))
            put(KMAX + q, cosine + sine)
            put(KMAX - q, cosine - sine)

    sections[Q_SLOTS // 2 - 1, :, LANES:] = jnp.zeros((DEPTH, LANES), jnp.bfloat16)
    def clear(k, carry):
        rows = pl.ds(pl.multiple_of(k * WAVE_ROWS, 8), WAVE_ROWS)
        waves[rows, :] = jnp.zeros((WAVE_ROWS, LANES), jnp.float32)
        return carry

    lax.fori_loop(0, Q_SLOTS, clear, 0)
    landed(far_level, far_sems.at[PLANES])

    @pl.when(core == 0)
    def _():
        to_sibling(far_level, near_level, PLANES).start()

    def each_batch(batch, carry):
        def each_plane(spot, carry):
            one_plane(batch * BATCH + spot, spot)
            return carry

        lax.fori_loop(0, BATCH, each_plane, 0)

        def slot_pair(k, carry):
            product = jnp.dot(xytab[batch], sections[k], preferred_element_type=jnp.float32)
            first = pl.multiple_of(k * 2 * WAVE_ROWS, 8)
            for half in range(2):
                rows = pl.ds(first + half * WAVE_ROWS, WAVE_ROWS)
                waves[rows, :] += product[:, half * LANES : (half + 1) * LANES]
            return carry

        lax.fori_loop(0, Q_SLOTS // 2, slot_pair, 0)
        return carry

    lax.fori_loop(0, PLANES // BATCH, each_batch, 0)
    landed(near_level, near_sems.at[PLANES])
    occ_level = jnp.where(lane < LANES // 2, near_level[...], far_level[...])
    scale = jnp.sqrt(2.0 / (emp_level - occ_level + omega_shift))[0:1]

    def chunk(yy, xx):
        base = (yy * 4 + xx) * 512

        def pick(step, carry):
            first = step * 16
            for i in range(16):
                row = index_s[0, base + first + i]
                picked[pl.ds((first + i) * 2, 2), :] = waves[pl.ds(row, 2), :]
            return carry

        lax.fori_loop(0, 32, pick, 0)
        for part in range(4):
            cosine = picked[pl.ds(part * 256, 128, stride=2), :]
            sine = picked[pl.ds(part * 256 + 1, 128, stride=2), :]
            first = pl.multiple_of(base + part * 128, 128)
            sign = jnp.broadcast_to(sign_v[:, pl.ds(first, 128)], (128, LANES)).T
            total = (cosine + sign * turned(sine)) * scale
            rows = slice((part % 2) * 128, (part % 2) * 128 + 128)
            part_ref[yy, xx, part // 2, rows, :] = total.astype(bf16)

    def both_chunks(xx):
        def one(yy, carry):
            chunk(yy, xx)
            return carry

        lax.fori_loop(0, 2, one, 0)

    sends = []

    def copy(source, target, arrival, device):
        return pltpu.make_async_remote_copy(
            src_ref=source, dst_ref=target, send_sem=send_sems.at[len(sends)], recv_sem=arrival,
            device_id=device, device_id_type=MESH,
        )

    def send(source, target, arrival, device):
        moving = copy(source, target, arrival, device)
        moving.start()
        sends.append(moving)

    out_ref[...] = jnp.zeros_like(out_ref)
    rows = everyone.shape[4] * 2
    half_rows, quarter = rows // 2, rows // 4

    xn, xl, xo = (x + 1) % 4, (x + 3) % 4, (x + 2) % 4
    both_chunks(xo)
    send(part_ref.at[:, xo, 0], relay.at[0], sum_sems.at[0], x_next)
    send(part_ref.at[:, xo, 1], relay.at[1], sum_sems.at[1], x_last)
    both_chunks(xn)
    send(part_ref.at[:, xn, 1], arrived.at[0], sum_sems.at[2], x_next)
    both_chunks(xl)
    send(part_ref.at[:, xl, 0], arrived.at[1], sum_sems.at[3], x_last)
    landed(relay.at[0], sum_sems.at[0])
    passed[0] = (part_ref[:, xn, 0].astype(f32) + relay[0].astype(f32)).astype(bf16)
    send(passed.at[0], arrived.at[2], sum_sems.at[4], x_next)
    landed(relay.at[1], sum_sems.at[1])
    passed[1] = (part_ref[:, xl, 1].astype(f32) + relay[1].astype(f32)).astype(bf16)
    send(passed.at[1], arrived.at[3], sum_sems.at[5], x_last)
    both_chunks(x)
    landed(arrived.at[0], sum_sems.at[2])
    landed(arrived.at[1], sum_sems.at[3])
    landed(arrived.at[2], sum_sems.at[4])
    landed(arrived.at[3], sum_sems.at[5])

    def x_total(y_hi, half):
        first, second = (2, 1) if half == 0 else (0, 3)
        return (
            part_ref[y_hi, x, half].astype(f32)
            + arrived[first, y_hi].astype(f32)
            + arrived[second, y_hi].astype(f32)
        )

    for half in range(2):
        plane_sum[half] = x_total(1 - y_hi, half).astype(bf16)
    send(plane_sum, other, sum_sems.at[6], facing)
    landed(other, sum_sems.at[6])
    mine = everyone.at[z, y, core]
    for half in range(2):
        total = x_total(y_hi, half) + other[half].astype(f32)
        everyone[z, y, core, half] = total.astype(bf16)

    send(mine, mine, side_sems.at[0], beside)
    send(mine, mine, side_sems.at[1], sibling)
    upper = lambda zz: everyone.at[zz, :, core, 0]
    lower = lambda zz, yy: everyone.at[zz, yy, core, 1]
    send(lower(z, y), lower(z, y), ring_sems.at[1, 0, 1], z_next)
    send(lower(z, y), lower(z, y), ring_sems.at[1, 1, 1], z_last)
    theirs = everyone.at[z, 1 - y, core]
    landed(theirs, side_sems.at[0])
    send(upper(z), upper(z), ring_sems.at[0, 0, 1], z_next)
    send(upper(z), upper(z), ring_sems.at[0, 1, 1], z_last)
    send(theirs, theirs, side_sems.at[2], sibling)

    longest = {(0, 0): n_z // 2, (0, 1): n_z // 2 - 1, (1, 0): n_z // 2 - 1, (1, 1): n_z // 2}

    def ring_step(step):
        for half in (1, 0):
            for way in (0, 1):
                if step > longest[half, way]:
                    continue
                origin = (z + n_z - step) % n_z if way == 0 else (z + step) % n_z
                piece = upper(origin) if half == 0 else lower(origin, y)
                landed(piece, ring_sems.at[half, way, step])
                if step < longest[half, way]:
                    send(piece, piece, ring_sems.at[half, way, step + 1], z_next if way == 0 else z_last)
                if half == 1:
                    send(piece, piece, ring_sems.at[2, way, step], beside)
                send(piece, piece, ring_sems.at[3 + half, way, step], sibling)

    def side_step(step):
        for way in (0, 1):
            if step > longest[1, way]:
                continue
            origin = (z + n_z - step) % n_z if way == 0 else (z + step) % n_z
            piece = lower(origin, 1 - y)
            landed(piece, ring_sems.at[2, way, step])
            send(piece, piece, ring_sems.at[5, way, step], sibling)

    def rest_step(step):
        if step == 0:
            for yy, spot in ((y, 1), (1 - y, 2)):
                landed(everyone.at[z, yy, 1 - core], side_sems.at[spot])
            return
        for way in (0, 1):
            origin = (z + n_z - step) % n_z if way == 0 else (z + step) % n_z
            if step <= longest[0, way]:
                landed(everyone.at[origin, :, 1 - core, 0], ring_sems.at[3, way, step])
            if step <= longest[1, way]:
                landed(everyone.at[origin, y, 1 - core, 1], ring_sems.at[4, way, step])
                landed(everyone.at[origin, 1 - y, 1 - core, 1], ring_sems.at[5, way, step])

    dx = (x + 4 - z % 4) % 4
    root = z // 4 == y_hi
    first = core * quarter
    eighth = quarter // 2

    def group_origins(step):
        if step == 0:
            return ((z, 0),)
        if step == n_z // 2:
            return (((z + step) % n_z, step),)
        return (((z + n_z - step) % n_z, step), ((z + step) % n_z, n_z - step))

    held = lambda zz, part: left.at[zz, :, :, pl.ds(part * eighth, eighth)]
    late = []

    def left_copies(step):
        made = []
        for zz, tag in group_origins(step):
            base = len(sends)

            def numbered(source, target, arrival, device, offset):
                return pltpu.make_async_remote_copy(
                    src_ref=source, dst_ref=target, send_sem=send_sems.at[base + offset],
                    recv_sem=arrival, device_id=device, device_id_type=MESH,
                )

            there = everyone.at[zz, :, :, 1 - y, pl.ds(first, quarter)]
            to_next = numbered(held(zz, 0), held(zz, 0), left_sems.at[0, tag], x_next, 0)
            to_last = numbered(held(zz, 1), held(zz, 1), left_sems.at[1, tag], x_last, 1)
            to_across = numbered(there, left.at[zz], left_sems.at[2, tag], across, 2)
            made.append((zz, tag, to_next, to_last, to_across))
            sends.extend([None] * 3)
        late.extend(made)
        return made

    def left_from_root(made):
        @pl.when((dx == 0) & root)
        def _():
            for zz, tag, to_next, to_last, to_across in made:
                to_across.start()
                left[zz] = everyone[zz, :, :, y, pl.ds(first, quarter)]
                to_next.start()
                to_last.start()

    def left_onward(made):
        @pl.when((dx == 0) & jnp.logical_not(root))
        def _():
            for zz, tag, to_next, to_last, to_across in made:
                landed(left.at[zz], left_sems.at[2, tag])
                to_next.start()
                to_last.start()

        @pl.when(dx == 1)
        def _():
            for zz, tag, to_next, to_last, to_across in made:
                landed(held(zz, 0), left_sems.at[0, tag])
                to_next.start()

        @pl.when(dx == 3)
        def _():
            for zz, tag, to_next, to_last, to_across in made:
                landed(held(zz, 1), left_sems.at[1, tag])
                to_last.start()

    def left_middle(made):
        @pl.when(dx == 2)
        def _():
            for zz, tag, to_next, to_last, to_across in made:
                landed(held(zz, 0), left_sems.at[0, tag])
                to_next.start()
                landed(held(zz, 1), left_sems.at[1, tag])
                to_last.start()

    parts = [left_copies(step) for step in range(n_z // 2 + 1)]
    rest_step(0)
    ring_step(1)
    left_from_root(parts[0])
    ring_step(2)
    side_step(1)
    rest_step(1)
    left_from_root(parts[1])
    ring_step(3)
    side_step(2)
    rest_step(2)
    left_from_root(parts[2])
    left_onward(parts[0])
    ring_step(4)
    side_step(3)
    rest_step(3)
    left_from_root(parts[3])
    left_onward(parts[1])
    left_middle(parts[0])
    side_step(4)
    rest_step(4)
    left_from_root(parts[4])
    for step in range(2, n_z // 2 + 1):
        left_onward(parts[step])
        left_middle(parts[step - 1])
    left_middle(parts[n_z // 2])

    def group_product(k, carry):
        odd = k % 2
        tag = (odd * ((k + 1) // 2) + (1 - odd) * (n_z - k // 2)) % n_z
        zz = (z + n_z - tag) % n_z

        @pl.when(dx == 1)
        def _():
            landed(held(zz, 1), left_sems.at[1, tag])

        @pl.when(dx == 3)
        def _():
            landed(held(zz, 0), left_sems.at[0, tag])

        straight = [left[zz, i // 2, i % 2].astype(f32) for i in range(4)]
        side = jnp.concatenate([turned(value) for value in straight], axis=1)
        both = jnp.concatenate([-jnp.concatenate(straight, axis=1), side], axis=0)
        both = both.astype(bf16)
        for half in range(2):
            right = jnp.concatenate([everyone[zz, i // 2, i % 2, half] for i in range(4)], axis=1)
            product = lax.dot_general(
                both, right, (((1,), (1,)), ((), ())), preferred_element_type=f32
            )
            for part in range(2):
                spot = (part, slice(None), slice(half * half_rows, (half + 1) * half_rows))
                out_ref[spot] += product[part * quarter : (part + 1) * quarter]
        return carry

    lax.fori_loop(0, n_z, group_product, 0)

    for moving in sends:
        if moving is not None:
            moving.wait_send()
    for zz, tag, to_next, to_last, to_across in late:
        pl.when(dx != 3)(lambda: to_next.wait_send())
        pl.when(dx != 1)(lambda: to_last.wait_send())
        pl.when((dx == 0) & root)(lambda: to_across.wait_send())

    def sent_plane(x, carry):
        to_behind(occ_ref.at[:, x], far.at[x], x).wait_send()
        return carry

    def passed_plane(x, carry):
        to_sibling(occ_ref.at[:, x], near.at[x], x).wait_send()
        return carry

    def passed_far(x, carry):
        to_sibling(far.at[x], near.at[x], x).wait_send()
        return carry

    to_behind(level_ref, far_level, PLANES).wait_send()
    lax.fori_loop(0, PLANES, sent_plane, 0)

    @pl.when(core == 1)
    def _():
        to_sibling(level_ref, near_level, PLANES).wait_send()
        lax.fori_loop(0, PLANES, passed_plane, 0)

    @pl.when(core == 0)
    def _():
        to_sibling(far_level, near_level, PLANES).wait_send()
        lax.fori_loop(0, PLANES, passed_far, 0)


def whole_response(occ, emp, gvectors, energies, ztab, xytabs, n_z):
    bf16, f32 = jnp.bfloat16, jnp.float32
    half = NG // 16
    anywhere, vmem = pl.BlockSpec(memory_space=pl.ANY), pl.BlockSpec(memory_space=pltpu.VMEM)
    return pl.pallas_call(
        response_kernel,
        out_shape=jax.ShapeDtypeStruct((2, half // 2, 2 * half), f32),
        in_specs=[anywhere, anywhere, vmem, vmem, vmem, anywhere, anywhere],
        out_specs=vmem,
        scratch_shapes=[
            pltpu.VMEM((PLANES, 2, 4, CELLS), bf16),
            pltpu.VMEM((PLANES, 2, 4, CELLS), bf16),
            pltpu.VMEM((8, LANES), f32),
            pltpu.VMEM((8, LANES), f32),
            pltpu.VMEM((8, LANES), f32),
            pltpu.VMEM((2, PLANES, 8, CELLS), bf16),
            pltpu.VMEM((Z_ROWS, GROUP_CELLS), bf16),
            pltpu.VMEM((PLANES // BATCH, WAVE_ROWS, DEPTH), bf16),
            pltpu.VMEM((16, CELLS), f32),
            pltpu.VMEM((GROUPS * LANES, GROUP_CELLS), bf16),
            pltpu.VMEM((Z_ROWS, GROUPS * LANES), f32),
            pltpu.VMEM((Q_SLOTS // 2, DEPTH, 2 * LANES), bf16),
            pltpu.VMEM((Q_SLOTS * WAVE_ROWS, LANES), f32),
            pltpu.VMEM((1024, LANES), f32),
            pltpu.VMEM((1, NG), jnp.int32),
            pltpu.SMEM((1, NG), jnp.int32),
            pltpu.VMEM((1, NG), f32),
            pltpu.VMEM((2, 4, 2, half, LANES), bf16),
            pltpu.VMEM((n_z, 2, 2, 2, half, LANES), bf16),
            pltpu.VMEM((n_z, 2, 2, half // 2, LANES), bf16),
            pltpu.VMEM((2, 2, half, LANES), bf16),
            pltpu.VMEM((2, 2, half, LANES), bf16),
            pltpu.VMEM((4, 2, half, LANES), bf16),
            pltpu.VMEM((2, half, LANES), bf16),
            pltpu.VMEM((2, half, LANES), bf16),
            pltpu.SemaphoreType.DMA((PLANES + 1,)),
            pltpu.SemaphoreType.DMA((PLANES + 1,)),
            pltpu.SemaphoreType.DMA((PLANES + 1,)),
            pltpu.SemaphoreType.DMA((PLANES + 1,)),
            pltpu.SemaphoreType.DMA((4,)),
            pltpu.SemaphoreType.DMA((128,)),
            pltpu.SemaphoreType.DMA((8,)),
            pltpu.SemaphoreType.DMA((6, 2, n_z // 2 + 1)),
            pltpu.SemaphoreType.DMA((3,)),
            pltpu.SemaphoreType.DMA((3, n_z)),
        ],
        compiler_params=pltpu.CompilerParams(
            collective_id=0, has_side_effects=True, vmem_limit_bytes=60 * 2**20
        ),
        cost_estimate=pl.CostEstimate(
            flops=16_000_000_000, bytes_accessed=12_000_000, transcendentals=0
        ),
    )(occ, emp, gvectors, *energies, ztab, xytabs)


def shards(ztab, xytabs, occupied_states, empty_states, occ_energy, empty_energy, gvectors):
    occ = jnp.transpose(occupied_states, (0, 2, 1, 3))
    emp = jnp.transpose(empty_states, (0, 2, 1, 3))
    energies = occ_energy.reshape(1, -1), empty_energy.reshape(1, -1)
    n_z = lax.axis_size("blk") // 4
    out = whole_response(occ, emp, gvectors, energies, ztab, xytabs, n_z)
    return jnp.transpose(out, (1, 0, 2))


def solution(mesh):
    ztab = z_table()
    xytabs = plane_table(mesh.shape["pw"])
    return jax.shard_map(
        lambda *args: shards(jnp.asarray(ztab), jnp.asarray(xytabs), *args),
        mesh=mesh,
        in_specs=(P(None, "blk", "pw", None), P(None, "blk", "pw", None), P("blk"), P("blk"), P()),
        out_specs=P("blk", None, "pw"),
        check_vma=False,
    )
```

```python
import math

import jax
import jax.numpy as jnp
import numpy as np
from jax import lax
from jax.experimental import pallas as pl
from jax.experimental.pallas import tpu as pltpu
from jax.sharding import PartitionSpec as P
import ml_dtypes

GX = 72
GY = 72
GZ = 144
KMAX = 16
SIDE = 2 * KMAX + 1
PLANES = 9
CELLS = GY * GZ
NG = 4096
GROUPS = 9
GROUP_CELLS = 8 * GZ
Z_ROWS = SIDE * 8
ROWS_X = 80
BATCH = 3
DEPTH = BATCH * ROWS_X
HALF = (SIDE * SIDE + 1) // 2
WAVE_ROWS = 1096
Q_SLOTS = 34
LANES = 128
omega_shift = 0.5


def z_table():
    z = np.arange(GZ)
    out = np.zeros((Z_ROWS, GROUP_CELLS), np.float64)
    for q in range(KMAX + 1):
        angle = 2 * np.pi * ((q * z) % GZ) / GZ
        for y in range(8):
            out[q * 8 + y, y * GZ : (y + 1) * GZ] = np.cos(angle)
            if q:
                out[(KMAX + q) * 8 + y, y * GZ : (y + 1) * GZ] = np.sin(angle)
    return out.astype(np.float32).astype(ml_dtypes.bfloat16)


def plane_table(groups):
    h = np.arange(HALF)
    p = (h + KMAX) // SIDE
    a = h - SIDE * p
    out = np.zeros((groups, WAVE_ROWS, PLANES, ROWS_X), np.float64)
    y = np.arange(GY)
    for group in range(groups):
        for plane in range(PLANES):
            x = group * PLANES + plane
            steps = (p[:, None] * y[None, :] + a[:, None] * x) % GX
            out[group, 0 : 2 * HALF : 2, plane, :GY] = np.cos(2 * np.pi * steps / GX)
            out[group, 1 : 2 * HALF : 2, plane, :GY] = np.sin(2 * np.pi * steps / GX)
    out = out.reshape(groups, WAVE_ROWS, PLANES // BATCH, DEPTH).transpose(0, 2, 1, 3)
    return out.astype(np.float32).astype(ml_dtypes.bfloat16)


def turned(value):
    lane = lax.broadcasted_iota(jnp.int32, value.shape, 1)
    ahead = pltpu.roll(value, LANES - 8, 1)
    behind = pltpu.roll(value, 8, 1)
    return jnp.where((lane & 8) == 0, ahead, -behind)


MESH = pl.DeviceIdType.MESH


def response_kernel(
    occ_ref, emp_ref, wave_ref, occ_energy_ref, emp_energy_ref, ztab_ref, xytab_ref, out_ref,
    near, far, level_ref, near_level, far_level, emp, ztab, xytab, occ_f, pairs, depth_out, sections, waves,
    picked, index_v, index_s, sign_v, sign_rows, part_ref, everyone, left, relay, passed, arrived, plane_sum,
    other, ahead_sems, far_sems, pass_sems, near_sems, load_sems, send_sems, sum_sems, ring_sems,
    side_sems, left_sems,
):
    blk, pw = lax.axis_index("blk"), lax.axis_index("pw")
    count = lax.axis_size("blk")
    n_z = count // 4
    z, y, core = blk // 4, (blk // 2) % 2, blk % 2
    x, y_hi = pw % 4, pw // 4
    f32, bf16 = jnp.float32, jnp.bfloat16

    def place(z=z, y=y, core=core, x=x, y_hi=y_hi):
        return {"blk": z * 4 + y * 2 + core, "pw": y_hi * 4 + x}

    x_next, x_last = place(x=(x + 1) % 4), place(x=(x + 3) % 4)
    z_next, z_last = place(z=(z + 1) % n_z), place(z=(z + n_z - 1) % n_z)
    sibling, beside = place(core=1 - core), place(y=1 - y)
    facing, across = place(y_hi=1 - y_hi), place(y=1 - y, y_hi=1 - y_hi)
    behind = {"blk": (blk + count - 2) % count, "pw": pw}
    ahead = {"blk": (blk + 2) % count, "pw": pw}

    barrier = pltpu.get_barrier_semaphore()
    neighbours = (
        x_next, x_last, z_next, z_last, sibling, beside, facing, across, behind, ahead
    )
    for device in neighbours:
        pl.semaphore_signal(barrier, inc=1, device_id=device, device_id_type=MESH)
    pl.semaphore_wait(barrier, len(neighbours))

    def to_behind(source, target, spot):
        return pltpu.make_async_remote_copy(
            src_ref=source, dst_ref=target, send_sem=ahead_sems.at[spot],
            recv_sem=far_sems.at[spot], device_id=behind, device_id_type=MESH,
        )

    def to_sibling(source, target, spot):
        return pltpu.make_async_remote_copy(
            src_ref=source, dst_ref=target, send_sem=pass_sems.at[spot],
            recv_sem=near_sems.at[spot], device_id=sibling, device_id_type=MESH,
        )

    def landed(target, arrival):
        pltpu.make_async_copy(target, target, arrival).wait()

    def send_plane(x, carry):
        to_behind(occ_ref.at[:, x], far.at[x], x).start()
        return carry

    def pass_plane(x, carry):
        to_sibling(occ_ref.at[:, x], near.at[x], x).start()
        return carry

    lane = lax.broadcasted_iota(jnp.int32, (8, LANES), 1)
    occ_energy = occ_energy_ref[...].astype(f32)
    emp_energy = emp_energy_ref[...].astype(f32)
    spread = jnp.zeros((8, LANES), f32)
    for v in range(4):
        spread = jnp.where((lane // 16) % 4 == v, occ_energy[:, v : v + 1], spread)
    level_ref[...] = spread
    emp_level = jnp.zeros((8, LANES), f32)
    for c in range(8):
        emp_level = jnp.where(lane % 8 == c, emp_energy[:, c : c + 1], emp_level)
    to_behind(level_ref, far_level, PLANES).start()
    lax.fori_loop(0, PLANES, send_plane, 0)

    @pl.when(core == 1)
    def _():
        to_sibling(level_ref, near_level, PLANES).start()
        lax.fori_loop(0, PLANES, pass_plane, 0)

    loads = [
        pltpu.make_async_copy(emp_ref, emp, load_sems.at[0]),
        pltpu.make_async_copy(ztab_ref, ztab, load_sems.at[1]),
        pltpu.make_async_copy(xytab_ref.at[pw], xytab, load_sems.at[2]),
    ]
    for load in loads:
        load.start()

    flat = SIDE * wave_ref[1:2, :] + wave_ref[0:1, :]
    index_v[...] = (wave_ref[2:3, :] + KMAX) * WAVE_ROWS + 2 * jnp.abs(flat)
    sign_v[...] = jnp.where(flat < 0, -1.0, 1.0).astype(jnp.float32)
    index_move = pltpu.make_async_copy(index_v, index_s, load_sems.at[3])
    index_move.start()
    for load in loads:
        load.wait()
    index_move.wait()

    def group_pairs(x, group):
        for part in range(3):
            start = group * GROUP_CELLS + part * 384
            cells = slice(start, start + 384)
            emp_re = emp[0, x, :, cells].astype(jnp.float32)
            emp_im = emp[1, x, :, cells].astype(jnp.float32)
            for v in range(8):
                row = v if v < 4 else v + 4
                occ_re = occ_f[row : row + 1, cells]
                occ_im = occ_f[row + 4 : row + 5, cells]
                both = jnp.concatenate(
                    [occ_re * emp_re + occ_im * emp_im, occ_re * emp_im - occ_im * emp_re], axis=0
                )
                rows = slice(group * LANES + v * 16, group * LANES + v * 16 + 16)
                pairs[rows, part * 384 : part * 384 + 384] = both.astype(jnp.bfloat16)

    blank = jnp.zeros((ROWS_X - GY, LANES), jnp.float32)

    def rows_of(first):
        parts = [depth_out[first : first + 8, t * LANES : (t + 1) * LANES] for t in range(GROUPS)]
        return jnp.concatenate(parts + [blank], axis=0)

    def one_plane(x, spot):
        landed(far.at[x], far_sems.at[x])

        @pl.when(core == 0)
        def _():
            to_sibling(far.at[x], near.at[x], x).start()

        landed(near.at[x], near_sems.at[x])
        for part in range(2):
            occ_f[part * 4 : part * 4 + 4, :] = near[x, part].astype(jnp.float32)
            occ_f[part * 4 + 8 : part * 4 + 12, :] = far[x, part].astype(jnp.float32)

        for start in range(0, GROUPS, 2):
            stop = min(start + 2, GROUPS)
            for group in range(start, stop):
                group_pairs(x, group)
            lines = slice(start * LANES, stop * LANES)
            depth_out[:, lines] = lax.dot_general(
                ztab[...], pairs[lines, :], (((1,), (1,)), ((), ())),
                preferred_element_type=jnp.float32,
            )
        rows = pl.ds(pl.multiple_of(spot * ROWS_X, 16), ROWS_X)

        def put(slot, value):
            half = slot % 2
            sections[slot // 2, rows, half * LANES : (half + 1) * LANES] = value.astype(jnp.bfloat16)

        put(KMAX, rows_of(0))
        for q in range(1, KMAX + 1):
            cosine = rows_of(q * 8)
            sine = turned(rows_of((KMAX + q) * 8))
            put(KMAX + q, cosine + sine)
            put(KMAX - q, cosine - sine)

    sections[Q_SLOTS // 2 - 1, :, LANES:] = jnp.zeros((DEPTH, LANES), jnp.bfloat16)
    def clear(k, carry):
        rows = pl.ds(pl.multiple_of(k * WAVE_ROWS, 8), WAVE_ROWS)
        waves[rows, :] = jnp.zeros((WAVE_ROWS, LANES), jnp.float32)
        return carry

    lax.fori_loop(0, Q_SLOTS, clear, 0)

    def stand(step, carry):
        first = pl.multiple_of(step * 128, 128)
        row = sign_v[:, pl.ds(first, 128)]
        sign_rows[pl.ds(first, 128), :] = jnp.broadcast_to(row, (128, LANES)).T
        return carry

    lax.fori_loop(0, NG // 128, stand, 0)
    landed(far_level, far_sems.at[PLANES])

    @pl.when(core == 0)
    def _():
        to_sibling(far_level, near_level, PLANES).start()

    def each_batch(batch, carry):
        def each_plane(spot, carry):
            one_plane(batch * BATCH + spot, spot)
            return carry

        lax.fori_loop(0, BATCH, each_plane, 0)

        def slot_pair(k, carry):
            product = jnp.dot(xytab[batch], sections[k], preferred_element_type=jnp.float32)
            first = pl.multiple_of(k * 2 * WAVE_ROWS, 8)
            for half in range(2):
                rows = pl.ds(first + half * WAVE_ROWS, WAVE_ROWS)
                waves[rows, :] += product[:, half * LANES : (half + 1) * LANES]
            return carry

        lax.fori_loop(0, Q_SLOTS // 2, slot_pair, 0)
        return carry

    lax.fori_loop(0, PLANES // BATCH, each_batch, 0)
    landed(near_level, near_sems.at[PLANES])
    occ_level = jnp.where(lane < LANES // 2, near_level[...], far_level[...])
    scale = jnp.sqrt(2.0 / (emp_level - occ_level + omega_shift))[0:1]

    def chunk(yy, xx):
        base = (yy * 4 + xx) * 512

        def pick(step, carry):
            first = step * 16
            for i in range(16):
                row = index_s[0, base + first + i]
                picked[pl.ds((first + i) * 2, 2), :] = waves[pl.ds(row, 2), :]
            return carry

        lax.fori_loop(0, 32, pick, 0)
        for part in range(4):
            cosine = picked[pl.ds(part * 256, 128, stride=2), :]
            sine = picked[pl.ds(part * 256 + 1, 128, stride=2), :]
            first = pl.multiple_of(base + part * 128, 128)
            total = (cosine + sign_rows[pl.ds(first, 128), :] * turned(sine)) * scale
            rows = slice((part % 2) * 128, (part % 2) * 128 + 128)
            part_ref[yy, xx, part // 2, rows, :] = total.astype(bf16)

    def both_chunks(xx):
        def one(yy, carry):
            chunk(yy, xx)
            return carry

        lax.fori_loop(0, 2, one, 0)

    sends = []

    def copy(source, target, arrival, device):
        return pltpu.make_async_remote_copy(
            src_ref=source, dst_ref=target, send_sem=send_sems.at[len(sends)], recv_sem=arrival,
            device_id=device, device_id_type=MESH,
        )

    def send(source, target, arrival, device):
        moving = copy(source, target, arrival, device)
        moving.start()
        sends.append(moving)

    out_ref[...] = jnp.zeros_like(out_ref)
    rows = everyone.shape[4] * 2
    half_rows, quarter = rows // 2, rows // 4

    xn, xl, xo = (x + 1) % 4, (x + 3) % 4, (x + 2) % 4
    both_chunks(xo)
    send(part_ref.at[:, xo, 0], relay.at[0], sum_sems.at[0], x_next)
    send(part_ref.at[:, xo, 1], relay.at[1], sum_sems.at[1], x_last)
    both_chunks(xn)
    send(part_ref.at[:, xn, 1], arrived.at[0], sum_sems.at[2], x_next)
    both_chunks(xl)
    send(part_ref.at[:, xl, 0], arrived.at[1], sum_sems.at[3], x_last)
    landed(relay.at[0], sum_sems.at[0])
    passed[0] = (part_ref[:, xn, 0].astype(f32) + relay[0].astype(f32)).astype(bf16)
    send(passed.at[0], arrived.at[2], sum_sems.at[4], x_next)
    landed(relay.at[1], sum_sems.at[1])
    passed[1] = (part_ref[:, xl, 1].astype(f32) + relay[1].astype(f32)).astype(bf16)
    send(passed.at[1], arrived.at[3], sum_sems.at[5], x_last)
    both_chunks(x)
    landed(arrived.at[0], sum_sems.at[2])
    landed(arrived.at[1], sum_sems.at[3])
    landed(arrived.at[2], sum_sems.at[4])
    landed(arrived.at[3], sum_sems.at[5])

    def x_total(y_hi, half):
        first, second = (2, 1) if half == 0 else (0, 3)
        return (
            part_ref[y_hi, x, half].astype(f32)
            + arrived[first, y_hi].astype(f32)
            + arrived[second, y_hi].astype(f32)
        )

    for half in range(2):
        plane_sum[half] = x_total(1 - y_hi, half).astype(bf16)
    send(plane_sum, other, sum_sems.at[6], facing)
    landed(other, sum_sems.at[6])
    mine = everyone.at[z, y, core]
    for half in range(2):
        total = x_total(y_hi, half) + other[half].astype(f32)
        everyone[z, y, core, half] = total.astype(bf16)

    send(mine, mine, side_sems.at[0], beside)
    send(mine, mine, side_sems.at[1], sibling)
    upper = lambda zz: everyone.at[zz, :, core, 0]
    lower = lambda zz, yy: everyone.at[zz, yy, core, 1]
    send(lower(z, y), lower(z, y), ring_sems.at[1, 0, 1], z_next)
    send(lower(z, y), lower(z, y), ring_sems.at[1, 1, 1], z_last)
    theirs = everyone.at[z, 1 - y, core]
    landed(theirs, side_sems.at[0])
    send(upper(z), upper(z), ring_sems.at[0, 0, 1], z_next)
    send(upper(z), upper(z), ring_sems.at[0, 1, 1], z_last)
    send(theirs, theirs, side_sems.at[2], sibling)

    longest = {(0, 0): n_z // 2, (0, 1): n_z // 2 - 1, (1, 0): n_z // 2 - 1, (1, 1): n_z // 2}

    def ring_step(step):
        for half in (1, 0):
            for way in (0, 1):
                if step > longest[half, way]:
                    continue
                origin = (z + n_z - step) % n_z if way == 0 else (z + step) % n_z
                piece = upper(origin) if half == 0 else lower(origin, y)
                landed(piece, ring_sems.at[half, way, step])
                if step < longest[half, way]:
                    send(piece, piece, ring_sems.at[half, way, step + 1], z_next if way == 0 else z_last)
                if half == 1:
                    send(piece, piece, ring_sems.at[2, way, step], beside)
                send(piece, piece, ring_sems.at[3 + half, way, step], sibling)

    def side_step(step):
        for way in (0, 1):
            if step > longest[1, way]:
                continue
            origin = (z + n_z - step) % n_z if way == 0 else (z + step) % n_z
            piece = lower(origin, 1 - y)
            landed(piece, ring_sems.at[2, way, step])
            send(piece, piece, ring_sems.at[5, way, step], sibling)

    def rest_step(step):
        if step == 0:
            for yy, spot in ((y, 1), (1 - y, 2)):
                landed(everyone.at[z, yy, 1 - core], side_sems.at[spot])
            return
        for way in (0, 1):
            origin = (z + n_z - step) % n_z if way == 0 else (z + step) % n_z
            if step <= longest[0, way]:
                landed(everyone.at[origin, :, 1 - core, 0], ring_sems.at[3, way, step])
            if step <= longest[1, way]:
                landed(everyone.at[origin, y, 1 - core, 1], ring_sems.at[4, way, step])
                landed(everyone.at[origin, 1 - y, 1 - core, 1], ring_sems.at[5, way, step])

    dx = (x + 4 - z % 4) % 4
    root = z // 4 == y_hi
    first = core * quarter
    eighth = quarter // 2

    def group_origins(step):
        if step == 0:
            return ((z, 0),)
        if step == n_z // 2:
            return (((z + step) % n_z, step),)
        return (((z + n_z - step) % n_z, step), ((z + step) % n_z, n_z - step))

    held = lambda zz, part: left.at[zz, :, :, pl.ds(part * eighth, eighth)]
    late = []

    def left_copies(step):
        made = []
        for zz, tag in group_origins(step):
            base = len(sends)

            def numbered(source, target, arrival, device, offset):
                return pltpu.make_async_remote_copy(
                    src_ref=source, dst_ref=target, send_sem=send_sems.at[base + offset],
                    recv_sem=arrival, device_id=device, device_id_type=MESH,
                )

            there = everyone.at[zz, :, :, 1 - y, pl.ds(first, quarter)]
            to_next = numbered(held(zz, 0), held(zz, 0), left_sems.at[0, tag], x_next, 0)
            to_last = numbered(held(zz, 1), held(zz, 1), left_sems.at[1, tag], x_last, 1)
            to_across = numbered(there, left.at[zz], left_sems.at[2, tag], across, 2)
            made.append((zz, tag, to_next, to_last, to_across))
            sends.extend([None] * 3)
        late.extend(made)
        return made

    def left_from_root(made):
        @pl.when((dx == 0) & root)
        def _():
            for zz, tag, to_next, to_last, to_across in made:
                to_across.start()
                left[zz] = everyone[zz, :, :, y, pl.ds(first, quarter)]
                to_next.start()
                to_last.start()

    def left_onward(made):
        @pl.when((dx == 0) & jnp.logical_not(root))
        def _():
            for zz, tag, to_next, to_last, to_across in made:
                landed(left.at[zz], left_sems.at[2, tag])
                to_next.start()
                to_last.start()

        @pl.when(dx == 1)
        def _():
            for zz, tag, to_next, to_last, to_across in made:
                landed(held(zz, 0), left_sems.at[0, tag])
                to_next.start()

        @pl.when(dx == 3)
        def _():
            for zz, tag, to_next, to_last, to_across in made:
                landed(held(zz, 1), left_sems.at[1, tag])
                to_last.start()

    def left_middle(made):
        @pl.when(dx == 2)
        def _():
            for zz, tag, to_next, to_last, to_across in made:
                landed(held(zz, 0), left_sems.at[0, tag])
                to_next.start()
                landed(held(zz, 1), left_sems.at[1, tag])
                to_last.start()

    parts = [left_copies(step) for step in range(n_z // 2 + 1)]
    rest_step(0)
    ring_step(1)
    left_from_root(parts[0])
    ring_step(2)
    side_step(1)
    rest_step(1)
    left_from_root(parts[1])
    ring_step(3)
    side_step(2)
    rest_step(2)
    left_from_root(parts[2])
    left_onward(parts[0])
    ring_step(4)
    side_step(3)
    rest_step(3)
    left_from_root(parts[3])
    left_onward(parts[1])
    left_middle(parts[0])
    side_step(4)
    rest_step(4)
    left_from_root(parts[4])
    for step in range(2, n_z // 2 + 1):
        left_onward(parts[step])
        left_middle(parts[step - 1])
    left_middle(parts[n_z // 2])

    def group_product(k, carry):
        odd = k % 2
        tag = (odd * ((k + 1) // 2) + (1 - odd) * (n_z - k // 2)) % n_z
        zz = (z + n_z - tag) % n_z

        @pl.when(dx == 1)
        def _():
            landed(held(zz, 1), left_sems.at[1, tag])

        @pl.when(dx == 3)
        def _():
            landed(held(zz, 0), left_sems.at[0, tag])

        straight = [left[zz, i // 2, i % 2].astype(f32) for i in range(4)]
        side = jnp.concatenate([turned(value) for value in straight], axis=1)
        both = jnp.concatenate([-jnp.concatenate(straight, axis=1), side], axis=0)
        both = both.astype(bf16)
        for half in range(2):
            right = jnp.concatenate([everyone[zz, i // 2, i % 2, half] for i in range(4)], axis=1)
            product = lax.dot_general(
                both, right, (((1,), (1,)), ((), ())), preferred_element_type=f32
            )
            for part in range(2):
                spot = (part, slice(None), slice(half * half_rows, (half + 1) * half_rows))
                out_ref[spot] += product[part * quarter : (part + 1) * quarter]
        return carry

    lax.fori_loop(0, n_z, group_product, 0)

    for moving in sends:
        if moving is not None:
            moving.wait_send()
    for zz, tag, to_next, to_last, to_across in late:
        pl.when(dx != 3)(lambda: to_next.wait_send())
        pl.when(dx != 1)(lambda: to_last.wait_send())
        pl.when((dx == 0) & root)(lambda: to_across.wait_send())

    def sent_plane(x, carry):
        to_behind(occ_ref.at[:, x], far.at[x], x).wait_send()
        return carry

    def passed_plane(x, carry):
        to_sibling(occ_ref.at[:, x], near.at[x], x).wait_send()
        return carry

    def passed_far(x, carry):
        to_sibling(far.at[x], near.at[x], x).wait_send()
        return carry

    to_behind(level_ref, far_level, PLANES).wait_send()
    lax.fori_loop(0, PLANES, sent_plane, 0)

    @pl.when(core == 1)
    def _():
        to_sibling(level_ref, near_level, PLANES).wait_send()
        lax.fori_loop(0, PLANES, passed_plane, 0)

    @pl.when(core == 0)
    def _():
        to_sibling(far_level, near_level, PLANES).wait_send()
        lax.fori_loop(0, PLANES, passed_far, 0)


def whole_response(occ, emp, gvectors, energies, ztab, xytabs, n_z):
    bf16, f32 = jnp.bfloat16, jnp.float32
    half = NG // 16
    anywhere, vmem = pl.BlockSpec(memory_space=pl.ANY), pl.BlockSpec(memory_space=pltpu.VMEM)
    return pl.pallas_call(
        response_kernel,
        out_shape=jax.ShapeDtypeStruct((2, half // 2, 2 * half), f32),
        in_specs=[anywhere, anywhere, vmem, vmem, vmem, anywhere, anywhere],
        out_specs=vmem,
        scratch_shapes=[
            pltpu.VMEM((PLANES, 2, 4, CELLS), bf16),
            pltpu.VMEM((PLANES, 2, 4, CELLS), bf16),
            pltpu.VMEM((8, LANES), f32),
            pltpu.VMEM((8, LANES), f32),
            pltpu.VMEM((8, LANES), f32),
            pltpu.VMEM((2, PLANES, 8, CELLS), bf16),
            pltpu.VMEM((Z_ROWS, GROUP_CELLS), bf16),
            pltpu.VMEM((PLANES // BATCH, WAVE_ROWS, DEPTH), bf16),
            pltpu.VMEM((16, CELLS), f32),
            pltpu.VMEM((GROUPS * LANES, GROUP_CELLS), bf16),
            pltpu.VMEM((Z_ROWS, GROUPS * LANES), f32),
            pltpu.VMEM((Q_SLOTS // 2, DEPTH, 2 * LANES), bf16),
            pltpu.VMEM((Q_SLOTS * WAVE_ROWS, LANES), f32),
            pltpu.VMEM((1024, LANES), f32),
            pltpu.VMEM((1, NG), jnp.int32),
            pltpu.SMEM((1, NG), jnp.int32),
            pltpu.VMEM((1, NG), f32),
            pltpu.VMEM((NG, LANES), f32),
            pltpu.VMEM((2, 4, 2, half, LANES), bf16),
            pltpu.VMEM((n_z, 2, 2, 2, half, LANES), bf16),
            pltpu.VMEM((n_z, 2, 2, half // 2, LANES), bf16),
            pltpu.VMEM((2, 2, half, LANES), bf16),
            pltpu.VMEM((2, 2, half, LANES), bf16),
            pltpu.VMEM((4, 2, half, LANES), bf16),
            pltpu.VMEM((2, half, LANES), bf16),
            pltpu.VMEM((2, half, LANES), bf16),
            pltpu.SemaphoreType.DMA((PLANES + 1,)),
            pltpu.SemaphoreType.DMA((PLANES + 1,)),
            pltpu.SemaphoreType.DMA((PLANES + 1,)),
            pltpu.SemaphoreType.DMA((PLANES + 1,)),
            pltpu.SemaphoreType.DMA((4,)),
            pltpu.SemaphoreType.DMA((128,)),
            pltpu.SemaphoreType.DMA((8,)),
            pltpu.SemaphoreType.DMA((6, 2, n_z // 2 + 1)),
            pltpu.SemaphoreType.DMA((3,)),
            pltpu.SemaphoreType.DMA((3, n_z)),
        ],
        compiler_params=pltpu.CompilerParams(
            collective_id=0, has_side_effects=True, vmem_limit_bytes=60 * 2**20
        ),
        cost_estimate=pl.CostEstimate(
            flops=16_000_000_000, bytes_accessed=12_000_000, transcendentals=0
        ),
    )(occ, emp, gvectors, *energies, ztab, xytabs)


def shards(ztab, xytabs, occupied_states, empty_states, occ_energy, empty_energy, gvectors):
    occ = jnp.transpose(occupied_states, (0, 2, 1, 3))
    emp = jnp.transpose(empty_states, (0, 2, 1, 3))
    energies = occ_energy.reshape(1, -1), empty_energy.reshape(1, -1)
    n_z = lax.axis_size("blk") // 4
    out = whole_response(occ, emp, gvectors, energies, ztab, xytabs, n_z)
    return jnp.transpose(out, (1, 0, 2))


def solution(mesh):
    ztab = z_table()
    xytabs = plane_table(mesh.shape["pw"])
    return jax.shard_map(
        lambda *args: shards(jnp.asarray(ztab), jnp.asarray(xytabs), *args),
        mesh=mesh,
        in_specs=(P(None, "blk", "pw", None), P(None, "blk", "pw", None), P("blk"), P("blk"), P()),
        out_specs=P("blk", None, "pw"),
        check_vma=False,
    )
```

```python
import math

import jax
import jax.numpy as jnp
import numpy as np
from jax import lax
from jax.experimental import pallas as pl
from jax.experimental.pallas import tpu as pltpu
from jax.sharding import PartitionSpec as P
import ml_dtypes

GX = 72
GY = 72
GZ = 144
KMAX = 16
SIDE = 2 * KMAX + 1
PLANES = 9
CELLS = GY * GZ
NG = 4096
GROUPS = 9
GROUP_CELLS = 8 * GZ
Z_ROWS = SIDE * 8
ROWS_X = 80
BATCH = 3
DEPTH = BATCH * ROWS_X
HALF = (SIDE * SIDE + 1) // 2
WAVE_ROWS = 1096
Q_SLOTS = 34
LANES = 128
omega_shift = 0.5


def z_table():
    z = np.arange(GZ)
    out = np.zeros((Z_ROWS, GROUP_CELLS), np.float64)
    for q in range(KMAX + 1):
        angle = 2 * np.pi * ((q * z) % GZ) / GZ
        for y in range(8):
            out[q * 8 + y, y * GZ : (y + 1) * GZ] = np.cos(angle)
            if q:
                out[(KMAX + q) * 8 + y, y * GZ : (y + 1) * GZ] = np.sin(angle)
    return out.astype(np.float32).astype(ml_dtypes.bfloat16)


def plane_table(groups):
    h = np.arange(HALF)
    p = (h + KMAX) // SIDE
    a = h - SIDE * p
    out = np.zeros((groups, WAVE_ROWS, PLANES, ROWS_X), np.float64)
    y = np.arange(GY)
    for group in range(groups):
        for plane in range(PLANES):
            x = group * PLANES + plane
            steps = (p[:, None] * y[None, :] + a[:, None] * x) % GX
            out[group, 0 : 2 * HALF : 2, plane, :GY] = np.cos(2 * np.pi * steps / GX)
            out[group, 1 : 2 * HALF : 2, plane, :GY] = np.sin(2 * np.pi * steps / GX)
    out = out.reshape(groups, WAVE_ROWS, PLANES // BATCH, DEPTH).transpose(0, 2, 1, 3)
    return out.astype(np.float32).astype(ml_dtypes.bfloat16)


def turned(value):
    lane = lax.broadcasted_iota(jnp.int32, value.shape, 1)
    ahead = pltpu.roll(value, LANES - 8, 1)
    behind = pltpu.roll(value, 8, 1)
    return jnp.where((lane & 8) == 0, ahead, -behind)


MESH = pl.DeviceIdType.MESH


def response_kernel(
    occ_ref, emp_ref, wave_ref, occ_energy_ref, emp_energy_ref, ztab_ref, xytab_ref, out_ref,
    near, far, level_ref, near_level, far_level, emp, ztab, xytab, occ_f, pairs, depth_out, sections, waves,
    picked, index_v, index_s, sign_v, sign_rows, part_ref, everyone, left, relay, passed, arrived, plane_sum,
    other, ahead_sems, far_sems, pass_sems, near_sems, load_sems, send_sems, sum_sems, ring_sems,
    side_sems, left_sems,
):
    blk, pw = lax.axis_index("blk"), lax.axis_index("pw")
    count = lax.axis_size("blk")
    n_z = count // 4
    z, y, core = blk // 4, (blk // 2) % 2, blk % 2
    x, y_hi = pw % 4, pw // 4
    f32, bf16 = jnp.float32, jnp.bfloat16

    def place(z=z, y=y, core=core, x=x, y_hi=y_hi):
        return {"blk": z * 4 + y * 2 + core, "pw": y_hi * 4 + x}

    x_next, x_last = place(x=(x + 1) % 4), place(x=(x + 3) % 4)
    z_next, z_last = place(z=(z + 1) % n_z), place(z=(z + n_z - 1) % n_z)
    sibling, beside = place(core=1 - core), place(y=1 - y)
    facing, across = place(y_hi=1 - y_hi), place(y=1 - y, y_hi=1 - y_hi)
    behind = {"blk": (blk + count - 2) % count, "pw": pw}
    ahead = {"blk": (blk + 2) % count, "pw": pw}

    barrier = pltpu.get_barrier_semaphore()
    neighbours = (
        x_next, x_last, z_next, z_last, sibling, beside, facing, across, behind, ahead
    )
    for device in neighbours:
        pl.semaphore_signal(barrier, inc=1, device_id=device, device_id_type=MESH)
    pl.semaphore_wait(barrier, len(neighbours))

    def to_behind(source, target, spot):
        return pltpu.make_async_remote_copy(
            src_ref=source, dst_ref=target, send_sem=ahead_sems.at[spot],
            recv_sem=far_sems.at[spot], device_id=behind, device_id_type=MESH,
        )

    def to_sibling(source, target, spot):
        return pltpu.make_async_remote_copy(
            src_ref=source, dst_ref=target, send_sem=pass_sems.at[spot],
            recv_sem=near_sems.at[spot], device_id=sibling, device_id_type=MESH,
        )

    def landed(target, arrival):
        pltpu.make_async_copy(target, target, arrival).wait()

    def send_plane(x, carry):
        to_behind(occ_ref.at[:, x], far.at[x], x).start()
        return carry

    def pass_plane(x, carry):
        to_sibling(occ_ref.at[:, x], near.at[x], x).start()
        return carry

    lane = lax.broadcasted_iota(jnp.int32, (8, LANES), 1)
    occ_energy = occ_energy_ref[...].astype(f32)
    emp_energy = emp_energy_ref[...].astype(f32)
    spread = jnp.zeros((8, LANES), f32)
    for v in range(4):
        spread = jnp.where((lane // 16) % 4 == v, occ_energy[:, v : v + 1], spread)
    level_ref[...] = spread
    emp_level = jnp.zeros((8, LANES), f32)
    for c in range(8):
        emp_level = jnp.where(lane % 8 == c, emp_energy[:, c : c + 1], emp_level)
    to_behind(level_ref, far_level, PLANES).start()
    lax.fori_loop(0, PLANES, send_plane, 0)

    @pl.when(core == 1)
    def _():
        to_sibling(level_ref, near_level, PLANES).start()
        lax.fori_loop(0, PLANES, pass_plane, 0)

    loads = [
        pltpu.make_async_copy(emp_ref, emp, load_sems.at[0]),
        pltpu.make_async_copy(ztab_ref, ztab, load_sems.at[1]),
        pltpu.make_async_copy(xytab_ref.at[pw], xytab, load_sems.at[2]),
    ]
    for load in loads:
        load.start()

    flat = SIDE * wave_ref[1:2, :] + wave_ref[0:1, :]
    index_v[...] = (wave_ref[2:3, :] + KMAX) * WAVE_ROWS + 2 * jnp.abs(flat)
    sign_v[...] = jnp.where(flat < 0, -1.0, 1.0).astype(jnp.float32)
    index_move = pltpu.make_async_copy(index_v, index_s, load_sems.at[3])
    index_move.start()
    for load in loads:
        load.wait()
    index_move.wait()

    def group_pairs(x, group):
        for part in range(3):
            start = group * GROUP_CELLS + part * 384
            cells = slice(start, start + 384)
            emp_re = emp[0, x, :, cells].astype(jnp.float32)
            emp_im = emp[1, x, :, cells].astype(jnp.float32)
            for v in range(8):
                row = v if v < 4 else v + 4
                occ_re = occ_f[row : row + 1, cells]
                occ_im = occ_f[row + 4 : row + 5, cells]
                both = jnp.concatenate(
                    [occ_re * emp_re + occ_im * emp_im, occ_re * emp_im - occ_im * emp_re], axis=0
                )
                rows = slice(group * LANES + v * 16, group * LANES + v * 16 + 16)
                pairs[rows, part * 384 : part * 384 + 384] = both.astype(jnp.bfloat16)

    blank = jnp.zeros((ROWS_X - GY, LANES), jnp.float32)

    def rows_of(first):
        parts = [depth_out[first : first + 8, t * LANES : (t + 1) * LANES] for t in range(GROUPS)]
        return jnp.concatenate(parts + [blank], axis=0)

    def one_plane(x, spot):
        landed(far.at[x], far_sems.at[x])

        @pl.when(core == 0)
        def _():
            to_sibling(far.at[x], near.at[x], x).start()

        landed(near.at[x], near_sems.at[x])
        for part in range(2):
            occ_f[part * 4 : part * 4 + 4, :] = near[x, part].astype(jnp.float32)
            occ_f[part * 4 + 8 : part * 4 + 12, :] = far[x, part].astype(jnp.float32)

        for start in range(0, GROUPS, 2):
            stop = min(start + 2, GROUPS)
            for group in range(start, stop):
                group_pairs(x, group)
            lines = slice(start * LANES, stop * LANES)
            depth_out[:, lines] = lax.dot_general(
                ztab[...], pairs[lines, :], (((1,), (1,)), ((), ())),
                preferred_element_type=jnp.float32,
            )
        rows = pl.ds(pl.multiple_of(spot * ROWS_X, 16), ROWS_X)

        def put(slot, value):
            half = slot % 2
            sections[slot // 2, rows, half * LANES : (half + 1) * LANES] = value.astype(jnp.bfloat16)

        put(KMAX, rows_of(0))
        for q in range(1, KMAX + 1):
            cosine = rows_of(q * 8)
            sine = turned(rows_of((KMAX + q) * 8))
            put(KMAX + q, cosine + sine)
            put(KMAX - q, cosine - sine)

    sections[Q_SLOTS // 2 - 1, :, LANES:] = jnp.zeros((DEPTH, LANES), jnp.bfloat16)
    def clear(k, carry):
        rows = pl.ds(pl.multiple_of(k * WAVE_ROWS, 8), WAVE_ROWS)
        waves[rows, :] = jnp.zeros((WAVE_ROWS, LANES), jnp.float32)
        return carry

    lax.fori_loop(0, Q_SLOTS, clear, 0)

    def stand(step, carry):
        first = pl.multiple_of(step * 128, 128)
        row = sign_v[:, pl.ds(first, 128)]
        sign_rows[pl.ds(first, 128), :] = jnp.broadcast_to(row, (128, LANES)).T
        return carry

    lax.fori_loop(0, NG // 128, stand, 0)
    landed(far_level, far_sems.at[PLANES])

    @pl.when(core == 0)
    def _():
        to_sibling(far_level, near_level, PLANES).start()

    def each_batch(batch, carry):
        def each_plane(spot, carry):
            one_plane(batch * BATCH + spot, spot)
            return carry

        lax.fori_loop(0, BATCH, each_plane, 0)

        def slot_pair(k, carry):
            product = jnp.dot(xytab[batch], sections[k], preferred_element_type=jnp.float32)
            first = pl.multiple_of(k * 2 * WAVE_ROWS, 8)
            for half in range(2):
                rows = pl.ds(first + half * WAVE_ROWS, WAVE_ROWS)
                waves[rows, :] += product[:, half * LANES : (half + 1) * LANES]
            return carry

        lax.fori_loop(0, Q_SLOTS // 2, slot_pair, 0)
        return carry

    lax.fori_loop(0, PLANES // BATCH, each_batch, 0)
    landed(near_level, near_sems.at[PLANES])
    occ_level = jnp.where(lane < LANES // 2, near_level[...], far_level[...])
    scale = jnp.sqrt(2.0 / (emp_level - occ_level + omega_shift))[0:1]

    def chunk(yy, xx, half):
        base = (yy * 4 + xx) * 512 + half * 256

        def pick(step, carry):
            first = step * 16
            for i in range(16):
                row = index_s[0, base + first + i]
                picked[pl.ds((first + i) * 2, 2), :] = waves[pl.ds(row, 2), :]
            return carry

        lax.fori_loop(0, 16, pick, 0)
        for part in range(2):
            cosine = picked[pl.ds(part * 256, 128, stride=2), :]
            sine = picked[pl.ds(part * 256 + 1, 128, stride=2), :]
            first = pl.multiple_of(base + part * 128, 128)
            total = (cosine + sign_rows[pl.ds(first, 128), :] * turned(sine)) * scale
            part_ref[yy, xx, half, part * 128 : part * 128 + 128, :] = total.astype(bf16)

    def both_chunks(xx, half):
        def one(yy, carry):
            chunk(yy, xx, half)
            return carry

        lax.fori_loop(0, 2, one, 0)

    sends = []

    def copy(source, target, arrival, device):
        return pltpu.make_async_remote_copy(
            src_ref=source, dst_ref=target, send_sem=send_sems.at[len(sends)], recv_sem=arrival,
            device_id=device, device_id_type=MESH,
        )

    def send(source, target, arrival, device):
        moving = copy(source, target, arrival, device)
        moving.start()
        sends.append(moving)

    out_ref[...] = jnp.zeros_like(out_ref)
    rows = everyone.shape[4] * 2
    half_rows, quarter = rows // 2, rows // 4

    xn, xl, xo = (x + 1) % 4, (x + 3) % 4, (x + 2) % 4

    def pass_on(half, xx, device):
        landed(relay.at[half], sum_sems.at[half])
        share = part_ref[:, xx, half].astype(f32) + relay[half].astype(f32)
        passed[half] = share.astype(bf16)
        send(passed.at[half], arrived.at[2 + half], sum_sems.at[4 + half], device)

    def x_total(yy, half):
        first, second = (2, 1) if half == 0 else (0, 3)
        return (
            part_ref[yy, x, half].astype(f32)
            + arrived[first, yy].astype(f32)
            + arrived[second, yy].astype(f32)
        )

    def cross_over(half):
        for spot in (2, 1) if half == 0 else (0, 3):
            landed(arrived.at[spot], sum_sems.at[2 + spot])
        plane_sum[half] = x_total(1 - y_hi, half).astype(bf16)
        send(plane_sum.at[half], other.at[half], sum_sems.at[6 + half], facing)

    def own_rho(half):
        landed(other.at[half], sum_sems.at[6 + half])
        total = x_total(y_hi, half) + other[half].astype(f32)
        everyone[z, y, core, half] = total.astype(bf16)

    both_chunks(xo, 0)
    send(part_ref.at[:, xo, 0], relay.at[0], sum_sems.at[0], x_next)
    both_chunks(xl, 0)
    send(part_ref.at[:, xl, 0], arrived.at[1], sum_sems.at[3], x_last)
    both_chunks(xn, 0)
    both_chunks(x, 0)
    pass_on(0, xn, x_next)
    both_chunks(xo, 1)
    send(part_ref.at[:, xo, 1], relay.at[1], sum_sems.at[1], x_last)
    both_chunks(xn, 1)
    send(part_ref.at[:, xn, 1], arrived.at[0], sum_sems.at[2], x_next)
    both_chunks(xl, 1)
    cross_over(0)
    both_chunks(x, 1)
    pass_on(1, xl, x_last)

    own_rho(0)
    mine = lambda half: everyone.at[z, y, core, half]
    theirs = lambda half: everyone.at[z, 1 - y, core, half]
    upper = lambda zz: everyone.at[zz, :, core, 0]
    lower = lambda zz, yy: everyone.at[zz, yy, core, 1]
    send(mine(0), mine(0), side_sems.at[0, 0], beside)
    send(mine(0), mine(0), side_sems.at[1, 0], sibling)
    cross_over(1)
    landed(theirs(0), side_sems.at[0, 0])
    send(upper(z), upper(z), ring_sems.at[0, 0, 1], z_next)
    send(upper(z), upper(z), ring_sems.at[0, 1, 1], z_last)
    send(theirs(0), theirs(0), side_sems.at[2, 0], sibling)
    own_rho(1)
    send(lower(z, y), lower(z, y), ring_sems.at[1, 0, 1], z_next)
    send(lower(z, y), lower(z, y), ring_sems.at[1, 1, 1], z_last)
    send(mine(1), mine(1), side_sems.at[0, 1], beside)
    send(mine(1), mine(1), side_sems.at[1, 1], sibling)

    longest = {(0, 0): n_z // 2, (0, 1): n_z // 2 - 1, (1, 0): n_z // 2 - 1, (1, 1): n_z // 2}

    def ring_step(step):
        for half in (0, 1):
            for way in (0, 1):
                if step > longest[half, way]:
                    continue
                origin = (z + n_z - step) % n_z if way == 0 else (z + step) % n_z
                piece = upper(origin) if half == 0 else lower(origin, y)
                landed(piece, ring_sems.at[half, way, step])
                if step < longest[half, way]:
                    send(piece, piece, ring_sems.at[half, way, step + 1], z_next if way == 0 else z_last)
                if half == 1:
                    send(piece, piece, ring_sems.at[2, way, step], beside)
                send(piece, piece, ring_sems.at[3 + half, way, step], sibling)

    def side_step(step):
        for way in (0, 1):
            if step > longest[1, way]:
                continue
            origin = (z + n_z - step) % n_z if way == 0 else (z + step) % n_z
            piece = lower(origin, 1 - y)
            landed(piece, ring_sems.at[2, way, step])
            send(piece, piece, ring_sems.at[5, way, step], sibling)

    def rest_step(step):
        if step == 0:
            for yy, spot in ((y, 1), (1 - y, 2)):
                for half in range(2):
                    landed(everyone.at[z, yy, 1 - core, half], side_sems.at[spot, half])
            return
        for way in (0, 1):
            origin = (z + n_z - step) % n_z if way == 0 else (z + step) % n_z
            if step <= longest[0, way]:
                landed(everyone.at[origin, :, 1 - core, 0], ring_sems.at[3, way, step])
            if step <= longest[1, way]:
                landed(everyone.at[origin, y, 1 - core, 1], ring_sems.at[4, way, step])
                landed(everyone.at[origin, 1 - y, 1 - core, 1], ring_sems.at[5, way, step])

    dx = (x + 4 - z % 4) % 4
    root = z // 4 == y_hi
    first = core * quarter
    eighth = quarter // 2

    def group_origins(step):
        if step == 0:
            return ((z, 0),)
        if step == n_z // 2:
            return (((z + step) % n_z, step),)
        return (((z + n_z - step) % n_z, step), ((z + step) % n_z, n_z - step))

    held = lambda zz, part: left.at[zz, :, :, pl.ds(part * eighth, eighth)]
    late = []

    def left_copies(step):
        made = []
        for zz, tag in group_origins(step):
            base = len(sends)

            def numbered(source, target, arrival, device, offset):
                return pltpu.make_async_remote_copy(
                    src_ref=source, dst_ref=target, send_sem=send_sems.at[base + offset],
                    recv_sem=arrival, device_id=device, device_id_type=MESH,
                )

            there = everyone.at[zz, :, :, 1 - y, pl.ds(first, quarter)]
            to_next = numbered(held(zz, 0), held(zz, 0), left_sems.at[0, tag], x_next, 0)
            to_last = numbered(held(zz, 1), held(zz, 1), left_sems.at[1, tag], x_last, 1)
            to_across = numbered(there, left.at[zz], left_sems.at[2, tag], across, 2)
            made.append((zz, tag, to_next, to_last, to_across))
            sends.extend([None] * 3)
        late.extend(made)
        return made

    def left_from_root(made):
        @pl.when((dx == 0) & root)
        def _():
            for zz, tag, to_next, to_last, to_across in made:
                to_across.start()
                left[zz] = everyone[zz, :, :, y, pl.ds(first, quarter)]
                to_next.start()
                to_last.start()

    def left_onward(made):
        @pl.when((dx == 0) & jnp.logical_not(root))
        def _():
            for zz, tag, to_next, to_last, to_across in made:
                landed(left.at[zz], left_sems.at[2, tag])
                to_next.start()
                to_last.start()

        @pl.when(dx == 1)
        def _():
            for zz, tag, to_next, to_last, to_across in made:
                landed(held(zz, 0), left_sems.at[0, tag])
                to_next.start()

        @pl.when(dx == 3)
        def _():
            for zz, tag, to_next, to_last, to_across in made:
                landed(held(zz, 1), left_sems.at[1, tag])
                to_last.start()

    def left_middle(made):
        @pl.when(dx == 2)
        def _():
            for zz, tag, to_next, to_last, to_across in made:
                landed(held(zz, 0), left_sems.at[0, tag])
                to_next.start()
                landed(held(zz, 1), left_sems.at[1, tag])
                to_last.start()

    parts = [left_copies(step) for step in range(n_z // 2 + 1)]
    ring_step(1)
    landed(theirs(1), side_sems.at[0, 1])
    send(theirs(1), theirs(1), side_sems.at[2, 1], sibling)
    rest_step(0)
    left_from_root(parts[0])
    ring_step(2)
    side_step(1)
    rest_step(1)
    left_from_root(parts[1])
    ring_step(3)
    side_step(2)
    rest_step(2)
    left_from_root(parts[2])
    left_onward(parts[0])
    ring_step(4)
    side_step(3)
    rest_step(3)
    left_from_root(parts[3])
    left_onward(parts[1])
    left_middle(parts[0])
    side_step(4)
    rest_step(4)
    left_from_root(parts[4])
    for step in range(2, n_z // 2 + 1):
        left_onward(parts[step])
        left_middle(parts[step - 1])
    left_middle(parts[n_z // 2])

    def group_product(k, carry):
        odd = k % 2
        tag = (odd * ((k + 1) // 2) + (1 - odd) * (n_z - k // 2)) % n_z
        zz = (z + n_z - tag) % n_z

        @pl.when(dx == 1)
        def _():
            landed(held(zz, 1), left_sems.at[1, tag])

        @pl.when(dx == 3)
        def _():
            landed(held(zz, 0), left_sems.at[0, tag])

        straight = [left[zz, i // 2, i % 2].astype(f32) for i in range(4)]
        side = jnp.concatenate([turned(value) for value in straight], axis=1)
        both = jnp.concatenate([-jnp.concatenate(straight, axis=1), side], axis=0)
        both = both.astype(bf16)
        for half in range(2):
            right = jnp.concatenate([everyone[zz, i // 2, i % 2, half] for i in range(4)], axis=1)
            product = lax.dot_general(
                both, right, (((1,), (1,)), ((), ())), preferred_element_type=f32
            )
            for part in range(2):
                spot = (part, slice(None), slice(half * half_rows, (half + 1) * half_rows))
                out_ref[spot] += product[part * quarter : (part + 1) * quarter]
        return carry

    lax.fori_loop(0, n_z, group_product, 0)

    for moving in sends:
        if moving is not None:
            moving.wait_send()
    for zz, tag, to_next, to_last, to_across in late:
        pl.when(dx != 3)(lambda: to_next.wait_send())
        pl.when(dx != 1)(lambda: to_last.wait_send())
        pl.when((dx == 0) & root)(lambda: to_across.wait_send())

    def sent_plane(x, carry):
        to_behind(occ_ref.at[:, x], far.at[x], x).wait_send()
        return carry

    def passed_plane(x, carry):
        to_sibling(occ_ref.at[:, x], near.at[x], x).wait_send()
        return carry

    def passed_far(x, carry):
        to_sibling(far.at[x], near.at[x], x).wait_send()
        return carry

    to_behind(level_ref, far_level, PLANES).wait_send()
    lax.fori_loop(0, PLANES, sent_plane, 0)

    @pl.when(core == 1)
    def _():
        to_sibling(level_ref, near_level, PLANES).wait_send()
        lax.fori_loop(0, PLANES, passed_plane, 0)

    @pl.when(core == 0)
    def _():
        to_sibling(far_level, near_level, PLANES).wait_send()
        lax.fori_loop(0, PLANES, passed_far, 0)


def whole_response(occ, emp, gvectors, energies, ztab, xytabs, n_z):
    bf16, f32 = jnp.bfloat16, jnp.float32
    half = NG // 16
    anywhere, vmem = pl.BlockSpec(memory_space=pl.ANY), pl.BlockSpec(memory_space=pltpu.VMEM)
    return pl.pallas_call(
        response_kernel,
        out_shape=jax.ShapeDtypeStruct((2, half // 2, 2 * half), f32),
        in_specs=[anywhere, anywhere, vmem, vmem, vmem, anywhere, anywhere],
        out_specs=vmem,
        scratch_shapes=[
            pltpu.VMEM((PLANES, 2, 4, CELLS), bf16),
            pltpu.VMEM((PLANES, 2, 4, CELLS), bf16),
            pltpu.VMEM((8, LANES), f32),
            pltpu.VMEM((8, LANES), f32),
            pltpu.VMEM((8, LANES), f32),
            pltpu.VMEM((2, PLANES, 8, CELLS), bf16),
            pltpu.VMEM((Z_ROWS, GROUP_CELLS), bf16),
            pltpu.VMEM((PLANES // BATCH, WAVE_ROWS, DEPTH), bf16),
            pltpu.VMEM((16, CELLS), f32),
            pltpu.VMEM((GROUPS * LANES, GROUP_CELLS), bf16),
            pltpu.VMEM((Z_ROWS, GROUPS * LANES), f32),
            pltpu.VMEM((Q_SLOTS // 2, DEPTH, 2 * LANES), bf16),
            pltpu.VMEM((Q_SLOTS * WAVE_ROWS, LANES), f32),
            pltpu.VMEM((512, LANES), f32),
            pltpu.VMEM((1, NG), jnp.int32),
            pltpu.SMEM((1, NG), jnp.int32),
            pltpu.VMEM((1, NG), f32),
            pltpu.VMEM((NG, LANES), f32),
            pltpu.VMEM((2, 4, 2, half, LANES), bf16),
            pltpu.VMEM((n_z, 2, 2, 2, half, LANES), bf16),
            pltpu.VMEM((n_z, 2, 2, half // 2, LANES), bf16),
            pltpu.VMEM((2, 2, half, LANES), bf16),
            pltpu.VMEM((2, 2, half, LANES), bf16),
            pltpu.VMEM((4, 2, half, LANES), bf16),
            pltpu.VMEM((2, half, LANES), bf16),
            pltpu.VMEM((2, half, LANES), bf16),
            pltpu.SemaphoreType.DMA((PLANES + 1,)),
            pltpu.SemaphoreType.DMA((PLANES + 1,)),
            pltpu.SemaphoreType.DMA((PLANES + 1,)),
            pltpu.SemaphoreType.DMA((PLANES + 1,)),
            pltpu.SemaphoreType.DMA((4,)),
            pltpu.SemaphoreType.DMA((128,)),
            pltpu.SemaphoreType.DMA((8,)),
            pltpu.SemaphoreType.DMA((6, 2, n_z // 2 + 1)),
            pltpu.SemaphoreType.DMA((3, 2)),
            pltpu.SemaphoreType.DMA((3, n_z)),
        ],
        compiler_params=pltpu.CompilerParams(
            collective_id=0, has_side_effects=True, vmem_limit_bytes=60 * 2**20
        ),
        cost_estimate=pl.CostEstimate(
            flops=16_000_000_000, bytes_accessed=12_000_000, transcendentals=0
        ),
    )(occ, emp, gvectors, *energies, ztab, xytabs)


def shards(ztab, xytabs, occupied_states, empty_states, occ_energy, empty_energy, gvectors):
    occ = jnp.transpose(occupied_states, (0, 2, 1, 3))
    emp = jnp.transpose(empty_states, (0, 2, 1, 3))
    energies = occ_energy.reshape(1, -1), empty_energy.reshape(1, -1)
    n_z = lax.axis_size("blk") // 4
    out = whole_response(occ, emp, gvectors, energies, ztab, xytabs, n_z)
    return jnp.transpose(out, (1, 0, 2))


def solution(mesh):
    ztab = z_table()
    xytabs = plane_table(mesh.shape["pw"])
    return jax.shard_map(
        lambda *args: shards(jnp.asarray(ztab), jnp.asarray(xytabs), *args),
        mesh=mesh,
        in_specs=(P(None, "blk", "pw", None), P(None, "blk", "pw", None), P("blk"), P("blk"), P()),
        out_specs=P("blk", None, "pw"),
        check_vma=False,
    )
```

```python
import math

import jax
import jax.numpy as jnp
import numpy as np
from jax import lax
from jax.experimental import pallas as pl
from jax.experimental.pallas import tpu as pltpu
from jax.sharding import PartitionSpec as P
import ml_dtypes

GX = 72
GY = 72
GZ = 144
KMAX = 16
SIDE = 2 * KMAX + 1
PLANES = 9
CELLS = GY * GZ
NG = 4096
GROUPS = 9
GROUP_CELLS = 8 * GZ
Z_ROWS = SIDE * 8
ROWS_X = 80
BATCH = 3
DEPTH = BATCH * ROWS_X
HALF = (SIDE * SIDE + 1) // 2
WAVE_ROWS = 1096
Q_SLOTS = 34
LANES = 128
omega_shift = 0.5


def z_table():
    z = np.arange(GZ)
    out = np.zeros((Z_ROWS, GROUP_CELLS), np.float64)
    for q in range(KMAX + 1):
        angle = 2 * np.pi * ((q * z) % GZ) / GZ
        for y in range(8):
            out[q * 8 + y, y * GZ : (y + 1) * GZ] = np.cos(angle)
            if q:
                out[(KMAX + q) * 8 + y, y * GZ : (y + 1) * GZ] = np.sin(angle)
    return out.astype(np.float32).astype(ml_dtypes.bfloat16)


def plane_table(groups):
    h = np.arange(HALF)
    p = (h + KMAX) // SIDE
    a = h - SIDE * p
    out = np.zeros((groups, WAVE_ROWS, PLANES, ROWS_X), np.float64)
    y = np.arange(GY)
    for group in range(groups):
        for plane in range(PLANES):
            x = group * PLANES + plane
            steps = (p[:, None] * y[None, :] + a[:, None] * x) % GX
            out[group, 0 : 2 * HALF : 2, plane, :GY] = np.cos(2 * np.pi * steps / GX)
            out[group, 1 : 2 * HALF : 2, plane, :GY] = np.sin(2 * np.pi * steps / GX)
    out = out.reshape(groups, WAVE_ROWS, PLANES // BATCH, DEPTH).transpose(0, 2, 1, 3)
    return out.astype(np.float32).astype(ml_dtypes.bfloat16)


def turned(value):
    lane = lax.broadcasted_iota(jnp.int32, value.shape, 1)
    ahead = pltpu.roll(value, LANES - 8, 1)
    behind = pltpu.roll(value, 8, 1)
    return jnp.where((lane & 8) == 0, ahead, -behind)


MESH = pl.DeviceIdType.MESH


def response_kernel(
    occ_ref, emp_ref, wave_ref, occ_energy_ref, emp_energy_ref, ztab_ref, xytab_ref, out_ref,
    near, far, level_ref, near_level, far_level, emp, ztab, xytab, occ_f, pairs, depth_out, sections, waves,
    picked, index_v, index_s, sign_v, sign_rows, part_ref, everyone, left, transit, relay, passed, arrived, plane_sum,
    other, ahead_sems, far_sems, pass_sems, near_sems, load_sems, send_sems, sum_sems, ring_sems,
    side_sems, left_sems,
):
    blk, pw = lax.axis_index("blk"), lax.axis_index("pw")
    count = lax.axis_size("blk")
    n_z = count // 4
    z, y, core = blk // 4, (blk // 2) % 2, blk % 2
    x, y_hi = pw % 4, pw // 4
    f32, bf16 = jnp.float32, jnp.bfloat16

    def place(z=z, y=y, core=core, x=x, y_hi=y_hi):
        return {"blk": z * 4 + y * 2 + core, "pw": y_hi * 4 + x}

    x_next, x_last = place(x=(x + 1) % 4), place(x=(x + 3) % 4)
    z_next, z_last = place(z=(z + 1) % n_z), place(z=(z + n_z - 1) % n_z)
    sibling, beside = place(core=1 - core), place(y=1 - y)
    facing, across = place(y_hi=1 - y_hi), place(y=1 - y, y_hi=1 - y_hi)
    behind = {"blk": (blk + count - 2) % count, "pw": pw}
    ahead = {"blk": (blk + 2) % count, "pw": pw}

    barrier = pltpu.get_barrier_semaphore()
    neighbours = (
        x_next, x_last, z_next, z_last, sibling, beside, facing, across, behind, ahead
    )
    for device in neighbours:
        pl.semaphore_signal(barrier, inc=1, device_id=device, device_id_type=MESH)
    pl.semaphore_wait(barrier, len(neighbours))

    def to_behind(source, target, spot):
        return pltpu.make_async_remote_copy(
            src_ref=source, dst_ref=target, send_sem=ahead_sems.at[spot],
            recv_sem=far_sems.at[spot], device_id=behind, device_id_type=MESH,
        )

    def to_sibling(source, target, spot):
        return pltpu.make_async_remote_copy(
            src_ref=source, dst_ref=target, send_sem=pass_sems.at[spot],
            recv_sem=near_sems.at[spot], device_id=sibling, device_id_type=MESH,
        )

    def landed(target, arrival):
        pltpu.make_async_copy(target, target, arrival).wait()

    def send_plane(x, carry):
        to_behind(occ_ref.at[:, x], far.at[x], x).start()
        return carry

    def pass_plane(x, carry):
        to_sibling(occ_ref.at[:, x], near.at[x], x).start()
        return carry

    lane = lax.broadcasted_iota(jnp.int32, (8, LANES), 1)
    occ_energy = occ_energy_ref[...].astype(f32)
    emp_energy = emp_energy_ref[...].astype(f32)
    spread = jnp.zeros((8, LANES), f32)
    for v in range(4):
        spread = jnp.where((lane // 16) % 4 == v, occ_energy[:, v : v + 1], spread)
    level_ref[...] = spread
    emp_level = jnp.zeros((8, LANES), f32)
    for c in range(8):
        emp_level = jnp.where(lane % 8 == c, emp_energy[:, c : c + 1], emp_level)
    to_behind(level_ref, far_level, PLANES).start()
    lax.fori_loop(0, PLANES, send_plane, 0)

    @pl.when(core == 1)
    def _():
        to_sibling(level_ref, near_level, PLANES).start()
        lax.fori_loop(0, PLANES, pass_plane, 0)

    loads = [
        pltpu.make_async_copy(emp_ref, emp, load_sems.at[0]),
        pltpu.make_async_copy(ztab_ref, ztab, load_sems.at[1]),
        pltpu.make_async_copy(xytab_ref.at[pw], xytab, load_sems.at[2]),
    ]
    for load in loads:
        load.start()

    flat = SIDE * wave_ref[1:2, :] + wave_ref[0:1, :]
    index_v[...] = (wave_ref[2:3, :] + KMAX) * WAVE_ROWS + 2 * jnp.abs(flat)
    sign_v[...] = jnp.where(flat < 0, -1.0, 1.0).astype(jnp.float32)
    index_move = pltpu.make_async_copy(index_v, index_s, load_sems.at[3])
    index_move.start()
    for load in loads:
        load.wait()
    index_move.wait()

    def group_pairs(x, group):
        for part in range(3):
            start = group * GROUP_CELLS + part * 384
            cells = slice(start, start + 384)
            emp_re = emp[0, x, :, cells].astype(jnp.float32)
            emp_im = emp[1, x, :, cells].astype(jnp.float32)
            for v in range(8):
                row = v if v < 4 else v + 4
                occ_re = occ_f[row : row + 1, cells]
                occ_im = occ_f[row + 4 : row + 5, cells]
                both = jnp.concatenate(
                    [occ_re * emp_re + occ_im * emp_im, occ_re * emp_im - occ_im * emp_re], axis=0
                )
                rows = slice(group * LANES + v * 16, group * LANES + v * 16 + 16)
                pairs[rows, part * 384 : part * 384 + 384] = both.astype(jnp.bfloat16)

    blank = jnp.zeros((ROWS_X - GY, LANES), jnp.float32)

    def rows_of(first):
        parts = [depth_out[first : first + 8, t * LANES : (t + 1) * LANES] for t in range(GROUPS)]
        return jnp.concatenate(parts + [blank], axis=0)

    def one_plane(x, spot):
        landed(far.at[x], far_sems.at[x])

        @pl.when(core == 0)
        def _():
            to_sibling(far.at[x], near.at[x], x).start()

        landed(near.at[x], near_sems.at[x])
        for part in range(2):
            occ_f[part * 4 : part * 4 + 4, :] = near[x, part].astype(jnp.float32)
            occ_f[part * 4 + 8 : part * 4 + 12, :] = far[x, part].astype(jnp.float32)

        for start in range(0, GROUPS, 2):
            stop = min(start + 2, GROUPS)
            for group in range(start, stop):
                group_pairs(x, group)
            lines = slice(start * LANES, stop * LANES)
            depth_out[:, lines] = lax.dot_general(
                ztab[...], pairs[lines, :], (((1,), (1,)), ((), ())),
                preferred_element_type=jnp.float32,
            )
        rows = pl.ds(pl.multiple_of(spot * ROWS_X, 16), ROWS_X)

        def put(slot, value):
            half = slot % 2
            sections[slot // 2, rows, half * LANES : (half + 1) * LANES] = value.astype(jnp.bfloat16)

        put(KMAX, rows_of(0))
        for q in range(1, KMAX + 1):
            cosine = rows_of(q * 8)
            sine = turned(rows_of((KMAX + q) * 8))
            put(KMAX + q, cosine + sine)
            put(KMAX - q, cosine - sine)

    sections[Q_SLOTS // 2 - 1, :, LANES:] = jnp.zeros((DEPTH, LANES), jnp.bfloat16)
    def clear(k, carry):
        rows = pl.ds(pl.multiple_of(k * WAVE_ROWS, 8), WAVE_ROWS)
        waves[rows, :] = jnp.zeros((WAVE_ROWS, LANES), jnp.float32)
        return carry

    lax.fori_loop(0, Q_SLOTS, clear, 0)

    def stand(step, carry):
        first = pl.multiple_of(step * 128, 128)
        row = sign_v[:, pl.ds(first, 128)]
        sign_rows[pl.ds(first, 128), :] = jnp.broadcast_to(row, (128, LANES)).T
        return carry

    lax.fori_loop(0, NG // 128, stand, 0)
    landed(far_level, far_sems.at[PLANES])

    @pl.when(core == 0)
    def _():
        to_sibling(far_level, near_level, PLANES).start()

    def each_batch(batch, carry):
        def each_plane(spot, carry):
            one_plane(batch * BATCH + spot, spot)
            return carry

        lax.fori_loop(0, BATCH, each_plane, 0)

        def slot_pair(k, carry):
            product = jnp.dot(xytab[batch], sections[k], preferred_element_type=jnp.float32)
            first = pl.multiple_of(k * 2 * WAVE_ROWS, 8)
            for half in range(2):
                rows = pl.ds(first + half * WAVE_ROWS, WAVE_ROWS)
                waves[rows, :] += product[:, half * LANES : (half + 1) * LANES]
            return carry

        lax.fori_loop(0, Q_SLOTS // 2, slot_pair, 0)
        return carry

    lax.fori_loop(0, PLANES // BATCH, each_batch, 0)
    landed(near_level, near_sems.at[PLANES])
    occ_level = jnp.where(lane < LANES // 2, near_level[...], far_level[...])
    scale = jnp.sqrt(2.0 / (emp_level - occ_level + omega_shift))[0:1]

    def chunk(yy, xx, half):
        base = (yy * 4 + xx) * 512 + half * 256

        def pick(step, carry):
            first = step * 16
            for i in range(16):
                row = index_s[0, base + first + i]
                picked[pl.ds((first + i) * 2, 2), :] = waves[pl.ds(row, 2), :]
            return carry

        lax.fori_loop(0, 16, pick, 0)
        for part in range(2):
            cosine = picked[pl.ds(part * 256, 128, stride=2), :]
            sine = picked[pl.ds(part * 256 + 1, 128, stride=2), :]
            first = pl.multiple_of(base + part * 128, 128)
            total = (cosine + sign_rows[pl.ds(first, 128), :] * turned(sine)) * scale
            part_ref[yy, xx, half, part * 128 : part * 128 + 128, :] = total.astype(bf16)

    def both_chunks(xx, half):
        def one(yy, carry):
            chunk(yy, xx, half)
            return carry

        lax.fori_loop(0, 2, one, 0)

    sends = []

    def copy(source, target, arrival, device):
        return pltpu.make_async_remote_copy(
            src_ref=source, dst_ref=target, send_sem=send_sems.at[len(sends)], recv_sem=arrival,
            device_id=device, device_id_type=MESH,
        )

    def send(source, target, arrival, device):
        moving = copy(source, target, arrival, device)
        moving.start()
        sends.append(moving)

    out_ref[...] = jnp.zeros_like(out_ref)
    rows = everyone.shape[4] * 2
    half_rows, quarter = rows // 2, rows // 4

    xn, xl, xo = (x + 1) % 4, (x + 3) % 4, (x + 2) % 4

    def pass_on(half, xx, device):
        landed(relay.at[half], sum_sems.at[half])
        share = part_ref[:, xx, half].astype(f32) + relay[half].astype(f32)
        passed[half] = share.astype(bf16)
        send(passed.at[half], arrived.at[2 + half], sum_sems.at[4 + half], device)

    def x_total(yy, half):
        first, second = (2, 1) if half == 0 else (0, 3)
        return (
            part_ref[yy, x, half].astype(f32)
            + arrived[first, yy].astype(f32)
            + arrived[second, yy].astype(f32)
        )

    def cross_over(half):
        for spot in (2, 1) if half == 0 else (0, 3):
            landed(arrived.at[spot], sum_sems.at[2 + spot])
        plane_sum[half] = x_total(1 - y_hi, half).astype(bf16)
        send(plane_sum.at[half], other.at[half], sum_sems.at[6 + half], facing)

    def own_rho(half):
        landed(other.at[half], sum_sems.at[6 + half])
        total = x_total(y_hi, half) + other[half].astype(f32)
        everyone[z, y, core, half] = total.astype(bf16)

    both_chunks(xo, 0)
    send(part_ref.at[:, xo, 0], relay.at[0], sum_sems.at[0], x_next)
    both_chunks(xl, 0)
    send(part_ref.at[:, xl, 0], arrived.at[1], sum_sems.at[3], x_last)
    both_chunks(xn, 0)
    both_chunks(x, 0)
    pass_on(0, xn, x_next)
    both_chunks(xo, 1)
    send(part_ref.at[:, xo, 1], relay.at[1], sum_sems.at[1], x_last)
    both_chunks(xn, 1)
    send(part_ref.at[:, xn, 1], arrived.at[0], sum_sems.at[2], x_next)
    both_chunks(xl, 1)
    cross_over(0)
    both_chunks(x, 1)
    pass_on(1, xl, x_last)

    own_rho(0)
    mine = lambda half: everyone.at[z, y, core, half]
    theirs = lambda half: everyone.at[z, 1 - y, core, half]
    upper = lambda zz: everyone.at[zz, :, core, 0]
    lower = lambda zz, yy: everyone.at[zz, yy, core, 1]
    send(mine(0), mine(0), side_sems.at[0, 0], beside)
    send(mine(0), mine(0), side_sems.at[1, 0], sibling)
    cross_over(1)
    landed(theirs(0), side_sems.at[0, 0])
    send(upper(z), upper(z), ring_sems.at[0, 0, 1], z_next)
    send(upper(z), upper(z), ring_sems.at[0, 1, 1], z_last)
    send(theirs(0), theirs(0), side_sems.at[2, 0], sibling)
    own_rho(1)
    send(lower(z, y), lower(z, y), ring_sems.at[1, 0, 1], z_next)
    send(lower(z, y), lower(z, y), ring_sems.at[1, 1, 1], z_last)
    send(mine(1), mine(1), side_sems.at[0, 1], beside)
    send(mine(1), mine(1), side_sems.at[1, 1], sibling)

    longest = {(0, 0): n_z // 2, (0, 1): n_z // 2 - 1, (1, 0): n_z // 2 - 1, (1, 1): n_z // 2}

    def ring_step(step):
        for half in (0, 1):
            for way in (0, 1):
                if step > longest[half, way]:
                    continue
                origin = (z + n_z - step) % n_z if way == 0 else (z + step) % n_z
                piece = upper(origin) if half == 0 else lower(origin, y)
                landed(piece, ring_sems.at[half, way, step])
                if step < longest[half, way]:
                    send(piece, piece, ring_sems.at[half, way, step + 1], z_next if way == 0 else z_last)
                if half == 1:
                    send(piece, piece, ring_sems.at[2, way, step], beside)
                send(piece, piece, ring_sems.at[3 + half, way, step], sibling)

    def side_step(step):
        for way in (0, 1):
            if step > longest[1, way]:
                continue
            origin = (z + n_z - step) % n_z if way == 0 else (z + step) % n_z
            piece = lower(origin, 1 - y)
            landed(piece, ring_sems.at[2, way, step])
            send(piece, piece, ring_sems.at[5, way, step], sibling)

    def rest_step(step):
        if step == 0:
            for yy, spot in ((y, 1), (1 - y, 2)):
                for half in range(2):
                    landed(everyone.at[z, yy, 1 - core, half], side_sems.at[spot, half])
            return
        for way in (0, 1):
            origin = (z + n_z - step) % n_z if way == 0 else (z + step) % n_z
            if step <= longest[0, way]:
                landed(everyone.at[origin, :, 1 - core, 0], ring_sems.at[3, way, step])
            if step <= longest[1, way]:
                landed(everyone.at[origin, y, 1 - core, 1], ring_sems.at[4, way, step])
                landed(everyone.at[origin, 1 - y, 1 - core, 1], ring_sems.at[5, way, step])

    dx = (x + 4 - z % 4) % 4
    root = z // 4 == y_hi
    first = core * quarter
    eighth = quarter // 2

    def group_origins(step):
        if step == 0:
            return ((z, 0),)
        if step == n_z // 2:
            return (((z + step) % n_z, step),)
        return (((z + n_z - step) % n_z, step), ((z + step) % n_z, n_z - step))

    piece_rows = quarter // 4
    held = lambda zz, part: left.at[zz, :, :, pl.ds(part * eighth, eighth)]
    piece = lambda zz, q: left.at[zz, :, :, pl.ds(q * piece_rows, piece_rows)]
    far_row = jnp.logical_not(root)
    late = []

    def left_copies(step):
        made = []
        for zz, tag in group_origins(step):
            base = len(sends)

            def numbered(source, target, spot, device, offset):
                return pltpu.make_async_remote_copy(
                    src_ref=source, dst_ref=target, send_sem=send_sems.at[base + offset],
                    recv_sem=left_sems.at[spot, tag], device_id=device, device_id_type=MESH,
                )

            there = lambda start, count: everyone.at[zz, :, :, 1 - y, pl.ds(first + start, count)]
            made.append(dict(
                zz=zz,
                tag=tag,
                next_half=numbered(held(zz, 0), held(zz, 0), 0, x_next, 0),
                last_half=numbered(held(zz, 1), held(zz, 1), 1, x_last, 1),
                cross_half=numbered(there(0, eighth), held(zz, 0), 4, across, 2),
                lend_next=numbered(there(eighth, piece_rows), transit.at[zz], 5, x_next, 3),
                lend_last=numbered(
                    there(eighth + piece_rows, piece_rows), transit.at[zz], 5, x_last, 4
                ),
                cross_next=numbered(transit.at[zz], piece(zz, 2), 4, across, 2),
                cross_last=numbered(transit.at[zz], piece(zz, 3), 4, across, 2),
                next_0=numbered(piece(zz, 0), piece(zz, 0), 0, x_next, 0),
                last_1=numbered(piece(zz, 1), piece(zz, 1), 1, x_last, 1),
                next_2=numbered(piece(zz, 2), piece(zz, 2), 2, x_next, 3),
                last_3=numbered(piece(zz, 3), piece(zz, 3), 3, x_last, 4),
            ))
            sends.extend([None] * 5)
        late.extend(made)
        return made

    def left_from_root(made):
        @pl.when((dx == 0) & root)
        def _():
            for group in made:
                zz = group["zz"]
                group["cross_half"].start()
                group["lend_next"].start()
                group["lend_last"].start()
                left[zz] = everyone[zz, :, :, y, pl.ds(first, quarter)]
                group["next_half"].start()
                group["last_half"].start()

    def got(group, target, spot):
        landed(target, left_sems.at[spot, group["tag"]])

    def beside_root(made):
        @pl.when((dx == 1) & root)
        def _():
            for group in made:
                got(group, transit.at[group["zz"]], 5)
                group["cross_next"].start()
                got(group, held(group["zz"], 0), 0)
                group["next_half"].start()

        @pl.when((dx == 3) & root)
        def _():
            for group in made:
                got(group, transit.at[group["zz"]], 5)
                group["cross_last"].start()
                got(group, held(group["zz"], 1), 1)
                group["last_half"].start()

    def opposite_root(made):
        @pl.when((dx == 2) & root)
        def _():
            for group in made:
                got(group, held(group["zz"], 0), 0)
                group["next_half"].start()
                got(group, held(group["zz"], 1), 1)
                group["last_half"].start()

    def far_heads(made):
        @pl.when((dx == 0) & far_row)
        def _():
            for group in made:
                got(group, held(group["zz"], 0), 4)
                group["next_0"].start()
                group["last_1"].start()

        @pl.when((dx == 1) & far_row)
        def _():
            for group in made:
                got(group, piece(group["zz"], 2), 4)
                group["next_2"].start()
                got(group, piece(group["zz"], 0), 0)
                group["next_0"].start()

        @pl.when((dx == 3) & far_row)
        def _():
            for group in made:
                got(group, piece(group["zz"], 3), 4)
                group["last_3"].start()
                got(group, piece(group["zz"], 1), 1)
                group["last_1"].start()

    def far_opposite(made):
        @pl.when((dx == 2) & far_row)
        def _():
            for group in made:
                for q, name in ((2, "next_2"), (3, "last_3"), (0, "next_0"), (1, "last_1")):
                    got(group, piece(group["zz"], q), q)
                    group[name].start()

    def far_back(made):
        @pl.when((dx == 1) & far_row)
        def _():
            for group in made:
                got(group, piece(group["zz"], 3), 3)
                group["last_3"].start()

        @pl.when((dx == 3) & far_row)
        def _():
            for group in made:
                got(group, piece(group["zz"], 2), 2)
                group["next_2"].start()

    parts = [left_copies(step) for step in range(n_z // 2 + 1)]
    ring_step(1)
    landed(theirs(1), side_sems.at[0, 1])
    send(theirs(1), theirs(1), side_sems.at[2, 1], sibling)
    rest_step(0)
    left_from_root(parts[0])
    ring_step(2)
    side_step(1)
    rest_step(1)
    left_from_root(parts[1])
    ring_step(3)
    side_step(2)
    rest_step(2)
    left_from_root(parts[2])
    beside_root(parts[0])
    ring_step(4)
    side_step(3)
    rest_step(3)
    left_from_root(parts[3])
    beside_root(parts[1])
    opposite_root(parts[0])
    far_heads(parts[0])
    side_step(4)
    rest_step(4)
    left_from_root(parts[4])
    last = n_z // 2
    for step in range(2, last + 4):
        for job, lag, begin in (
            (beside_root, 0, 2), (opposite_root, 1, 1), (far_heads, 1, 1), (far_opposite, 2, 0),
            (far_back, 2, 0),
        ):
            if begin <= step - lag <= last:
                job(parts[step - lag])

    def group_product(k, carry):
        odd = k % 2
        tag = (odd * ((k + 1) // 2) + (1 - odd) * (n_z - k // 2)) % n_z
        zz = (z + n_z - tag) % n_z

        @pl.when((dx == 1) & root)
        def _():
            landed(held(zz, 1), left_sems.at[1, tag])

        @pl.when((dx == 3) & root)
        def _():
            landed(held(zz, 0), left_sems.at[0, tag])

        @pl.when((dx == 0) & far_row)
        def _():
            landed(piece(zz, 2), left_sems.at[2, tag])
            landed(piece(zz, 3), left_sems.at[3, tag])

        @pl.when((dx == 1) & far_row)
        def _():
            landed(piece(zz, 1), left_sems.at[1, tag])

        @pl.when((dx == 3) & far_row)
        def _():
            landed(piece(zz, 0), left_sems.at[0, tag])

        straight = [left[zz, i // 2, i % 2].astype(f32) for i in range(4)]
        side = jnp.concatenate([turned(value) for value in straight], axis=1)
        both = jnp.concatenate([-jnp.concatenate(straight, axis=1), side], axis=0)
        both = both.astype(bf16)
        for half in range(2):
            right = jnp.concatenate([everyone[zz, i // 2, i % 2, half] for i in range(4)], axis=1)
            product = lax.dot_general(
                both, right, (((1,), (1,)), ((), ())), preferred_element_type=f32
            )
            for part in range(2):
                spot = (part, slice(None), slice(half * half_rows, (half + 1) * half_rows))
                out_ref[spot] += product[part * quarter : (part + 1) * quarter]
        return carry

    lax.fori_loop(0, n_z, group_product, 0)

    for moving in sends:
        if moving is not None:
            moving.wait_send()
    roles = (
        ("next_half", root & (dx != 3)), ("last_half", root & (dx != 1)),
        ("cross_half", root & (dx == 0)), ("lend_next", root & (dx == 0)),
        ("lend_last", root & (dx == 0)), ("cross_next", root & (dx == 1)),
        ("cross_last", root & (dx == 3)), ("next_0", far_row & (dx != 3)),
        ("last_1", far_row & (dx != 1)), ("next_2", far_row & (dx != 0)),
        ("last_3", far_row & (dx != 0)),
    )
    for name, mine_to_send in roles:

        @pl.when(mine_to_send)
        def _():
            for group in late:
                group[name].wait_send()

    def sent_plane(x, carry):
        to_behind(occ_ref.at[:, x], far.at[x], x).wait_send()
        return carry

    def passed_plane(x, carry):
        to_sibling(occ_ref.at[:, x], near.at[x], x).wait_send()
        return carry

    def passed_far(x, carry):
        to_sibling(far.at[x], near.at[x], x).wait_send()
        return carry

    to_behind(level_ref, far_level, PLANES).wait_send()
    lax.fori_loop(0, PLANES, sent_plane, 0)

    @pl.when(core == 1)
    def _():
        to_sibling(level_ref, near_level, PLANES).wait_send()
        lax.fori_loop(0, PLANES, passed_plane, 0)

    @pl.when(core == 0)
    def _():
        to_sibling(far_level, near_level, PLANES).wait_send()
        lax.fori_loop(0, PLANES, passed_far, 0)


def whole_response(occ, emp, gvectors, energies, ztab, xytabs, n_z):
    bf16, f32 = jnp.bfloat16, jnp.float32
    half = NG // 16
    anywhere, vmem = pl.BlockSpec(memory_space=pl.ANY), pl.BlockSpec(memory_space=pltpu.VMEM)
    return pl.pallas_call(
        response_kernel,
        out_shape=jax.ShapeDtypeStruct((2, half // 2, 2 * half), f32),
        in_specs=[anywhere, anywhere, vmem, vmem, vmem, anywhere, anywhere],
        out_specs=vmem,
        scratch_shapes=[
            pltpu.VMEM((PLANES, 2, 4, CELLS), bf16),
            pltpu.VMEM((PLANES, 2, 4, CELLS), bf16),
            pltpu.VMEM((8, LANES), f32),
            pltpu.VMEM((8, LANES), f32),
            pltpu.VMEM((8, LANES), f32),
            pltpu.VMEM((2, PLANES, 8, CELLS), bf16),
            pltpu.VMEM((Z_ROWS, GROUP_CELLS), bf16),
            pltpu.VMEM((PLANES // BATCH, WAVE_ROWS, DEPTH), bf16),
            pltpu.VMEM((16, CELLS), f32),
            pltpu.VMEM((GROUPS * LANES, GROUP_CELLS), bf16),
            pltpu.VMEM((Z_ROWS, GROUPS * LANES), f32),
            pltpu.VMEM((Q_SLOTS // 2, DEPTH, 2 * LANES), bf16),
            pltpu.VMEM((Q_SLOTS * WAVE_ROWS, LANES), f32),
            pltpu.VMEM((512, LANES), f32),
            pltpu.VMEM((1, NG), jnp.int32),
            pltpu.SMEM((1, NG), jnp.int32),
            pltpu.VMEM((1, NG), f32),
            pltpu.VMEM((NG, LANES), f32),
            pltpu.VMEM((2, 4, 2, half, LANES), bf16),
            pltpu.VMEM((n_z, 2, 2, 2, half, LANES), bf16),
            pltpu.VMEM((n_z, 2, 2, half // 2, LANES), bf16),
            pltpu.VMEM((n_z, 2, 2, half // 8, LANES), bf16),
            pltpu.VMEM((2, 2, half, LANES), bf16),
            pltpu.VMEM((2, 2, half, LANES), bf16),
            pltpu.VMEM((4, 2, half, LANES), bf16),
            pltpu.VMEM((2, half, LANES), bf16),
            pltpu.VMEM((2, half, LANES), bf16),
            pltpu.SemaphoreType.DMA((PLANES + 1,)),
            pltpu.SemaphoreType.DMA((PLANES + 1,)),
            pltpu.SemaphoreType.DMA((PLANES + 1,)),
            pltpu.SemaphoreType.DMA((PLANES + 1,)),
            pltpu.SemaphoreType.DMA((4,)),
            pltpu.SemaphoreType.DMA((144,)),
            pltpu.SemaphoreType.DMA((8,)),
            pltpu.SemaphoreType.DMA((6, 2, n_z // 2 + 1)),
            pltpu.SemaphoreType.DMA((3, 2)),
            pltpu.SemaphoreType.DMA((6, n_z)),
        ],
        compiler_params=pltpu.CompilerParams(
            collective_id=0, has_side_effects=True, vmem_limit_bytes=60 * 2**20
        ),
        cost_estimate=pl.CostEstimate(
            flops=16_000_000_000, bytes_accessed=12_000_000, transcendentals=0
        ),
    )(occ, emp, gvectors, *energies, ztab, xytabs)


def shards(ztab, xytabs, occupied_states, empty_states, occ_energy, empty_energy, gvectors):
    occ = jnp.transpose(occupied_states, (0, 2, 1, 3))
    emp = jnp.transpose(empty_states, (0, 2, 1, 3))
    energies = occ_energy.reshape(1, -1), empty_energy.reshape(1, -1)
    n_z = lax.axis_size("blk") // 4
    out = whole_response(occ, emp, gvectors, energies, ztab, xytabs, n_z)
    return jnp.transpose(out, (1, 0, 2))


def solution(mesh):
    ztab = z_table()
    xytabs = plane_table(mesh.shape["pw"])
    return jax.shard_map(
        lambda *args: shards(jnp.asarray(ztab), jnp.asarray(xytabs), *args),
        mesh=mesh,
        in_specs=(P(None, "blk", "pw", None), P(None, "blk", "pw", None), P("blk"), P("blk"), P()),
        out_specs=P("blk", None, "pw"),
        check_vma=False,
    )
```

```python
import math

import jax
import jax.numpy as jnp
import numpy as np
from jax import lax
from jax.experimental import pallas as pl
from jax.experimental.pallas import tpu as pltpu
from jax.sharding import PartitionSpec as P
import ml_dtypes

GX = 72
GY = 72
GZ = 144
KMAX = 16
SIDE = 2 * KMAX + 1
PLANES = 9
CELLS = GY * GZ
NG = 4096
GROUPS = 9
GROUP_CELLS = 8 * GZ
Z_ROWS = SIDE * 8
ROWS_X = 80
BATCH = 3
DEPTH = BATCH * ROWS_X
HALF = (SIDE * SIDE + 1) // 2
WAVE_ROWS = 1096
Q_SLOTS = 34
LANES = 128
omega_shift = 0.5


def z_table():
    z = np.arange(GZ)
    out = np.zeros((Z_ROWS, GROUP_CELLS), np.float64)
    for q in range(KMAX + 1):
        angle = 2 * np.pi * ((q * z) % GZ) / GZ
        for y in range(8):
            out[q * 8 + y, y * GZ : (y + 1) * GZ] = np.cos(angle)
            if q:
                out[(KMAX + q) * 8 + y, y * GZ : (y + 1) * GZ] = np.sin(angle)
    return out.astype(np.float32).astype(ml_dtypes.bfloat16)


def plane_table(groups):
    h = np.arange(HALF)
    p = (h + KMAX) // SIDE
    a = h - SIDE * p
    out = np.zeros((groups, WAVE_ROWS, PLANES, ROWS_X), np.float64)
    y = np.arange(GY)
    for group in range(groups):
        for plane in range(PLANES):
            x = group * PLANES + plane
            steps = (p[:, None] * y[None, :] + a[:, None] * x) % GX
            out[group, 0 : 2 * HALF : 2, plane, :GY] = np.cos(2 * np.pi * steps / GX)
            out[group, 1 : 2 * HALF : 2, plane, :GY] = np.sin(2 * np.pi * steps / GX)
    out = out.reshape(groups, WAVE_ROWS, PLANES // BATCH, DEPTH).transpose(0, 2, 1, 3)
    return out.astype(np.float32).astype(ml_dtypes.bfloat16)


def turned(value):
    lane = lax.broadcasted_iota(jnp.int32, value.shape, 1)
    ahead = pltpu.roll(value, LANES - 8, 1)
    behind = pltpu.roll(value, 8, 1)
    return jnp.where((lane & 8) == 0, ahead, -behind)


MESH = pl.DeviceIdType.MESH


def response_kernel(
    occ_ref, emp_ref, wave_ref, occ_energy_ref, emp_energy_ref, ztab_ref, xytab_ref, out_ref,
    near, far, level_ref, near_level, far_level, emp, ztab, xytab, occ_f, pairs, depth_out, sections, waves,
    picked, index_v, index_s, sign_v, sign_rows, part_ref, everyone, left, relay, passed, arrived, plane_sum,
    other, ahead_sems, far_sems, pass_sems, near_sems, load_sems, send_sems, sum_sems, ring_sems,
    side_sems, left_sems,
):
    blk, pw = lax.axis_index("blk"), lax.axis_index("pw")
    count = lax.axis_size("blk")
    n_z = count // 4
    z, y, core = blk // 4, (blk // 2) % 2, blk % 2
    x, y_hi = pw % 4, pw // 4
    f32, bf16 = jnp.float32, jnp.bfloat16

    def place(z=z, y=y, core=core, x=x, y_hi=y_hi):
        return {"blk": z * 4 + y * 2 + core, "pw": y_hi * 4 + x}

    x_next, x_last = place(x=(x + 1) % 4), place(x=(x + 3) % 4)
    z_next, z_last = place(z=(z + 1) % n_z), place(z=(z + n_z - 1) % n_z)
    sibling, beside = place(core=1 - core), place(y=1 - y)
    facing, across = place(y_hi=1 - y_hi), place(y=1 - y, y_hi=1 - y_hi)
    behind = {"blk": (blk + count - 2) % count, "pw": pw}
    ahead = {"blk": (blk + 2) % count, "pw": pw}

    barrier = pltpu.get_barrier_semaphore()
    neighbours = (
        x_next, x_last, z_next, z_last, sibling, beside, facing, across, behind, ahead
    )
    for device in neighbours:
        pl.semaphore_signal(barrier, inc=1, device_id=device, device_id_type=MESH)
    pl.semaphore_wait(barrier, len(neighbours))

    def to_behind(source, target, spot):
        return pltpu.make_async_remote_copy(
            src_ref=source, dst_ref=target, send_sem=ahead_sems.at[spot],
            recv_sem=far_sems.at[spot], device_id=behind, device_id_type=MESH,
        )

    def to_sibling(source, target, spot):
        return pltpu.make_async_remote_copy(
            src_ref=source, dst_ref=target, send_sem=pass_sems.at[spot],
            recv_sem=near_sems.at[spot], device_id=sibling, device_id_type=MESH,
        )

    def landed(target, arrival):
        pltpu.make_async_copy(target, target, arrival).wait()

    def send_plane(x, carry):
        to_behind(occ_ref.at[:, x], far.at[x], x).start()
        return carry

    def pass_plane(x, carry):
        to_sibling(occ_ref.at[:, x], near.at[x], x).start()
        return carry

    lane = lax.broadcasted_iota(jnp.int32, (8, LANES), 1)
    occ_energy = occ_energy_ref[...].astype(f32)
    emp_energy = emp_energy_ref[...].astype(f32)
    spread = jnp.zeros((8, LANES), f32)
    for v in range(4):
        spread = jnp.where((lane // 16) % 4 == v, occ_energy[:, v : v + 1], spread)
    level_ref[...] = spread
    emp_level = jnp.zeros((8, LANES), f32)
    for c in range(8):
        emp_level = jnp.where(lane % 8 == c, emp_energy[:, c : c + 1], emp_level)
    to_behind(level_ref, far_level, PLANES).start()
    lax.fori_loop(0, PLANES, send_plane, 0)

    @pl.when(core == 1)
    def _():
        to_sibling(level_ref, near_level, PLANES).start()
        lax.fori_loop(0, PLANES, pass_plane, 0)

    loads = [
        pltpu.make_async_copy(emp_ref, emp, load_sems.at[0]),
        pltpu.make_async_copy(ztab_ref, ztab, load_sems.at[1]),
        pltpu.make_async_copy(xytab_ref.at[pw], xytab, load_sems.at[2]),
    ]
    for load in loads:
        load.start()

    flat = SIDE * wave_ref[1:2, :] + wave_ref[0:1, :]
    index_v[...] = (wave_ref[2:3, :] + KMAX) * WAVE_ROWS + 2 * jnp.abs(flat)
    sign_v[...] = jnp.where(flat < 0, -1.0, 1.0).astype(jnp.float32)
    index_move = pltpu.make_async_copy(index_v, index_s, load_sems.at[3])
    index_move.start()
    for load in loads:
        load.wait()
    index_move.wait()

    def group_pairs(x, group):
        for part in range(3):
            start = group * GROUP_CELLS + part * 384
            cells = slice(start, start + 384)
            emp_re = emp[0, x, :, cells].astype(jnp.float32)
            emp_im = emp[1, x, :, cells].astype(jnp.float32)
            for v in range(8):
                row = v if v < 4 else v + 4
                occ_re = occ_f[row : row + 1, cells]
                occ_im = occ_f[row + 4 : row + 5, cells]
                both = jnp.concatenate(
                    [occ_re * emp_re + occ_im * emp_im, occ_re * emp_im - occ_im * emp_re], axis=0
                )
                rows = slice(group * LANES + v * 16, group * LANES + v * 16 + 16)
                pairs[rows, part * 384 : part * 384 + 384] = both.astype(jnp.bfloat16)

    blank = jnp.zeros((ROWS_X - GY, LANES), jnp.float32)

    def rows_of(first):
        parts = [depth_out[first : first + 8, t * LANES : (t + 1) * LANES] for t in range(GROUPS)]
        return jnp.concatenate(parts + [blank], axis=0)

    def one_plane(x, spot):
        landed(far.at[x], far_sems.at[x])

        @pl.when(core == 0)
        def _():
            to_sibling(far.at[x], near.at[x], x).start()

        landed(near.at[x], near_sems.at[x])
        for part in range(2):
            occ_f[part * 4 : part * 4 + 4, :] = near[x, part].astype(jnp.float32)
            occ_f[part * 4 + 8 : part * 4 + 12, :] = far[x, part].astype(jnp.float32)

        for start in range(0, GROUPS, 2):
            stop = min(start + 2, GROUPS)
            for group in range(start, stop):
                group_pairs(x, group)
            lines = slice(start * LANES, stop * LANES)
            depth_out[:, lines] = lax.dot_general(
                ztab[...], pairs[lines, :], (((1,), (1,)), ((), ())),
                preferred_element_type=jnp.float32,
            )
        rows = pl.ds(pl.multiple_of(spot * ROWS_X, 16), ROWS_X)

        def put(slot, value):
            half = slot % 2
            sections[slot // 2, rows, half * LANES : (half + 1) * LANES] = value.astype(jnp.bfloat16)

        put(KMAX, rows_of(0))
        for q in range(1, KMAX + 1):
            cosine = rows_of(q * 8)
            sine = turned(rows_of((KMAX + q) * 8))
            put(KMAX + q, cosine + sine)
            put(KMAX - q, cosine - sine)

    sections[Q_SLOTS // 2 - 1, :, LANES:] = jnp.zeros((DEPTH, LANES), jnp.bfloat16)
    def clear(k, carry):
        rows = pl.ds(pl.multiple_of(k * WAVE_ROWS, 8), WAVE_ROWS)
        waves[rows, :] = jnp.zeros((WAVE_ROWS, LANES), jnp.float32)
        return carry

    lax.fori_loop(0, Q_SLOTS, clear, 0)

    def stand(step, carry):
        first = pl.multiple_of(step * 128, 128)
        row = sign_v[:, pl.ds(first, 128)]
        sign_rows[pl.ds(first, 128), :] = jnp.broadcast_to(row, (128, LANES)).T
        return carry

    lax.fori_loop(0, NG // 128, stand, 0)
    landed(far_level, far_sems.at[PLANES])

    @pl.when(core == 0)
    def _():
        to_sibling(far_level, near_level, PLANES).start()

    def each_batch(batch, carry):
        def each_plane(spot, carry):
            one_plane(batch * BATCH + spot, spot)
            return carry

        lax.fori_loop(0, BATCH, each_plane, 0)

        def slot_pair(k, carry):
            product = jnp.dot(xytab[batch], sections[k], preferred_element_type=jnp.float32)
            first = pl.multiple_of(k * 2 * WAVE_ROWS, 8)
            for half in range(2):
                rows = pl.ds(first + half * WAVE_ROWS, WAVE_ROWS)
                waves[rows, :] += product[:, half * LANES : (half + 1) * LANES]
            return carry

        lax.fori_loop(0, Q_SLOTS // 2, slot_pair, 0)
        return carry

    lax.fori_loop(0, PLANES // BATCH, each_batch, 0)
    landed(near_level, near_sems.at[PLANES])
    occ_level = jnp.where(lane < LANES // 2, near_level[...], far_level[...])
    scale = jnp.sqrt(2.0 / (emp_level - occ_level + omega_shift))[0:1]

    def chunk(yy, xx, half):
        base = (yy * 4 + xx) * 512 + half * 256

        def pick(step, carry):
            first = step * 32
            for i in range(32):
                row = index_s[0, base + first + i]
                picked[pl.ds((first + i) * 2, 2), :] = waves[pl.ds(row, 2), :]
            return carry

        lax.fori_loop(0, 8, pick, 0)
        for part in range(2):
            cosine = picked[pl.ds(part * 256, 128, stride=2), :]
            sine = picked[pl.ds(part * 256 + 1, 128, stride=2), :]
            first = pl.multiple_of(base + part * 128, 128)
            total = (cosine + sign_rows[pl.ds(first, 128), :] * turned(sine)) * scale
            part_ref[yy, xx, half, part * 128 : part * 128 + 128, :] = total.astype(bf16)

    def both_chunks(xx, half):
        def one(yy, carry):
            chunk(yy, xx, half)
            return carry

        lax.fori_loop(0, 2, one, 0)

    sends = []

    def copy(source, target, arrival, device):
        return pltpu.make_async_remote_copy(
            src_ref=source, dst_ref=target, send_sem=send_sems.at[len(sends)], recv_sem=arrival,
            device_id=device, device_id_type=MESH,
        )

    def send(source, target, arrival, device):
        moving = copy(source, target, arrival, device)
        moving.start()
        sends.append(moving)

    out_ref[...] = jnp.zeros_like(out_ref)
    rows = everyone.shape[4] * 2
    half_rows, quarter = rows // 2, rows // 4

    xn, xl, xo = (x + 1) % 4, (x + 3) % 4, (x + 2) % 4

    def pass_on(half, xx, device):
        landed(relay.at[half], sum_sems.at[half])
        share = part_ref[:, xx, half].astype(f32) + relay[half].astype(f32)
        passed[half] = share.astype(bf16)
        send(passed.at[half], arrived.at[2 + half], sum_sems.at[4 + half], device)

    def x_total(yy, half):
        first, second = (2, 1) if half == 0 else (0, 3)
        return (
            part_ref[yy, x, half].astype(f32)
            + arrived[first, yy].astype(f32)
            + arrived[second, yy].astype(f32)
        )

    def cross_over(half):
        for spot in (2, 1) if half == 0 else (0, 3):
            landed(arrived.at[spot], sum_sems.at[2 + spot])
        plane_sum[half] = x_total(1 - y_hi, half).astype(bf16)
        send(plane_sum.at[half], other.at[half], sum_sems.at[6 + half], facing)

    def own_rho(half):
        landed(other.at[half], sum_sems.at[6 + half])
        total = x_total(y_hi, half) + other[half].astype(f32)
        everyone[z, y, core, half] = total.astype(bf16)

    both_chunks(xo, 0)
    send(part_ref.at[:, xo, 0], relay.at[0], sum_sems.at[0], x_next)
    both_chunks(xl, 0)
    send(part_ref.at[:, xl, 0], arrived.at[1], sum_sems.at[3], x_last)
    both_chunks(xn, 0)
    both_chunks(x, 0)
    pass_on(0, xn, x_next)
    both_chunks(xo, 1)
    send(part_ref.at[:, xo, 1], relay.at[1], sum_sems.at[1], x_last)
    both_chunks(xn, 1)
    send(part_ref.at[:, xn, 1], arrived.at[0], sum_sems.at[2], x_next)
    both_chunks(xl, 1)
    cross_over(0)
    both_chunks(x, 1)
    pass_on(1, xl, x_last)

    own_rho(0)
    mine = lambda half: everyone.at[z, y, core, half]
    theirs = lambda half: everyone.at[z, 1 - y, core, half]
    upper = lambda zz: everyone.at[zz, :, core, 0]
    lower = lambda zz, yy: everyone.at[zz, yy, core, 1]
    send(mine(0), mine(0), side_sems.at[0, 0], beside)
    send(mine(0), mine(0), side_sems.at[1, 0], sibling)
    cross_over(1)
    landed(theirs(0), side_sems.at[0, 0])
    send(upper(z), upper(z), ring_sems.at[0, 0, 1], z_next)
    send(upper(z), upper(z), ring_sems.at[0, 1, 1], z_last)
    send(theirs(0), theirs(0), side_sems.at[2, 0], sibling)
    own_rho(1)
    send(lower(z, y), lower(z, y), ring_sems.at[1, 0, 1], z_next)
    send(lower(z, y), lower(z, y), ring_sems.at[1, 1, 1], z_last)
    send(mine(1), mine(1), side_sems.at[0, 1], beside)
    send(mine(1), mine(1), side_sems.at[1, 1], sibling)

    longest = {(0, 0): n_z // 2, (0, 1): n_z // 2 - 1, (1, 0): n_z // 2 - 1, (1, 1): n_z // 2}

    def ring_step(step):
        for half in (0, 1):
            for way in (0, 1):
                if step > longest[half, way]:
                    continue
                origin = (z + n_z - step) % n_z if way == 0 else (z + step) % n_z
                piece = upper(origin) if half == 0 else lower(origin, y)
                landed(piece, ring_sems.at[half, way, step])
                if step < longest[half, way]:
                    send(piece, piece, ring_sems.at[half, way, step + 1], z_next if way == 0 else z_last)
                if half == 1:
                    send(piece, piece, ring_sems.at[2, way, step], beside)
                send(piece, piece, ring_sems.at[3 + half, way, step], sibling)

    def side_step(step):
        for way in (0, 1):
            if step > longest[1, way]:
                continue
            origin = (z + n_z - step) % n_z if way == 0 else (z + step) % n_z
            piece = lower(origin, 1 - y)
            landed(piece, ring_sems.at[2, way, step])
            send(piece, piece, ring_sems.at[5, way, step], sibling)

    def rest_step(step):
        if step == 0:
            for yy, spot in ((y, 1), (1 - y, 2)):
                for half in range(2):
                    landed(everyone.at[z, yy, 1 - core, half], side_sems.at[spot, half])
            return
        for way in (0, 1):
            origin = (z + n_z - step) % n_z if way == 0 else (z + step) % n_z
            if step <= longest[0, way]:
                landed(everyone.at[origin, :, 1 - core, 0], ring_sems.at[3, way, step])
            if step <= longest[1, way]:
                landed(everyone.at[origin, y, 1 - core, 1], ring_sems.at[4, way, step])
                landed(everyone.at[origin, 1 - y, 1 - core, 1], ring_sems.at[5, way, step])

    dx = (x + 4 - z % 4) % 4
    root = z // 4 == y_hi
    first = core * quarter
    eighth = quarter // 2

    def group_origins(step):
        if step == 0:
            return ((z, 0),)
        if step == n_z // 2:
            return (((z + step) % n_z, step),)
        return (((z + n_z - step) % n_z, step), ((z + step) % n_z, n_z - step))

    held = lambda zz, part: left.at[zz, :, :, pl.ds(part * eighth, eighth)]
    late = []

    def left_copies(step):
        made = []
        for zz, tag in group_origins(step):
            base = len(sends)

            def numbered(source, target, arrival, device, offset):
                return pltpu.make_async_remote_copy(
                    src_ref=source, dst_ref=target, send_sem=send_sems.at[base + offset],
                    recv_sem=arrival, device_id=device, device_id_type=MESH,
                )

            there = everyone.at[zz, :, :, 1 - y, pl.ds(first, quarter)]
            to_next = numbered(held(zz, 0), held(zz, 0), left_sems.at[0, tag], x_next, 0)
            to_last = numbered(held(zz, 1), held(zz, 1), left_sems.at[1, tag], x_last, 1)
            to_across = numbered(there, left.at[zz], left_sems.at[2, tag], across, 2)
            made.append((zz, tag, to_next, to_last, to_across))
            sends.extend([None] * 3)
        late.extend(made)
        return made

    def left_from_root(made):
        @pl.when((dx == 0) & root)
        def _():
            for zz, tag, to_next, to_last, to_across in made:
                to_across.start()
                left[zz] = everyone[zz, :, :, y, pl.ds(first, quarter)]
                to_next.start()
                to_last.start()

    def left_onward(made):
        @pl.when((dx == 0) & jnp.logical_not(root))
        def _():
            for zz, tag, to_next, to_last, to_across in made:
                landed(left.at[zz], left_sems.at[2, tag])
                to_next.start()
                to_last.start()

        @pl.when(dx == 1)
        def _():
            for zz, tag, to_next, to_last, to_across in made:
                landed(held(zz, 0), left_sems.at[0, tag])
                to_next.start()

        @pl.when(dx == 3)
        def _():
            for zz, tag, to_next, to_last, to_across in made:
                landed(held(zz, 1), left_sems.at[1, tag])
                to_last.start()

    def left_middle(made):
        @pl.when(dx == 2)
        def _():
            for zz, tag, to_next, to_last, to_across in made:
                landed(held(zz, 0), left_sems.at[0, tag])
                to_next.start()
                landed(held(zz, 1), left_sems.at[1, tag])
                to_last.start()

    def group_product(k, carry):
        odd = k % 2
        tag = (odd * ((k + 1) // 2) + (1 - odd) * (n_z - k // 2)) % n_z
        zz = (z + n_z - tag) % n_z

        @pl.when(dx == 1)
        def _():
            landed(held(zz, 1), left_sems.at[1, tag])

        @pl.when(dx == 3)
        def _():
            landed(held(zz, 0), left_sems.at[0, tag])

        straight = [left[zz, i // 2, i % 2].astype(f32) for i in range(4)]
        side = jnp.concatenate([turned(value) for value in straight], axis=1)
        both = jnp.concatenate([-jnp.concatenate(straight, axis=1), side], axis=0)
        both = both.astype(bf16)
        for half in range(2):
            right = jnp.concatenate([everyone[zz, i // 2, i % 2, half] for i in range(4)], axis=1)
            product = lax.dot_general(
                both, right, (((1,), (1,)), ((), ())), preferred_element_type=f32
            )
            for part in range(2):
                spot = (part, slice(None), slice(half * half_rows, (half + 1) * half_rows))
                out_ref[spot] += product[part * quarter : (part + 1) * quarter]
        return carry

    def products(begin, end):
        lax.fori_loop(begin, end, group_product, 0)

    parts = [left_copies(step) for step in range(n_z // 2 + 1)]
    ring_step(1)
    landed(theirs(1), side_sems.at[0, 1])
    send(theirs(1), theirs(1), side_sems.at[2, 1], sibling)
    rest_step(0)
    left_from_root(parts[0])
    side_step(1)
    rest_step(1)
    left_from_root(parts[1])
    ring_step(2)
    side_step(2)
    rest_step(2)
    left_from_root(parts[2])
    ring_step(3)
    left_onward(parts[0])
    side_step(3)
    rest_step(3)
    left_from_root(parts[3])
    ring_step(4)
    side_step(4)
    left_onward(parts[1])
    left_middle(parts[0])
    rest_step(4)
    left_from_root(parts[4])
    left_onward(parts[2])
    left_middle(parts[1])
    products(0, 3)
    left_onward(parts[3])
    left_middle(parts[2])
    products(3, 5)
    left_onward(parts[4])
    left_middle(parts[3])
    left_middle(parts[4])
    products(5, n_z)

    for moving in sends:
        if moving is not None:
            moving.wait_send()
    for zz, tag, to_next, to_last, to_across in late:
        pl.when(dx != 3)(lambda: to_next.wait_send())
        pl.when(dx != 1)(lambda: to_last.wait_send())
        pl.when((dx == 0) & root)(lambda: to_across.wait_send())

    def sent_plane(x, carry):
        to_behind(occ_ref.at[:, x], far.at[x], x).wait_send()
        return carry

    def passed_plane(x, carry):
        to_sibling(occ_ref.at[:, x], near.at[x], x).wait_send()
        return carry

    def passed_far(x, carry):
        to_sibling(far.at[x], near.at[x], x).wait_send()
        return carry

    to_behind(level_ref, far_level, PLANES).wait_send()
    lax.fori_loop(0, PLANES, sent_plane, 0)

    @pl.when(core == 1)
    def _():
        to_sibling(level_ref, near_level, PLANES).wait_send()
        lax.fori_loop(0, PLANES, passed_plane, 0)

    @pl.when(core == 0)
    def _():
        to_sibling(far_level, near_level, PLANES).wait_send()
        lax.fori_loop(0, PLANES, passed_far, 0)


def whole_response(occ, emp, gvectors, energies, ztab, xytabs, n_z):
    bf16, f32 = jnp.bfloat16, jnp.float32
    half = NG // 16
    anywhere, vmem = pl.BlockSpec(memory_space=pl.ANY), pl.BlockSpec(memory_space=pltpu.VMEM)
    return pl.pallas_call(
        response_kernel,
        out_shape=jax.ShapeDtypeStruct((2, half // 2, 2 * half), f32),
        in_specs=[anywhere, anywhere, vmem, vmem, vmem, anywhere, anywhere],
        out_specs=vmem,
        scratch_shapes=[
            pltpu.VMEM((PLANES, 2, 4, CELLS), bf16),
            pltpu.VMEM((PLANES, 2, 4, CELLS), bf16),
            pltpu.VMEM((8, LANES), f32),
            pltpu.VMEM((8, LANES), f32),
            pltpu.VMEM((8, LANES), f32),
            pltpu.VMEM((2, PLANES, 8, CELLS), bf16),
            pltpu.VMEM((Z_ROWS, GROUP_CELLS), bf16),
            pltpu.VMEM((PLANES // BATCH, WAVE_ROWS, DEPTH), bf16),
            pltpu.VMEM((16, CELLS), f32),
            pltpu.VMEM((GROUPS * LANES, GROUP_CELLS), bf16),
            pltpu.VMEM((Z_ROWS, GROUPS * LANES), f32),
            pltpu.VMEM((Q_SLOTS // 2, DEPTH, 2 * LANES), bf16),
            pltpu.VMEM((Q_SLOTS * WAVE_ROWS, LANES), f32),
            pltpu.VMEM((512, LANES), f32),
            pltpu.VMEM((1, NG), jnp.int32),
            pltpu.SMEM((1, NG), jnp.int32),
            pltpu.VMEM((1, NG), f32),
            pltpu.VMEM((NG, LANES), f32),
            pltpu.VMEM((2, 4, 2, half, LANES), bf16),
            pltpu.VMEM((n_z, 2, 2, 2, half, LANES), bf16),
            pltpu.VMEM((n_z, 2, 2, half // 2, LANES), bf16),
            pltpu.VMEM((2, 2, half, LANES), bf16),
            pltpu.VMEM((2, 2, half, LANES), bf16),
            pltpu.VMEM((4, 2, half, LANES), bf16),
            pltpu.VMEM((2, half, LANES), bf16),
            pltpu.VMEM((2, half, LANES), bf16),
            pltpu.SemaphoreType.DMA((PLANES + 1,)),
            pltpu.SemaphoreType.DMA((PLANES + 1,)),
            pltpu.SemaphoreType.DMA((PLANES + 1,)),
            pltpu.SemaphoreType.DMA((PLANES + 1,)),
            pltpu.SemaphoreType.DMA((4,)),
            pltpu.SemaphoreType.DMA((128,)),
            pltpu.SemaphoreType.DMA((8,)),
            pltpu.SemaphoreType.DMA((6, 2, n_z // 2 + 1)),
            pltpu.SemaphoreType.DMA((3, 2)),
            pltpu.SemaphoreType.DMA((3, n_z)),
        ],
        compiler_params=pltpu.CompilerParams(
            collective_id=0, has_side_effects=True, vmem_limit_bytes=60 * 2**20
        ),
        cost_estimate=pl.CostEstimate(
            flops=16_000_000_000, bytes_accessed=12_000_000, transcendentals=0
        ),
    )(occ, emp, gvectors, *energies, ztab, xytabs)


def shards(ztab, xytabs, occupied_states, empty_states, occ_energy, empty_energy, gvectors):
    occ = jnp.transpose(occupied_states, (0, 2, 1, 3))
    emp = jnp.transpose(empty_states, (0, 2, 1, 3))
    energies = occ_energy.reshape(1, -1), empty_energy.reshape(1, -1)
    n_z = lax.axis_size("blk") // 4
    out = whole_response(occ, emp, gvectors, energies, ztab, xytabs, n_z)
    return jnp.transpose(out, (1, 0, 2))


def solution(mesh):
    ztab = z_table()
    xytabs = plane_table(mesh.shape["pw"])
    return jax.shard_map(
        lambda *args: shards(jnp.asarray(ztab), jnp.asarray(xytabs), *args),
        mesh=mesh,
        in_specs=(P(None, "blk", "pw", None), P(None, "blk", "pw", None), P("blk"), P("blk"), P()),
        out_specs=P("blk", None, "pw"),
        check_vma=False,
    )
```

```python
import math

import jax
import jax.numpy as jnp
import numpy as np
from jax import lax
from jax.experimental import pallas as pl
from jax.experimental.pallas import tpu as pltpu
from jax.sharding import PartitionSpec as P
import ml_dtypes

GX = 72
GY = 72
GZ = 144
KMAX = 16
SIDE = 2 * KMAX + 1
PLANES = 9
CELLS = GY * GZ
NG = 4096
GROUPS = 9
GROUP_CELLS = 8 * GZ
Z_ROWS = SIDE * 8
ROWS_X = 80
BATCH = 3
DEPTH = BATCH * ROWS_X
HALF = (SIDE * SIDE + 1) // 2
WAVE_ROWS = 1096
Q_SLOTS = 34
LANES = 128
omega_shift = 0.5


def z_table():
    z = np.arange(GZ)
    out = np.zeros((Z_ROWS, GROUP_CELLS), np.float64)
    for q in range(KMAX + 1):
        angle = 2 * np.pi * ((q * z) % GZ) / GZ
        for y in range(8):
            out[q * 8 + y, y * GZ : (y + 1) * GZ] = np.cos(angle)
            if q:
                out[(KMAX + q) * 8 + y, y * GZ : (y + 1) * GZ] = np.sin(angle)
    return out.astype(np.float32).astype(ml_dtypes.bfloat16)


def plane_table(groups):
    h = np.arange(HALF)
    p = (h + KMAX) // SIDE
    a = h - SIDE * p
    out = np.zeros((groups, WAVE_ROWS, PLANES, ROWS_X), np.float64)
    y = np.arange(GY)
    for group in range(groups):
        for plane in range(PLANES):
            x = group * PLANES + plane
            steps = (p[:, None] * y[None, :] + a[:, None] * x) % GX
            out[group, 0 : 2 * HALF : 2, plane, :GY] = np.cos(2 * np.pi * steps / GX)
            out[group, 1 : 2 * HALF : 2, plane, :GY] = np.sin(2 * np.pi * steps / GX)
    out = out.reshape(groups, WAVE_ROWS, PLANES // BATCH, DEPTH).transpose(0, 2, 1, 3)
    return out.astype(np.float32).astype(ml_dtypes.bfloat16)


def turned(value):
    lane = lax.broadcasted_iota(jnp.int32, value.shape, 1)
    ahead = pltpu.roll(value, LANES - 8, 1)
    behind = pltpu.roll(value, 8, 1)
    return jnp.where((lane & 8) == 0, ahead, -behind)


MESH = pl.DeviceIdType.MESH


def response_kernel(
    occ_ref, emp_ref, wave_ref, occ_energy_ref, emp_energy_ref, ztab_ref, xytab_ref, out_ref,
    near, far, level_ref, near_level, far_level, emp, ztab, xytab, occ_f, pairs, depth_out, sections, waves,
    picked, index_v, index_s, sign_v, sign_rows, part_ref, everyone, left, relay, passed, arrived, plane_sum,
    other, ahead_sems, far_sems, pass_sems, near_sems, load_sems, send_sems, sum_sems, ring_sems,
    side_sems, left_sems,
):
    blk, pw = lax.axis_index("blk"), lax.axis_index("pw")
    count = lax.axis_size("blk")
    n_z = count // 4
    z, y, core = blk // 4, (blk // 2) % 2, blk % 2
    x, y_hi = pw % 4, pw // 4
    f32, bf16 = jnp.float32, jnp.bfloat16

    def place(z=z, y=y, core=core, x=x, y_hi=y_hi):
        return {"blk": z * 4 + y * 2 + core, "pw": y_hi * 4 + x}

    x_next, x_last = place(x=(x + 1) % 4), place(x=(x + 3) % 4)
    z_next, z_last = place(z=(z + 1) % n_z), place(z=(z + n_z - 1) % n_z)
    sibling, beside = place(core=1 - core), place(y=1 - y)
    facing, across = place(y_hi=1 - y_hi), place(y=1 - y, y_hi=1 - y_hi)
    behind = {"blk": (blk + count - 2) % count, "pw": pw}
    ahead = {"blk": (blk + 2) % count, "pw": pw}

    barrier = pltpu.get_barrier_semaphore()
    neighbours = (
        x_next, x_last, z_next, z_last, sibling, beside, facing, across, behind, ahead
    )
    for device in neighbours:
        pl.semaphore_signal(barrier, inc=1, device_id=device, device_id_type=MESH)
    pl.semaphore_wait(barrier, len(neighbours))

    def to_behind(source, target, spot):
        return pltpu.make_async_remote_copy(
            src_ref=source, dst_ref=target, send_sem=ahead_sems.at[spot],
            recv_sem=far_sems.at[spot], device_id=behind, device_id_type=MESH,
        )

    def to_sibling(source, target, spot):
        return pltpu.make_async_remote_copy(
            src_ref=source, dst_ref=target, send_sem=pass_sems.at[spot],
            recv_sem=near_sems.at[spot], device_id=sibling, device_id_type=MESH,
        )

    def landed(target, arrival):
        pltpu.make_async_copy(target, target, arrival).wait()

    def send_plane(x, carry):
        to_behind(occ_ref.at[:, x], far.at[x], x).start()
        return carry

    def pass_plane(x, carry):
        to_sibling(occ_ref.at[:, x], near.at[x], x).start()
        return carry

    lane = lax.broadcasted_iota(jnp.int32, (8, LANES), 1)
    occ_energy = occ_energy_ref[...].astype(f32)
    emp_energy = emp_energy_ref[...].astype(f32)
    spread = jnp.zeros((8, LANES), f32)
    for v in range(4):
        spread = jnp.where((lane // 16) % 4 == v, occ_energy[:, v : v + 1], spread)
    level_ref[...] = spread
    emp_level = jnp.zeros((8, LANES), f32)
    for c in range(8):
        emp_level = jnp.where(lane % 8 == c, emp_energy[:, c : c + 1], emp_level)
    to_behind(level_ref, far_level, PLANES).start()
    lax.fori_loop(0, PLANES, send_plane, 0)

    @pl.when(core == 1)
    def _():
        to_sibling(level_ref, near_level, PLANES).start()
        lax.fori_loop(0, PLANES, pass_plane, 0)

    loads = [
        pltpu.make_async_copy(emp_ref, emp, load_sems.at[0]),
        pltpu.make_async_copy(ztab_ref, ztab, load_sems.at[1]),
        pltpu.make_async_copy(xytab_ref.at[pw], xytab, load_sems.at[2]),
    ]
    for load in loads:
        load.start()

    flat = SIDE * wave_ref[1:2, :] + wave_ref[0:1, :]
    index_v[...] = (wave_ref[2:3, :] + KMAX) * WAVE_ROWS + 2 * jnp.abs(flat)
    sign_v[...] = jnp.where(flat < 0, -1.0, 1.0).astype(jnp.float32)
    index_move = pltpu.make_async_copy(index_v, index_s, load_sems.at[3])
    index_move.start()
    for load in loads:
        load.wait()
    index_move.wait()

    def group_pairs(x, group):
        for part in range(3):
            start = group * GROUP_CELLS + part * 384
            cells = slice(start, start + 384)
            emp_re = emp[0, x, :, cells].astype(jnp.float32)
            emp_im = emp[1, x, :, cells].astype(jnp.float32)
            for v in range(8):
                row = v if v < 4 else v + 4
                occ_re = occ_f[row : row + 1, cells]
                occ_im = occ_f[row + 4 : row + 5, cells]
                both = jnp.concatenate(
                    [occ_re * emp_re + occ_im * emp_im, occ_re * emp_im - occ_im * emp_re], axis=0
                )
                rows = slice(group * LANES + v * 16, group * LANES + v * 16 + 16)
                pairs[rows, part * 384 : part * 384 + 384] = both.astype(jnp.bfloat16)

    blank = jnp.zeros((ROWS_X - GY, LANES), jnp.float32)

    def rows_of(first):
        parts = [depth_out[first : first + 8, t * LANES : (t + 1) * LANES] for t in range(GROUPS)]
        return jnp.concatenate(parts + [blank], axis=0)

    def one_plane(x, spot):
        landed(far.at[x], far_sems.at[x])

        @pl.when(core == 0)
        def _():
            to_sibling(far.at[x], near.at[x], x).start()

        landed(near.at[x], near_sems.at[x])
        for part in range(2):
            occ_f[part * 4 : part * 4 + 4, :] = near[x, part].astype(jnp.float32)
            occ_f[part * 4 + 8 : part * 4 + 12, :] = far[x, part].astype(jnp.float32)

        for start in range(0, GROUPS, 2):
            stop = min(start + 2, GROUPS)
            for group in range(start, stop):
                group_pairs(x, group)
            lines = slice(start * LANES, stop * LANES)
            depth_out[:, lines] = lax.dot_general(
                ztab[...], pairs[lines, :], (((1,), (1,)), ((), ())),
                preferred_element_type=jnp.float32,
            )
        rows = pl.ds(pl.multiple_of(spot * ROWS_X, 16), ROWS_X)

        def put(slot, value):
            half = slot % 2
            sections[slot // 2, rows, half * LANES : (half + 1) * LANES] = value.astype(jnp.bfloat16)

        put(KMAX, rows_of(0))
        for q in range(1, KMAX + 1):
            cosine = rows_of(q * 8)
            sine = turned(rows_of((KMAX + q) * 8))
            put(KMAX + q, cosine + sine)
            put(KMAX - q, cosine - sine)

    sections[Q_SLOTS // 2 - 1, :, LANES:] = jnp.zeros((DEPTH, LANES), jnp.bfloat16)
    def clear(k, carry):
        rows = pl.ds(pl.multiple_of(k * WAVE_ROWS, 8), WAVE_ROWS)
        waves[rows, :] = jnp.zeros((WAVE_ROWS, LANES), jnp.float32)
        return carry

    lax.fori_loop(0, Q_SLOTS, clear, 0)

    def stand(step, carry):
        first = pl.multiple_of(step * 128, 128)
        row = sign_v[:, pl.ds(first, 128)]
        sign_rows[pl.ds(first, 128), :] = jnp.broadcast_to(row, (128, LANES)).T
        return carry

    lax.fori_loop(0, NG // 128, stand, 0)
    landed(far_level, far_sems.at[PLANES])

    @pl.when(core == 0)
    def _():
        to_sibling(far_level, near_level, PLANES).start()

    def each_batch(batch, carry):
        def each_plane(spot, carry):
            one_plane(batch * BATCH + spot, spot)
            return carry

        lax.fori_loop(0, BATCH, each_plane, 0)

        def slot_pair(k, carry):
            product = jnp.dot(xytab[batch], sections[k], preferred_element_type=jnp.float32)
            first = pl.multiple_of(k * 2 * WAVE_ROWS, 8)
            for half in range(2):
                rows = pl.ds(first + half * WAVE_ROWS, WAVE_ROWS)
                waves[rows, :] += product[:, half * LANES : (half + 1) * LANES]
            return carry

        lax.fori_loop(0, Q_SLOTS // 2, slot_pair, 0)
        return carry

    lax.fori_loop(0, PLANES // BATCH, each_batch, 0)
    landed(near_level, near_sems.at[PLANES])
    occ_level = jnp.where(lane < LANES // 2, near_level[...], far_level[...])
    scale = jnp.sqrt(2.0 / (emp_level - occ_level + omega_shift))[0:1]

    def chunk(yy, xx, half):
        base = (yy * 4 + xx) * 512 + half * 256

        def pick(step, carry):
            first = step * 16
            for i in range(16):
                row = index_s[0, base + first + i]
                picked[pl.ds((first + i) * 2, 2), :] = waves[pl.ds(row, 2), :]
            return carry

        lax.fori_loop(0, 16, pick, 0)
        for part in range(2):
            cosine = picked[pl.ds(part * 256, 128, stride=2), :]
            sine = picked[pl.ds(part * 256 + 1, 128, stride=2), :]
            first = pl.multiple_of(base + part * 128, 128)
            total = (cosine + sign_rows[pl.ds(first, 128), :] * turned(sine)) * scale
            part_ref[yy, xx, half, part * 128 : part * 128 + 128, :] = total.astype(bf16)

    def both_chunks(xx, half):
        def one(yy, carry):
            chunk(yy, xx, half)
            return carry

        lax.fori_loop(0, 2, one, 0)

    sends = []

    def copy(source, target, arrival, device):
        return pltpu.make_async_remote_copy(
            src_ref=source, dst_ref=target, send_sem=send_sems.at[len(sends)], recv_sem=arrival,
            device_id=device, device_id_type=MESH,
        )

    def send(source, target, arrival, device):
        moving = copy(source, target, arrival, device)
        moving.start()
        sends.append(moving)

    out_ref[...] = jnp.zeros_like(out_ref)
    rows = everyone.shape[4] * 2
    half_rows, quarter = rows // 2, rows // 4

    xn, xl, xo = (x + 1) % 4, (x + 3) % 4, (x + 2) % 4

    def pass_on(half, xx, device):
        landed(relay.at[half], sum_sems.at[half])
        share = part_ref[:, xx, half].astype(f32) + relay[half].astype(f32)
        passed[half] = share.astype(bf16)
        send(passed.at[half], arrived.at[2 + half], sum_sems.at[4 + half], device)

    def x_total(yy, half):
        first, second = (2, 1) if half == 0 else (0, 3)
        return (
            part_ref[yy, x, half].astype(f32)
            + arrived[first, yy].astype(f32)
            + arrived[second, yy].astype(f32)
        )

    def cross_over(half):
        for spot in (2, 1) if half == 0 else (0, 3):
            landed(arrived.at[spot], sum_sems.at[2 + spot])
        plane_sum[half] = x_total(1 - y_hi, half).astype(bf16)
        send(plane_sum.at[half], other.at[half], sum_sems.at[6 + half], facing)

    def own_rho(half):
        landed(other.at[half], sum_sems.at[6 + half])
        total = x_total(y_hi, half) + other[half].astype(f32)
        everyone[z, y, core, half] = total.astype(bf16)

    both_chunks(xo, 0)
    send(part_ref.at[:, xo, 0], relay.at[0], sum_sems.at[0], x_next)
    both_chunks(xl, 0)
    send(part_ref.at[:, xl, 0], arrived.at[1], sum_sems.at[3], x_last)
    both_chunks(xn, 0)
    both_chunks(x, 0)
    pass_on(0, xn, x_next)
    both_chunks(xo, 1)
    send(part_ref.at[:, xo, 1], relay.at[1], sum_sems.at[1], x_last)
    both_chunks(xn, 1)
    send(part_ref.at[:, xn, 1], arrived.at[0], sum_sems.at[2], x_next)
    both_chunks(xl, 1)
    cross_over(0)
    both_chunks(x, 1)
    pass_on(1, xl, x_last)

    own_rho(0)
    mine = lambda half: everyone.at[z, y, core, half]
    theirs = lambda half: everyone.at[z, 1 - y, core, half]
    upper = lambda zz: everyone.at[zz, :, core, 0]
    lower = lambda zz, yy: everyone.at[zz, yy, core, 1]
    send(mine(0), mine(0), side_sems.at[0, 0], beside)
    send(mine(0), mine(0), side_sems.at[1, 0], sibling)
    cross_over(1)
    landed(theirs(0), side_sems.at[0, 0])
    send(upper(z), upper(z), ring_sems.at[0, 0, 1], z_next)
    send(upper(z), upper(z), ring_sems.at[0, 1, 1], z_last)
    send(theirs(0), theirs(0), side_sems.at[2, 0], sibling)
    own_rho(1)
    send(lower(z, y), lower(z, y), ring_sems.at[1, 0, 1], z_next)
    send(lower(z, y), lower(z, y), ring_sems.at[1, 1, 1], z_last)
    send(mine(1), mine(1), side_sems.at[0, 1], beside)
    send(mine(1), mine(1), side_sems.at[1, 1], sibling)

    longest = {(0, 0): n_z // 2, (0, 1): n_z // 2 - 1, (1, 0): n_z // 2 - 1, (1, 1): n_z // 2}

    def ring_step(step):
        for half in (0, 1):
            for way in (0, 1):
                if step > longest[half, way]:
                    continue
                origin = (z + n_z - step) % n_z if way == 0 else (z + step) % n_z
                piece = upper(origin) if half == 0 else lower(origin, y)
                landed(piece, ring_sems.at[half, way, step])
                if step < longest[half, way]:
                    send(piece, piece, ring_sems.at[half, way, step + 1], z_next if way == 0 else z_last)
                if half == 1:
                    send(piece, piece, ring_sems.at[2, way, step], beside)
                send(piece, piece, ring_sems.at[3 + half, way, step], sibling)

    def side_step(step):
        for way in (0, 1):
            if step > longest[1, way]:
                continue
            origin = (z + n_z - step) % n_z if way == 0 else (z + step) % n_z
            piece = lower(origin, 1 - y)
            landed(piece, ring_sems.at[2, way, step])
            send(piece, piece, ring_sems.at[5, way, step], sibling)

    def rest_step(step):
        if step == 0:
            for yy, spot in ((y, 1), (1 - y, 2)):
                for half in range(2):
                    landed(everyone.at[z, yy, 1 - core, half], side_sems.at[spot, half])
            return
        for way in (0, 1):
            origin = (z + n_z - step) % n_z if way == 0 else (z + step) % n_z
            if step <= longest[0, way]:
                landed(everyone.at[origin, :, 1 - core, 0], ring_sems.at[3, way, step])
            if step <= longest[1, way]:
                landed(everyone.at[origin, y, 1 - core, 1], ring_sems.at[4, way, step])
                landed(everyone.at[origin, 1 - y, 1 - core, 1], ring_sems.at[5, way, step])

    dx = (x + 4 - z % 4) % 4
    root = z // 4 == y_hi
    first = core * quarter
    eighth = quarter // 2

    def group_origins(step):
        if step == 0:
            return ((z, 0),)
        if step == n_z // 2:
            return (((z + step) % n_z, step),)
        return (((z + n_z - step) % n_z, step), ((z + step) % n_z, n_z - step))

    held = lambda zz, part: left.at[zz, :, :, pl.ds(part * eighth, eighth)]
    late = []

    def left_copies(step):
        made = []
        for zz, tag in group_origins(step):
            base = len(sends)

            def numbered(source, target, arrival, device, offset):
                return pltpu.make_async_remote_copy(
                    src_ref=source, dst_ref=target, send_sem=send_sems.at[base + offset],
                    recv_sem=arrival, device_id=device, device_id_type=MESH,
                )

            there = everyone.at[zz, :, :, 1 - y, pl.ds(first, quarter)]
            to_next = numbered(held(zz, 0), held(zz, 0), left_sems.at[0, tag], x_next, 0)
            to_last = numbered(held(zz, 1), held(zz, 1), left_sems.at[1, tag], x_last, 1)
            to_across = numbered(there, left.at[zz], left_sems.at[2, tag], across, 2)
            made.append((zz, tag, to_next, to_last, to_across))
            sends.extend([None] * 3)
        late.extend(made)
        return made

    def left_from_root(made):
        @pl.when((dx == 0) & root)
        def _():
            for zz, tag, to_next, to_last, to_across in made:
                to_across.start()
                left[zz] = everyone[zz, :, :, y, pl.ds(first, quarter)]
                to_next.start()
                to_last.start()

    def left_onward(made):
        @pl.when((dx == 0) & jnp.logical_not(root))
        def _():
            for zz, tag, to_next, to_last, to_across in made:
                landed(left.at[zz], left_sems.at[2, tag])
                to_next.start()
                to_last.start()

        @pl.when(dx == 1)
        def _():
            for zz, tag, to_next, to_last, to_across in made:
                landed(held(zz, 0), left_sems.at[0, tag])
                to_next.start()

        @pl.when(dx == 3)
        def _():
            for zz, tag, to_next, to_last, to_across in made:
                landed(held(zz, 1), left_sems.at[1, tag])
                to_last.start()

    def left_middle(made):
        @pl.when(dx == 2)
        def _():
            for zz, tag, to_next, to_last, to_across in made:
                landed(held(zz, 0), left_sems.at[0, tag])
                to_next.start()
                landed(held(zz, 1), left_sems.at[1, tag])
                to_last.start()

    parts = [left_copies(step) for step in range(n_z // 2 + 1)]
    ring_step(1)
    landed(theirs(1), side_sems.at[0, 1])
    send(theirs(1), theirs(1), side_sems.at[2, 1], sibling)
    rest_step(0)
    left_from_root(parts[0])
    side_step(1)
    rest_step(1)
    left_from_root(parts[1])
    ring_step(2)
    side_step(2)
    rest_step(2)
    left_from_root(parts[2])
    ring_step(3)
    side_step(3)
    rest_step(3)
    left_from_root(parts[3])
    left_onward(parts[0])
    ring_step(4)
    side_step(4)
    left_onward(parts[1])
    left_middle(parts[0])
    rest_step(4)
    left_from_root(parts[4])
    for step in range(2, n_z // 2 + 1):
        left_onward(parts[step])
        left_middle(parts[step - 1])
    left_middle(parts[n_z // 2])

    def group_product(k, carry):
        odd = k % 2
        tag = (odd * ((k + 1) // 2) + (1 - odd) * (n_z - k // 2)) % n_z
        zz = (z + n_z - tag) % n_z

        @pl.when(dx == 1)
        def _():
            landed(held(zz, 1), left_sems.at[1, tag])

        @pl.when(dx == 3)
        def _():
            landed(held(zz, 0), left_sems.at[0, tag])

        straight = [left[zz, i // 2, i % 2].astype(f32) for i in range(4)]
        side = jnp.concatenate([turned(value) for value in straight], axis=1)
        both = jnp.concatenate([-jnp.concatenate(straight, axis=1), side], axis=0)
        both = both.astype(bf16)
        for half in range(2):
            right = jnp.concatenate([everyone[zz, i // 2, i % 2, half] for i in range(4)], axis=1)
            product = lax.dot_general(
                both, right, (((1,), (1,)), ((), ())), preferred_element_type=f32
            )
            for part in range(2):
                spot = (part, slice(None), slice(half * half_rows, (half + 1) * half_rows))
                out_ref[spot] += product[part * quarter : (part + 1) * quarter]
        return carry

    lax.fori_loop(0, n_z, group_product, 0)

    for moving in sends:
        if moving is not None:
            moving.wait_send()
    for zz, tag, to_next, to_last, to_across in late:
        pl.when(dx != 3)(lambda: to_next.wait_send())
        pl.when(dx != 1)(lambda: to_last.wait_send())
        pl.when((dx == 0) & root)(lambda: to_across.wait_send())

    def sent_plane(x, carry):
        to_behind(occ_ref.at[:, x], far.at[x], x).wait_send()
        return carry

    def passed_plane(x, carry):
        to_sibling(occ_ref.at[:, x], near.at[x], x).wait_send()
        return carry

    def passed_far(x, carry):
        to_sibling(far.at[x], near.at[x], x).wait_send()
        return carry

    to_behind(level_ref, far_level, PLANES).wait_send()
    lax.fori_loop(0, PLANES, sent_plane, 0)

    @pl.when(core == 1)
    def _():
        to_sibling(level_ref, near_level, PLANES).wait_send()
        lax.fori_loop(0, PLANES, passed_plane, 0)

    @pl.when(core == 0)
    def _():
        to_sibling(far_level, near_level, PLANES).wait_send()
        lax.fori_loop(0, PLANES, passed_far, 0)


def whole_response(occ, emp, gvectors, energies, ztab, xytabs, n_z):
    bf16, f32 = jnp.bfloat16, jnp.float32
    half = NG // 16
    anywhere, vmem = pl.BlockSpec(memory_space=pl.ANY), pl.BlockSpec(memory_space=pltpu.VMEM)
    return pl.pallas_call(
        response_kernel,
        out_shape=jax.ShapeDtypeStruct((2, half // 2, 2 * half), f32),
        in_specs=[anywhere, anywhere, vmem, vmem, vmem, anywhere, anywhere],
        out_specs=vmem,
        scratch_shapes=[
            pltpu.VMEM((PLANES, 2, 4, CELLS), bf16),
            pltpu.VMEM((PLANES, 2, 4, CELLS), bf16),
            pltpu.VMEM((8, LANES), f32),
            pltpu.VMEM((8, LANES), f32),
            pltpu.VMEM((8, LANES), f32),
            pltpu.VMEM((2, PLANES, 8, CELLS), bf16),
            pltpu.VMEM((Z_ROWS, GROUP_CELLS), bf16),
            pltpu.VMEM((PLANES // BATCH, WAVE_ROWS, DEPTH), bf16),
            pltpu.VMEM((16, CELLS), f32),
            pltpu.VMEM((GROUPS * LANES, GROUP_CELLS), bf16),
            pltpu.VMEM((Z_ROWS, GROUPS * LANES), f32),
            pltpu.VMEM((Q_SLOTS // 2, DEPTH, 2 * LANES), bf16),
            pltpu.VMEM((Q_SLOTS * WAVE_ROWS, LANES), f32),
            pltpu.VMEM((512, LANES), f32),
            pltpu.VMEM((1, NG), jnp.int32),
            pltpu.SMEM((1, NG), jnp.int32),
            pltpu.VMEM((1, NG), f32),
            pltpu.VMEM((NG, LANES), f32),
            pltpu.VMEM((2, 4, 2, half, LANES), bf16),
            pltpu.VMEM((n_z, 2, 2, 2, half, LANES), bf16),
            pltpu.VMEM((n_z, 2, 2, half // 2, LANES), bf16),
            pltpu.VMEM((2, 2, half, LANES), bf16),
            pltpu.VMEM((2, 2, half, LANES), bf16),
            pltpu.VMEM((4, 2, half, LANES), bf16),
            pltpu.VMEM((2, half, LANES), bf16),
            pltpu.VMEM((2, half, LANES), bf16),
            pltpu.SemaphoreType.DMA((PLANES + 1,)),
            pltpu.SemaphoreType.DMA((PLANES + 1,)),
            pltpu.SemaphoreType.DMA((PLANES + 1,)),
            pltpu.SemaphoreType.DMA((PLANES + 1,)),
            pltpu.SemaphoreType.DMA((4,)),
            pltpu.SemaphoreType.DMA((128,)),
            pltpu.SemaphoreType.DMA((8,)),
            pltpu.SemaphoreType.DMA((6, 2, n_z // 2 + 1)),
            pltpu.SemaphoreType.DMA((3, 2)),
            pltpu.SemaphoreType.DMA((3, n_z)),
        ],
        compiler_params=pltpu.CompilerParams(
            collective_id=0, has_side_effects=True, vmem_limit_bytes=60 * 2**20
        ),
        cost_estimate=pl.CostEstimate(
            flops=16_000_000_000, bytes_accessed=12_000_000, transcendentals=0
        ),
    )(occ, emp, gvectors, *energies, ztab, xytabs)


def shards(ztab, xytabs, occupied_states, empty_states, occ_energy, empty_energy, gvectors):
    occ = jnp.transpose(occupied_states, (0, 2, 1, 3))
    emp = jnp.transpose(empty_states, (0, 2, 1, 3))
    energies = occ_energy.reshape(1, -1), empty_energy.reshape(1, -1)
    n_z = lax.axis_size("blk") // 4
    out = whole_response(occ, emp, gvectors, energies, ztab, xytabs, n_z)
    return jnp.transpose(out, (1, 0, 2))


def solution(mesh):
    ztab = z_table()
    xytabs = plane_table(mesh.shape["pw"])
    return jax.shard_map(
        lambda *args: shards(jnp.asarray(ztab), jnp.asarray(xytabs), *args),
        mesh=mesh,
        in_specs=(P(None, "blk", "pw", None), P(None, "blk", "pw", None), P("blk"), P("blk"), P()),
        out_specs=P("blk", None, "pw"),
        check_vma=False,
    )
```

```python
import math

import jax
import jax.numpy as jnp
import numpy as np
from jax import lax
from jax.experimental import pallas as pl
from jax.experimental.pallas import tpu as pltpu
from jax.sharding import PartitionSpec as P
import ml_dtypes

GX = 72
GY = 72
GZ = 144
KMAX = 16
SIDE = 2 * KMAX + 1
PLANES = 9
CELLS = GY * GZ
NG = 4096
GROUPS = 9
GROUP_CELLS = 8 * GZ
Z_ROWS = SIDE * 8
ROWS_X = 80
BATCH = 3
DEPTH = BATCH * ROWS_X
HALF = (SIDE * SIDE + 1) // 2
WAVE_ROWS = 1096
Q_SLOTS = 34
LANES = 128
omega_shift = 0.5


def z_table():
    z = np.arange(GZ)
    out = np.zeros((Z_ROWS, GROUP_CELLS), np.float64)
    for q in range(KMAX + 1):
        angle = 2 * np.pi * ((q * z) % GZ) / GZ
        for y in range(8):
            out[q * 8 + y, y * GZ : (y + 1) * GZ] = np.cos(angle)
            if q:
                out[(KMAX + q) * 8 + y, y * GZ : (y + 1) * GZ] = np.sin(angle)
    return out.astype(np.float32).astype(ml_dtypes.bfloat16)


def plane_table(groups):
    h = np.arange(HALF)
    p = (h + KMAX) // SIDE
    a = h - SIDE * p
    out = np.zeros((groups, WAVE_ROWS, PLANES, ROWS_X), np.float64)
    y = np.arange(GY)
    for group in range(groups):
        for plane in range(PLANES):
            x = group * PLANES + plane
            steps = (p[:, None] * y[None, :] + a[:, None] * x) % GX
            out[group, 0 : 2 * HALF : 2, plane, :GY] = np.cos(2 * np.pi * steps / GX)
            out[group, 1 : 2 * HALF : 2, plane, :GY] = np.sin(2 * np.pi * steps / GX)
    out = out.reshape(groups, WAVE_ROWS, PLANES // BATCH, DEPTH).transpose(0, 2, 1, 3)
    return out.astype(np.float32).astype(ml_dtypes.bfloat16)


def turned(value):
    lane = lax.broadcasted_iota(jnp.int32, value.shape, 1)
    ahead = pltpu.roll(value, LANES - 8, 1)
    behind = pltpu.roll(value, 8, 1)
    return jnp.where((lane & 8) == 0, ahead, -behind)


MESH = pl.DeviceIdType.MESH


def response_kernel(
    occ_ref, emp_ref, wave_ref, occ_energy_ref, emp_energy_ref, ztab_ref, xytab_ref, out_ref,
    near, far, level_ref, near_level, far_level, emp, ztab, xytab, occ_f, pairs, depth_out, sections, waves,
    picked, index_v, index_s, sign_v, sign_rows, part_ref, everyone, left, relay, passed, arrived, plane_sum,
    other, ahead_sems, far_sems, pass_sems, near_sems, load_sems, send_sems, sum_sems, ring_sems,
    side_sems, left_sems,
):
    blk, pw = lax.axis_index("blk"), lax.axis_index("pw")
    count = lax.axis_size("blk")
    n_z = count // 4
    z, y, core = blk // 4, (blk // 2) % 2, blk % 2
    x, y_hi = pw % 4, pw // 4
    f32, bf16 = jnp.float32, jnp.bfloat16

    def place(z=z, y=y, core=core, x=x, y_hi=y_hi):
        return {"blk": z * 4 + y * 2 + core, "pw": y_hi * 4 + x}

    x_next, x_last = place(x=(x + 1) % 4), place(x=(x + 3) % 4)
    z_next, z_last = place(z=(z + 1) % n_z), place(z=(z + n_z - 1) % n_z)
    sibling, beside = place(core=1 - core), place(y=1 - y)
    facing, across = place(y_hi=1 - y_hi), place(y=1 - y, y_hi=1 - y_hi)
    behind = {"blk": (blk + count - 2) % count, "pw": pw}
    ahead = {"blk": (blk + 2) % count, "pw": pw}

    barrier = pltpu.get_barrier_semaphore()
    neighbours = (
        x_next, x_last, z_next, z_last, sibling, beside, facing, across, behind, ahead
    )
    for device in neighbours:
        pl.semaphore_signal(barrier, inc=1, device_id=device, device_id_type=MESH)
    pl.semaphore_wait(barrier, len(neighbours))

    def to_behind(source, target, spot):
        return pltpu.make_async_remote_copy(
            src_ref=source, dst_ref=target, send_sem=ahead_sems.at[spot],
            recv_sem=far_sems.at[spot], device_id=behind, device_id_type=MESH,
        )

    def to_sibling(source, target, spot):
        return pltpu.make_async_remote_copy(
            src_ref=source, dst_ref=target, send_sem=pass_sems.at[spot],
            recv_sem=near_sems.at[spot], device_id=sibling, device_id_type=MESH,
        )

    def landed(target, arrival):
        pltpu.make_async_copy(target, target, arrival).wait()

    def send_plane(x, carry):
        to_behind(occ_ref.at[:, x], far.at[x], x).start()
        return carry

    def pass_plane(x, carry):
        to_sibling(occ_ref.at[:, x], near.at[x], x).start()
        return carry

    lane = lax.broadcasted_iota(jnp.int32, (8, LANES), 1)
    occ_energy = occ_energy_ref[...].astype(f32)
    emp_energy = emp_energy_ref[...].astype(f32)
    spread = jnp.zeros((8, LANES), f32)
    for v in range(4):
        spread = jnp.where((lane // 16) % 4 == v, occ_energy[:, v : v + 1], spread)
    level_ref[...] = spread
    emp_level = jnp.zeros((8, LANES), f32)
    for c in range(8):
        emp_level = jnp.where(lane % 8 == c, emp_energy[:, c : c + 1], emp_level)
    to_behind(level_ref, far_level, PLANES).start()
    lax.fori_loop(0, PLANES, send_plane, 0)

    @pl.when(core == 1)
    def _():
        to_sibling(level_ref, near_level, PLANES).start()
        lax.fori_loop(0, PLANES, pass_plane, 0)

    loads = [
        pltpu.make_async_copy(emp_ref, emp, load_sems.at[0]),
        pltpu.make_async_copy(ztab_ref, ztab, load_sems.at[1]),
        pltpu.make_async_copy(xytab_ref.at[pw], xytab, load_sems.at[2]),
    ]
    for load in loads:
        load.start()

    flat = SIDE * wave_ref[1:2, :] + wave_ref[0:1, :]
    index_v[...] = (wave_ref[2:3, :] + KMAX) * WAVE_ROWS + 2 * jnp.abs(flat)
    sign_v[...] = jnp.where(flat < 0, -1.0, 1.0).astype(jnp.float32)
    index_move = pltpu.make_async_copy(index_v, index_s, load_sems.at[3])
    index_move.start()
    for load in loads:
        load.wait()
    index_move.wait()

    def group_pairs(x, group):
        for part in range(3):
            start = group * GROUP_CELLS + part * 384
            cells = slice(start, start + 384)
            emp_re = emp[0, x, :, cells].astype(jnp.float32)
            emp_im = emp[1, x, :, cells].astype(jnp.float32)
            for v in range(8):
                row = v if v < 4 else v + 4
                occ_re = occ_f[row : row + 1, cells]
                occ_im = occ_f[row + 4 : row + 5, cells]
                both = jnp.concatenate(
                    [occ_re * emp_re + occ_im * emp_im, occ_re * emp_im - occ_im * emp_re], axis=0
                )
                rows = slice(group * LANES + v * 16, group * LANES + v * 16 + 16)
                pairs[rows, part * 384 : part * 384 + 384] = both.astype(jnp.bfloat16)

    blank = jnp.zeros((ROWS_X - GY, LANES), jnp.float32)

    def rows_of(first):
        parts = [depth_out[first : first + 8, t * LANES : (t + 1) * LANES] for t in range(GROUPS)]
        return jnp.concatenate(parts + [blank], axis=0)

    def one_plane(x, spot):
        landed(far.at[x], far_sems.at[x])

        @pl.when(core == 0)
        def _():
            to_sibling(far.at[x], near.at[x], x).start()

        landed(near.at[x], near_sems.at[x])
        for part in range(2):
            occ_f[part * 4 : part * 4 + 4, :] = near[x, part].astype(jnp.float32)
            occ_f[part * 4 + 8 : part * 4 + 12, :] = far[x, part].astype(jnp.float32)

        for start in range(0, GROUPS, 2):
            stop = min(start + 2, GROUPS)
            for group in range(start, stop):
                group_pairs(x, group)
            lines = slice(start * LANES, stop * LANES)
            depth_out[:, lines] = lax.dot_general(
                ztab[...], pairs[lines, :], (((1,), (1,)), ((), ())),
                preferred_element_type=jnp.float32,
            )
        rows = pl.ds(pl.multiple_of(spot * ROWS_X, 16), ROWS_X)

        def put(slot, value):
            half = slot % 2
            sections[slot // 2, rows, half * LANES : (half + 1) * LANES] = value.astype(jnp.bfloat16)

        put(KMAX, rows_of(0))
        for q in range(1, KMAX + 1):
            cosine = rows_of(q * 8)
            sine = turned(rows_of((KMAX + q) * 8))
            put(KMAX + q, cosine + sine)
            put(KMAX - q, cosine - sine)

    sections[Q_SLOTS // 2 - 1, :, LANES:] = jnp.zeros((DEPTH, LANES), jnp.bfloat16)
    def clear(k, carry):
        rows = pl.ds(pl.multiple_of(k * WAVE_ROWS, 8), WAVE_ROWS)
        waves[rows, :] = jnp.zeros((WAVE_ROWS, LANES), jnp.float32)
        return carry

    lax.fori_loop(0, Q_SLOTS, clear, 0)

    def stand(step, carry):
        first = pl.multiple_of(step * 128, 128)
        row = sign_v[:, pl.ds(first, 128)]
        sign_rows[pl.ds(first, 128), :] = jnp.broadcast_to(row, (128, LANES)).T
        return carry

    lax.fori_loop(0, NG // 128, stand, 0)
    landed(far_level, far_sems.at[PLANES])

    @pl.when(core == 0)
    def _():
        to_sibling(far_level, near_level, PLANES).start()

    def each_batch(batch, carry):
        def each_plane(spot, carry):
            one_plane(batch * BATCH + spot, spot)
            return carry

        lax.fori_loop(0, BATCH, each_plane, 0)

        def slot_pair(k, carry):
            product = jnp.dot(xytab[batch], sections[k], preferred_element_type=jnp.float32)
            first = pl.multiple_of(k * 2 * WAVE_ROWS, 8)
            for half in range(2):
                rows = pl.ds(first + half * WAVE_ROWS, WAVE_ROWS)
                waves[rows, :] += product[:, half * LANES : (half + 1) * LANES]
            return carry

        lax.fori_loop(0, Q_SLOTS // 2, slot_pair, 0)
        return carry

    lax.fori_loop(0, PLANES // BATCH, each_batch, 0)
    landed(near_level, near_sems.at[PLANES])
    occ_level = jnp.where(lane < LANES // 2, near_level[...], far_level[...])
    scale = jnp.sqrt(2.0 / (emp_level - occ_level + omega_shift))[0:1]

    def chunk(yy, xx, half):
        base = (yy * 4 + xx) * 512 + half * 256

        def pick(step, carry):
            first = step * 16
            for i in range(16):
                row = index_s[0, base + first + i]
                picked[pl.ds((first + i) * 2, 2), :] = waves[pl.ds(row, 2), :]
            return carry

        lax.fori_loop(0, 16, pick, 0)
        for part in range(2):
            cosine = picked[pl.ds(part * 256, 128, stride=2), :]
            sine = picked[pl.ds(part * 256 + 1, 128, stride=2), :]
            first = pl.multiple_of(base + part * 128, 128)
            total = (cosine + sign_rows[pl.ds(first, 128), :] * turned(sine)) * scale
            part_ref[yy, xx, half, part * 128 : part * 128 + 128, :] = total.astype(bf16)

    def both_chunks(xx, half):
        def one(yy, carry):
            chunk(yy, xx, half)
            return carry

        lax.fori_loop(0, 2, one, 0)

    sends = []

    def copy(source, target, arrival, device):
        return pltpu.make_async_remote_copy(
            src_ref=source, dst_ref=target, send_sem=send_sems.at[len(sends)], recv_sem=arrival,
            device_id=device, device_id_type=MESH,
        )

    def send(source, target, arrival, device):
        moving = copy(source, target, arrival, device)
        moving.start()
        sends.append(moving)

    out_ref[...] = jnp.zeros_like(out_ref)
    rows = everyone.shape[4] * 2
    half_rows, quarter = rows // 2, rows // 4

    xn, xl, xo = (x + 1) % 4, (x + 3) % 4, (x + 2) % 4

    def pass_on(half, xx, device):
        landed(relay.at[half], sum_sems.at[half])
        share = part_ref[:, xx, half].astype(f32) + relay[half].astype(f32)
        passed[half] = share.astype(bf16)
        send(passed.at[half], arrived.at[2 + half], sum_sems.at[4 + half], device)

    def x_total(yy, half):
        first, second = (2, 1) if half == 0 else (0, 3)
        return (
            part_ref[yy, x, half].astype(f32)
            + arrived[first, yy].astype(f32)
            + arrived[second, yy].astype(f32)
        )

    def cross_over(half):
        for spot in (2, 1) if half == 0 else (0, 3):
            landed(arrived.at[spot], sum_sems.at[2 + spot])
        plane_sum[half] = x_total(1 - y_hi, half).astype(bf16)
        send(plane_sum.at[half], other.at[half], sum_sems.at[6 + half], facing)

    def own_rho(half):
        landed(other.at[half], sum_sems.at[6 + half])
        total = x_total(y_hi, half) + other[half].astype(f32)
        everyone[z, y, core, half] = total.astype(bf16)

    both_chunks(xo, 0)
    send(part_ref.at[:, xo, 0], relay.at[0], sum_sems.at[0], x_next)
    both_chunks(xl, 0)
    send(part_ref.at[:, xl, 0], arrived.at[1], sum_sems.at[3], x_last)
    both_chunks(xn, 0)
    both_chunks(x, 0)
    pass_on(0, xn, x_next)
    both_chunks(xo, 1)
    send(part_ref.at[:, xo, 1], relay.at[1], sum_sems.at[1], x_last)
    both_chunks(xn, 1)
    send(part_ref.at[:, xn, 1], arrived.at[0], sum_sems.at[2], x_next)
    both_chunks(xl, 1)
    cross_over(0)
    both_chunks(x, 1)
    pass_on(1, xl, x_last)

    own_rho(0)
    mine = lambda half: everyone.at[z, y, core, half]
    theirs = lambda half: everyone.at[z, 1 - y, core, half]
    upper = lambda zz: everyone.at[zz, :, core, 0]
    lower = lambda zz, yy: everyone.at[zz, yy, core, 1]
    send(mine(0), mine(0), side_sems.at[0, 0], beside)
    send(mine(0), mine(0), side_sems.at[1, 0], sibling)
    cross_over(1)
    landed(theirs(0), side_sems.at[0, 0])
    send(upper(z), upper(z), ring_sems.at[0, 0, 1], z_next)
    send(upper(z), upper(z), ring_sems.at[0, 1, 1], z_last)
    send(theirs(0), theirs(0), side_sems.at[2, 0], sibling)
    own_rho(1)
    send(lower(z, y), lower(z, y), ring_sems.at[1, 0, 1], z_next)
    send(lower(z, y), lower(z, y), ring_sems.at[1, 1, 1], z_last)
    send(mine(1), mine(1), side_sems.at[0, 1], beside)
    send(mine(1), mine(1), side_sems.at[1, 1], sibling)

    longest = {(0, 0): n_z // 2, (0, 1): n_z // 2 - 1, (1, 0): n_z // 2 - 1, (1, 1): n_z // 2}

    def ring_step(step):
        for half in (0, 1):
            for way in (0, 1):
                if step > longest[half, way]:
                    continue
                origin = (z + n_z - step) % n_z if way == 0 else (z + step) % n_z
                piece = upper(origin) if half == 0 else lower(origin, y)
                landed(piece, ring_sems.at[half, way, step])
                if step < longest[half, way]:
                    send(piece, piece, ring_sems.at[half, way, step + 1], z_next if way == 0 else z_last)
                if half == 1:
                    send(piece, piece, ring_sems.at[2, way, step], beside)
                send(piece, piece, ring_sems.at[3 + half, way, step], sibling)

    def side_step(step):
        for way in (0, 1):
            if step > longest[1, way]:
                continue
            origin = (z + n_z - step) % n_z if way == 0 else (z + step) % n_z
            piece = lower(origin, 1 - y)
            landed(piece, ring_sems.at[2, way, step])
            send(piece, piece, ring_sems.at[5, way, step], sibling)

    def rest_step(step):
        if step == 0:
            for yy, spot in ((y, 1), (1 - y, 2)):
                for half in range(2):
                    landed(everyone.at[z, yy, 1 - core, half], side_sems.at[spot, half])
            return
        for way in (0, 1):
            origin = (z + n_z - step) % n_z if way == 0 else (z + step) % n_z
            if step <= longest[0, way]:
                landed(everyone.at[origin, :, 1 - core, 0], ring_sems.at[3, way, step])
            if step <= longest[1, way]:
                landed(everyone.at[origin, y, 1 - core, 1], ring_sems.at[4, way, step])
                landed(everyone.at[origin, 1 - y, 1 - core, 1], ring_sems.at[5, way, step])

    dx = (x + 4 - z % 4) % 4
    root = z // 4 == y_hi
    first = core * quarter
    eighth = quarter // 2

    def group_origins(step):
        if step == 0:
            return ((z, 0),)
        if step == n_z // 2:
            return (((z + step) % n_z, step),)
        return (((z + n_z - step) % n_z, step), ((z + step) % n_z, n_z - step))

    held = lambda zz, part: left.at[zz, :, :, pl.ds(part * eighth, eighth)]
    late = []

    def left_copies(step):
        made = []
        for zz, tag in group_origins(step):
            base = len(sends)

            def numbered(source, target, arrival, device, offset):
                return pltpu.make_async_remote_copy(
                    src_ref=source, dst_ref=target, send_sem=send_sems.at[base + offset],
                    recv_sem=arrival, device_id=device, device_id_type=MESH,
                )

            there = everyone.at[zz, :, :, 1 - y, pl.ds(first, quarter)]
            to_next = numbered(held(zz, 0), held(zz, 0), left_sems.at[0, tag], x_next, 0)
            to_last = numbered(held(zz, 1), held(zz, 1), left_sems.at[1, tag], x_last, 1)
            to_across = numbered(there, left.at[zz], left_sems.at[2, tag], across, 2)
            made.append((zz, tag, to_next, to_last, to_across))
            sends.extend([None] * 3)
        late.extend(made)
        return made

    def left_from_root(made):
        @pl.when((dx == 0) & root)
        def _():
            for zz, tag, to_next, to_last, to_across in made:
                to_across.start()
                left[zz] = everyone[zz, :, :, y, pl.ds(first, quarter)]
                to_next.start()
                to_last.start()

    def left_onward(made):
        @pl.when((dx == 0) & jnp.logical_not(root))
        def _():
            for zz, tag, to_next, to_last, to_across in made:
                landed(left.at[zz], left_sems.at[2, tag])
                to_next.start()
                to_last.start()

        @pl.when(dx == 1)
        def _():
            for zz, tag, to_next, to_last, to_across in made:
                landed(held(zz, 0), left_sems.at[0, tag])
                to_next.start()

        @pl.when(dx == 3)
        def _():
            for zz, tag, to_next, to_last, to_across in made:
                landed(held(zz, 1), left_sems.at[1, tag])
                to_last.start()

    def left_middle(made):
        @pl.when(dx == 2)
        def _():
            for zz, tag, to_next, to_last, to_across in made:
                landed(held(zz, 0), left_sems.at[0, tag])
                to_next.start()
                landed(held(zz, 1), left_sems.at[1, tag])
                to_last.start()

    parts = [left_copies(step) for step in range(n_z // 2 + 1)]
    ring_step(1)
    landed(theirs(1), side_sems.at[0, 1])
    send(theirs(1), theirs(1), side_sems.at[2, 1], sibling)
    rest_step(0)
    left_from_root(parts[0])
    ring_step(2)
    side_step(1)
    rest_step(1)
    left_from_root(parts[1])
    ring_step(3)
    side_step(2)
    rest_step(2)
    left_from_root(parts[2])
    left_onward(parts[0])
    ring_step(4)
    left_onward(parts[1])
    left_middle(parts[0])
    side_step(3)
    rest_step(3)
    left_from_root(parts[3])
    left_onward(parts[2])
    left_middle(parts[1])
    side_step(4)
    rest_step(4)
    left_from_root(parts[4])
    left_onward(parts[3])
    left_middle(parts[2])
    left_onward(parts[4])
    left_middle(parts[3])
    left_middle(parts[4])

    def group_product(k, carry):
        odd = k % 2
        tag = (odd * ((k + 1) // 2) + (1 - odd) * (n_z - k // 2)) % n_z
        zz = (z + n_z - tag) % n_z

        @pl.when(dx == 1)
        def _():
            landed(held(zz, 1), left_sems.at[1, tag])

        @pl.when(dx == 3)
        def _():
            landed(held(zz, 0), left_sems.at[0, tag])

        straight = [left[zz, i // 2, i % 2].astype(f32) for i in range(4)]
        side = jnp.concatenate([turned(value) for value in straight], axis=1)
        both = jnp.concatenate([-jnp.concatenate(straight, axis=1), side], axis=0)
        both = both.astype(bf16)
        for half in range(2):
            right = jnp.concatenate([everyone[zz, i // 2, i % 2, half] for i in range(4)], axis=1)
            product = lax.dot_general(
                both, right, (((1,), (1,)), ((), ())), preferred_element_type=f32
            )
            for part in range(2):
                spot = (part, slice(None), slice(half * half_rows, (half + 1) * half_rows))
                out_ref[spot] += product[part * quarter : (part + 1) * quarter]
        return carry

    lax.fori_loop(0, n_z, group_product, 0)

    for moving in sends:
        if moving is not None:
            moving.wait_send()
    for zz, tag, to_next, to_last, to_across in late:
        pl.when(dx != 3)(lambda: to_next.wait_send())
        pl.when(dx != 1)(lambda: to_last.wait_send())
        pl.when((dx == 0) & root)(lambda: to_across.wait_send())

    def sent_plane(x, carry):
        to_behind(occ_ref.at[:, x], far.at[x], x).wait_send()
        return carry

    def passed_plane(x, carry):
        to_sibling(occ_ref.at[:, x], near.at[x], x).wait_send()
        return carry

    def passed_far(x, carry):
        to_sibling(far.at[x], near.at[x], x).wait_send()
        return carry

    to_behind(level_ref, far_level, PLANES).wait_send()
    lax.fori_loop(0, PLANES, sent_plane, 0)

    @pl.when(core == 1)
    def _():
        to_sibling(level_ref, near_level, PLANES).wait_send()
        lax.fori_loop(0, PLANES, passed_plane, 0)

    @pl.when(core == 0)
    def _():
        to_sibling(far_level, near_level, PLANES).wait_send()
        lax.fori_loop(0, PLANES, passed_far, 0)


def whole_response(occ, emp, gvectors, energies, ztab, xytabs, n_z):
    bf16, f32 = jnp.bfloat16, jnp.float32
    half = NG // 16
    anywhere, vmem = pl.BlockSpec(memory_space=pl.ANY), pl.BlockSpec(memory_space=pltpu.VMEM)
    return pl.pallas_call(
        response_kernel,
        out_shape=jax.ShapeDtypeStruct((2, half // 2, 2 * half), f32),
        in_specs=[anywhere, anywhere, vmem, vmem, vmem, anywhere, anywhere],
        out_specs=vmem,
        scratch_shapes=[
            pltpu.VMEM((PLANES, 2, 4, CELLS), bf16),
            pltpu.VMEM((PLANES, 2, 4, CELLS), bf16),
            pltpu.VMEM((8, LANES), f32),
            pltpu.VMEM((8, LANES), f32),
            pltpu.VMEM((8, LANES), f32),
            pltpu.VMEM((2, PLANES, 8, CELLS), bf16),
            pltpu.VMEM((Z_ROWS, GROUP_CELLS), bf16),
            pltpu.VMEM((PLANES // BATCH, WAVE_ROWS, DEPTH), bf16),
            pltpu.VMEM((16, CELLS), f32),
            pltpu.VMEM((GROUPS * LANES, GROUP_CELLS), bf16),
            pltpu.VMEM((Z_ROWS, GROUPS * LANES), f32),
            pltpu.VMEM((Q_SLOTS // 2, DEPTH, 2 * LANES), bf16),
            pltpu.VMEM((Q_SLOTS * WAVE_ROWS, LANES), f32),
            pltpu.VMEM((512, LANES), f32),
            pltpu.VMEM((1, NG), jnp.int32),
            pltpu.SMEM((1, NG), jnp.int32),
            pltpu.VMEM((1, NG), f32),
            pltpu.VMEM((NG, LANES), f32),
            pltpu.VMEM((2, 4, 2, half, LANES), bf16),
            pltpu.VMEM((n_z, 2, 2, 2, half, LANES), bf16),
            pltpu.VMEM((n_z, 2, 2, half // 2, LANES), bf16),
            pltpu.VMEM((2, 2, half, LANES), bf16),
            pltpu.VMEM((2, 2, half, LANES), bf16),
            pltpu.VMEM((4, 2, half, LANES), bf16),
            pltpu.VMEM((2, half, LANES), bf16),
            pltpu.VMEM((2, half, LANES), bf16),
            pltpu.SemaphoreType.DMA((PLANES + 1,)),
            pltpu.SemaphoreType.DMA((PLANES + 1,)),
            pltpu.SemaphoreType.DMA((PLANES + 1,)),
            pltpu.SemaphoreType.DMA((PLANES + 1,)),
            pltpu.SemaphoreType.DMA((4,)),
            pltpu.SemaphoreType.DMA((128,)),
            pltpu.SemaphoreType.DMA((8,)),
            pltpu.SemaphoreType.DMA((6, 2, n_z // 2 + 1)),
            pltpu.SemaphoreType.DMA((3, 2)),
            pltpu.SemaphoreType.DMA((3, n_z)),
        ],
        compiler_params=pltpu.CompilerParams(
            collective_id=0, has_side_effects=True, vmem_limit_bytes=60 * 2**20
        ),
        cost_estimate=pl.CostEstimate(
            flops=16_000_000_000, bytes_accessed=12_000_000, transcendentals=0
        ),
    )(occ, emp, gvectors, *energies, ztab, xytabs)


def shards(ztab, xytabs, occupied_states, empty_states, occ_energy, empty_energy, gvectors):
    occ = jnp.transpose(occupied_states, (0, 2, 1, 3))
    emp = jnp.transpose(empty_states, (0, 2, 1, 3))
    energies = occ_energy.reshape(1, -1), empty_energy.reshape(1, -1)
    n_z = lax.axis_size("blk") // 4
    out = whole_response(occ, emp, gvectors, energies, ztab, xytabs, n_z)
    return jnp.transpose(out, (1, 0, 2))


def solution(mesh):
    ztab = z_table()
    xytabs = plane_table(mesh.shape["pw"])
    return jax.shard_map(
        lambda *args: shards(jnp.asarray(ztab), jnp.asarray(xytabs), *args),
        mesh=mesh,
        in_specs=(P(None, "blk", "pw", None), P(None, "blk", "pw", None), P("blk"), P("blk"), P()),
        out_specs=P("blk", None, "pw"),
        check_vma=False,
    )
```

```python
import math

import jax
import jax.numpy as jnp
import numpy as np
from jax import lax
from jax.experimental import pallas as pl
from jax.experimental.pallas import tpu as pltpu
from jax.sharding import PartitionSpec as P
import ml_dtypes

GX = 72
GY = 72
GZ = 144
KMAX = 16
SIDE = 2 * KMAX + 1
PLANES = 9
CELLS = GY * GZ
NG = 4096
GROUPS = 9
GROUP_CELLS = 8 * GZ
Z_ROWS = SIDE * 8
ROWS_X = 80
BATCH = 3
DEPTH = BATCH * ROWS_X
HALF = (SIDE * SIDE + 1) // 2
WAVE_ROWS = 1096
Q_SLOTS = 34
LANES = 128
omega_shift = 0.5


def z_table():
    z = np.arange(GZ)
    out = np.zeros((Z_ROWS, GROUP_CELLS), np.float64)
    for q in range(KMAX + 1):
        angle = 2 * np.pi * ((q * z) % GZ) / GZ
        for y in range(8):
            out[q * 8 + y, y * GZ : (y + 1) * GZ] = np.cos(angle)
            if q:
                out[(KMAX + q) * 8 + y, y * GZ : (y + 1) * GZ] = np.sin(angle)
    return out.astype(np.float32).astype(ml_dtypes.bfloat16)


def plane_table(groups):
    h = np.arange(HALF)
    p = (h + KMAX) // SIDE
    a = h - SIDE * p
    out = np.zeros((groups, WAVE_ROWS, PLANES, ROWS_X), np.float64)
    y = np.arange(GY)
    for group in range(groups):
        for plane in range(PLANES):
            x = group * PLANES + plane
            steps = (p[:, None] * y[None, :] + a[:, None] * x) % GX
            out[group, 0 : 2 * HALF : 2, plane, :GY] = np.cos(2 * np.pi * steps / GX)
            out[group, 1 : 2 * HALF : 2, plane, :GY] = np.sin(2 * np.pi * steps / GX)
    out = out.reshape(groups, WAVE_ROWS, PLANES // BATCH, DEPTH).transpose(0, 2, 1, 3)
    return out.astype(np.float32).astype(ml_dtypes.bfloat16)


def turned(value):
    lane = lax.broadcasted_iota(jnp.int32, value.shape, 1)
    ahead = pltpu.roll(value, LANES - 8, 1)
    behind = pltpu.roll(value, 8, 1)
    return jnp.where((lane & 8) == 0, ahead, -behind)


MESH = pl.DeviceIdType.MESH


def response_kernel(
    occ_ref, emp_ref, wave_ref, occ_energy_ref, emp_energy_ref, ztab_ref, xytab_ref, out_ref,
    near, far, level_ref, near_level, far_level, emp, ztab, xytab, occ_f, pairs, depth_out, sections, waves,
    picked, index_v, index_s, sign_v, sign_rows, part_ref, everyone, left, relay, passed, arrived, plane_sum,
    other, ahead_sems, far_sems, pass_sems, near_sems, load_sems, send_sems, sum_sems, ring_sems,
    side_sems, left_sems,
):
    blk, pw = lax.axis_index("blk"), lax.axis_index("pw")
    count = lax.axis_size("blk")
    n_z = count // 4
    z, y, core = blk // 4, (blk // 2) % 2, blk % 2
    x, y_hi = pw % 4, pw // 4
    f32, bf16 = jnp.float32, jnp.bfloat16

    def place(z=z, y=y, core=core, x=x, y_hi=y_hi):
        return {"blk": z * 4 + y * 2 + core, "pw": y_hi * 4 + x}

    x_next, x_last = place(x=(x + 1) % 4), place(x=(x + 3) % 4)
    z_next, z_last = place(z=(z + 1) % n_z), place(z=(z + n_z - 1) % n_z)
    sibling, beside = place(core=1 - core), place(y=1 - y)
    facing, across = place(y_hi=1 - y_hi), place(y=1 - y, y_hi=1 - y_hi)
    behind = {"blk": (blk + count - 2) % count, "pw": pw}
    ahead = {"blk": (blk + 2) % count, "pw": pw}

    barrier = pltpu.get_barrier_semaphore()
    neighbours = (
        x_next, x_last, z_next, z_last, sibling, beside, facing, across, behind, ahead
    )
    for device in neighbours:
        pl.semaphore_signal(barrier, inc=1, device_id=device, device_id_type=MESH)
    pl.semaphore_wait(barrier, len(neighbours))

    def to_behind(source, target, spot):
        return pltpu.make_async_remote_copy(
            src_ref=source, dst_ref=target, send_sem=ahead_sems.at[spot],
            recv_sem=far_sems.at[spot], device_id=behind, device_id_type=MESH,
        )

    def to_sibling(source, target, spot):
        return pltpu.make_async_remote_copy(
            src_ref=source, dst_ref=target, send_sem=pass_sems.at[spot],
            recv_sem=near_sems.at[spot], device_id=sibling, device_id_type=MESH,
        )

    def landed(target, arrival):
        pltpu.make_async_copy(target, target, arrival).wait()

    def send_plane(x, carry):
        to_behind(occ_ref.at[:, x], far.at[x], x).start()
        return carry

    def pass_plane(x, carry):
        to_sibling(occ_ref.at[:, x], near.at[x], x).start()
        return carry

    lane = lax.broadcasted_iota(jnp.int32, (8, LANES), 1)
    occ_energy = occ_energy_ref[...].astype(f32)
    emp_energy = emp_energy_ref[...].astype(f32)
    spread = jnp.zeros((8, LANES), f32)
    for v in range(4):
        spread = jnp.where((lane // 16) % 4 == v, occ_energy[:, v : v + 1], spread)
    level_ref[...] = spread
    emp_level = jnp.zeros((8, LANES), f32)
    for c in range(8):
        emp_level = jnp.where(lane % 8 == c, emp_energy[:, c : c + 1], emp_level)
    to_behind(level_ref, far_level, PLANES).start()
    lax.fori_loop(0, PLANES, send_plane, 0)

    @pl.when(core == 1)
    def _():
        to_sibling(level_ref, near_level, PLANES).start()
        lax.fori_loop(0, PLANES, pass_plane, 0)

    loads = [
        pltpu.make_async_copy(emp_ref, emp, load_sems.at[0]),
        pltpu.make_async_copy(ztab_ref, ztab, load_sems.at[1]),
        pltpu.make_async_copy(xytab_ref.at[pw], xytab, load_sems.at[2]),
    ]
    for load in loads:
        load.start()

    flat = SIDE * wave_ref[1:2, :] + wave_ref[0:1, :]
    index_v[...] = (wave_ref[2:3, :] + KMAX) * WAVE_ROWS + 2 * jnp.abs(flat)
    sign_v[...] = jnp.where(flat < 0, -1.0, 1.0).astype(jnp.float32)
    index_move = pltpu.make_async_copy(index_v, index_s, load_sems.at[3])
    index_move.start()
    for load in loads:
        load.wait()
    index_move.wait()

    def group_pairs(x, group):
        for part in range(3):
            start = group * GROUP_CELLS + part * 384
            cells = slice(start, start + 384)
            emp_re = emp[0, x, :, cells].astype(jnp.float32)
            emp_im = emp[1, x, :, cells].astype(jnp.float32)
            for v in range(8):
                row = v if v < 4 else v + 4
                occ_re = occ_f[row : row + 1, cells]
                occ_im = occ_f[row + 4 : row + 5, cells]
                both = jnp.concatenate(
                    [occ_re * emp_re + occ_im * emp_im, occ_re * emp_im - occ_im * emp_re], axis=0
                )
                rows = slice(group * LANES + v * 16, group * LANES + v * 16 + 16)
                pairs[rows, part * 384 : part * 384 + 384] = both.astype(jnp.bfloat16)

    blank = jnp.zeros((ROWS_X - GY, LANES), jnp.float32)

    def rows_of(first):
        parts = [depth_out[first : first + 8, t * LANES : (t + 1) * LANES] for t in range(GROUPS)]
        return jnp.concatenate(parts + [blank], axis=0)

    def one_plane(x, spot):
        landed(far.at[x], far_sems.at[x])

        @pl.when(core == 0)
        def _():
            to_sibling(far.at[x], near.at[x], x).start()

        landed(near.at[x], near_sems.at[x])
        for part in range(2):
            occ_f[part * 4 : part * 4 + 4, :] = near[x, part].astype(jnp.float32)
            occ_f[part * 4 + 8 : part * 4 + 12, :] = far[x, part].astype(jnp.float32)

        for start in range(0, GROUPS, 2):
            stop = min(start + 2, GROUPS)
            for group in range(start, stop):
                group_pairs(x, group)
            lines = slice(start * LANES, stop * LANES)
            depth_out[:, lines] = lax.dot_general(
                ztab[...], pairs[lines, :], (((1,), (1,)), ((), ())),
                preferred_element_type=jnp.float32,
            )
        rows = pl.ds(pl.multiple_of(spot * ROWS_X, 16), ROWS_X)

        def put(slot, value):
            half = slot % 2
            sections[slot // 2, rows, half * LANES : (half + 1) * LANES] = value.astype(jnp.bfloat16)

        put(KMAX, rows_of(0))
        for q in range(1, KMAX + 1):
            cosine = rows_of(q * 8)
            sine = turned(rows_of((KMAX + q) * 8))
            put(KMAX + q, cosine + sine)
            put(KMAX - q, cosine - sine)

    sections[Q_SLOTS // 2 - 1, :, LANES:] = jnp.zeros((DEPTH, LANES), jnp.bfloat16)
    def clear(k, carry):
        rows = pl.ds(pl.multiple_of(k * WAVE_ROWS, 8), WAVE_ROWS)
        waves[rows, :] = jnp.zeros((WAVE_ROWS, LANES), jnp.float32)
        return carry

    lax.fori_loop(0, Q_SLOTS, clear, 0)

    def stand(step, carry):
        first = pl.multiple_of(step * 128, 128)
        row = sign_v[:, pl.ds(first, 128)]
        sign_rows[pl.ds(first, 128), :] = jnp.broadcast_to(row, (128, LANES)).T
        return carry

    lax.fori_loop(0, NG // 128, stand, 0)
    landed(far_level, far_sems.at[PLANES])

    @pl.when(core == 0)
    def _():
        to_sibling(far_level, near_level, PLANES).start()

    def each_batch(batch, carry):
        def each_plane(spot, carry):
            one_plane(batch * BATCH + spot, spot)
            return carry

        lax.fori_loop(0, BATCH, each_plane, 0)

        def slot_pair(k, carry):
            product = jnp.dot(xytab[batch], sections[k], preferred_element_type=jnp.float32)
            first = pl.multiple_of(k * 2 * WAVE_ROWS, 8)
            for half in range(2):
                rows = pl.ds(first + half * WAVE_ROWS, WAVE_ROWS)
                waves[rows, :] += product[:, half * LANES : (half + 1) * LANES]
            return carry

        lax.fori_loop(0, Q_SLOTS // 2, slot_pair, 0)
        return carry

    lax.fori_loop(0, PLANES // BATCH, each_batch, 0)
    landed(near_level, near_sems.at[PLANES])
    occ_level = jnp.where(lane < LANES // 2, near_level[...], far_level[...])
    scale = jnp.sqrt(2.0 / (emp_level - occ_level + omega_shift))[0:1]

    def chunk(yy, xx, half):
        base = (yy * 4 + xx) * 512 + half * 256

        def pick(step, carry):
            first = step * 16
            for i in range(16):
                row = index_s[0, base + first + i]
                picked[pl.ds((first + i) * 2, 2), :] = waves[pl.ds(row, 2), :]
            return carry

        lax.fori_loop(0, 16, pick, 0)
        for part in range(2):
            cosine = picked[pl.ds(part * 256, 128, stride=2), :]
            sine = picked[pl.ds(part * 256 + 1, 128, stride=2), :]
            first = pl.multiple_of(base + part * 128, 128)
            total = (cosine + sign_rows[pl.ds(first, 128), :] * turned(sine)) * scale
            part_ref[yy, xx, half, part * 128 : part * 128 + 128, :] = total.astype(bf16)

    def both_chunks(xx, half):
        def one(yy, carry):
            chunk(yy, xx, half)
            return carry

        lax.fori_loop(0, 2, one, 0)

    sends = []

    def copy(source, target, arrival, device):
        return pltpu.make_async_remote_copy(
            src_ref=source, dst_ref=target, send_sem=send_sems.at[len(sends)], recv_sem=arrival,
            device_id=device, device_id_type=MESH,
        )

    def send(source, target, arrival, device):
        moving = copy(source, target, arrival, device)
        moving.start()
        sends.append(moving)

    out_ref[...] = jnp.zeros_like(out_ref)
    rows = everyone.shape[4] * 2
    half_rows, quarter = rows // 2, rows // 4

    xn, xl, xo = (x + 1) % 4, (x + 3) % 4, (x + 2) % 4

    def pass_on(half, xx, device):
        landed(relay.at[half], sum_sems.at[half])
        share = part_ref[:, xx, half].astype(f32) + relay[half].astype(f32)
        passed[half] = share.astype(bf16)
        send(passed.at[half], arrived.at[2 + half], sum_sems.at[4 + half], device)

    def x_total(yy, half):
        first, second = (2, 1) if half == 0 else (0, 3)
        return (
            part_ref[yy, x, half].astype(f32)
            + arrived[first, yy].astype(f32)
            + arrived[second, yy].astype(f32)
        )

    def cross_over(half):
        for spot in (2, 1) if half == 0 else (0, 3):
            landed(arrived.at[spot], sum_sems.at[2 + spot])
        plane_sum[half] = x_total(1 - y_hi, half).astype(bf16)
        send(plane_sum.at[half], other.at[half], sum_sems.at[6 + half], facing)

    def own_rho(half):
        landed(other.at[half], sum_sems.at[6 + half])
        total = x_total(y_hi, half) + other[half].astype(f32)
        everyone[z, y, core, half] = total.astype(bf16)

    both_chunks(xo, 0)
    send(part_ref.at[:, xo, 0], relay.at[0], sum_sems.at[0], x_next)
    both_chunks(xl, 0)
    send(part_ref.at[:, xl, 0], arrived.at[1], sum_sems.at[3], x_last)
    both_chunks(xn, 0)
    both_chunks(x, 0)
    pass_on(0, xn, x_next)
    both_chunks(xo, 1)
    send(part_ref.at[:, xo, 1], relay.at[1], sum_sems.at[1], x_last)
    both_chunks(xn, 1)
    send(part_ref.at[:, xn, 1], arrived.at[0], sum_sems.at[2], x_next)
    both_chunks(xl, 1)
    cross_over(0)
    both_chunks(x, 1)
    pass_on(1, xl, x_last)

    own_rho(0)
    mine = lambda half: everyone.at[z, y, core, half]
    theirs = lambda half: everyone.at[z, 1 - y, core, half]
    upper = lambda zz: everyone.at[zz, :, core, 0]
    lower = lambda zz, yy: everyone.at[zz, yy, core, 1]
    send(mine(0), mine(0), side_sems.at[0, 0], beside)
    send(mine(0), mine(0), side_sems.at[1, 0], sibling)
    cross_over(1)
    landed(theirs(0), side_sems.at[0, 0])
    send(upper(z), upper(z), ring_sems.at[0, 0, 1], z_next)
    send(upper(z), upper(z), ring_sems.at[0, 1, 1], z_last)
    send(theirs(0), theirs(0), side_sems.at[2, 0], sibling)
    own_rho(1)
    send(lower(z, y), lower(z, y), ring_sems.at[1, 0, 1], z_next)
    send(lower(z, y), lower(z, y), ring_sems.at[1, 1, 1], z_last)
    send(mine(1), mine(1), side_sems.at[0, 1], beside)
    send(mine(1), mine(1), side_sems.at[1, 1], sibling)

    longest = {(0, 0): n_z // 2, (0, 1): n_z // 2 - 1, (1, 0): n_z // 2 - 1, (1, 1): n_z // 2}

    def ring_step(step):
        for half in (0, 1):
            for way in (0, 1):
                if step > longest[half, way]:
                    continue
                origin = (z + n_z - step) % n_z if way == 0 else (z + step) % n_z
                piece = upper(origin) if half == 0 else lower(origin, y)
                landed(piece, ring_sems.at[half, way, step])
                if step < longest[half, way]:
                    send(piece, piece, ring_sems.at[half, way, step + 1], z_next if way == 0 else z_last)
                if half == 1:
                    send(piece, piece, ring_sems.at[2, way, step], beside)
                send(piece, piece, ring_sems.at[3 + half, way, step], sibling)

    def side_step(step):
        for way in (0, 1):
            if step > longest[1, way]:
                continue
            origin = (z + n_z - step) % n_z if way == 0 else (z + step) % n_z
            piece = lower(origin, 1 - y)
            landed(piece, ring_sems.at[2, way, step])
            send(piece, piece, ring_sems.at[5, way, step], sibling)

    def rest_step(step):
        if step == 0:
            for yy, spot in ((y, 1), (1 - y, 2)):
                for half in range(2):
                    landed(everyone.at[z, yy, 1 - core, half], side_sems.at[spot, half])
            return
        for way in (0, 1):
            origin = (z + n_z - step) % n_z if way == 0 else (z + step) % n_z
            if step <= longest[0, way]:
                landed(everyone.at[origin, :, 1 - core, 0], ring_sems.at[3, way, step])
            if step <= longest[1, way]:
                landed(everyone.at[origin, y, 1 - core, 1], ring_sems.at[4, way, step])
                landed(everyone.at[origin, 1 - y, 1 - core, 1], ring_sems.at[5, way, step])

    dx = (x + 4 - z % 4) % 4
    root = z // 4 == y_hi
    first = core * quarter
    eighth = quarter // 2

    def group_origins(step):
        if step == 0:
            return ((z, 0),)
        if step == n_z // 2:
            return (((z + step) % n_z, step),)
        return (((z + n_z - step) % n_z, step), ((z + step) % n_z, n_z - step))

    held = lambda zz, part: left.at[zz, :, :, pl.ds(part * eighth, eighth)]
    late = []

    def left_copies(step):
        made = []
        for zz, tag in group_origins(step):
            base = len(sends)

            def numbered(source, target, arrival, device, offset):
                return pltpu.make_async_remote_copy(
                    src_ref=source, dst_ref=target, send_sem=send_sems.at[base + offset],
                    recv_sem=arrival, device_id=device, device_id_type=MESH,
                )

            there = lambda part: everyone.at[
                zz, :, :, 1 - y, pl.ds(first + part * eighth, eighth)
            ]
            to_next = numbered(held(zz, 0), held(zz, 0), left_sems.at[0, tag], x_next, 0)
            to_last = numbered(held(zz, 1), held(zz, 1), left_sems.at[1, tag], x_last, 1)
            to_across = [
                numbered(there(part), held(zz, part), left_sems.at[2 + part, tag], across, 2 + part)
                for part in range(2)
            ]
            also_next = numbered(held(zz, 1), held(zz, 1), left_sems.at[1, tag], x_next, 4)
            also_last = numbered(held(zz, 0), held(zz, 0), left_sems.at[0, tag], x_last, 5)
            made.append((zz, tag, to_next, to_last, to_across, also_next, also_last))
            sends.extend([None] * 6)
        late.extend(made)
        return made

    def left_from_root(made):
        @pl.when((dx == 0) & root)
        def _():
            for zz, tag, to_next, to_last, to_across, also_next, also_last in made:
                to_across[0].start()
                to_across[1].start()
                left[zz] = everyone[zz, :, :, y, pl.ds(first, quarter)]
                to_next.start()
                to_last.start()

    def left_onward(made):
        @pl.when((dx == 0) & jnp.logical_not(root))
        def _():
            for zz, tag, to_next, to_last, to_across, also_next, also_last in made:
                landed(held(zz, 0), left_sems.at[2, tag])
                to_next.start()
                also_last.start()
                landed(held(zz, 1), left_sems.at[3, tag])
                to_last.start()
                also_next.start()

        @pl.when(dx == 1)
        def _():
            for zz, tag, to_next, to_last, to_across, also_next, also_last in made:
                landed(held(zz, 0), left_sems.at[0, tag])
                to_next.start()

        @pl.when(dx == 3)
        def _():
            for zz, tag, to_next, to_last, to_across, also_next, also_last in made:
                landed(held(zz, 1), left_sems.at[1, tag])
                to_last.start()

    def left_middle(made):
        @pl.when((dx == 2) & root)
        def _():
            for zz, tag, to_next, to_last, to_across, also_next, also_last in made:
                landed(held(zz, 0), left_sems.at[0, tag])
                to_next.start()
                landed(held(zz, 1), left_sems.at[1, tag])
                to_last.start()

    parts = [left_copies(step) for step in range(n_z // 2 + 1)]
    ring_step(1)
    landed(theirs(1), side_sems.at[0, 1])
    send(theirs(1), theirs(1), side_sems.at[2, 1], sibling)
    rest_step(0)
    left_from_root(parts[0])
    ring_step(2)
    side_step(1)
    rest_step(1)
    left_from_root(parts[1])
    ring_step(3)
    side_step(2)
    rest_step(2)
    left_from_root(parts[2])
    left_onward(parts[0])
    ring_step(4)
    left_onward(parts[1])
    left_middle(parts[0])
    side_step(3)
    rest_step(3)
    left_from_root(parts[3])
    left_onward(parts[2])
    left_middle(parts[1])
    side_step(4)
    rest_step(4)
    left_from_root(parts[4])
    left_onward(parts[3])
    left_middle(parts[2])
    left_onward(parts[4])
    left_middle(parts[3])
    left_middle(parts[4])

    def group_product(k, carry):
        odd = k % 2
        tag = (odd * ((k + 1) // 2) + (1 - odd) * (n_z - k // 2)) % n_z
        zz = (z + n_z - tag) % n_z

        @pl.when(dx == 1)
        def _():
            landed(held(zz, 1), left_sems.at[1, tag])

        @pl.when(dx == 3)
        def _():
            landed(held(zz, 0), left_sems.at[0, tag])

        @pl.when((dx == 2) & jnp.logical_not(root))
        def _():
            landed(held(zz, 0), left_sems.at[0, tag])
            landed(held(zz, 1), left_sems.at[1, tag])

        straight = [left[zz, i // 2, i % 2].astype(f32) for i in range(4)]
        side = jnp.concatenate([turned(value) for value in straight], axis=1)
        both = jnp.concatenate([-jnp.concatenate(straight, axis=1), side], axis=0)
        both = both.astype(bf16)
        for half in range(2):
            right = jnp.concatenate([everyone[zz, i // 2, i % 2, half] for i in range(4)], axis=1)
            product = lax.dot_general(
                both, right, (((1,), (1,)), ((), ())), preferred_element_type=f32
            )
            for part in range(2):
                spot = (part, slice(None), slice(half * half_rows, (half + 1) * half_rows))
                out_ref[spot] += product[part * quarter : (part + 1) * quarter]
        return carry

    lax.fori_loop(0, n_z, group_product, 0)

    for moving in sends:
        if moving is not None:
            moving.wait_send()
    far_row = jnp.logical_not(root)
    from_next = (dx < 2) | ((dx == 2) & root)
    from_last = (dx == 0) | (dx == 3) | ((dx == 2) & root)
    for zz, tag, to_next, to_last, to_across, also_next, also_last in late:
        pl.when(from_next)(lambda: to_next.wait_send())
        pl.when(from_last)(lambda: to_last.wait_send())
        for part in range(2):
            pl.when((dx == 0) & root)(lambda: to_across[part].wait_send())
        pl.when((dx == 0) & far_row)(lambda: also_next.wait_send())
        pl.when((dx == 0) & far_row)(lambda: also_last.wait_send())

    def sent_plane(x, carry):
        to_behind(occ_ref.at[:, x], far.at[x], x).wait_send()
        return carry

    def passed_plane(x, carry):
        to_sibling(occ_ref.at[:, x], near.at[x], x).wait_send()
        return carry

    def passed_far(x, carry):
        to_sibling(far.at[x], near.at[x], x).wait_send()
        return carry

    to_behind(level_ref, far_level, PLANES).wait_send()
    lax.fori_loop(0, PLANES, sent_plane, 0)

    @pl.when(core == 1)
    def _():
        to_sibling(level_ref, near_level, PLANES).wait_send()
        lax.fori_loop(0, PLANES, passed_plane, 0)

    @pl.when(core == 0)
    def _():
        to_sibling(far_level, near_level, PLANES).wait_send()
        lax.fori_loop(0, PLANES, passed_far, 0)


def whole_response(occ, emp, gvectors, energies, ztab, xytabs, n_z):
    bf16, f32 = jnp.bfloat16, jnp.float32
    half = NG // 16
    anywhere, vmem = pl.BlockSpec(memory_space=pl.ANY), pl.BlockSpec(memory_space=pltpu.VMEM)
    return pl.pallas_call(
        response_kernel,
        out_shape=jax.ShapeDtypeStruct((2, half // 2, 2 * half), f32),
        in_specs=[anywhere, anywhere, vmem, vmem, vmem, anywhere, anywhere],
        out_specs=vmem,
        scratch_shapes=[
            pltpu.VMEM((PLANES, 2, 4, CELLS), bf16),
            pltpu.VMEM((PLANES, 2, 4, CELLS), bf16),
            pltpu.VMEM((8, LANES), f32),
            pltpu.VMEM((8, LANES), f32),
            pltpu.VMEM((8, LANES), f32),
            pltpu.VMEM((2, PLANES, 8, CELLS), bf16),
            pltpu.VMEM((Z_ROWS, GROUP_CELLS), bf16),
            pltpu.VMEM((PLANES // BATCH, WAVE_ROWS, DEPTH), bf16),
            pltpu.VMEM((16, CELLS), f32),
            pltpu.VMEM((GROUPS * LANES, GROUP_CELLS), bf16),
            pltpu.VMEM((Z_ROWS, GROUPS * LANES), f32),
            pltpu.VMEM((Q_SLOTS // 2, DEPTH, 2 * LANES), bf16),
            pltpu.VMEM((Q_SLOTS * WAVE_ROWS, LANES), f32),
            pltpu.VMEM((512, LANES), f32),
            pltpu.VMEM((1, NG), jnp.int32),
            pltpu.SMEM((1, NG), jnp.int32),
            pltpu.VMEM((1, NG), f32),
            pltpu.VMEM((NG, LANES), f32),
            pltpu.VMEM((2, 4, 2, half, LANES), bf16),
            pltpu.VMEM((n_z, 2, 2, 2, half, LANES), bf16),
            pltpu.VMEM((n_z, 2, 2, half // 2, LANES), bf16),
            pltpu.VMEM((2, 2, half, LANES), bf16),
            pltpu.VMEM((2, 2, half, LANES), bf16),
            pltpu.VMEM((4, 2, half, LANES), bf16),
            pltpu.VMEM((2, half, LANES), bf16),
            pltpu.VMEM((2, half, LANES), bf16),
            pltpu.SemaphoreType.DMA((PLANES + 1,)),
            pltpu.SemaphoreType.DMA((PLANES + 1,)),
            pltpu.SemaphoreType.DMA((PLANES + 1,)),
            pltpu.SemaphoreType.DMA((PLANES + 1,)),
            pltpu.SemaphoreType.DMA((4,)),
            pltpu.SemaphoreType.DMA((160,)),
            pltpu.SemaphoreType.DMA((8,)),
            pltpu.SemaphoreType.DMA((6, 2, n_z // 2 + 1)),
            pltpu.SemaphoreType.DMA((3, 2)),
            pltpu.SemaphoreType.DMA((4, n_z)),
        ],
        compiler_params=pltpu.CompilerParams(
            collective_id=0, has_side_effects=True, vmem_limit_bytes=60 * 2**20
        ),
        cost_estimate=pl.CostEstimate(
            flops=16_000_000_000, bytes_accessed=12_000_000, transcendentals=0
        ),
    )(occ, emp, gvectors, *energies, ztab, xytabs)


def shards(ztab, xytabs, occupied_states, empty_states, occ_energy, empty_energy, gvectors):
    occ = jnp.transpose(occupied_states, (0, 2, 1, 3))
    emp = jnp.transpose(empty_states, (0, 2, 1, 3))
    energies = occ_energy.reshape(1, -1), empty_energy.reshape(1, -1)
    n_z = lax.axis_size("blk") // 4
    out = whole_response(occ, emp, gvectors, energies, ztab, xytabs, n_z)
    return jnp.transpose(out, (1, 0, 2))


def solution(mesh):
    ztab = z_table()
    xytabs = plane_table(mesh.shape["pw"])
    return jax.shard_map(
        lambda *args: shards(jnp.asarray(ztab), jnp.asarray(xytabs), *args),
        mesh=mesh,
        in_specs=(P(None, "blk", "pw", None), P(None, "blk", "pw", None), P("blk"), P("blk"), P()),
        out_specs=P("blk", None, "pw"),
        check_vma=False,
    )
```

```python
import math

import jax
import jax.numpy as jnp
import numpy as np
from jax import lax
from jax.experimental import pallas as pl
from jax.experimental.pallas import tpu as pltpu
from jax.sharding import PartitionSpec as P
import ml_dtypes

GX = 72
GY = 72
GZ = 144
KMAX = 16
SIDE = 2 * KMAX + 1
PLANES = 9
CELLS = GY * GZ
NG = 4096
GROUPS = 9
GROUP_CELLS = 8 * GZ
Z_ROWS = SIDE * 8
ROWS_X = 80
BATCH = 3
DEPTH = BATCH * ROWS_X
HALF = (SIDE * SIDE + 1) // 2
WAVE_ROWS = 1096
Q_SLOTS = 34
LANES = 128
omega_shift = 0.5


def z_table():
    z = np.arange(GZ)
    out = np.zeros((Z_ROWS, GROUP_CELLS), np.float64)
    for q in range(KMAX + 1):
        angle = 2 * np.pi * ((q * z) % GZ) / GZ
        for y in range(8):
            out[q * 8 + y, y * GZ : (y + 1) * GZ] = np.cos(angle)
            if q:
                out[(KMAX + q) * 8 + y, y * GZ : (y + 1) * GZ] = np.sin(angle)
    return out.astype(np.float32).astype(ml_dtypes.bfloat16)


def plane_table(groups):
    h = np.arange(HALF)
    p = (h + KMAX) // SIDE
    a = h - SIDE * p
    out = np.zeros((groups, WAVE_ROWS, PLANES, ROWS_X), np.float64)
    y = np.arange(GY)
    for group in range(groups):
        for plane in range(PLANES):
            x = group * PLANES + plane
            steps = (p[:, None] * y[None, :] + a[:, None] * x) % GX
            out[group, 0 : 2 * HALF : 2, plane, :GY] = np.cos(2 * np.pi * steps / GX)
            out[group, 1 : 2 * HALF : 2, plane, :GY] = np.sin(2 * np.pi * steps / GX)
    out = out.reshape(groups, WAVE_ROWS, PLANES // BATCH, DEPTH).transpose(0, 2, 1, 3)
    return out.astype(np.float32).astype(ml_dtypes.bfloat16)


def turned(value):
    lane = lax.broadcasted_iota(jnp.int32, value.shape, 1)
    ahead = pltpu.roll(value, LANES - 8, 1)
    behind = pltpu.roll(value, 8, 1)
    return jnp.where((lane & 8) == 0, ahead, -behind)


MESH = pl.DeviceIdType.MESH


def response_kernel(
    occ_ref, emp_ref, wave_ref, occ_energy_ref, emp_energy_ref, ztab_ref, xytab_ref, out_ref,
    near, far, level_ref, near_level, far_level, emp, ztab, xytab, occ_f, pairs, depth_out, sections, waves,
    picked, index_v, index_s, sign_v, sign_rows, part_ref, everyone, left, relay, passed, arrived, plane_sum,
    other, ahead_sems, far_sems, pass_sems, near_sems, load_sems, send_sems, sum_sems, ring_sems,
    side_sems, left_sems,
):
    blk, pw = lax.axis_index("blk"), lax.axis_index("pw")
    count = lax.axis_size("blk")
    n_z = count // 4
    z, y, core = blk // 4, (blk // 2) % 2, blk % 2
    x, y_hi = pw % 4, pw // 4
    f32, bf16 = jnp.float32, jnp.bfloat16

    def place(z=z, y=y, core=core, x=x, y_hi=y_hi):
        return {"blk": z * 4 + y * 2 + core, "pw": y_hi * 4 + x}

    x_next, x_last = place(x=(x + 1) % 4), place(x=(x + 3) % 4)
    z_next, z_last = place(z=(z + 1) % n_z), place(z=(z + n_z - 1) % n_z)
    sibling, beside = place(core=1 - core), place(y=1 - y)
    facing, across = place(y_hi=1 - y_hi), place(y=1 - y, y_hi=1 - y_hi)
    behind = {"blk": (blk + count - 2) % count, "pw": pw}
    ahead = {"blk": (blk + 2) % count, "pw": pw}

    barrier = pltpu.get_barrier_semaphore()
    neighbours = (
        x_next, x_last, z_next, z_last, sibling, beside, facing, across, behind, ahead
    )
    for device in neighbours:
        pl.semaphore_signal(barrier, inc=1, device_id=device, device_id_type=MESH)
    pl.semaphore_wait(barrier, len(neighbours))

    def to_behind(source, target, spot):
        return pltpu.make_async_remote_copy(
            src_ref=source, dst_ref=target, send_sem=ahead_sems.at[spot],
            recv_sem=far_sems.at[spot], device_id=behind, device_id_type=MESH,
        )

    def to_sibling(source, target, spot):
        return pltpu.make_async_remote_copy(
            src_ref=source, dst_ref=target, send_sem=pass_sems.at[spot],
            recv_sem=near_sems.at[spot], device_id=sibling, device_id_type=MESH,
        )

    def landed(target, arrival):
        pltpu.make_async_copy(target, target, arrival).wait()

    def send_plane(x, carry):
        to_behind(occ_ref.at[:, x], far.at[x], x).start()
        return carry

    def pass_plane(x, carry):
        to_sibling(occ_ref.at[:, x], near.at[x], x).start()
        return carry

    lane = lax.broadcasted_iota(jnp.int32, (8, LANES), 1)
    occ_energy = occ_energy_ref[...].astype(f32)
    emp_energy = emp_energy_ref[...].astype(f32)
    spread = jnp.zeros((8, LANES), f32)
    for v in range(4):
        spread = jnp.where((lane // 16) % 4 == v, occ_energy[:, v : v + 1], spread)
    level_ref[...] = spread
    emp_level = jnp.zeros((8, LANES), f32)
    for c in range(8):
        emp_level = jnp.where(lane % 8 == c, emp_energy[:, c : c + 1], emp_level)
    to_behind(level_ref, far_level, PLANES).start()
    lax.fori_loop(0, PLANES, send_plane, 0)

    @pl.when(core == 1)
    def _():
        to_sibling(level_ref, near_level, PLANES).start()
        lax.fori_loop(0, PLANES, pass_plane, 0)

    loads = [
        pltpu.make_async_copy(emp_ref, emp, load_sems.at[0]),
        pltpu.make_async_copy(ztab_ref, ztab, load_sems.at[1]),
        pltpu.make_async_copy(xytab_ref.at[pw], xytab, load_sems.at[2]),
    ]
    for load in loads:
        load.start()

    flat = SIDE * wave_ref[1:2, :] + wave_ref[0:1, :]
    index_v[...] = (wave_ref[2:3, :] + KMAX) * WAVE_ROWS + 2 * jnp.abs(flat)
    sign_v[...] = jnp.where(flat < 0, -1.0, 1.0).astype(jnp.float32)
    index_move = pltpu.make_async_copy(index_v, index_s, load_sems.at[3])
    index_move.start()
    for load in loads:
        load.wait()
    index_move.wait()

    def group_pairs(x, group):
        for part in range(3):
            start = group * GROUP_CELLS + part * 384
            cells = slice(start, start + 384)
            emp_re = emp[0, x, :, cells].astype(jnp.float32)
            emp_im = emp[1, x, :, cells].astype(jnp.float32)
            for v in range(8):
                row = v if v < 4 else v + 4
                occ_re = occ_f[row : row + 1, cells]
                occ_im = occ_f[row + 4 : row + 5, cells]
                both = jnp.concatenate(
                    [occ_re * emp_re + occ_im * emp_im, occ_re * emp_im - occ_im * emp_re], axis=0
                )
                rows = slice(group * LANES + v * 16, group * LANES + v * 16 + 16)
                pairs[rows, part * 384 : part * 384 + 384] = both.astype(jnp.bfloat16)

    blank = jnp.zeros((ROWS_X - GY, LANES), jnp.float32)

    def rows_of(first):
        parts = [depth_out[first : first + 8, t * LANES : (t + 1) * LANES] for t in range(GROUPS)]
        return jnp.concatenate(parts + [blank], axis=0)

    def one_plane(x, spot):
        landed(far.at[x], far_sems.at[x])

        @pl.when(core == 0)
        def _():
            to_sibling(far.at[x], near.at[x], x).start()

        landed(near.at[x], near_sems.at[x])
        for part in range(2):
            occ_f[part * 4 : part * 4 + 4, :] = near[x, part].astype(jnp.float32)
            occ_f[part * 4 + 8 : part * 4 + 12, :] = far[x, part].astype(jnp.float32)

        for start in range(0, GROUPS, 2):
            stop = min(start + 2, GROUPS)
            for group in range(start, stop):
                group_pairs(x, group)
            lines = slice(start * LANES, stop * LANES)
            depth_out[:, lines] = lax.dot_general(
                ztab[...], pairs[lines, :], (((1,), (1,)), ((), ())),
                preferred_element_type=jnp.float32,
            )
        rows = pl.ds(pl.multiple_of(spot * ROWS_X, 16), ROWS_X)

        def put(slot, value):
            half = slot % 2
            sections[slot // 2, rows, half * LANES : (half + 1) * LANES] = value.astype(jnp.bfloat16)

        put(KMAX, rows_of(0))
        for q in range(1, KMAX + 1):
            cosine = rows_of(q * 8)
            sine = turned(rows_of((KMAX + q) * 8))
            put(KMAX + q, cosine + sine)
            put(KMAX - q, cosine - sine)

    sections[Q_SLOTS // 2 - 1, :, LANES:] = jnp.zeros((DEPTH, LANES), jnp.bfloat16)
    def clear(k, carry):
        rows = pl.ds(pl.multiple_of(k * WAVE_ROWS, 8), WAVE_ROWS)
        waves[rows, :] = jnp.zeros((WAVE_ROWS, LANES), jnp.float32)
        return carry

    lax.fori_loop(0, Q_SLOTS, clear, 0)

    def stand(step, carry):
        first = pl.multiple_of(step * 128, 128)
        row = sign_v[:, pl.ds(first, 128)]
        sign_rows[pl.ds(first, 128), :] = jnp.broadcast_to(row, (128, LANES)).T
        return carry

    lax.fori_loop(0, NG // 128, stand, 0)
    landed(far_level, far_sems.at[PLANES])

    @pl.when(core == 0)
    def _():
        to_sibling(far_level, near_level, PLANES).start()

    def each_batch(batch, carry):
        def each_plane(spot, carry):
            one_plane(batch * BATCH + spot, spot)
            return carry

        lax.fori_loop(0, BATCH, each_plane, 0)

        def slot_pairs(start, width):
            made = [
                jnp.dot(xytab[batch], sections[start + i], preferred_element_type=jnp.float32)
                for i in range(width)
            ]
            for i, product in enumerate(made):
                first = pl.multiple_of((start + i) * 2 * WAVE_ROWS, 8)
                for half in range(2):
                    rows = pl.ds(first + half * WAVE_ROWS, WAVE_ROWS)
                    waves[rows, :] += product[:, half * LANES : (half + 1) * LANES]

        def four_pairs(k, carry):
            slot_pairs(k * 4, 4)
            return carry

        lax.fori_loop(0, Q_SLOTS // 8, four_pairs, 0)
        slot_pairs(Q_SLOTS // 8 * 4, Q_SLOTS // 2 - Q_SLOTS // 8 * 4)
        return carry

    lax.fori_loop(0, PLANES // BATCH, each_batch, 0)
    landed(near_level, near_sems.at[PLANES])
    occ_level = jnp.where(lane < LANES // 2, near_level[...], far_level[...])
    scale = jnp.sqrt(2.0 / (emp_level - occ_level + omega_shift))[0:1]

    def chunk(yy, xx, half):
        base = (yy * 4 + xx) * 512 + half * 256

        def pick(step, carry):
            first = step * 16
            for i in range(16):
                row = index_s[0, base + first + i]
                picked[pl.ds((first + i) * 2, 2), :] = waves[pl.ds(row, 2), :]
            return carry

        lax.fori_loop(0, 16, pick, 0)
        for part in range(2):
            cosine = picked[pl.ds(part * 256, 128, stride=2), :]
            sine = picked[pl.ds(part * 256 + 1, 128, stride=2), :]
            first = pl.multiple_of(base + part * 128, 128)
            total = (cosine + sign_rows[pl.ds(first, 128), :] * turned(sine)) * scale
            part_ref[yy, xx, half, part * 128 : part * 128 + 128, :] = total.astype(bf16)

    def both_chunks(xx, half):
        def one(yy, carry):
            chunk(yy, xx, half)
            return carry

        lax.fori_loop(0, 2, one, 0)

    sends = []

    def copy(source, target, arrival, device):
        return pltpu.make_async_remote_copy(
            src_ref=source, dst_ref=target, send_sem=send_sems.at[len(sends)], recv_sem=arrival,
            device_id=device, device_id_type=MESH,
        )

    def send(source, target, arrival, device):
        moving = copy(source, target, arrival, device)
        moving.start()
        sends.append(moving)

    out_ref[...] = jnp.zeros_like(out_ref)
    rows = everyone.shape[4] * 2
    half_rows, quarter = rows // 2, rows // 4

    xn, xl, xo = (x + 1) % 4, (x + 3) % 4, (x + 2) % 4

    def pass_on(half, xx, device):
        landed(relay.at[half], sum_sems.at[half])
        share = part_ref[:, xx, half].astype(f32) + relay[half].astype(f32)
        passed[half] = share.astype(bf16)
        send(passed.at[half], arrived.at[2 + half], sum_sems.at[4 + half], device)

    def x_total(yy, half):
        first, second = (2, 1) if half == 0 else (0, 3)
        return (
            part_ref[yy, x, half].astype(f32)
            + arrived[first, yy].astype(f32)
            + arrived[second, yy].astype(f32)
        )

    def cross_over(half):
        for spot in (2, 1) if half == 0 else (0, 3):
            landed(arrived.at[spot], sum_sems.at[2 + spot])
        plane_sum[half] = x_total(1 - y_hi, half).astype(bf16)
        send(plane_sum.at[half], other.at[half], sum_sems.at[6 + half], facing)

    def own_rho(half):
        landed(other.at[half], sum_sems.at[6 + half])
        total = x_total(y_hi, half) + other[half].astype(f32)
        everyone[z, y, core, half] = total.astype(bf16)

    both_chunks(xo, 0)
    send(part_ref.at[:, xo, 0], relay.at[0], sum_sems.at[0], x_next)
    both_chunks(xl, 0)
    send(part_ref.at[:, xl, 0], arrived.at[1], sum_sems.at[3], x_last)
    both_chunks(xn, 0)
    both_chunks(x, 0)
    pass_on(0, xn, x_next)
    both_chunks(xo, 1)
    send(part_ref.at[:, xo, 1], relay.at[1], sum_sems.at[1], x_last)
    both_chunks(xn, 1)
    send(part_ref.at[:, xn, 1], arrived.at[0], sum_sems.at[2], x_next)
    both_chunks(xl, 1)
    cross_over(0)
    both_chunks(x, 1)
    pass_on(1, xl, x_last)

    own_rho(0)
    mine = lambda half: everyone.at[z, y, core, half]
    theirs = lambda half: everyone.at[z, 1 - y, core, half]
    upper = lambda zz: everyone.at[zz, :, core, 0]
    lower = lambda zz, yy: everyone.at[zz, yy, core, 1]
    send(mine(0), mine(0), side_sems.at[0, 0], beside)
    send(mine(0), mine(0), side_sems.at[1, 0], sibling)
    cross_over(1)
    landed(theirs(0), side_sems.at[0, 0])
    send(upper(z), upper(z), ring_sems.at[0, 0, 1], z_next)
    send(upper(z), upper(z), ring_sems.at[0, 1, 1], z_last)
    send(theirs(0), theirs(0), side_sems.at[2, 0], sibling)
    own_rho(1)
    send(lower(z, y), lower(z, y), ring_sems.at[1, 0, 1], z_next)
    send(lower(z, y), lower(z, y), ring_sems.at[1, 1, 1], z_last)
    send(mine(1), mine(1), side_sems.at[0, 1], beside)
    send(mine(1), mine(1), side_sems.at[1, 1], sibling)

    longest = {(0, 0): n_z // 2, (0, 1): n_z // 2 - 1, (1, 0): n_z // 2 - 1, (1, 1): n_z // 2}

    def ring_step(step):
        for half in (0, 1):
            for way in (0, 1):
                if step > longest[half, way]:
                    continue
                origin = (z + n_z - step) % n_z if way == 0 else (z + step) % n_z
                piece = upper(origin) if half == 0 else lower(origin, y)
                landed(piece, ring_sems.at[half, way, step])
                if step < longest[half, way]:
                    send(piece, piece, ring_sems.at[half, way, step + 1], z_next if way == 0 else z_last)
                if half == 1:
                    send(piece, piece, ring_sems.at[2, way, step], beside)
                send(piece, piece, ring_sems.at[3 + half, way, step], sibling)

    def side_step(step):
        for way in (0, 1):
            if step > longest[1, way]:
                continue
            origin = (z + n_z - step) % n_z if way == 0 else (z + step) % n_z
            piece = lower(origin, 1 - y)
            landed(piece, ring_sems.at[2, way, step])
            send(piece, piece, ring_sems.at[5, way, step], sibling)

    def rest_step(step):
        if step == 0:
            for yy, spot in ((y, 1), (1 - y, 2)):
                for half in range(2):
                    landed(everyone.at[z, yy, 1 - core, half], side_sems.at[spot, half])
            return
        for way in (0, 1):
            origin = (z + n_z - step) % n_z if way == 0 else (z + step) % n_z
            if step <= longest[0, way]:
                landed(everyone.at[origin, :, 1 - core, 0], ring_sems.at[3, way, step])
            if step <= longest[1, way]:
                landed(everyone.at[origin, y, 1 - core, 1], ring_sems.at[4, way, step])
                landed(everyone.at[origin, 1 - y, 1 - core, 1], ring_sems.at[5, way, step])

    dx = (x + 4 - z % 4) % 4
    root = z // 4 == y_hi
    first = core * quarter
    eighth = quarter // 2

    def group_origins(step):
        if step == 0:
            return ((z, 0),)
        if step == n_z // 2:
            return (((z + step) % n_z, step),)
        return (((z + n_z - step) % n_z, step), ((z + step) % n_z, n_z - step))

    held = lambda zz, part: left.at[zz, :, :, pl.ds(part * eighth, eighth)]
    late = []

    def left_copies(step):
        made = []
        for zz, tag in group_origins(step):
            base = len(sends)

            def numbered(source, target, arrival, device, offset):
                return pltpu.make_async_remote_copy(
                    src_ref=source, dst_ref=target, send_sem=send_sems.at[base + offset],
                    recv_sem=arrival, device_id=device, device_id_type=MESH,
                )

            there = everyone.at[zz, :, :, 1 - y, pl.ds(first, quarter)]
            to_next = numbered(held(zz, 0), held(zz, 0), left_sems.at[0, tag], x_next, 0)
            to_last = numbered(held(zz, 1), held(zz, 1), left_sems.at[1, tag], x_last, 1)
            to_across = numbered(there, left.at[zz], left_sems.at[2, tag], across, 2)
            made.append((zz, tag, to_next, to_last, to_across))
            sends.extend([None] * 3)
        late.extend(made)
        return made

    def left_from_root(made):
        @pl.when((dx == 0) & root)
        def _():
            for zz, tag, to_next, to_last, to_across in made:
                to_across.start()
                left[zz] = everyone[zz, :, :, y, pl.ds(first, quarter)]
                to_next.start()
                to_last.start()

    def left_onward(made):
        @pl.when((dx == 0) & jnp.logical_not(root))
        def _():
            for zz, tag, to_next, to_last, to_across in made:
                landed(left.at[zz], left_sems.at[2, tag])
                to_next.start()
                to_last.start()

        @pl.when(dx == 1)
        def _():
            for zz, tag, to_next, to_last, to_across in made:
                landed(held(zz, 0), left_sems.at[0, tag])
                to_next.start()

        @pl.when(dx == 3)
        def _():
            for zz, tag, to_next, to_last, to_across in made:
                landed(held(zz, 1), left_sems.at[1, tag])
                to_last.start()

    def left_middle(made):
        @pl.when(dx == 2)
        def _():
            for zz, tag, to_next, to_last, to_across in made:
                landed(held(zz, 0), left_sems.at[0, tag])
                to_next.start()
                landed(held(zz, 1), left_sems.at[1, tag])
                to_last.start()

    parts = [left_copies(step) for step in range(n_z // 2 + 1)]
    ring_step(1)
    landed(theirs(1), side_sems.at[0, 1])
    send(theirs(1), theirs(1), side_sems.at[2, 1], sibling)
    rest_step(0)
    left_from_root(parts[0])
    ring_step(2)
    side_step(1)
    rest_step(1)
    left_from_root(parts[1])
    ring_step(3)
    side_step(2)
    rest_step(2)
    left_from_root(parts[2])
    left_onward(parts[0])
    ring_step(4)
    left_onward(parts[1])
    left_middle(parts[0])
    side_step(3)
    rest_step(3)
    left_from_root(parts[3])
    left_onward(parts[2])
    left_middle(parts[1])
    side_step(4)
    rest_step(4)
    left_from_root(parts[4])
    left_onward(parts[3])
    left_middle(parts[2])
    left_onward(parts[4])
    left_middle(parts[3])
    left_middle(parts[4])

    def group_product(k, carry):
        odd = k % 2
        tag = (odd * ((k + 1) // 2) + (1 - odd) * (n_z - k // 2)) % n_z
        zz = (z + n_z - tag) % n_z

        @pl.when(dx == 1)
        def _():
            landed(held(zz, 1), left_sems.at[1, tag])

        @pl.when(dx == 3)
        def _():
            landed(held(zz, 0), left_sems.at[0, tag])

        straight = [left[zz, i // 2, i % 2].astype(f32) for i in range(4)]
        side = jnp.concatenate([turned(value) for value in straight], axis=1)
        both = jnp.concatenate([-jnp.concatenate(straight, axis=1), side], axis=0)
        both = both.astype(bf16)
        for half in range(2):
            right = jnp.concatenate([everyone[zz, i // 2, i % 2, half] for i in range(4)], axis=1)
            product = lax.dot_general(
                both, right, (((1,), (1,)), ((), ())), preferred_element_type=f32
            )
            for part in range(2):
                spot = (part, slice(None), slice(half * half_rows, (half + 1) * half_rows))
                out_ref[spot] += product[part * quarter : (part + 1) * quarter]
        return carry

    lax.fori_loop(0, n_z, group_product, 0)

    for moving in sends:
        if moving is not None:
            moving.wait_send()
    for zz, tag, to_next, to_last, to_across in late:
        pl.when(dx != 3)(lambda: to_next.wait_send())
        pl.when(dx != 1)(lambda: to_last.wait_send())
        pl.when((dx == 0) & root)(lambda: to_across.wait_send())

    def sent_plane(x, carry):
        to_behind(occ_ref.at[:, x], far.at[x], x).wait_send()
        return carry

    def passed_plane(x, carry):
        to_sibling(occ_ref.at[:, x], near.at[x], x).wait_send()
        return carry

    def passed_far(x, carry):
        to_sibling(far.at[x], near.at[x], x).wait_send()
        return carry

    to_behind(level_ref, far_level, PLANES).wait_send()
    lax.fori_loop(0, PLANES, sent_plane, 0)

    @pl.when(core == 1)
    def _():
        to_sibling(level_ref, near_level, PLANES).wait_send()
        lax.fori_loop(0, PLANES, passed_plane, 0)

    @pl.when(core == 0)
    def _():
        to_sibling(far_level, near_level, PLANES).wait_send()
        lax.fori_loop(0, PLANES, passed_far, 0)


def whole_response(occ, emp, gvectors, energies, ztab, xytabs, n_z):
    bf16, f32 = jnp.bfloat16, jnp.float32
    half = NG // 16
    anywhere, vmem = pl.BlockSpec(memory_space=pl.ANY), pl.BlockSpec(memory_space=pltpu.VMEM)
    return pl.pallas_call(
        response_kernel,
        out_shape=jax.ShapeDtypeStruct((2, half // 2, 2 * half), f32),
        in_specs=[anywhere, anywhere, vmem, vmem, vmem, anywhere, anywhere],
        out_specs=vmem,
        scratch_shapes=[
            pltpu.VMEM((PLANES, 2, 4, CELLS), bf16),
            pltpu.VMEM((PLANES, 2, 4, CELLS), bf16),
            pltpu.VMEM((8, LANES), f32),
            pltpu.VMEM((8, LANES), f32),
            pltpu.VMEM((8, LANES), f32),
            pltpu.VMEM((2, PLANES, 8, CELLS), bf16),
            pltpu.VMEM((Z_ROWS, GROUP_CELLS), bf16),
            pltpu.VMEM((PLANES // BATCH, WAVE_ROWS, DEPTH), bf16),
            pltpu.VMEM((16, CELLS), f32),
            pltpu.VMEM((GROUPS * LANES, GROUP_CELLS), bf16),
            pltpu.VMEM((Z_ROWS, GROUPS * LANES), f32),
            pltpu.VMEM((Q_SLOTS // 2, DEPTH, 2 * LANES), bf16),
            pltpu.VMEM((Q_SLOTS * WAVE_ROWS, LANES), f32),
            pltpu.VMEM((512, LANES), f32),
            pltpu.VMEM((1, NG), jnp.int32),
            pltpu.SMEM((1, NG), jnp.int32),
            pltpu.VMEM((1, NG), f32),
            pltpu.VMEM((NG, LANES), f32),
            pltpu.VMEM((2, 4, 2, half, LANES), bf16),
            pltpu.VMEM((n_z, 2, 2, 2, half, LANES), bf16),
            pltpu.VMEM((n_z, 2, 2, half // 2, LANES), bf16),
            pltpu.VMEM((2, 2, half, LANES), bf16),
            pltpu.VMEM((2, 2, half, LANES), bf16),
            pltpu.VMEM((4, 2, half, LANES), bf16),
            pltpu.VMEM((2, half, LANES), bf16),
            pltpu.VMEM((2, half, LANES), bf16),
            pltpu.SemaphoreType.DMA((PLANES + 1,)),
            pltpu.SemaphoreType.DMA((PLANES + 1,)),
            pltpu.SemaphoreType.DMA((PLANES + 1,)),
            pltpu.SemaphoreType.DMA((PLANES + 1,)),
            pltpu.SemaphoreType.DMA((4,)),
            pltpu.SemaphoreType.DMA((128,)),
            pltpu.SemaphoreType.DMA((8,)),
            pltpu.SemaphoreType.DMA((6, 2, n_z // 2 + 1)),
            pltpu.SemaphoreType.DMA((3, 2)),
            pltpu.SemaphoreType.DMA((3, n_z)),
        ],
        compiler_params=pltpu.CompilerParams(
            collective_id=0, has_side_effects=True, vmem_limit_bytes=60 * 2**20
        ),
        cost_estimate=pl.CostEstimate(
            flops=16_000_000_000, bytes_accessed=12_000_000, transcendentals=0
        ),
    )(occ, emp, gvectors, *energies, ztab, xytabs)


def shards(ztab, xytabs, occupied_states, empty_states, occ_energy, empty_energy, gvectors):
    occ = jnp.transpose(occupied_states, (0, 2, 1, 3))
    emp = jnp.transpose(empty_states, (0, 2, 1, 3))
    energies = occ_energy.reshape(1, -1), empty_energy.reshape(1, -1)
    n_z = lax.axis_size("blk") // 4
    out = whole_response(occ, emp, gvectors, energies, ztab, xytabs, n_z)
    return jnp.transpose(out, (1, 0, 2))


def solution(mesh):
    ztab = z_table()
    xytabs = plane_table(mesh.shape["pw"])
    return jax.shard_map(
        lambda *args: shards(jnp.asarray(ztab), jnp.asarray(xytabs), *args),
        mesh=mesh,
        in_specs=(P(None, "blk", "pw", None), P(None, "blk", "pw", None), P("blk"), P("blk"), P()),
        out_specs=P("blk", None, "pw"),
        check_vma=False,
    )
```

```python
import math

import jax
import jax.numpy as jnp
import numpy as np
from jax import lax
from jax.experimental import pallas as pl
from jax.experimental.pallas import tpu as pltpu
from jax.sharding import PartitionSpec as P
import ml_dtypes

GX = 72
GY = 72
GZ = 144
KMAX = 16
SIDE = 2 * KMAX + 1
PLANES = 9
CELLS = GY * GZ
NG = 4096
GROUPS = 9
GROUP_CELLS = 8 * GZ
Z_ROWS = SIDE * 8
ROWS_X = 80
BATCH = 3
DEPTH = BATCH * ROWS_X
HALF = (SIDE * SIDE + 1) // 2
WAVE_ROWS = 1096
Q_SLOTS = 34
LANES = 128
omega_shift = 0.5


def z_table():
    z = np.arange(GZ)
    out = np.zeros((Z_ROWS, GROUP_CELLS), np.float64)
    for q in range(KMAX + 1):
        angle = 2 * np.pi * ((q * z) % GZ) / GZ
        for y in range(8):
            out[q * 8 + y, y * GZ : (y + 1) * GZ] = np.cos(angle)
            if q:
                out[(KMAX + q) * 8 + y, y * GZ : (y + 1) * GZ] = np.sin(angle)
    return out.astype(np.float32).astype(ml_dtypes.bfloat16)


def plane_table(groups):
    h = np.arange(HALF)
    p = (h + KMAX) // SIDE
    a = h - SIDE * p
    out = np.zeros((groups, WAVE_ROWS, PLANES, ROWS_X), np.float64)
    y = np.arange(GY)
    for group in range(groups):
        for plane in range(PLANES):
            x = group * PLANES + plane
            steps = (p[:, None] * y[None, :] + a[:, None] * x) % GX
            out[group, 0 : 2 * HALF : 2, plane, :GY] = np.cos(2 * np.pi * steps / GX)
            out[group, 1 : 2 * HALF : 2, plane, :GY] = np.sin(2 * np.pi * steps / GX)
    out = out.reshape(groups, WAVE_ROWS, PLANES // BATCH, DEPTH).transpose(0, 2, 1, 3)
    return out.astype(np.float32).astype(ml_dtypes.bfloat16)


def turned(value):
    lane = lax.broadcasted_iota(jnp.int32, value.shape, 1)
    ahead = pltpu.roll(value, LANES - 8, 1)
    behind = pltpu.roll(value, 8, 1)
    return jnp.where((lane & 8) == 0, ahead, -behind)


MESH = pl.DeviceIdType.MESH


def response_kernel(
    occ_ref, emp_ref, wave_ref, occ_energy_ref, emp_energy_ref, ztab_ref, xytab_ref, out_ref,
    near, far, level_ref, near_level, far_level, emp, ztab, xytab, occ_f, pairs, depth_out, sections, waves,
    picked, index_v, index_s, sign_v, sign_rows, part_ref, everyone, left, relay, passed, arrived, plane_sum,
    other, ahead_sems, far_sems, pass_sems, near_sems, load_sems, send_sems, sum_sems, ring_sems,
    side_sems, left_sems,
):
    blk, pw = lax.axis_index("blk"), lax.axis_index("pw")
    count = lax.axis_size("blk")
    n_z = count // 4
    z, y, core = blk // 4, (blk // 2) % 2, blk % 2
    x, y_hi = pw % 4, pw // 4
    f32, bf16 = jnp.float32, jnp.bfloat16

    def place(z=z, y=y, core=core, x=x, y_hi=y_hi):
        return {"blk": z * 4 + y * 2 + core, "pw": y_hi * 4 + x}

    x_next, x_last = place(x=(x + 1) % 4), place(x=(x + 3) % 4)
    z_next, z_last = place(z=(z + 1) % n_z), place(z=(z + n_z - 1) % n_z)
    sibling, beside = place(core=1 - core), place(y=1 - y)
    facing, across = place(y_hi=1 - y_hi), place(y=1 - y, y_hi=1 - y_hi)
    behind = {"blk": (blk + count - 2) % count, "pw": pw}
    ahead = {"blk": (blk + 2) % count, "pw": pw}

    barrier = pltpu.get_barrier_semaphore()
    neighbours = (
        x_next, x_last, z_next, z_last, sibling, beside, facing, across, behind, ahead
    )
    for device in neighbours:
        pl.semaphore_signal(barrier, inc=1, device_id=device, device_id_type=MESH)
    pl.semaphore_wait(barrier, len(neighbours))

    def to_behind(source, target, spot):
        return pltpu.make_async_remote_copy(
            src_ref=source, dst_ref=target, send_sem=ahead_sems.at[spot],
            recv_sem=far_sems.at[spot], device_id=behind, device_id_type=MESH,
        )

    def to_sibling(source, target, spot):
        return pltpu.make_async_remote_copy(
            src_ref=source, dst_ref=target, send_sem=pass_sems.at[spot],
            recv_sem=near_sems.at[spot], device_id=sibling, device_id_type=MESH,
        )

    def landed(target, arrival):
        pltpu.make_async_copy(target, target, arrival).wait()

    def send_plane(x, carry):
        to_behind(occ_ref.at[:, x], far.at[x], x).start()
        return carry

    def pass_plane(x, carry):
        to_sibling(occ_ref.at[:, x], near.at[x], x).start()
        return carry

    lane = lax.broadcasted_iota(jnp.int32, (8, LANES), 1)
    occ_energy = occ_energy_ref[...].astype(f32)
    emp_energy = emp_energy_ref[...].astype(f32)
    spread = jnp.zeros((8, LANES), f32)
    for v in range(4):
        spread = jnp.where((lane // 16) % 4 == v, occ_energy[:, v : v + 1], spread)
    level_ref[...] = spread
    emp_level = jnp.zeros((8, LANES), f32)
    for c in range(8):
        emp_level = jnp.where(lane % 8 == c, emp_energy[:, c : c + 1], emp_level)
    to_behind(level_ref, far_level, PLANES).start()
    lax.fori_loop(0, PLANES, send_plane, 0)

    @pl.when(core == 1)
    def _():
        to_sibling(level_ref, near_level, PLANES).start()
        lax.fori_loop(0, PLANES, pass_plane, 0)

    loads = [
        pltpu.make_async_copy(emp_ref, emp, load_sems.at[0]),
        pltpu.make_async_copy(ztab_ref, ztab, load_sems.at[1]),
        pltpu.make_async_copy(xytab_ref.at[pw], xytab, load_sems.at[2]),
    ]
    for load in loads:
        load.start()

    flat = SIDE * wave_ref[1:2, :] + wave_ref[0:1, :]
    index_v[...] = (wave_ref[2:3, :] + KMAX) * WAVE_ROWS + 2 * jnp.abs(flat)
    sign_v[...] = jnp.where(flat < 0, -1.0, 1.0).astype(jnp.float32)
    index_move = pltpu.make_async_copy(index_v, index_s, load_sems.at[3])
    index_move.start()
    for load in loads:
        load.wait()
    index_move.wait()

    def group_pairs(x, group):
        for part in range(3):
            start = group * GROUP_CELLS + part * 384
            cells = slice(start, start + 384)
            emp_re = emp[0, x, :, cells].astype(jnp.float32)
            emp_im = emp[1, x, :, cells].astype(jnp.float32)
            for v in range(8):
                row = v if v < 4 else v + 4
                occ_re = occ_f[row : row + 1, cells]
                occ_im = occ_f[row + 4 : row + 5, cells]
                both = jnp.concatenate(
                    [occ_re * emp_re + occ_im * emp_im, occ_re * emp_im - occ_im * emp_re], axis=0
                )
                rows = slice(group * LANES + v * 16, group * LANES + v * 16 + 16)
                pairs[rows, part * 384 : part * 384 + 384] = both.astype(jnp.bfloat16)

    blank = jnp.zeros((ROWS_X - GY, LANES), jnp.float32)

    def rows_of(first):
        parts = [depth_out[first : first + 8, t * LANES : (t + 1) * LANES] for t in range(GROUPS)]
        return jnp.concatenate(parts + [blank], axis=0)

    def one_plane(x, spot):
        landed(far.at[x], far_sems.at[x])

        @pl.when(core == 0)
        def _():
            to_sibling(far.at[x], near.at[x], x).start()

        landed(near.at[x], near_sems.at[x])
        for part in range(2):
            occ_f[part * 4 : part * 4 + 4, :] = near[x, part].astype(jnp.float32)
            occ_f[part * 4 + 8 : part * 4 + 12, :] = far[x, part].astype(jnp.float32)

        for start in range(0, GROUPS, 2):
            stop = min(start + 2, GROUPS)
            for group in range(start, stop):
                group_pairs(x, group)
            lines = slice(start * LANES, stop * LANES)
            depth_out[:, lines] = lax.dot_general(
                ztab[...], pairs[lines, :], (((1,), (1,)), ((), ())),
                preferred_element_type=jnp.float32,
            )
        rows = pl.ds(pl.multiple_of(spot * ROWS_X, 16), ROWS_X)

        def put(slot, value):
            half = slot % 2
            sections[slot // 2, rows, half * LANES : (half + 1) * LANES] = value.astype(jnp.bfloat16)

        put(KMAX, rows_of(0))
        for q in range(1, KMAX + 1):
            cosine = rows_of(q * 8)
            sine = turned(rows_of((KMAX + q) * 8))
            put(KMAX + q, cosine + sine)
            put(KMAX - q, cosine - sine)

    sections[Q_SLOTS // 2 - 1, :, LANES:] = jnp.zeros((DEPTH, LANES), jnp.bfloat16)
    def clear(k, carry):
        rows = pl.ds(pl.multiple_of(k * WAVE_ROWS, 8), WAVE_ROWS)
        waves[rows, :] = jnp.zeros((WAVE_ROWS, LANES), jnp.float32)
        return carry

    lax.fori_loop(0, Q_SLOTS, clear, 0)

    def stand(step, carry):
        first = pl.multiple_of(step * 128, 128)
        row = sign_v[:, pl.ds(first, 128)]
        sign_rows[pl.ds(first, 128), :] = jnp.broadcast_to(row, (128, LANES)).T
        return carry

    lax.fori_loop(0, NG // 128, stand, 0)
    landed(far_level, far_sems.at[PLANES])

    @pl.when(core == 0)
    def _():
        to_sibling(far_level, near_level, PLANES).start()

    def each_batch(batch, carry):
        def each_plane(spot, carry):
            one_plane(batch * BATCH + spot, spot)
            return carry

        lax.fori_loop(0, BATCH, each_plane, 0)

        def slot_pairs(start, width):
            made = [
                jnp.dot(xytab[batch], sections[start + i], preferred_element_type=jnp.float32)
                for i in range(width)
            ]
            for i, product in enumerate(made):
                first = pl.multiple_of((start + i) * 2 * WAVE_ROWS, 8)
                for half in range(2):
                    rows = pl.ds(first + half * WAVE_ROWS, WAVE_ROWS)
                    waves[rows, :] += product[:, half * LANES : (half + 1) * LANES]

        def four_pairs(k, carry):
            slot_pairs(k * 4, 4)
            return carry

        lax.fori_loop(0, Q_SLOTS // 8, four_pairs, 0)
        slot_pairs(Q_SLOTS // 8 * 4, Q_SLOTS // 2 - Q_SLOTS // 8 * 4)
        return carry

    lax.fori_loop(0, PLANES // BATCH, each_batch, 0)
    landed(near_level, near_sems.at[PLANES])
    occ_level = jnp.where(lane < LANES // 2, near_level[...], far_level[...])
    scale = jnp.sqrt(2.0 / (emp_level - occ_level + omega_shift))[0:1]

    def chunk(yy, xx, half):
        base = (yy * 4 + xx) * 512 + half * 256

        def two_blocks(step, carry):
            begin = pl.multiple_of(base + step * 128, 128)
            for block in range(2):
                for i in range(block * 64, block * 64 + 64):
                    picked[2 * i : 2 * i + 2, :] = waves[pl.ds(index_s[0, begin + i], 2), :]
            for block in range(2):
                cosine = picked[pl.ds(block * 128, 64, stride=2), :]
                sine = picked[pl.ds(block * 128 + 1, 64, stride=2), :]
                signs = sign_rows[pl.ds(begin + block * 64, 64), :]
                total = (cosine + signs * turned(sine)) * scale
                rows = pl.ds(pl.multiple_of(step * 128 + block * 64, 64), 64)
                part_ref[yy, xx, half, rows, :] = total.astype(bf16)
            return carry

        lax.fori_loop(0, 2, two_blocks, 0)

    def both_chunks(xx, half):
        def one(yy, carry):
            chunk(yy, xx, half)
            return carry

        lax.fori_loop(0, 2, one, 0)

    sends = []

    def copy(source, target, arrival, device):
        return pltpu.make_async_remote_copy(
            src_ref=source, dst_ref=target, send_sem=send_sems.at[len(sends)], recv_sem=arrival,
            device_id=device, device_id_type=MESH,
        )

    def send(source, target, arrival, device):
        moving = copy(source, target, arrival, device)
        moving.start()
        sends.append(moving)

    out_ref[...] = jnp.zeros_like(out_ref)
    rows = everyone.shape[4] * 2
    half_rows, quarter = rows // 2, rows // 4

    xn, xl, xo = (x + 1) % 4, (x + 3) % 4, (x + 2) % 4

    def pass_on(half, xx, device):
        landed(relay.at[half], sum_sems.at[half])
        share = part_ref[:, xx, half].astype(f32) + relay[half].astype(f32)
        passed[half] = share.astype(bf16)
        send(passed.at[half], arrived.at[2 + half], sum_sems.at[4 + half], device)

    def x_total(yy, half):
        first, second = (2, 1) if half == 0 else (0, 3)
        return (
            part_ref[yy, x, half].astype(f32)
            + arrived[first, yy].astype(f32)
            + arrived[second, yy].astype(f32)
        )

    def cross_over(half):
        for spot in (2, 1) if half == 0 else (0, 3):
            landed(arrived.at[spot], sum_sems.at[2 + spot])
        plane_sum[half] = x_total(1 - y_hi, half).astype(bf16)
        send(plane_sum.at[half], other.at[half], sum_sems.at[6 + half], facing)

    def own_rho(half):
        landed(other.at[half], sum_sems.at[6 + half])
        total = x_total(y_hi, half) + other[half].astype(f32)
        everyone[z, y, core, half] = total.astype(bf16)

    both_chunks(xo, 0)
    send(part_ref.at[:, xo, 0], relay.at[0], sum_sems.at[0], x_next)
    both_chunks(xl, 0)
    send(part_ref.at[:, xl, 0], arrived.at[1], sum_sems.at[3], x_last)
    both_chunks(xn, 0)
    both_chunks(x, 0)
    pass_on(0, xn, x_next)
    both_chunks(xo, 1)
    send(part_ref.at[:, xo, 1], relay.at[1], sum_sems.at[1], x_last)
    both_chunks(xn, 1)
    send(part_ref.at[:, xn, 1], arrived.at[0], sum_sems.at[2], x_next)
    both_chunks(xl, 1)
    cross_over(0)
    both_chunks(x, 1)
    pass_on(1, xl, x_last)

    own_rho(0)
    mine = lambda half: everyone.at[z, y, core, half]
    theirs = lambda half: everyone.at[z, 1 - y, core, half]
    upper = lambda zz: everyone.at[zz, :, core, 0]
    lower = lambda zz, yy: everyone.at[zz, yy, core, 1]
    send(mine(0), mine(0), side_sems.at[0, 0], beside)
    send(mine(0), mine(0), side_sems.at[1, 0], sibling)
    cross_over(1)
    landed(theirs(0), side_sems.at[0, 0])
    send(upper(z), upper(z), ring_sems.at[0, 0, 1], z_next)
    send(upper(z), upper(z), ring_sems.at[0, 1, 1], z_last)
    send(theirs(0), theirs(0), side_sems.at[2, 0], sibling)
    own_rho(1)
    send(lower(z, y), lower(z, y), ring_sems.at[1, 0, 1], z_next)
    send(lower(z, y), lower(z, y), ring_sems.at[1, 1, 1], z_last)
    send(mine(1), mine(1), side_sems.at[0, 1], beside)
    send(mine(1), mine(1), side_sems.at[1, 1], sibling)

    longest = {(0, 0): n_z // 2, (0, 1): n_z // 2 - 1, (1, 0): n_z // 2 - 1, (1, 1): n_z // 2}

    def ring_step(step):
        for half in (0, 1):
            for way in (0, 1):
                if step > longest[half, way]:
                    continue
                origin = (z + n_z - step) % n_z if way == 0 else (z + step) % n_z
                piece = upper(origin) if half == 0 else lower(origin, y)
                landed(piece, ring_sems.at[half, way, step])
                if step < longest[half, way]:
                    send(piece, piece, ring_sems.at[half, way, step + 1], z_next if way == 0 else z_last)
                if half == 1:
                    send(piece, piece, ring_sems.at[2, way, step], beside)
                send(piece, piece, ring_sems.at[3 + half, way, step], sibling)

    def side_step(step):
        for way in (0, 1):
            if step > longest[1, way]:
                continue
            origin = (z + n_z - step) % n_z if way == 0 else (z + step) % n_z
            piece = lower(origin, 1 - y)
            landed(piece, ring_sems.at[2, way, step])
            send(piece, piece, ring_sems.at[5, way, step], sibling)

    def rest_step(step):
        if step == 0:
            for yy, spot in ((y, 1), (1 - y, 2)):
                for half in range(2):
                    landed(everyone.at[z, yy, 1 - core, half], side_sems.at[spot, half])
            return
        for way in (0, 1):
            origin = (z + n_z - step) % n_z if way == 0 else (z + step) % n_z
            if step <= longest[0, way]:
                landed(everyone.at[origin, :, 1 - core, 0], ring_sems.at[3, way, step])
            if step <= longest[1, way]:
                landed(everyone.at[origin, y, 1 - core, 1], ring_sems.at[4, way, step])
                landed(everyone.at[origin, 1 - y, 1 - core, 1], ring_sems.at[5, way, step])

    dx = (x + 4 - z % 4) % 4
    root = z // 4 == y_hi
    first = core * quarter
    eighth = quarter // 2

    def group_origins(step):
        if step == 0:
            return ((z, 0),)
        if step == n_z // 2:
            return (((z + step) % n_z, step),)
        return (((z + n_z - step) % n_z, step), ((z + step) % n_z, n_z - step))

    held = lambda zz, part: left.at[zz, :, :, pl.ds(part * eighth, eighth)]
    late = []

    def left_copies(step):
        made = []
        for zz, tag in group_origins(step):
            base = len(sends)

            def numbered(source, target, arrival, device, offset):
                return pltpu.make_async_remote_copy(
                    src_ref=source, dst_ref=target, send_sem=send_sems.at[base + offset],
                    recv_sem=arrival, device_id=device, device_id_type=MESH,
                )

            there = everyone.at[zz, :, :, 1 - y, pl.ds(first, quarter)]
            to_next = numbered(held(zz, 0), held(zz, 0), left_sems.at[0, tag], x_next, 0)
            to_last = numbered(held(zz, 1), held(zz, 1), left_sems.at[1, tag], x_last, 1)
            to_across = numbered(there, left.at[zz], left_sems.at[2, tag], across, 2)
            made.append((zz, tag, to_next, to_last, to_across))
            sends.extend([None] * 3)
        late.extend(made)
        return made

    def left_from_root(made):
        @pl.when((dx == 0) & root)
        def _():
            for zz, tag, to_next, to_last, to_across in made:
                to_across.start()
                left[zz] = everyone[zz, :, :, y, pl.ds(first, quarter)]
                to_next.start()
                to_last.start()

    def left_onward(made):
        @pl.when((dx == 0) & jnp.logical_not(root))
        def _():
            for zz, tag, to_next, to_last, to_across in made:
                landed(left.at[zz], left_sems.at[2, tag])
                to_next.start()
                to_last.start()

        @pl.when(dx == 1)
        def _():
            for zz, tag, to_next, to_last, to_across in made:
                landed(held(zz, 0), left_sems.at[0, tag])
                to_next.start()

        @pl.when(dx == 3)
        def _():
            for zz, tag, to_next, to_last, to_across in made:
                landed(held(zz, 1), left_sems.at[1, tag])
                to_last.start()

    def left_middle(made):
        @pl.when(dx == 2)
        def _():
            for zz, tag, to_next, to_last, to_across in made:
                landed(held(zz, 0), left_sems.at[0, tag])
                to_next.start()
                landed(held(zz, 1), left_sems.at[1, tag])
                to_last.start()

    parts = [left_copies(step) for step in range(n_z // 2 + 1)]
    ring_step(1)
    landed(theirs(1), side_sems.at[0, 1])
    send(theirs(1), theirs(1), side_sems.at[2, 1], sibling)
    rest_step(0)
    left_from_root(parts[0])
    ring_step(2)
    side_step(1)
    rest_step(1)
    left_from_root(parts[1])
    ring_step(3)
    side_step(2)
    rest_step(2)
    left_from_root(parts[2])
    left_onward(parts[0])
    ring_step(4)
    left_onward(parts[1])
    left_middle(parts[0])
    side_step(3)
    rest_step(3)
    left_from_root(parts[3])
    left_onward(parts[2])
    left_middle(parts[1])
    side_step(4)
    rest_step(4)
    left_from_root(parts[4])
    left_onward(parts[3])
    left_middle(parts[2])
    left_onward(parts[4])
    left_middle(parts[3])
    left_middle(parts[4])

    def group_product(k, carry):
        odd = k % 2
        tag = (odd * ((k + 1) // 2) + (1 - odd) * (n_z - k // 2)) % n_z
        zz = (z + n_z - tag) % n_z

        @pl.when(dx == 1)
        def _():
            landed(held(zz, 1), left_sems.at[1, tag])

        @pl.when(dx == 3)
        def _():
            landed(held(zz, 0), left_sems.at[0, tag])

        straight = [left[zz, i // 2, i % 2].astype(f32) for i in range(4)]
        side = jnp.concatenate([turned(value) for value in straight], axis=1)
        both = jnp.concatenate([-jnp.concatenate(straight, axis=1), side], axis=0)
        both = both.astype(bf16)
        for half in range(2):
            right = jnp.concatenate([everyone[zz, i // 2, i % 2, half] for i in range(4)], axis=1)
            product = lax.dot_general(
                both, right, (((1,), (1,)), ((), ())), preferred_element_type=f32
            )
            for part in range(2):
                spot = (part, slice(None), slice(half * half_rows, (half + 1) * half_rows))
                out_ref[spot] += product[part * quarter : (part + 1) * quarter]
        return carry

    lax.fori_loop(0, n_z, group_product, 0)

    for moving in sends:
        if moving is not None:
            moving.wait_send()
    for zz, tag, to_next, to_last, to_across in late:
        pl.when(dx != 3)(lambda: to_next.wait_send())
        pl.when(dx != 1)(lambda: to_last.wait_send())
        pl.when((dx == 0) & root)(lambda: to_across.wait_send())

    def sent_plane(x, carry):
        to_behind(occ_ref.at[:, x], far.at[x], x).wait_send()
        return carry

    def passed_plane(x, carry):
        to_sibling(occ_ref.at[:, x], near.at[x], x).wait_send()
        return carry

    def passed_far(x, carry):
        to_sibling(far.at[x], near.at[x], x).wait_send()
        return carry

    to_behind(level_ref, far_level, PLANES).wait_send()
    lax.fori_loop(0, PLANES, sent_plane, 0)

    @pl.when(core == 1)
    def _():
        to_sibling(level_ref, near_level, PLANES).wait_send()
        lax.fori_loop(0, PLANES, passed_plane, 0)

    @pl.when(core == 0)
    def _():
        to_sibling(far_level, near_level, PLANES).wait_send()
        lax.fori_loop(0, PLANES, passed_far, 0)


def whole_response(occ, emp, gvectors, energies, ztab, xytabs, n_z):
    bf16, f32 = jnp.bfloat16, jnp.float32
    half = NG // 16
    anywhere, vmem = pl.BlockSpec(memory_space=pl.ANY), pl.BlockSpec(memory_space=pltpu.VMEM)
    return pl.pallas_call(
        response_kernel,
        out_shape=jax.ShapeDtypeStruct((2, half // 2, 2 * half), f32),
        in_specs=[anywhere, anywhere, vmem, vmem, vmem, anywhere, anywhere],
        out_specs=vmem,
        scratch_shapes=[
            pltpu.VMEM((PLANES, 2, 4, CELLS), bf16),
            pltpu.VMEM((PLANES, 2, 4, CELLS), bf16),
            pltpu.VMEM((8, LANES), f32),
            pltpu.VMEM((8, LANES), f32),
            pltpu.VMEM((8, LANES), f32),
            pltpu.VMEM((2, PLANES, 8, CELLS), bf16),
            pltpu.VMEM((Z_ROWS, GROUP_CELLS), bf16),
            pltpu.VMEM((PLANES // BATCH, WAVE_ROWS, DEPTH), bf16),
            pltpu.VMEM((16, CELLS), f32),
            pltpu.VMEM((GROUPS * LANES, GROUP_CELLS), bf16),
            pltpu.VMEM((Z_ROWS, GROUPS * LANES), f32),
            pltpu.VMEM((Q_SLOTS // 2, DEPTH, 2 * LANES), bf16),
            pltpu.VMEM((Q_SLOTS * WAVE_ROWS, LANES), f32),
            pltpu.VMEM((256, LANES), f32),
            pltpu.VMEM((1, NG), jnp.int32),
            pltpu.SMEM((1, NG), jnp.int32),
            pltpu.VMEM((1, NG), f32),
            pltpu.VMEM((NG, LANES), f32),
            pltpu.VMEM((2, 4, 2, half, LANES), bf16),
            pltpu.VMEM((n_z, 2, 2, 2, half, LANES), bf16),
            pltpu.VMEM((n_z, 2, 2, half // 2, LANES), bf16),
            pltpu.VMEM((2, 2, half, LANES), bf16),
            pltpu.VMEM((2, 2, half, LANES), bf16),
            pltpu.VMEM((4, 2, half, LANES), bf16),
            pltpu.VMEM((2, half, LANES), bf16),
            pltpu.VMEM((2, half, LANES), bf16),
            pltpu.SemaphoreType.DMA((PLANES + 1,)),
            pltpu.SemaphoreType.DMA((PLANES + 1,)),
            pltpu.SemaphoreType.DMA((PLANES + 1,)),
            pltpu.SemaphoreType.DMA((PLANES + 1,)),
            pltpu.SemaphoreType.DMA((4,)),
            pltpu.SemaphoreType.DMA((128,)),
            pltpu.SemaphoreType.DMA((8,)),
            pltpu.SemaphoreType.DMA((6, 2, n_z // 2 + 1)),
            pltpu.SemaphoreType.DMA((3, 2)),
            pltpu.SemaphoreType.DMA((3, n_z)),
        ],
        compiler_params=pltpu.CompilerParams(
            collective_id=0, has_side_effects=True, vmem_limit_bytes=60 * 2**20
        ),
        cost_estimate=pl.CostEstimate(
            flops=16_000_000_000, bytes_accessed=12_000_000, transcendentals=0
        ),
    )(occ, emp, gvectors, *energies, ztab, xytabs)


def shards(ztab, xytabs, occupied_states, empty_states, occ_energy, empty_energy, gvectors):
    occ = jnp.transpose(occupied_states, (0, 2, 1, 3))
    emp = jnp.transpose(empty_states, (0, 2, 1, 3))
    energies = occ_energy.reshape(1, -1), empty_energy.reshape(1, -1)
    n_z = lax.axis_size("blk") // 4
    out = whole_response(occ, emp, gvectors, energies, ztab, xytabs, n_z)
    return jnp.transpose(out, (1, 0, 2))


def solution(mesh):
    ztab = z_table()
    xytabs = plane_table(mesh.shape["pw"])
    return jax.shard_map(
        lambda *args: shards(jnp.asarray(ztab), jnp.asarray(xytabs), *args),
        mesh=mesh,
        in_specs=(P(None, "blk", "pw", None), P(None, "blk", "pw", None), P("blk"), P("blk"), P()),
        out_specs=P("blk", None, "pw"),
        check_vma=False,
    )
```

```python
import math

import jax
import jax.numpy as jnp
import numpy as np
from jax import lax
from jax.experimental import pallas as pl
from jax.experimental.pallas import tpu as pltpu
from jax.sharding import PartitionSpec as P
import ml_dtypes

GX = 72
GY = 72
GZ = 144
KMAX = 16
SIDE = 2 * KMAX + 1
PLANES = 9
CELLS = GY * GZ
NG = 4096
GROUPS = 9
GROUP_CELLS = 8 * GZ
Z_ROWS = SIDE * 8
ROWS_X = 80
BATCH = 3
DEPTH = BATCH * ROWS_X
HALF = (SIDE * SIDE + 1) // 2
WAVE_ROWS = 1096
Q_SLOTS = 34
LANES = 128
omega_shift = 0.5


def z_table():
    z = np.arange(GZ)
    out = np.zeros((Z_ROWS, GROUP_CELLS), np.float64)
    for q in range(KMAX + 1):
        angle = 2 * np.pi * ((q * z) % GZ) / GZ
        for y in range(8):
            out[q * 8 + y, y * GZ : (y + 1) * GZ] = np.cos(angle)
            if q:
                out[(KMAX + q) * 8 + y, y * GZ : (y + 1) * GZ] = np.sin(angle)
    return out.astype(np.float32).astype(ml_dtypes.bfloat16)


def plane_table(groups):
    h = np.arange(HALF)
    p = (h + KMAX) // SIDE
    a = h - SIDE * p
    out = np.zeros((groups, WAVE_ROWS, PLANES, ROWS_X), np.float64)
    y = np.arange(GY)
    for group in range(groups):
        for plane in range(PLANES):
            x = group * PLANES + plane
            steps = (p[:, None] * y[None, :] + a[:, None] * x) % GX
            out[group, 0 : 2 * HALF : 2, plane, :GY] = np.cos(2 * np.pi * steps / GX)
            out[group, 1 : 2 * HALF : 2, plane, :GY] = np.sin(2 * np.pi * steps / GX)
    out = out.reshape(groups, WAVE_ROWS, PLANES // BATCH, DEPTH).transpose(0, 2, 1, 3)
    return out.astype(np.float32).astype(ml_dtypes.bfloat16)


def turned(value):
    lane = lax.broadcasted_iota(jnp.int32, value.shape, 1)
    ahead = pltpu.roll(value, LANES - 8, 1)
    behind = pltpu.roll(value, 8, 1)
    return jnp.where((lane & 8) == 0, ahead, -behind)


MESH = pl.DeviceIdType.MESH


def response_kernel(
    occ_ref, emp_ref, wave_ref, occ_energy_ref, emp_energy_ref, ztab_ref, xytab_ref, out_ref,
    near, far, level_ref, near_level, far_level, emp, ztab, xytab, occ_f, pairs, depth_out, sections, waves,
    picked, index_v, index_s, sign_v, sign_rows, part_ref, everyone, left, relay, passed, arrived, plane_sum,
    other, ahead_sems, far_sems, pass_sems, near_sems, load_sems, send_sems, sum_sems, ring_sems,
    side_sems, left_sems,
):
    blk, pw = lax.axis_index("blk"), lax.axis_index("pw")
    count = lax.axis_size("blk")
    n_z = count // 4
    z, y, core = blk // 4, (blk // 2) % 2, blk % 2
    x, y_hi = pw % 4, pw // 4
    f32, bf16 = jnp.float32, jnp.bfloat16

    def place(z=z, y=y, core=core, x=x, y_hi=y_hi):
        return {"blk": z * 4 + y * 2 + core, "pw": y_hi * 4 + x}

    x_next, x_last = place(x=(x + 1) % 4), place(x=(x + 3) % 4)
    z_next, z_last = place(z=(z + 1) % n_z), place(z=(z + n_z - 1) % n_z)
    sibling, beside = place(core=1 - core), place(y=1 - y)
    facing, across = place(y_hi=1 - y_hi), place(y=1 - y, y_hi=1 - y_hi)
    behind = {"blk": (blk + count - 2) % count, "pw": pw}
    ahead = {"blk": (blk + 2) % count, "pw": pw}

    barrier = pltpu.get_barrier_semaphore()
    neighbours = (
        x_next, x_last, z_next, z_last, sibling, beside, facing, across, behind, ahead
    )
    for device in neighbours:
        pl.semaphore_signal(barrier, inc=1, device_id=device, device_id_type=MESH)
    pl.semaphore_wait(barrier, len(neighbours))

    def to_behind(source, target, spot):
        return pltpu.make_async_remote_copy(
            src_ref=source, dst_ref=target, send_sem=ahead_sems.at[spot],
            recv_sem=far_sems.at[spot], device_id=behind, device_id_type=MESH,
        )

    def to_sibling(source, target, spot):
        return pltpu.make_async_remote_copy(
            src_ref=source, dst_ref=target, send_sem=pass_sems.at[spot],
            recv_sem=near_sems.at[spot], device_id=sibling, device_id_type=MESH,
        )

    def landed(target, arrival):
        pltpu.make_async_copy(target, target, arrival).wait()

    def send_plane(x, carry):
        to_behind(occ_ref.at[:, x], far.at[x], x).start()
        return carry

    def pass_plane(x, carry):
        to_sibling(occ_ref.at[:, x], near.at[x], x).start()
        return carry

    lane = lax.broadcasted_iota(jnp.int32, (8, LANES), 1)
    occ_energy = occ_energy_ref[...].astype(f32)
    emp_energy = emp_energy_ref[...].astype(f32)
    spread = jnp.zeros((8, LANES), f32)
    for v in range(4):
        spread = jnp.where((lane // 16) % 4 == v, occ_energy[:, v : v + 1], spread)
    level_ref[...] = spread
    emp_level = jnp.zeros((8, LANES), f32)
    for c in range(8):
        emp_level = jnp.where(lane % 8 == c, emp_energy[:, c : c + 1], emp_level)
    to_behind(level_ref, far_level, PLANES).start()
    lax.fori_loop(0, PLANES, send_plane, 0)

    @pl.when(core == 1)
    def _():
        to_sibling(level_ref, near_level, PLANES).start()
        lax.fori_loop(0, PLANES, pass_plane, 0)

    loads = [
        pltpu.make_async_copy(emp_ref, emp, load_sems.at[0]),
        pltpu.make_async_copy(ztab_ref, ztab, load_sems.at[1]),
        pltpu.make_async_copy(xytab_ref.at[pw], xytab, load_sems.at[2]),
    ]
    for load in loads:
        load.start()

    flat = SIDE * wave_ref[1:2, :] + wave_ref[0:1, :]
    index_v[...] = (wave_ref[2:3, :] + KMAX) * WAVE_ROWS + 2 * jnp.abs(flat)
    sign_v[...] = jnp.where(flat < 0, -1.0, 1.0).astype(jnp.float32)
    index_move = pltpu.make_async_copy(index_v, index_s, load_sems.at[3])
    index_move.start()
    for load in loads:
        load.wait()
    index_move.wait()

    def group_pairs(x, group):
        for part in range(3):
            start = group * GROUP_CELLS + part * 384
            cells = slice(start, start + 384)
            emp_re = emp[0, x, :, cells].astype(jnp.float32)
            emp_im = emp[1, x, :, cells].astype(jnp.float32)
            for v in range(8):
                row = v if v < 4 else v + 4
                occ_re = occ_f[row : row + 1, cells]
                occ_im = occ_f[row + 4 : row + 5, cells]
                both = jnp.concatenate(
                    [occ_re * emp_re + occ_im * emp_im, occ_re * emp_im - occ_im * emp_re], axis=0
                )
                rows = slice(group * LANES + v * 16, group * LANES + v * 16 + 16)
                pairs[rows, part * 384 : part * 384 + 384] = both.astype(jnp.bfloat16)

    blank = jnp.zeros((ROWS_X - GY, LANES), jnp.float32)

    def rows_of(first):
        parts = [depth_out[first : first + 8, t * LANES : (t + 1) * LANES] for t in range(GROUPS)]
        return jnp.concatenate(parts + [blank], axis=0)

    def one_plane(x, spot):
        landed(far.at[x], far_sems.at[x])

        @pl.when(core == 0)
        def _():
            to_sibling(far.at[x], near.at[x], x).start()

        landed(near.at[x], near_sems.at[x])
        for part in range(2):
            occ_f[part * 4 : part * 4 + 4, :] = near[x, part].astype(jnp.float32)
            occ_f[part * 4 + 8 : part * 4 + 12, :] = far[x, part].astype(jnp.float32)

        for start in range(0, GROUPS, 2):
            stop = min(start + 2, GROUPS)
            for group in range(start, stop):
                group_pairs(x, group)
            lines = slice(start * LANES, stop * LANES)
            depth_out[:, lines] = lax.dot_general(
                ztab[...], pairs[lines, :], (((1,), (1,)), ((), ())),
                preferred_element_type=jnp.float32,
            )
        rows = pl.ds(pl.multiple_of(spot * ROWS_X, 16), ROWS_X)

        def put(slot, value):
            half = slot % 2
            sections[slot // 2, rows, half * LANES : (half + 1) * LANES] = value.astype(jnp.bfloat16)

        put(KMAX, rows_of(0))
        for q in range(1, KMAX + 1):
            cosine = rows_of(q * 8)
            sine = turned(rows_of((KMAX + q) * 8))
            put(KMAX + q, cosine + sine)
            put(KMAX - q, cosine - sine)

    sections[Q_SLOTS // 2 - 1, :, LANES:] = jnp.zeros((DEPTH, LANES), jnp.bfloat16)
    def clear(k, carry):
        rows = pl.ds(pl.multiple_of(k * WAVE_ROWS, 8), WAVE_ROWS)
        waves[rows, :] = jnp.zeros((WAVE_ROWS, LANES), jnp.float32)
        return carry

    lax.fori_loop(0, Q_SLOTS, clear, 0)

    def stand(step, carry):
        first = pl.multiple_of(step * 128, 128)
        row = sign_v[:, pl.ds(first, 128)]
        sign_rows[pl.ds(first, 128), :] = jnp.broadcast_to(row, (128, LANES)).T
        return carry

    lax.fori_loop(0, NG // 128, stand, 0)
    landed(far_level, far_sems.at[PLANES])

    @pl.when(core == 0)
    def _():
        to_sibling(far_level, near_level, PLANES).start()

    def each_batch(batch, carry):
        def each_plane(spot, carry):
            one_plane(batch * BATCH + spot, spot)
            return carry

        lax.fori_loop(0, BATCH, each_plane, 0)

        def slot_pairs(start, width):
            made = [
                jnp.dot(xytab[batch], sections[start + i], preferred_element_type=jnp.float32)
                for i in range(width)
            ]
            for i, product in enumerate(made):
                first = pl.multiple_of((start + i) * 2 * WAVE_ROWS, 8)
                for half in range(2):
                    rows = pl.ds(first + half * WAVE_ROWS, WAVE_ROWS)
                    waves[rows, :] += product[:, half * LANES : (half + 1) * LANES]

        def four_pairs(k, carry):
            slot_pairs(k * 4, 4)
            return carry

        lax.fori_loop(0, Q_SLOTS // 8, four_pairs, 0)
        slot_pairs(Q_SLOTS // 8 * 4, Q_SLOTS // 2 - Q_SLOTS // 8 * 4)
        return carry

    lax.fori_loop(0, PLANES // BATCH, each_batch, 0)
    landed(near_level, near_sems.at[PLANES])
    occ_level = jnp.where(lane < LANES // 2, near_level[...], far_level[...])
    scale = jnp.sqrt(2.0 / (emp_level - occ_level + omega_shift))[0:1]

    def chunk(yy, xx, half):
        base = (yy * 4 + xx) * 512 + half * 256

        def pick(step, carry):
            first = step * 16
            for i in range(16):
                row = index_s[0, base + first + i]
                picked[pl.ds((first + i) * 2, 2), :] = waves[pl.ds(row, 2), :]
            return carry

        lax.fori_loop(0, 16, pick, 0)
        for part in range(2):
            cosine = picked[pl.ds(part * 256, 128, stride=2), :]
            sine = picked[pl.ds(part * 256 + 1, 128, stride=2), :]
            first = pl.multiple_of(base + part * 128, 128)
            total = (cosine + sign_rows[pl.ds(first, 128), :] * turned(sine)) * scale
            part_ref[yy, xx, half, part * 128 : part * 128 + 128, :] = total.astype(bf16)

    def both_chunks(xx, half):
        def one(yy, carry):
            chunk(yy, xx, half)
            return carry

        lax.fori_loop(0, 2, one, 0)

    sends = []

    def copy(source, target, arrival, device):
        return pltpu.make_async_remote_copy(
            src_ref=source, dst_ref=target, send_sem=send_sems.at[len(sends)], recv_sem=arrival,
            device_id=device, device_id_type=MESH,
        )

    def send(source, target, arrival, device):
        moving = copy(source, target, arrival, device)
        moving.start()
        sends.append(moving)

    out_ref[...] = jnp.zeros_like(out_ref)
    rows = everyone.shape[4] * 2
    half_rows, quarter = rows // 2, rows // 4

    xn, xl, xo = (x + 1) % 4, (x + 3) % 4, (x + 2) % 4

    def pass_on(half, xx, device):
        landed(relay.at[half], sum_sems.at[half])
        share = part_ref[:, xx, half].astype(f32) + relay[half].astype(f32)
        passed[half] = share.astype(bf16)
        send(passed.at[half], arrived.at[2 + half], sum_sems.at[4 + half], device)

    def x_total(yy, half):
        first, second = (2, 1) if half == 0 else (0, 3)
        return (
            part_ref[yy, x, half].astype(f32)
            + arrived[first, yy].astype(f32)
            + arrived[second, yy].astype(f32)
        )

    def cross_over(half):
        for spot in (2, 1) if half == 0 else (0, 3):
            landed(arrived.at[spot], sum_sems.at[2 + spot])
        plane_sum[half] = x_total(1 - y_hi, half).astype(bf16)
        send(plane_sum.at[half], other.at[half], sum_sems.at[6 + half], facing)

    def own_rho(half):
        landed(other.at[half], sum_sems.at[6 + half])
        total = x_total(y_hi, half) + other[half].astype(f32)
        everyone[z, y, core, half] = total.astype(bf16)

    both_chunks(xo, 0)
    send(part_ref.at[:, xo, 0], relay.at[0], sum_sems.at[0], x_next)
    both_chunks(xl, 0)
    send(part_ref.at[:, xl, 0], arrived.at[1], sum_sems.at[3], x_last)
    both_chunks(xn, 0)
    both_chunks(x, 0)
    pass_on(0, xn, x_next)
    both_chunks(xo, 1)
    send(part_ref.at[:, xo, 1], relay.at[1], sum_sems.at[1], x_last)
    both_chunks(xn, 1)
    send(part_ref.at[:, xn, 1], arrived.at[0], sum_sems.at[2], x_next)
    both_chunks(xl, 1)
    cross_over(0)
    both_chunks(x, 1)
    pass_on(1, xl, x_last)

    own_rho(0)
    mine = lambda half: everyone.at[z, y, core, half]
    theirs = lambda half: everyone.at[z, 1 - y, core, half]
    upper = lambda zz: everyone.at[zz, :, core, 0]
    lower = lambda zz, yy: everyone.at[zz, yy, core, 1]
    send(mine(0), mine(0), side_sems.at[0, 0], beside)
    send(mine(0), mine(0), side_sems.at[1, 0], sibling)
    cross_over(1)
    landed(theirs(0), side_sems.at[0, 0])
    send(upper(z), upper(z), ring_sems.at[0, 0, 1], z_next)
    send(upper(z), upper(z), ring_sems.at[0, 1, 1], z_last)
    send(theirs(0), theirs(0), side_sems.at[2, 0], sibling)
    own_rho(1)
    send(lower(z, y), lower(z, y), ring_sems.at[1, 0, 1], z_next)
    send(lower(z, y), lower(z, y), ring_sems.at[1, 1, 1], z_last)
    send(mine(1), mine(1), side_sems.at[0, 1], beside)
    send(mine(1), mine(1), side_sems.at[1, 1], sibling)

    longest = {(0, 0): n_z // 2, (0, 1): n_z // 2 - 1, (1, 0): n_z // 2 - 1, (1, 1): n_z // 2}

    def ring_step(step):
        for half in (0, 1):
            for way in (0, 1):
                if step > longest[half, way]:
                    continue
                origin = (z + n_z - step) % n_z if way == 0 else (z + step) % n_z
                piece = upper(origin) if half == 0 else lower(origin, y)
                landed(piece, ring_sems.at[half, way, step])
                if step < longest[half, way]:
                    send(piece, piece, ring_sems.at[half, way, step + 1], z_next if way == 0 else z_last)
                if half == 1:
                    send(piece, piece, ring_sems.at[2, way, step], beside)
                send(piece, piece, ring_sems.at[3 + half, way, step], sibling)

    def side_step(step):
        for way in (0, 1):
            if step > longest[1, way]:
                continue
            origin = (z + n_z - step) % n_z if way == 0 else (z + step) % n_z
            piece = lower(origin, 1 - y)
            landed(piece, ring_sems.at[2, way, step])
            send(piece, piece, ring_sems.at[5, way, step], sibling)

    def rest_step(step):
        if step == 0:
            for yy, spot in ((y, 1), (1 - y, 2)):
                for half in range(2):
                    landed(everyone.at[z, yy, 1 - core, half], side_sems.at[spot, half])
            return
        for way in (0, 1):
            origin = (z + n_z - step) % n_z if way == 0 else (z + step) % n_z
            if step <= longest[0, way]:
                landed(everyone.at[origin, :, 1 - core, 0], ring_sems.at[3, way, step])
            if step <= longest[1, way]:
                landed(everyone.at[origin, y, 1 - core, 1], ring_sems.at[4, way, step])
                landed(everyone.at[origin, 1 - y, 1 - core, 1], ring_sems.at[5, way, step])

    dx = (x + 4 - z % 4) % 4
    root = z // 4 == y_hi
    first = core * quarter
    eighth = quarter // 2

    def group_origins(step):
        if step == 0:
            return ((z, 0),)
        if step == n_z // 2:
            return (((z + step) % n_z, step),)
        return (((z + n_z - step) % n_z, step), ((z + step) % n_z, n_z - step))

    held = lambda zz, part: left.at[zz, :, :, pl.ds(part * eighth, eighth)]
    late = []

    def left_copies(step):
        made = []
        for zz, tag in group_origins(step):
            base = len(sends)

            def numbered(source, target, arrival, device, offset):
                return pltpu.make_async_remote_copy(
                    src_ref=source, dst_ref=target, send_sem=send_sems.at[base + offset],
                    recv_sem=arrival, device_id=device, device_id_type=MESH,
                )

            there = lambda part: everyone.at[
                zz, :, :, 1 - y, pl.ds(first + part * eighth, eighth)
            ]
            to_next = numbered(held(zz, 0), held(zz, 0), left_sems.at[0, tag], x_next, 0)
            to_last = numbered(held(zz, 1), held(zz, 1), left_sems.at[1, tag], x_last, 1)
            to_across = [
                numbered(there(part), held(zz, part), left_sems.at[2 + part, tag], across, 2 + part)
                for part in range(2)
            ]
            also_next = numbered(held(zz, 1), held(zz, 1), left_sems.at[1, tag], x_next, 4)
            also_last = numbered(held(zz, 0), held(zz, 0), left_sems.at[0, tag], x_last, 5)
            made.append((zz, tag, to_next, to_last, to_across, also_next, also_last))
            sends.extend([None] * 6)
        late.extend(made)
        return made

    def left_from_root(made):
        @pl.when((dx == 0) & root)
        def _():
            for zz, tag, to_next, to_last, to_across, also_next, also_last in made:
                to_across[0].start()
                to_across[1].start()
                left[zz] = everyone[zz, :, :, y, pl.ds(first, quarter)]
                to_next.start()
                to_last.start()

    def left_onward(made):
        @pl.when((dx == 0) & jnp.logical_not(root))
        def _():
            for zz, tag, to_next, to_last, to_across, also_next, also_last in made:
                landed(held(zz, 0), left_sems.at[2, tag])
                to_next.start()
                also_last.start()
                landed(held(zz, 1), left_sems.at[3, tag])
                to_last.start()
                also_next.start()

        @pl.when(dx == 1)
        def _():
            for zz, tag, to_next, to_last, to_across, also_next, also_last in made:
                landed(held(zz, 0), left_sems.at[0, tag])
                to_next.start()

        @pl.when(dx == 3)
        def _():
            for zz, tag, to_next, to_last, to_across, also_next, also_last in made:
                landed(held(zz, 1), left_sems.at[1, tag])
                to_last.start()

    def left_middle(made):
        @pl.when((dx == 2) & root)
        def _():
            for zz, tag, to_next, to_last, to_across, also_next, also_last in made:
                landed(held(zz, 0), left_sems.at[0, tag])
                to_next.start()
                landed(held(zz, 1), left_sems.at[1, tag])
                to_last.start()

    parts = [left_copies(step) for step in range(n_z // 2 + 1)]
    ring_step(1)
    landed(theirs(1), side_sems.at[0, 1])
    send(theirs(1), theirs(1), side_sems.at[2, 1], sibling)
    rest_step(0)
    left_from_root(parts[0])
    ring_step(2)
    side_step(1)
    rest_step(1)
    left_from_root(parts[1])
    ring_step(3)
    side_step(2)
    rest_step(2)
    left_from_root(parts[2])
    left_onward(parts[0])
    ring_step(4)
    left_onward(parts[1])
    left_middle(parts[0])
    side_step(3)
    rest_step(3)
    left_from_root(parts[3])
    left_onward(parts[2])
    left_middle(parts[1])
    side_step(4)
    rest_step(4)
    left_from_root(parts[4])
    left_onward(parts[3])
    left_middle(parts[2])
    left_onward(parts[4])
    left_middle(parts[3])
    left_middle(parts[4])

    def group_product(k, carry):
        odd = k % 2
        tag = (odd * ((k + 1) // 2) + (1 - odd) * (n_z - k // 2)) % n_z
        zz = (z + n_z - tag) % n_z

        @pl.when(dx == 1)
        def _():
            landed(held(zz, 1), left_sems.at[1, tag])

        @pl.when(dx == 3)
        def _():
            landed(held(zz, 0), left_sems.at[0, tag])

        @pl.when((dx == 2) & jnp.logical_not(root))
        def _():
            landed(held(zz, 0), left_sems.at[0, tag])
            landed(held(zz, 1), left_sems.at[1, tag])

        straight = [left[zz, i // 2, i % 2].astype(f32) for i in range(4)]
        side = jnp.concatenate([turned(value) for value in straight], axis=1)
        both = jnp.concatenate([-jnp.concatenate(straight, axis=1), side], axis=0)
        both = both.astype(bf16)
        for half in range(2):
            right = jnp.concatenate([everyone[zz, i // 2, i % 2, half] for i in range(4)], axis=1)
            product = lax.dot_general(
                both, right, (((1,), (1,)), ((), ())), preferred_element_type=f32
            )
            for part in range(2):
                spot = (part, slice(None), slice(half * half_rows, (half + 1) * half_rows))
                out_ref[spot] += product[part * quarter : (part + 1) * quarter]
        return carry

    lax.fori_loop(0, n_z, group_product, 0)

    for moving in sends:
        if moving is not None:
            moving.wait_send()
    far_row = jnp.logical_not(root)
    from_next = (dx < 2) | ((dx == 2) & root)
    from_last = (dx == 0) | (dx == 3) | ((dx == 2) & root)
    for zz, tag, to_next, to_last, to_across, also_next, also_last in late:
        pl.when(from_next)(lambda: to_next.wait_send())
        pl.when(from_last)(lambda: to_last.wait_send())
        for part in range(2):
            pl.when((dx == 0) & root)(lambda: to_across[part].wait_send())
        pl.when((dx == 0) & far_row)(lambda: also_next.wait_send())
        pl.when((dx == 0) & far_row)(lambda: also_last.wait_send())

    def sent_plane(x, carry):
        to_behind(occ_ref.at[:, x], far.at[x], x).wait_send()
        return carry

    def passed_plane(x, carry):
        to_sibling(occ_ref.at[:, x], near.at[x], x).wait_send()
        return carry

    def passed_far(x, carry):
        to_sibling(far.at[x], near.at[x], x).wait_send()
        return carry

    to_behind(level_ref, far_level, PLANES).wait_send()
    lax.fori_loop(0, PLANES, sent_plane, 0)

    @pl.when(core == 1)
    def _():
        to_sibling(level_ref, near_level, PLANES).wait_send()
        lax.fori_loop(0, PLANES, passed_plane, 0)

    @pl.when(core == 0)
    def _():
        to_sibling(far_level, near_level, PLANES).wait_send()
        lax.fori_loop(0, PLANES, passed_far, 0)


def whole_response(occ, emp, gvectors, energies, ztab, xytabs, n_z):
    bf16, f32 = jnp.bfloat16, jnp.float32
    half = NG // 16
    anywhere, vmem = pl.BlockSpec(memory_space=pl.ANY), pl.BlockSpec(memory_space=pltpu.VMEM)
    return pl.pallas_call(
        response_kernel,
        out_shape=jax.ShapeDtypeStruct((2, half // 2, 2 * half), f32),
        in_specs=[anywhere, anywhere, vmem, vmem, vmem, anywhere, anywhere],
        out_specs=vmem,
        scratch_shapes=[
            pltpu.VMEM((PLANES, 2, 4, CELLS), bf16),
            pltpu.VMEM((PLANES, 2, 4, CELLS), bf16),
            pltpu.VMEM((8, LANES), f32),
            pltpu.VMEM((8, LANES), f32),
            pltpu.VMEM((8, LANES), f32),
            pltpu.VMEM((2, PLANES, 8, CELLS), bf16),
            pltpu.VMEM((Z_ROWS, GROUP_CELLS), bf16),
            pltpu.VMEM((PLANES // BATCH, WAVE_ROWS, DEPTH), bf16),
            pltpu.VMEM((16, CELLS), f32),
            pltpu.VMEM((GROUPS * LANES, GROUP_CELLS), bf16),
            pltpu.VMEM((Z_ROWS, GROUPS * LANES), f32),
            pltpu.VMEM((Q_SLOTS // 2, DEPTH, 2 * LANES), bf16),
            pltpu.VMEM((Q_SLOTS * WAVE_ROWS, LANES), f32),
            pltpu.VMEM((512, LANES), f32),
            pltpu.VMEM((1, NG), jnp.int32),
            pltpu.SMEM((1, NG), jnp.int32),
            pltpu.VMEM((1, NG), f32),
            pltpu.VMEM((NG, LANES), f32),
            pltpu.VMEM((2, 4, 2, half, LANES), bf16),
            pltpu.VMEM((n_z, 2, 2, 2, half, LANES), bf16),
            pltpu.VMEM((n_z, 2, 2, half // 2, LANES), bf16),
            pltpu.VMEM((2, 2, half, LANES), bf16),
            pltpu.VMEM((2, 2, half, LANES), bf16),
            pltpu.VMEM((4, 2, half, LANES), bf16),
            pltpu.VMEM((2, half, LANES), bf16),
            pltpu.VMEM((2, half, LANES), bf16),
            pltpu.SemaphoreType.DMA((PLANES + 1,)),
            pltpu.SemaphoreType.DMA((PLANES + 1,)),
            pltpu.SemaphoreType.DMA((PLANES + 1,)),
            pltpu.SemaphoreType.DMA((PLANES + 1,)),
            pltpu.SemaphoreType.DMA((4,)),
            pltpu.SemaphoreType.DMA((160,)),
            pltpu.SemaphoreType.DMA((8,)),
            pltpu.SemaphoreType.DMA((6, 2, n_z // 2 + 1)),
            pltpu.SemaphoreType.DMA((3, 2)),
            pltpu.SemaphoreType.DMA((4, n_z)),
        ],
        compiler_params=pltpu.CompilerParams(
            collective_id=0, has_side_effects=True, vmem_limit_bytes=60 * 2**20
        ),
        cost_estimate=pl.CostEstimate(
            flops=16_000_000_000, bytes_accessed=12_000_000, transcendentals=0
        ),
    )(occ, emp, gvectors, *energies, ztab, xytabs)


def shards(ztab, xytabs, occupied_states, empty_states, occ_energy, empty_energy, gvectors):
    occ = jnp.transpose(occupied_states, (0, 2, 1, 3))
    emp = jnp.transpose(empty_states, (0, 2, 1, 3))
    energies = occ_energy.reshape(1, -1), empty_energy.reshape(1, -1)
    n_z = lax.axis_size("blk") // 4
    out = whole_response(occ, emp, gvectors, energies, ztab, xytabs, n_z)
    return jnp.transpose(out, (1, 0, 2))


def solution(mesh):
    ztab = z_table()
    xytabs = plane_table(mesh.shape["pw"])
    return jax.shard_map(
        lambda *args: shards(jnp.asarray(ztab), jnp.asarray(xytabs), *args),
        mesh=mesh,
        in_specs=(P(None, "blk", "pw", None), P(None, "blk", "pw", None), P("blk"), P("blk"), P()),
        out_specs=P("blk", None, "pw"),
        check_vma=False,
    )
```
